32 devices in a mesh: section: 2 (over core), blk: 16 (over z, y, x).
Axes of the slice: x: 2, y: 2, z: 4, core: 2. Of those that a mesh axis runs over, the one named last changes fastest.
Arguments:
- hidden: bfloat16 [2, 48, 3072], P(None, 'blk'), may hold values from -4 to 4
- qkv_weight: bfloat16 [2, 3072, 9216], P('section', None, 'blk'), may hold values from -0.109375 to 0.109375
- out_weight: bfloat16 [2, 3072, 3072], P('section', None, 'blk'), may hold values from -0.109375 to 0.109375
- modulation: float32 [2, 50, 3, 3072], P('section'), may hold values from -3 to 3
- timestep: int32 [1], replicated, may hold values from 0 to 49
- fresh: int32 [2, 2, 16], P('section'), may hold values 0 or 1
- live: int32 [2, 16], replicated, may hold values from 0 to 1, as said below
- k_stale: bfloat16 [2, 2, 48, 3072], P('section', None, 'blk'), may hold values from -6 to 6
- v_stale: bfloat16 [2, 2, 48, 3072], P('section', None, 'blk'), may hold values from -16 to 16
Outputs:
- layer_outputs: bfloat16 [2, 2, 48, 3072], P('section', None, 'blk')
The draws below stay inside these ranges and needn't reach their ends.
Inputs may be any that keep to these rules, and one draw needn't show every extreme that they name: Block 0 of every request is live.
All inputs are finite; a program needn't handle non-finite values. No bound on the sum of `fresh` on one device may be relied on, other than what follows from the above.
Results may differ from the reference program's by a relative error of at most 0.017.
Values may be sent and summed in bfloat16 or wider, within the bound.
No kernel may reach another device: no remote copies, remote signals or barrier semaphores. Data moves between devices by JAX's collectives and lax.ppermute only.
A program may use at most 64 MiB of HBM per device.

```python
import jax
import jax.numpy as jnp
from jax import lax

D = 3072
HEADS = 48
HEAD = 64
ROWS = 3
REQS = 2
TSTEPS = 50
NBLOCKS = 16
SEQ = 48


def draw_live(key, part):
    levels = jax.random.randint(key, (REQS, NBLOCKS), 0, 4)
    filled = (levels > 0).astype(jnp.int32)
    leading = (jnp.arange(NBLOCKS) == 0)[None, :]
    return jnp.where(leading, 1, filled).astype(jnp.int32)


def set_ends(entries, own_key, least, largest):
    spot = [jax.random.randint(jax.random.fold_in(own_key, axis), (), 0, length) for axis, length in enumerate(entries.shape)]
    widest = entries.shape.index(max(entries.shape))
    next_to = spot[:widest] + [(spot[widest] + 1) % entries.shape[widest]] + spot[widest + 1:]
    return entries.at[tuple(spot)].set(least).at[tuple(next_to)].set(largest)


def block_levels(key, extent, cuts, smallest, largest):
    factor_of = 1.0
    for position, shards_of in cuts:
        draws = jax.random.uniform(jax.random.fold_in(jax.random.fold_in(key, 6), position), (shards_of,), jnp.float32, smallest / len(cuts), largest / len(cuts))
        factor_of = factor_of * jnp.repeat(jnp.exp(draws), extent[position] // shards_of).reshape((-1,) + (1,) * (len(extent) - 1 - position))
    return factor_of


def scatter_about(rng, shape, scale, most, split=(), kind=jnp.bfloat16):
    level = block_levels(rng, shape, split, -0.22, 0.18) if split else 1.0
    values = jax.random.normal(rng, shape, jnp.float32) * scale * level
    return jnp.minimum(jnp.maximum(values, -most), most).astype(kind)


def setup_inputs(seed: int = 0) -> dict:
    seeds = jax.random.split(jax.random.key(seed), 10)
    return {
        "hidden": scatter_about(seeds[0], (REQS, SEQ, D), 0.3, 4.0, ((1, 16),)),
        "qkv_weight": scatter_about(seeds[1], (2, D, 3 * D), D ** -0.5, 0.109375, ((0, 2), (2, 16))),
        "out_weight": scatter_about(seeds[2], (2, D, D), D ** -0.5, 0.109375, ((0, 2), (2, 16))),
        "modulation": scatter_about(seeds[3], (2, TSTEPS, 3, D), 0.8, 3.0, ((0, 2),), jnp.float32),
        "timestep": jax.random.randint(seeds[4], (1,), 0, TSTEPS).astype(jnp.int32),
        "fresh": set_ends((jax.random.randint(seeds[5], (2, REQS, NBLOCKS), 0, 2) < 1).astype(jnp.int32), jax.random.fold_in(seeds[5], 1), 0, 1),
        "live": draw_live(jax.random.fold_in(seeds[9], 71), 0),
        "k_stale": scatter_about(seeds[7], (2, REQS, SEQ, D), 1.0, 6.0, ((0, 2), (2, 16))),
        "v_stale": scatter_about(seeds[8], (2, REQS, SEQ, D), 3.0, 16.0, ((0, 2), (2, 16))),
    }


def one_layer(stream_in, qkv_w, out_w, modulate, fresh_rows, old_keys, old_values, live):
    stream = stream_in.astype(jnp.float32)
    center = lax.optimization_barrier(jnp.mean(stream, axis=-1, keepdims=True))
    variance = lax.optimization_barrier(jnp.mean((stream - center) ** 2, axis=-1, keepdims=True))
    normed = (stream - center) / jnp.sqrt(variance + 1e-06) * (1.0 + modulate[0]) + modulate[1]
    normed_b = normed.astype(jnp.bfloat16)
    projected = jnp.dot(normed_b.reshape(REQS * SEQ, D), qkv_w, preferred_element_type=jnp.float32)
    projected = projected.astype(jnp.bfloat16).reshape(REQS, SEQ, 3 * D)
    queries = projected[:, :, :D]
    new_keys = projected[:, :, D:2 * D]
    new_values = projected[:, :, 2 * D:]
    use_fresh = jnp.repeat(fresh_rows, ROWS, axis=1)[:, :, None] == 1
    keys = jnp.where(use_fresh, new_keys, old_keys)
    values = jnp.where(use_fresh, new_values, old_values)
    usable = (jnp.repeat(live, ROWS, axis=1) == 1)[:, None, :]

    def split_heads(array):
        return jnp.transpose(array.reshape(REQS, SEQ, HEADS, HEAD), (2, 0, 1, 3))

    def per_head(triple):
        q_head, k_head, v_head = triple
        scores = jnp.einsum('rid,rjd->rij', q_head.astype(jnp.float32), k_head.astype(jnp.float32), precision=lax.Precision.HIGHEST) * 0.125
        scores = jnp.where(usable, scores, -1e+30)
        top_score = lax.optimization_barrier(jnp.max(scores, axis=-1, keepdims=True))
        weights = jnp.where(usable, jnp.exp(scores - top_score), 0.0)
        total = lax.optimization_barrier(jnp.sum(weights, axis=-1, keepdims=True))
        mixed = jnp.einsum('rij,rjd->rid', weights, v_head.astype(jnp.float32), precision=lax.Precision.HIGHEST)
        return mixed / total
    attn = lax.map(per_head, (split_heads(queries), split_heads(keys), split_heads(values)))
    attn = jnp.transpose(attn, (1, 2, 0, 3)).reshape(REQS, SEQ, D).astype(jnp.bfloat16)
    mixed_out = jnp.dot(attn.reshape(REQS * SEQ, D), out_w, preferred_element_type=jnp.float32)
    mixed_out = mixed_out.astype(jnp.bfloat16).reshape(REQS, SEQ, D)
    return (stream + modulate[2] * mixed_out.astype(jnp.float32)).astype(jnp.bfloat16)

def reference(hidden, qkv_weight, out_weight, modulation, timestep, fresh, live, k_stale, v_stale):
    step_idx = timestep[0]
    first_out = one_layer(hidden, qkv_weight[0], out_weight[0], modulation[0, step_idx], fresh[0], k_stale[0], v_stale[0], live)
    second_out = one_layer(first_out, qkv_weight[1], out_weight[1], modulation[1, step_idx], fresh[1], k_stale[1], v_stale[1], live)
    return jnp.stack([first_out, second_out])
```

```python
import functools

import jax
import jax.numpy as jnp
from jax import lax
from jax.experimental import pallas as pl
from jax.experimental.pallas import tpu as pltpu
from jax.sharding import PartitionSpec as P


def from_behind(shard, axis, by):
    count = lax.axis_size(axis)
    pairs = [(i, i + by) for i in range(count) if 0 <= i + by < count]
    return lax.ppermute(shard, axis, pairs)


def attend(layer_in, qkv_cols, out_cols, modulate, fresh_own, old_keys, old_values, live):
    stream = layer_in.astype(jnp.float32)
    center = jnp.mean(stream, axis=-1, keepdims=True)
    variance = jnp.mean((stream - center) ** 2, axis=-1, keepdims=True)
    normed = (stream - center) / jnp.sqrt(variance + 1e-06) * (1.0 + modulate[0]) + modulate[1]
    normed_b = normed.astype(jnp.bfloat16)
    columns = jnp.einsum(
        "rnd,dc->rnc",
        lax.all_gather(normed_b, "blk", axis=1, tiled=True),
        qkv_cols,
        preferred_element_type=jnp.float32,
    ).astype(jnp.bfloat16)
    projected = lax.all_to_all(columns, "blk", split_axis=1, concat_axis=2, tiled=True)
    num_req, num_rows, width = layer_in.shape
    queries = projected[:, :, :width]
    new_keys = projected[:, :, width : 2 * width]
    new_values = projected[:, :, 2 * width :]
    use_fresh = (fresh_own == 1)[:, None, None]
    keys = jnp.where(use_fresh, new_keys, old_keys)
    values = jnp.where(use_fresh, new_values, old_values)
    num_heads = width // 64
    num_blocks = live.shape[1]
    q_heads = queries.reshape(num_req, num_rows, num_heads, 64)
    live_float = live.astype(jnp.float32)
    run_max = jnp.full((num_req, num_heads, num_rows), -1e30, jnp.float32)
    key_piece = lax.all_gather(keys, "blk", axis=1, tiled=True)
    value_piece = lax.all_gather(values, "blk", axis=1, tiled=True)
    piece_rows = key_piece.shape[1]
    key_heads = key_piece.reshape(num_req, piece_rows, num_heads, 64)
    value_heads = value_piece.reshape(num_req, piece_rows, num_heads, 64)
    scores = (
        jnp.einsum("qrhd,qnhd->qhrn", q_heads, key_heads, preferred_element_type=jnp.float32)
        * 0.125
    )
    block_ids = jnp.arange(piece_rows) // num_rows
    one_hot = (block_ids[:, None] == jnp.arange(num_blocks)[None, :]).astype(jnp.float32)
    usable = jnp.einsum("qb,nb->qn", live_float, one_hot) > 0.5
    usable = usable[:, None, None, :]
    scores = jnp.where(usable, scores, -1e30)
    new_max = jnp.maximum(run_max, jnp.max(scores, axis=-1))
    weights = jnp.where(usable, jnp.exp(scores - new_max[..., None]), 0.0)
    new_sum = jnp.sum(weights, axis=-1)
    new_acc = jnp.einsum(
        "qhrn,qnhd->qhrd", weights, value_heads.astype(jnp.float32), precision=lax.Precision.HIGHEST
    )
    attn = new_acc / new_sum[..., None]
    attn = jnp.transpose(attn, (0, 2, 1, 3)).reshape(num_req, num_rows, width).astype(jnp.bfloat16)
    out_part = jnp.einsum(
        "rnd,dc->rnc",
        lax.all_gather(attn, "blk", axis=1, tiled=True),
        out_cols,
        preferred_element_type=jnp.float32,
    ).astype(jnp.bfloat16)
    mixed_back = lax.all_to_all(out_part, "blk", split_axis=1, concat_axis=2, tiled=True)
    return (stream + modulate[2] * mixed_back.astype(jnp.float32)).astype(jnp.bfloat16)


def pick_request(array, req_idx):
    return lax.dynamic_index_in_dim(array, req_idx, 0, keepdims=True)


def per_device_by_token(hidden, qkv_weight, out_weight, modulation, timestep, fresh, live, k_stale, v_stale):
    section_idx = lax.axis_index("section")
    block_idx = lax.axis_index("blk")
    steps_all = modulation.shape[1]
    pick_row = (jnp.arange(steps_all) == timestep[0]).astype(jnp.float32)
    modulate = jnp.einsum("t,tcd->cd", pick_row, modulation[0], precision=lax.Precision.HIGHEST)
    num_blocks = fresh.shape[2]
    own_column = (jnp.arange(num_blocks) == block_idx).astype(jnp.int32)
    fresh_own = jnp.sum(fresh[0] * own_column[None, :], axis=1)
    qkv_cols = qkv_weight[0]
    out_cols = out_weight[0]
    old_keys = k_stale[0]
    old_values = v_stale[0]
    num_req = hidden.shape[0]
    received = jnp.zeros_like(hidden[0:1])
    first_out = []
    second_out = []
    for tick_idx in range(num_req + 1):
        if tick_idx < num_req:
            own_input = hidden[tick_idx : tick_idx + 1]
        else:
            own_input = jnp.zeros_like(hidden[0:1])
        layer_in = jnp.where(section_idx == 0, own_input, received)
        req_idx = jnp.clip(tick_idx - section_idx, 0, num_req - 1)
        layer_out = attend(
            layer_in,
            qkv_cols,
            out_cols,
            modulate,
            pick_request(fresh_own, req_idx),
            pick_request(old_keys, req_idx),
            pick_request(old_values, req_idx),
            pick_request(live, req_idx),
        )
        if tick_idx < num_req:
            first_out.append(layer_out)
            received = from_behind(layer_out, "section", 1)
        if tick_idx >= 1:
            second_out.append(layer_out)
    result = jnp.where(
        section_idx == 0, jnp.concatenate(first_out, axis=0), jnp.concatenate(second_out, axis=0)
    )
    return result[None]


HEAD = 64
BF16 = jnp.bfloat16
F32 = jnp.float32
NT = (((1,), (1,)), ((), ()))
VMEM = pl.BlockSpec(memory_space=pltpu.VMEM)


def call(body, outs, scratch, cost, *args):
    flops, moved = cost
    return pl.pallas_call(
        body,
        out_shape=outs,
        in_specs=[VMEM] * len(args),
        out_specs=jax.tree.map(lambda _: VMEM, outs),
        scratch_shapes=scratch,
        compiler_params=pltpu.CompilerParams(vmem_limit_bytes=24 << 20),
        cost_estimate=pl.CostEstimate(flops=flops, bytes_accessed=moved, transcendentals=0),
    )(*args)


def dot_nt(left, right):
    return lax.dot_general(left, right, NT, preferred_element_type=F32)


def halves(columns):
    mid = columns.shape[0] // 2
    return jnp.concatenate([columns[:mid], columns[mid:]], axis=1)


def pack(cols):
    return jnp.concatenate([cols[:, :128], halves(cols[:, 128:])], axis=0)


def unpack(packed):
    tokens = packed.shape[0] // 3 * 2
    last = packed[tokens:]
    return jnp.concatenate(
        [packed[:tokens], jnp.concatenate([last[:, :HEAD], last[:, HEAD:]], axis=0)], axis=1
    )


def pack_by_parity(cols, odd):
    mid = cols.shape[0] // 2
    even_form = pack(cols)
    odd_form = jnp.concatenate(
        [
            cols[:, HEAD:],
            jnp.concatenate([cols[mid:, :HEAD], cols[:mid, :HEAD]], axis=1),
        ],
        axis=0,
    )
    return jnp.where(odd, odd_form, even_form)


def assemble(blocks, me, whole):
    odd = (me & 1) == 1
    tokens = whole.shape[0]
    for s in range(0, len(blocks), 2):
        mine, other = blocks[s][...].astype(F32), blocks[s + 1][...].astype(F32)
        even_block = jnp.where(odd, other, mine)
        odd_block = jnp.where(odd, mine, other)
        even_last, odd_last = even_block[tokens:], odd_block[tokens:]
        left = lax.broadcasted_iota(jnp.int32, even_last.shape, 1) < HEAD
        first = jnp.where(left, even_last, odd_last)
        second = pltpu.roll(jnp.where(left, odd_last, even_last), HEAD, 1)
        at = pl.multiple_of((me ^ s) // 2 * 384, 128)
        whole[:, pl.ds(at, 128)] = even_block[:tokens].astype(whole.dtype)
        whole[:, pl.ds(at + 128, 128)] = jnp.concatenate([first, second], axis=0).astype(whole.dtype)
        whole[:, pl.ds(at + 256, 128)] = odd_block[:tokens].astype(whole.dtype)


def own_columns(ref, rows, me):
    pair = ref[rows, pl.ds(pl.multiple_of(me // 2 * 384, 128), 384)]
    return jnp.where((me & 1) == 1, pair[:, 192:], pair[:, :192])


def norm_into(stream, mod, normed):
    tokens, width = stream.shape
    step = 128
    total = jnp.zeros((tokens, step), F32)
    for at in range(0, width, step):
        total += stream[:, at : at + step]
    center = jnp.sum(total, axis=-1, keepdims=True) / width
    total = jnp.zeros((tokens, step), F32)
    for at in range(0, width, step):
        off = stream[:, at : at + step] - center
        total += off * off
    variance = jnp.sum(total, axis=-1, keepdims=True) / width
    spread = 1.0 / jnp.sqrt(variance + 1e-06)
    for at in range(0, width, step):
        part = (stream[:, at : at + step] - center) * spread
        part = part * (1.0 + mod[0, :, at : at + step]) + mod[1, :, at : at + step]
        normed[:, at : at + step] = part.astype(BF16)


def first_projection(*refs):
    n = len(refs) - 9
    blocks, (weight, mod), chunks, (residual, stream, normed) = (
        refs[:n],
        refs[n : n + 2],
        refs[n + 2 : n + 5],
        refs[n + 5 : n + 8],
    )
    mixed_order = refs[n + 8]
    me = lax.axis_index("blk")
    rows, reqs, _ = blocks[0].shape
    for s in range(n):
        for i in range(rows):
            at = (s * rows + i) * reqs
            stream[at : at + reqs, :] = blocks[s][i].astype(F32)
    norm_into(stream, mod, normed)
    tokens = stream.shape[0]
    per = rows * reqs
    columns = weight.shape[0]
    mixed_order[:, :columns] = dot_nt(normed[...], weight[...]).astype(BF16)
    mixed_order[:, columns:] = own_columns(stream, slice(None), me).astype(BF16)
    held = lax.broadcasted_iota(jnp.int32, (tokens, tokens), 1)
    wanted = lax.broadcasted_iota(jnp.int32, (tokens, tokens), 0)
    holder = held // per
    pick = (wanted == (holder ^ me) * per + (held - holder * per)).astype(F32).astype(BF16)
    ordered = jnp.dot(pick, mixed_order[...], preferred_element_type=F32).astype(BF16)
    for j in range(3):
        chunks[j][...] = pack(ordered[:, 192 * j : 192 * j + 192])
    residual[...] = ordered[:, columns:]


def next_projection(*refs):
    n = len(refs) - 8
    blocks, (weight, mod), chunks, (residual, stream, normed) = (
        refs[:n],
        refs[n : n + 2],
        refs[n + 2 : n + 5],
        refs[n + 5 : n + 8],
    )
    me = lax.axis_index("blk")
    assemble(blocks, me, stream)
    norm_into(stream, mod, normed)
    columns = dot_nt(normed[...], weight[...]).astype(BF16)
    for j in range(3):
        chunks[j][...] = pack(columns[:, 192 * j : 192 * j + 192])
    residual[...] = own_columns(stream, slice(None), me).astype(BF16)


def attention(chunk0, chunk1, chunk2, old, fresh, usable, attn):
    me = lax.axis_index("blk")
    first = lax.rem(me, 3)
    got = [unpack(chunk[...]) for chunk in (chunk0, chunk1, chunk2)]

    def kind(of):
        at = lax.rem(first + of, 3)
        return jnp.where(at == 0, got[0], jnp.where(at == 1, got[1], got[2]))

    queries = kind(0)
    is_fresh = fresh[...] > 0.5
    keys = jnp.where(is_fresh, kind(1), old[0])
    values = jnp.where(is_fresh, kind(2), old[1])
    tokens, width = queries.shape
    heads = width // HEAD
    head_of = lax.broadcasted_iota(jnp.int32, (tokens, width), 1) // HEAD
    stacked = jnp.concatenate(
        [jnp.where(head_of == h, queries, jnp.zeros_like(queries)) for h in range(heads)], axis=0
    )
    scores = dot_nt(stacked, keys) * 0.125
    allowed = jnp.concatenate([usable[...]] * heads, axis=0) > 0.5
    scores = jnp.where(allowed, scores, -1e30)
    top = jnp.max(scores, axis=-1, keepdims=True)
    weights = jnp.where(allowed, jnp.exp(scores - top), 0.0)
    total = jnp.sum(weights, axis=-1, keepdims=True)
    mixed = jnp.dot(weights.astype(BF16), values, preferred_element_type=F32) / total
    result = jnp.zeros((tokens, width), F32)
    for h in range(heads):
        result = jnp.where(head_of == h, mixed[h * tokens : (h + 1) * tokens], result)
    attn[...] = pack_by_parity(result, (me & 1) == 1).astype(BF16)


def output_projection(layer, *refs):
    n = len(refs) - 8
    blocks, (weight, mod, residual, kept), (packed, by_token), (whole, rows) = (
        refs[:n],
        refs[n : n + 4],
        refs[n + 4 : n + 6],
        refs[n + 6 : n + 8],
    )
    me = lax.axis_index("blk")
    assemble(blocks, me, whole)
    mixed = dot_nt(whole[...], weight[...]).astype(BF16).astype(F32)
    gate = own_columns(mod.at[2], slice(None), me)
    layer_out = (residual[...].astype(F32) + gate * mixed).astype(BF16).astype(F32)
    packed[...] = pack_by_parity(layer_out, (me & 1) == 1).astype(BF16)
    rows[...] = layer_out
    per = rows.shape[0] // n
    keep = lax.axis_index("section") < layer
    for d in range(n):
        mine = rows[d * per : d * per + per, :].astype(BF16)
        by_token[d, :per, :] = jnp.where(keep, kept[d, :per, :], mine)


def stale_by_head(old_keys, old_values, by_head, rows):
    n = by_head.shape[0]
    for which, old in enumerate((old_keys, old_values)):
        for i in range(3):
            rows[which * 8 + 2 * i : which * 8 + 2 * i + 2, :] = old[i].astype(F32)
    for d in range(n):
        by_head[d] = rows[:, 192 * d : 192 * d + 192].astype(BF16)


def stale_by_token(by_head, old, rows):
    n = by_head.shape[0]
    for d in range(n):
        block = by_head[d].astype(F32)
        rows[0, 6 * d : 6 * d + 6, :] = block[0:6]
        rows[1, 6 * d : 6 * d + 6, :] = block[8:14]
    old[...] = rows[...].astype(BF16)


def to_rows(by_column, out, rows):
    n = by_column.shape[0]
    for d in range(n):
        rows[:, 192 * d : 192 * d + 192] = by_column[d].astype(F32)
    for i in range(3):
        out[i] = rows[2 * i : 2 * i + 2, :].astype(BF16)


def hop(block, pairs):
    return lax.ppermute(block, ("section", "blk"), pairs)


def gather(block, n, source, target):
    return [
        block
        if s == 0 and source == target
        else hop(block, [(source * n + i, target * n + (i ^ s)) for i in range(n)])
        for s in range(n)
    ]


def by_heads(chunks, n, section):
    return [
        hop(chunk, [(section * n + b, section * n + (3 * b + j) % n) for b in range(n)])
        for j, chunk in enumerate(chunks)
    ]


def per_device(hidden, qkv_weight, out_weight, modulation, timestep, fresh, live, k_stale, v_stale):
    n = lax.axis_size("blk")
    columns = out_weight.shape[2]
    reqs, rows, width = hidden.shape
    if not (columns == 3 * HEAD and n % 3 == 1 and n & (n - 1) == 0 and (reqs, rows) == (2, 3)):
        return per_device_by_token(
            hidden, qkv_weight, out_weight, modulation, timestep, fresh, live, k_stale, v_stale
        )
    per = reqs * rows
    tokens = n * per
    shape = jax.ShapeDtypeStruct
    weight = jnp.swapaxes(qkv_weight[0], 0, 1)
    out_cols = jnp.swapaxes(out_weight[0], 0, 1)
    packed = shape((tokens * 3 // 2, 128), BF16)
    cols = shape((tokens, columns), BF16)

    own = jnp.transpose(hidden, (1, 0, 2))
    blocks = gather(own, n, 0, 0)

    steps = jnp.transpose(modulation, (1, 2, 0, 3))
    mod = lax.dynamic_index_in_dim(steps, timestep[0], 0, keepdims=False)
    parity = jnp.arange(tokens) % reqs
    live_keys = jnp.broadcast_to(live.T[:, None, :], (n, rows, reqs)).reshape(1, tokens)
    usable = ((parity[:, None] == parity[None, :]) & (live_keys == 1)).astype(F32)
    fresh_rows = jnp.broadcast_to(fresh[0].T[:, None, :], (n, rows, reqs)).reshape(tokens, 1)
    fresh_rows = jnp.broadcast_to(fresh_rows, (tokens, columns)).astype(F32)
    by_head = call(
        stale_by_head,
        shape((n, 16, columns), BF16),
        [pltpu.VMEM((16, width), F32)],
        (0, 200000),
        jnp.transpose(k_stale[0], (1, 0, 2)),
        jnp.transpose(v_stale[0], (1, 0, 2)),
    )
    by_head = lax.all_to_all(by_head, "blk", split_axis=0, concat_axis=0, tiled=True)
    old = call(
        stale_by_token,
        shape((2, tokens, columns), BF16),
        [pltpu.VMEM((2, tokens, columns), F32)],
        (0, 200000),
        by_head,
    )

    kept = jnp.zeros((n, 8, columns), BF16)
    for layer in range(2):
        *chunks, residual = call(
            first_projection if layer == 0 else next_projection,
            [packed, packed, packed, cols],
            [pltpu.VMEM((tokens, width), F32), pltpu.VMEM((tokens, width), BF16)]
            + ([pltpu.VMEM((tokens, 4 * columns), BF16)] if layer == 0 else []),
            (2 * tokens * width * 3 * columns, 8 * width * columns),
            *blocks,
            weight,
            mod,
        )
        attn = call(
            attention,
            packed,
            [],
            (8 * tokens * tokens * columns, 300000),
            *by_heads(chunks, n, layer),
            old,
            fresh_rows,
            usable,
        )
        layer_out, kept = call(
            functools.partial(output_projection, layer),
            [packed, shape((n, 8, columns), BF16)],
            [pltpu.VMEM((tokens, width), BF16), pltpu.VMEM((tokens, columns), F32)],
            (2 * tokens * width * columns, 4 * width * columns),
            *gather(attn, n, layer, layer),
            out_cols,
            mod,
            residual,
            kept,
        )
        if layer == 0:
            blocks = gather(layer_out, n, 0, 1)
    by_column = lax.all_to_all(kept, "blk", split_axis=0, concat_axis=0, tiled=True)
    result = call(
        to_rows,
        shape((rows, reqs, width), BF16),
        [pltpu.VMEM((8, width), F32)],
        (0, 100000),
        by_column,
    )
    return jnp.transpose(result, (1, 0, 2))[None]


def solution(mesh):
    return jax.shard_map(
        per_device,
        mesh=mesh,
        in_specs=(
            P(None, "blk", None),
            P("section", None, "blk"),
            P("section", None, "blk"),
            P("section", None, None, None),
            P(),
            P("section", None, None),
            P(),
            P("section", None, "blk", None),
            P("section", None, "blk", None),
        ),
        out_specs=P("section", None, "blk", None),
        check_vma=False,
    )
```

```python
import functools

import jax
import jax.numpy as jnp
from jax import lax
from jax.experimental import pallas as pl
from jax.experimental.pallas import tpu as pltpu
from jax.sharding import PartitionSpec as P


def from_behind(shard, axis, by):
    count = lax.axis_size(axis)
    pairs = [(i, i + by) for i in range(count) if 0 <= i + by < count]
    return lax.ppermute(shard, axis, pairs)


def attend(layer_in, qkv_cols, out_cols, modulate, fresh_own, old_keys, old_values, live):
    stream = layer_in.astype(jnp.float32)
    center = jnp.mean(stream, axis=-1, keepdims=True)
    variance = jnp.mean((stream - center) ** 2, axis=-1, keepdims=True)
    normed = (stream - center) / jnp.sqrt(variance + 1e-06) * (1.0 + modulate[0]) + modulate[1]
    normed_b = normed.astype(jnp.bfloat16)
    columns = jnp.einsum(
        "rnd,dc->rnc",
        lax.all_gather(normed_b, "blk", axis=1, tiled=True),
        qkv_cols,
        preferred_element_type=jnp.float32,
    ).astype(jnp.bfloat16)
    projected = lax.all_to_all(columns, "blk", split_axis=1, concat_axis=2, tiled=True)
    num_req, num_rows, width = layer_in.shape
    queries = projected[:, :, :width]
    new_keys = projected[:, :, width : 2 * width]
    new_values = projected[:, :, 2 * width :]
    use_fresh = (fresh_own == 1)[:, None, None]
    keys = jnp.where(use_fresh, new_keys, old_keys)
    values = jnp.where(use_fresh, new_values, old_values)
    num_heads = width // 64
    num_blocks = live.shape[1]
    q_heads = queries.reshape(num_req, num_rows, num_heads, 64)
    live_float = live.astype(jnp.float32)
    run_max = jnp.full((num_req, num_heads, num_rows), -1e30, jnp.float32)
    key_piece = lax.all_gather(keys, "blk", axis=1, tiled=True)
    value_piece = lax.all_gather(values, "blk", axis=1, tiled=True)
    piece_rows = key_piece.shape[1]
    key_heads = key_piece.reshape(num_req, piece_rows, num_heads, 64)
    value_heads = value_piece.reshape(num_req, piece_rows, num_heads, 64)
    scores = (
        jnp.einsum("qrhd,qnhd->qhrn", q_heads, key_heads, preferred_element_type=jnp.float32)
        * 0.125
    )
    block_ids = jnp.arange(piece_rows) // num_rows
    one_hot = (block_ids[:, None] == jnp.arange(num_blocks)[None, :]).astype(jnp.float32)
    usable = jnp.einsum("qb,nb->qn", live_float, one_hot) > 0.5
    usable = usable[:, None, None, :]
    scores = jnp.where(usable, scores, -1e30)
    new_max = jnp.maximum(run_max, jnp.max(scores, axis=-1))
    weights = jnp.where(usable, jnp.exp(scores - new_max[..., None]), 0.0)
    new_sum = jnp.sum(weights, axis=-1)
    new_acc = jnp.einsum(
        "qhrn,qnhd->qhrd", weights, value_heads.astype(jnp.float32), precision=lax.Precision.HIGHEST
    )
    attn = new_acc / new_sum[..., None]
    attn = jnp.transpose(attn, (0, 2, 1, 3)).reshape(num_req, num_rows, width).astype(jnp.bfloat16)
    out_part = jnp.einsum(
        "rnd,dc->rnc",
        lax.all_gather(attn, "blk", axis=1, tiled=True),
        out_cols,
        preferred_element_type=jnp.float32,
    ).astype(jnp.bfloat16)
    mixed_back = lax.all_to_all(out_part, "blk", split_axis=1, concat_axis=2, tiled=True)
    return (stream + modulate[2] * mixed_back.astype(jnp.float32)).astype(jnp.bfloat16)


def pick_request(array, req_idx):
    return lax.dynamic_index_in_dim(array, req_idx, 0, keepdims=True)


def per_device_by_token(hidden, qkv_weight, out_weight, modulation, timestep, fresh, live, k_stale, v_stale):
    section_idx = lax.axis_index("section")
    block_idx = lax.axis_index("blk")
    steps_all = modulation.shape[1]
    pick_row = (jnp.arange(steps_all) == timestep[0]).astype(jnp.float32)
    modulate = jnp.einsum("t,tcd->cd", pick_row, modulation[0], precision=lax.Precision.HIGHEST)
    num_blocks = fresh.shape[2]
    own_column = (jnp.arange(num_blocks) == block_idx).astype(jnp.int32)
    fresh_own = jnp.sum(fresh[0] * own_column[None, :], axis=1)
    qkv_cols = qkv_weight[0]
    out_cols = out_weight[0]
    old_keys = k_stale[0]
    old_values = v_stale[0]
    num_req = hidden.shape[0]
    received = jnp.zeros_like(hidden[0:1])
    first_out = []
    second_out = []
    for tick_idx in range(num_req + 1):
        if tick_idx < num_req:
            own_input = hidden[tick_idx : tick_idx + 1]
        else:
            own_input = jnp.zeros_like(hidden[0:1])
        layer_in = jnp.where(section_idx == 0, own_input, received)
        req_idx = jnp.clip(tick_idx - section_idx, 0, num_req - 1)
        layer_out = attend(
            layer_in,
            qkv_cols,
            out_cols,
            modulate,
            pick_request(fresh_own, req_idx),
            pick_request(old_keys, req_idx),
            pick_request(old_values, req_idx),
            pick_request(live, req_idx),
        )
        if tick_idx < num_req:
            first_out.append(layer_out)
            received = from_behind(layer_out, "section", 1)
        if tick_idx >= 1:
            second_out.append(layer_out)
    result = jnp.where(
        section_idx == 0, jnp.concatenate(first_out, axis=0), jnp.concatenate(second_out, axis=0)
    )
    return result[None]


HEAD = 64
BF16 = jnp.bfloat16
F32 = jnp.float32
NT = (((1,), (1,)), ((), ()))
VMEM = pl.BlockSpec(memory_space=pltpu.VMEM)


def call(body, outs, scratch, cost, *args):
    flops, moved = cost
    return pl.pallas_call(
        body,
        out_shape=outs,
        in_specs=[VMEM] * len(args),
        out_specs=jax.tree.map(lambda _: VMEM, outs),
        scratch_shapes=scratch,
        compiler_params=pltpu.CompilerParams(vmem_limit_bytes=24 << 20),
        cost_estimate=pl.CostEstimate(flops=flops, bytes_accessed=moved, transcendentals=0),
    )(*args)


def dot_nt(left, right):
    return lax.dot_general(left, right, NT, preferred_element_type=F32)


def halves(columns):
    mid = columns.shape[0] // 2
    return jnp.concatenate([columns[:mid], columns[mid:]], axis=1)


def pack(cols):
    return jnp.concatenate([cols[:, :128], halves(cols[:, 128:])], axis=0)


def unpack(packed):
    tokens = packed.shape[0] // 3 * 2
    last = packed[tokens:]
    return jnp.concatenate(
        [packed[:tokens], jnp.concatenate([last[:, :HEAD], last[:, HEAD:]], axis=0)], axis=1
    )


def pack_by_parity(cols, odd):
    mid = cols.shape[0] // 2
    even_form = pack(cols)
    odd_form = jnp.concatenate(
        [
            cols[:, HEAD:],
            jnp.concatenate([cols[mid:, :HEAD], cols[:mid, :HEAD]], axis=1),
        ],
        axis=0,
    )
    return jnp.where(odd, odd_form, even_form)


def assemble(blocks, whole):
    tokens = whole.shape[0]
    for d in range(0, blocks.shape[0], 2):
        even_last, odd_last = blocks[d, tokens:].astype(F32), blocks[d + 1, tokens:].astype(F32)
        left = lax.broadcasted_iota(jnp.int32, even_last.shape, 1) < HEAD
        first = jnp.where(left, even_last, odd_last)
        second = pltpu.roll(jnp.where(left, odd_last, even_last), HEAD, 1)
        at = d // 2 * 384
        whole[:, at : at + 128] = blocks[d, :tokens].astype(whole.dtype)
        whole[:, at + 128 : at + 256] = jnp.concatenate([first, second], axis=0).astype(whole.dtype)
        whole[:, at + 256 : at + 384] = blocks[d + 1, :tokens].astype(whole.dtype)


def own_columns(ref, rows, me):
    pair = ref[rows, pl.ds(pl.multiple_of(me // 2 * 384, 128), 384)]
    return jnp.where((me & 1) == 1, pair[:, 192:], pair[:, :192])


def norm_into(stream, mod, normed):
    tokens, width = stream.shape
    step = 128
    total = jnp.zeros((tokens, step), F32)
    for at in range(0, width, step):
        total += stream[:, at : at + step]
    center = jnp.sum(total, axis=-1, keepdims=True) / width
    total = jnp.zeros((tokens, step), F32)
    for at in range(0, width, step):
        off = stream[:, at : at + step] - center
        total += off * off
    variance = jnp.sum(total, axis=-1, keepdims=True) / width
    spread = 1.0 / jnp.sqrt(variance + 1e-06)
    for at in range(0, width, step):
        part = (stream[:, at : at + step] - center) * spread
        part = part * (1.0 + mod[0, :, at : at + step]) + mod[1, :, at : at + step]
        normed[:, at : at + step] = part.astype(BF16)


def project(stream, weight, mod, chunks, residual, normed):
    me = lax.axis_index("blk")
    norm_into(stream, mod, normed)
    columns = dot_nt(normed[...], weight[...]).astype(BF16)
    for j in range(3):
        chunks[j][...] = pack(columns[:, 192 * j : 192 * j + 192])
    residual[...] = own_columns(stream, slice(None), me).astype(BF16)


def first_projection(blocks, weight, mod, chunk0, chunk1, chunk2, residual, stream, normed):
    for i in range(blocks.shape[0]):
        stream[2 * i : 2 * i + 2, :] = blocks[i].astype(F32)
    project(stream, weight, mod, (chunk0, chunk1, chunk2), residual, normed)


def next_projection(blocks, weight, mod, chunk0, chunk1, chunk2, residual, stream, normed):
    assemble(blocks, stream)
    project(stream, weight, mod, (chunk0, chunk1, chunk2), residual, normed)


def attention(chunk0, chunk1, chunk2, old, fresh, usable, attn):
    me = lax.axis_index("blk")
    first = lax.rem(me, 3)
    got = [unpack(chunk[...]) for chunk in (chunk0, chunk1, chunk2)]

    def kind(of):
        at = lax.rem(first + of, 3)
        return jnp.where(at == 0, got[0], jnp.where(at == 1, got[1], got[2]))

    queries = kind(0)
    is_fresh = fresh[...] > 0.5
    keys = jnp.where(is_fresh, kind(1), old[0])
    values = jnp.where(is_fresh, kind(2), old[1])
    tokens, width = queries.shape
    heads = width // HEAD
    head_of = lax.broadcasted_iota(jnp.int32, (tokens, width), 1) // HEAD
    stacked = jnp.concatenate(
        [jnp.where(head_of == h, queries, jnp.zeros_like(queries)) for h in range(heads)], axis=0
    )
    scores = dot_nt(stacked, keys) * 0.125
    allowed = jnp.concatenate([usable[...]] * heads, axis=0) > 0.5
    scores = jnp.where(allowed, scores, -1e30)
    top = jnp.max(scores, axis=-1, keepdims=True)
    weights = jnp.where(allowed, jnp.exp(scores - top), 0.0)
    total = jnp.sum(weights, axis=-1, keepdims=True)
    mixed = jnp.dot(weights.astype(BF16), values, preferred_element_type=F32) / total
    result = jnp.zeros((tokens, width), F32)
    for h in range(heads):
        result = jnp.where(head_of == h, mixed[h * tokens : (h + 1) * tokens], result)
    attn[...] = pack_by_parity(result, (me & 1) == 1).astype(BF16)


def output_projection(layer, blocks, weight, mod, residual, kept, packed, by_token, whole, rows):
    n = blocks.shape[0]
    me = lax.axis_index("blk")
    assemble(blocks, whole)
    mixed = dot_nt(whole[...], weight[...]).astype(BF16).astype(F32)
    gate = own_columns(mod.at[2], slice(None), me)
    layer_out = (residual[...].astype(F32) + gate * mixed).astype(BF16).astype(F32)
    packed[...] = pack_by_parity(layer_out, (me & 1) == 1).astype(BF16)
    rows[...] = layer_out
    per = rows.shape[0] // n
    keep = lax.axis_index("section") < layer
    for d in range(n):
        mine = rows[d * per : d * per + per, :].astype(BF16)
        by_token[d, :per, :] = jnp.where(keep, kept[d, :per, :], mine)


def stale_by_head(old_keys, old_values, by_head, rows):
    n = by_head.shape[0]
    for which, old in enumerate((old_keys, old_values)):
        for i in range(3):
            rows[which * 8 + 2 * i : which * 8 + 2 * i + 2, :] = old[i].astype(F32)
    for d in range(n):
        by_head[d] = rows[:, 192 * d : 192 * d + 192].astype(BF16)


def stale_by_token(by_head, old, rows):
    n = by_head.shape[0]
    for d in range(n):
        block = by_head[d].astype(F32)
        rows[0, 6 * d : 6 * d + 6, :] = block[0:6]
        rows[1, 6 * d : 6 * d + 6, :] = block[8:14]
    old[...] = rows[...].astype(BF16)


def to_rows(by_column, out, rows):
    n = by_column.shape[0]
    for d in range(n):
        rows[:, 192 * d : 192 * d + 192] = by_column[d].astype(F32)
    for i in range(3):
        out[i] = rows[2 * i : 2 * i + 2, :].astype(BF16)


def hop(block, pairs):
    return lax.ppermute(block, ("section", "blk"), pairs)


def gather(block):
    return lax.all_gather(block, "blk", axis=0, tiled=True)


def by_heads(chunks, n, section):
    return [
        hop(chunk, [(section * n + b, section * n + (3 * b + j) % n) for b in range(n)])
        for j, chunk in enumerate(chunks)
    ]


def per_device(hidden, qkv_weight, out_weight, modulation, timestep, fresh, live, k_stale, v_stale):
    n = lax.axis_size("blk")
    columns = out_weight.shape[2]
    reqs, rows, width = hidden.shape
    if not (columns == 3 * HEAD and n % 3 == 1 and n & (n - 1) == 0 and (reqs, rows) == (2, 3)):
        return per_device_by_token(
            hidden, qkv_weight, out_weight, modulation, timestep, fresh, live, k_stale, v_stale
        )
    per = reqs * rows
    tokens = n * per
    shape = jax.ShapeDtypeStruct
    weight = jnp.swapaxes(qkv_weight[0], 0, 1)
    out_cols = jnp.swapaxes(out_weight[0], 0, 1)
    packed = shape((tokens * 3 // 2, 128), BF16)
    cols = shape((tokens, columns), BF16)

    own = jnp.transpose(hidden, (1, 0, 2))
    blocks = gather(own)

    steps = jnp.transpose(modulation, (1, 2, 0, 3))
    mod = lax.dynamic_index_in_dim(steps, timestep[0], 0, keepdims=False)
    parity = jnp.arange(tokens) % reqs
    live_keys = jnp.broadcast_to(live.T[:, None, :], (n, rows, reqs)).reshape(1, tokens)
    usable = ((parity[:, None] == parity[None, :]) & (live_keys == 1)).astype(F32)
    fresh_rows = jnp.broadcast_to(fresh[0].T[:, None, :], (n, rows, reqs)).reshape(tokens, 1)
    fresh_rows = jnp.broadcast_to(fresh_rows, (tokens, columns)).astype(F32)
    by_head = call(
        stale_by_head,
        shape((n, 16, columns), BF16),
        [pltpu.VMEM((16, width), F32)],
        (0, 200000),
        jnp.transpose(k_stale[0], (1, 0, 2)),
        jnp.transpose(v_stale[0], (1, 0, 2)),
    )
    by_head = lax.all_to_all(by_head, "blk", split_axis=0, concat_axis=0, tiled=True)
    old = call(
        stale_by_token,
        shape((2, tokens, columns), BF16),
        [pltpu.VMEM((2, tokens, columns), F32)],
        (0, 200000),
        by_head,
    )

    kept = jnp.zeros((n, 8, columns), BF16)
    for layer in range(2):
        *chunks, residual = call(
            first_projection if layer == 0 else next_projection,
            [packed, packed, packed, cols],
            [pltpu.VMEM((tokens, width), F32), pltpu.VMEM((tokens, width), BF16)],
            (2 * tokens * width * 3 * columns, 8 * width * columns),
            blocks,
            weight,
            mod,
        )
        attn = call(
            attention,
            packed,
            [],
            (8 * tokens * tokens * columns, 300000),
            *by_heads(chunks, n, layer),
            old,
            fresh_rows,
            usable,
        )
        layer_out, kept = call(
            functools.partial(output_projection, layer),
            [packed, shape((n, 8, columns), BF16)],
            [pltpu.VMEM((tokens, width), BF16), pltpu.VMEM((tokens, columns), F32)],
            (2 * tokens * width * columns, 4 * width * columns),
            gather(attn).reshape(n, *packed.shape),
            out_cols,
            mod,
            residual,
            kept,
        )
        if layer == 0:
            across = hop(layer_out, [(b, n + b) for b in range(n)])
            blocks = gather(across).reshape(n, *packed.shape)
    by_column = lax.all_to_all(kept, "blk", split_axis=0, concat_axis=0, tiled=True)
    result = call(
        to_rows,
        shape((rows, reqs, width), BF16),
        [pltpu.VMEM((8, width), F32)],
        (0, 100000),
        by_column,
    )
    return jnp.transpose(result, (1, 0, 2))[None]


def solution(mesh):
    return jax.shard_map(
        per_device,
        mesh=mesh,
        in_specs=(
            P(None, "blk", None),
            P("section", None, "blk"),
            P("section", None, "blk"),
            P("section", None, None, None),
            P(),
            P("section", None, None),
            P(),
            P("section", None, "blk", None),
            P("section", None, "blk", None),
        ),
        out_specs=P("section", None, "blk", None),
        check_vma=False,
    )
```

```python
import functools

import jax
import jax.numpy as jnp
from jax import lax
from jax.experimental import pallas as pl
from jax.experimental.pallas import tpu as pltpu
from jax.sharding import PartitionSpec as P


def from_behind(shard, axis, by):
    count = lax.axis_size(axis)
    pairs = [(i, i + by) for i in range(count) if 0 <= i + by < count]
    return lax.ppermute(shard, axis, pairs)


def attend(layer_in, qkv_cols, out_cols, modulate, fresh_own, old_keys, old_values, live):
    stream = layer_in.astype(jnp.float32)
    center = jnp.mean(stream, axis=-1, keepdims=True)
    variance = jnp.mean((stream - center) ** 2, axis=-1, keepdims=True)
    normed = (stream - center) / jnp.sqrt(variance + 1e-06) * (1.0 + modulate[0]) + modulate[1]
    normed_b = normed.astype(jnp.bfloat16)
    columns = jnp.einsum(
        "rnd,dc->rnc",
        lax.all_gather(normed_b, "blk", axis=1, tiled=True),
        qkv_cols,
        preferred_element_type=jnp.float32,
    ).astype(jnp.bfloat16)
    projected = lax.all_to_all(columns, "blk", split_axis=1, concat_axis=2, tiled=True)
    num_req, num_rows, width = layer_in.shape
    queries = projected[:, :, :width]
    new_keys = projected[:, :, width : 2 * width]
    new_values = projected[:, :, 2 * width :]
    use_fresh = (fresh_own == 1)[:, None, None]
    keys = jnp.where(use_fresh, new_keys, old_keys)
    values = jnp.where(use_fresh, new_values, old_values)
    num_heads = width // 64
    num_blocks = live.shape[1]
    q_heads = queries.reshape(num_req, num_rows, num_heads, 64)
    live_float = live.astype(jnp.float32)
    run_max = jnp.full((num_req, num_heads, num_rows), -1e30, jnp.float32)
    key_piece = lax.all_gather(keys, "blk", axis=1, tiled=True)
    value_piece = lax.all_gather(values, "blk", axis=1, tiled=True)
    piece_rows = key_piece.shape[1]
    key_heads = key_piece.reshape(num_req, piece_rows, num_heads, 64)
    value_heads = value_piece.reshape(num_req, piece_rows, num_heads, 64)
    scores = (
        jnp.einsum("qrhd,qnhd->qhrn", q_heads, key_heads, preferred_element_type=jnp.float32)
        * 0.125
    )
    block_ids = jnp.arange(piece_rows) // num_rows
    one_hot = (block_ids[:, None] == jnp.arange(num_blocks)[None, :]).astype(jnp.float32)
    usable = jnp.einsum("qb,nb->qn", live_float, one_hot) > 0.5
    usable = usable[:, None, None, :]
    scores = jnp.where(usable, scores, -1e30)
    new_max = jnp.maximum(run_max, jnp.max(scores, axis=-1))
    weights = jnp.where(usable, jnp.exp(scores - new_max[..., None]), 0.0)
    new_sum = jnp.sum(weights, axis=-1)
    new_acc = jnp.einsum(
        "qhrn,qnhd->qhrd", weights, value_heads.astype(jnp.float32), precision=lax.Precision.HIGHEST
    )
    attn = new_acc / new_sum[..., None]
    attn = jnp.transpose(attn, (0, 2, 1, 3)).reshape(num_req, num_rows, width).astype(jnp.bfloat16)
    out_part = jnp.einsum(
        "rnd,dc->rnc",
        lax.all_gather(attn, "blk", axis=1, tiled=True),
        out_cols,
        preferred_element_type=jnp.float32,
    ).astype(jnp.bfloat16)
    mixed_back = lax.all_to_all(out_part, "blk", split_axis=1, concat_axis=2, tiled=True)
    return (stream + modulate[2] * mixed_back.astype(jnp.float32)).astype(jnp.bfloat16)


def pick_request(array, req_idx):
    return lax.dynamic_index_in_dim(array, req_idx, 0, keepdims=True)


def per_device_by_token(hidden, qkv_weight, out_weight, modulation, timestep, fresh, live, k_stale, v_stale):
    section_idx = lax.axis_index("section")
    block_idx = lax.axis_index("blk")
    steps_all = modulation.shape[1]
    pick_row = (jnp.arange(steps_all) == timestep[0]).astype(jnp.float32)
    modulate = jnp.einsum("t,tcd->cd", pick_row, modulation[0], precision=lax.Precision.HIGHEST)
    num_blocks = fresh.shape[2]
    own_column = (jnp.arange(num_blocks) == block_idx).astype(jnp.int32)
    fresh_own = jnp.sum(fresh[0] * own_column[None, :], axis=1)
    qkv_cols = qkv_weight[0]
    out_cols = out_weight[0]
    old_keys = k_stale[0]
    old_values = v_stale[0]
    num_req = hidden.shape[0]
    received = jnp.zeros_like(hidden[0:1])
    first_out = []
    second_out = []
    for tick_idx in range(num_req + 1):
        if tick_idx < num_req:
            own_input = hidden[tick_idx : tick_idx + 1]
        else:
            own_input = jnp.zeros_like(hidden[0:1])
        layer_in = jnp.where(section_idx == 0, own_input, received)
        req_idx = jnp.clip(tick_idx - section_idx, 0, num_req - 1)
        layer_out = attend(
            layer_in,
            qkv_cols,
            out_cols,
            modulate,
            pick_request(fresh_own, req_idx),
            pick_request(old_keys, req_idx),
            pick_request(old_values, req_idx),
            pick_request(live, req_idx),
        )
        if tick_idx < num_req:
            first_out.append(layer_out)
            received = from_behind(layer_out, "section", 1)
        if tick_idx >= 1:
            second_out.append(layer_out)
    result = jnp.where(
        section_idx == 0, jnp.concatenate(first_out, axis=0), jnp.concatenate(second_out, axis=0)
    )
    return result[None]


HEAD = 64
BF16 = jnp.bfloat16
F32 = jnp.float32
NT = (((1,), (1,)), ((), ()))
VMEM = pl.BlockSpec(memory_space=pltpu.VMEM)


def call(body, outs, scratch, cost, *args):
    flops, moved = cost
    return pl.pallas_call(
        body,
        out_shape=outs,
        in_specs=[VMEM] * len(args),
        out_specs=jax.tree.map(lambda _: VMEM, outs),
        scratch_shapes=scratch,
        compiler_params=pltpu.CompilerParams(vmem_limit_bytes=24 << 20),
        cost_estimate=pl.CostEstimate(flops=flops, bytes_accessed=moved, transcendentals=0),
    )(*args)


def dot_nt(left, right):
    return lax.dot_general(left, right, NT, preferred_element_type=F32)


def halves(columns):
    mid = columns.shape[0] // 2
    return jnp.concatenate([columns[:mid], columns[mid:]], axis=1)


def pack(cols):
    return jnp.concatenate([cols[:, :128], halves(cols[:, 128:])], axis=0)


def unpack(packed):
    tokens = packed.shape[0] // 3 * 2
    last = packed[tokens:]
    return jnp.concatenate(
        [packed[:tokens], jnp.concatenate([last[:, :HEAD], last[:, HEAD:]], axis=0)], axis=1
    )


def pack_by_parity(cols, odd):
    mid = cols.shape[0] // 2
    even_form = pack(cols)
    odd_form = jnp.concatenate(
        [
            cols[:, HEAD:],
            jnp.concatenate([cols[mid:, :HEAD], cols[:mid, :HEAD]], axis=1),
        ],
        axis=0,
    )
    return jnp.where(odd, odd_form, even_form)


def assemble(blocks, whole, by_heads=False):
    tokens = whole.shape[0]
    n = blocks.shape[0]
    for d in range(0, n, 2):
        even, odd = [group * pow(3, -1, n) % n if by_heads else group for group in (d, d + 1)]
        even_last, odd_last = blocks[even, tokens:].astype(F32), blocks[odd, tokens:].astype(F32)
        left = lax.broadcasted_iota(jnp.int32, even_last.shape, 1) < HEAD
        first = jnp.where(left, even_last, odd_last)
        second = pltpu.roll(jnp.where(left, odd_last, even_last), HEAD, 1)
        at = d // 2 * 384
        whole[:, at : at + 128] = blocks[even, :tokens].astype(whole.dtype)
        whole[:, at + 128 : at + 256] = jnp.concatenate([first, second], axis=0).astype(whole.dtype)
        whole[:, at + 256 : at + 384] = blocks[odd, :tokens].astype(whole.dtype)


def own_columns(ref, rows, me):
    pair = ref[rows, pl.ds(pl.multiple_of(me // 2 * 384, 128), 384)]
    return jnp.where((me & 1) == 1, pair[:, 192:], pair[:, :192])


def norm_into(stream, mod, normed):
    tokens, width = stream.shape
    step = 128
    total = jnp.zeros((tokens, step), F32)
    for at in range(0, width, step):
        total += stream[:, at : at + step]
    center = jnp.sum(total, axis=-1, keepdims=True) / width
    total = jnp.zeros((tokens, step), F32)
    for at in range(0, width, step):
        off = stream[:, at : at + step] - center
        total += off * off
    variance = jnp.sum(total, axis=-1, keepdims=True) / width
    spread = 1.0 / jnp.sqrt(variance + 1e-06)
    for at in range(0, width, step):
        part = (stream[:, at : at + step] - center) * spread
        part = part * (1.0 + mod[0, :, at : at + step]) + mod[1, :, at : at + step]
        normed[:, at : at + step] = part.astype(BF16)


def project(stream, weight, mod, chunks, residual, normed):
    me = lax.axis_index("blk")
    norm_into(stream, mod, normed)
    columns = dot_nt(normed[...], weight[...]).astype(BF16)
    for j in range(3):
        chunks[j][...] = pack(columns[:, 192 * j : 192 * j + 192])
    residual[...] = own_columns(stream, slice(None), me).astype(BF16)


def first_projection(blocks, weight, mod, chunk0, chunk1, chunk2, residual, stream, normed):
    for i in range(blocks.shape[0]):
        stream[2 * i : 2 * i + 2, :] = blocks[i].astype(F32)
    project(stream, weight, mod, (chunk0, chunk1, chunk2), residual, normed)


def next_projection(blocks, weight, mod, chunk0, chunk1, chunk2, residual, stream, normed):
    assemble(blocks, stream)
    project(stream, weight, mod, (chunk0, chunk1, chunk2), residual, normed)


def attention(chunk0, chunk1, chunk2, old, fresh, usable, attn):
    me = lax.axis_index("blk")
    first = lax.rem(lax.rem(3 * me, lax.axis_size("blk")), 3)
    got = [unpack(chunk[...]) for chunk in (chunk0, chunk1, chunk2)]

    def kind(of):
        at = lax.rem(first + of, 3)
        return jnp.where(at == 0, got[0], jnp.where(at == 1, got[1], got[2]))

    queries = kind(0)
    is_fresh = fresh[...] > 0.5
    keys = jnp.where(is_fresh, kind(1), old[0])
    values = jnp.where(is_fresh, kind(2), old[1])
    tokens, width = queries.shape
    heads = width // HEAD
    head_of = lax.broadcasted_iota(jnp.int32, (tokens, width), 1) // HEAD
    stacked = jnp.concatenate(
        [jnp.where(head_of == h, queries, jnp.zeros_like(queries)) for h in range(heads)], axis=0
    )
    scores = dot_nt(stacked, keys) * 0.125
    allowed = jnp.concatenate([usable[...]] * heads, axis=0) > 0.5
    scores = jnp.where(allowed, scores, -1e30)
    top = jnp.max(scores, axis=-1, keepdims=True)
    weights = jnp.where(allowed, jnp.exp(scores - top), 0.0)
    total = jnp.sum(weights, axis=-1, keepdims=True)
    mixed = jnp.dot(weights.astype(BF16), values, preferred_element_type=F32) / total
    result = jnp.zeros((tokens, width), F32)
    for h in range(heads):
        result = jnp.where(head_of == h, mixed[h * tokens : (h + 1) * tokens], result)
    attn[...] = pack_by_parity(result, (me & 1) == 1).astype(BF16)


def output_projection(layer, blocks, weight, mod, residual, kept, packed, by_token, whole, rows):
    n = blocks.shape[0]
    me = lax.axis_index("blk")
    assemble(blocks, whole, by_heads=True)
    mixed = dot_nt(whole[...], weight[...]).astype(BF16).astype(F32)
    gate = own_columns(mod.at[2], slice(None), me)
    layer_out = (residual[...].astype(F32) + gate * mixed).astype(BF16).astype(F32)
    packed[...] = pack_by_parity(layer_out, (me & 1) == 1).astype(BF16)
    rows[...] = layer_out
    per = rows.shape[0] // n
    keep = lax.axis_index("section") < layer
    for d in range(n):
        mine = rows[d * per : d * per + per, :].astype(BF16)
        by_token[d, :per, :] = jnp.where(keep, kept[d, :per, :], mine)


def stale_by_head(old_keys, old_values, by_head, rows):
    n = by_head.shape[0]
    for which, old in enumerate((old_keys, old_values)):
        for i in range(3):
            rows[which * 8 + 2 * i : which * 8 + 2 * i + 2, :] = old[i].astype(F32)
    for d in range(n):
        at = 192 * (3 * d % n)
        by_head[d] = rows[:, at : at + 192].astype(BF16)


def stale_by_token(by_head, old, rows):
    n = by_head.shape[0]
    for d in range(n):
        block = by_head[d].astype(F32)
        rows[0, 6 * d : 6 * d + 6, :] = block[0:6]
        rows[1, 6 * d : 6 * d + 6, :] = block[8:14]
    old[...] = rows[...].astype(BF16)


def to_rows(by_column, out, rows):
    n = by_column.shape[0]
    for d in range(n):
        rows[:, 192 * d : 192 * d + 192] = by_column[d].astype(F32)
    for i in range(3):
        out[i] = rows[2 * i : 2 * i + 2, :].astype(BF16)


def hop(block, pairs):
    return lax.ppermute(block, ("section", "blk"), pairs)


def gather(block, n):
    return lax.all_to_all(
        jnp.broadcast_to(block[None], (n, *block.shape)), "blk", split_axis=0, concat_axis=0, tiled=True
    )


def by_heads(chunks, n, section):
    inverse = pow(3, -1, n)
    return [
        hop(chunk, [(section * n + b, section * n + (b + inverse * j) % n) for b in range(n)]) if j else chunk
        for j, chunk in enumerate(chunks)
    ]


def per_device(hidden, qkv_weight, out_weight, modulation, timestep, fresh, live, k_stale, v_stale):
    n = lax.axis_size("blk")
    columns = out_weight.shape[2]
    reqs, rows, width = hidden.shape
    if not (columns == 3 * HEAD and n % 3 == 1 and n & (n - 1) == 0 and (reqs, rows) == (2, 3)):
        return per_device_by_token(
            hidden, qkv_weight, out_weight, modulation, timestep, fresh, live, k_stale, v_stale
        )
    per = reqs * rows
    tokens = n * per
    shape = jax.ShapeDtypeStruct
    weight = jnp.swapaxes(qkv_weight[0], 0, 1)
    out_cols = jnp.swapaxes(out_weight[0], 0, 1)
    packed = shape((tokens * 3 // 2, 128), BF16)
    cols = shape((tokens, columns), BF16)

    own = jnp.transpose(hidden, (1, 0, 2))
    blocks = gather(own, n).reshape(n * rows, reqs, width)

    steps = jnp.transpose(modulation, (1, 2, 0, 3))
    mod = lax.dynamic_index_in_dim(steps, timestep[0], 0, keepdims=False)
    parity = jnp.arange(tokens) % reqs
    live_keys = jnp.broadcast_to(live.T[:, None, :], (n, rows, reqs)).reshape(1, tokens)
    usable = ((parity[:, None] == parity[None, :]) & (live_keys == 1)).astype(F32)
    fresh_rows = jnp.broadcast_to(fresh[0].T[:, None, :], (n, rows, reqs)).reshape(tokens, 1)
    fresh_rows = jnp.broadcast_to(fresh_rows, (tokens, columns)).astype(F32)
    by_head = call(
        stale_by_head,
        shape((n, 16, columns), BF16),
        [pltpu.VMEM((16, width), F32)],
        (0, 200000),
        jnp.transpose(k_stale[0], (1, 0, 2)),
        jnp.transpose(v_stale[0], (1, 0, 2)),
    )
    by_head = lax.all_to_all(by_head, "blk", split_axis=0, concat_axis=0, tiled=True)
    old = call(
        stale_by_token,
        shape((2, tokens, columns), BF16),
        [pltpu.VMEM((2, tokens, columns), F32)],
        (0, 200000),
        by_head,
    )

    kept = jnp.zeros((n, 8, columns), BF16)
    for layer in range(2):
        *chunks, residual = call(
            first_projection if layer == 0 else next_projection,
            [packed, packed, packed, cols],
            [pltpu.VMEM((tokens, width), F32), pltpu.VMEM((tokens, width), BF16)],
            (2 * tokens * width * 3 * columns, 8 * width * columns),
            blocks,
            weight,
            mod,
        )
        attn = call(
            attention,
            packed,
            [],
            (8 * tokens * tokens * columns, 300000),
            *by_heads(chunks, n, layer),
            old,
            fresh_rows,
            usable,
        )
        layer_out, kept = call(
            functools.partial(output_projection, layer),
            [packed, shape((n, 8, columns), BF16)],
            [pltpu.VMEM((tokens, width), BF16), pltpu.VMEM((tokens, columns), F32)],
            (2 * tokens * width * columns, 4 * width * columns),
            gather(attn, n),
            out_cols,
            mod,
            residual,
            kept,
        )
        if layer == 0:
            across = hop(layer_out, [(b, n + b) for b in range(n)])
            blocks = gather(across, n)
    by_column = lax.all_to_all(kept, "blk", split_axis=0, concat_axis=0, tiled=True)
    result = call(
        to_rows,
        shape((rows, reqs, width), BF16),
        [pltpu.VMEM((8, width), F32)],
        (0, 100000),
        by_column,
    )
    return jnp.transpose(result, (1, 0, 2))[None]


def solution(mesh):
    return jax.shard_map(
        per_device,
        mesh=mesh,
        in_specs=(
            P(None, "blk", None),
            P("section", None, "blk"),
            P("section", None, "blk"),
            P("section", None, None, None),
            P(),
            P("section", None, None),
            P(),
            P("section", None, "blk", None),
            P("section", None, "blk", None),
        ),
        out_specs=P("section", None, "blk", None),
        check_vma=False,
    )
```

```python
import functools

import jax
import jax.numpy as jnp
from jax import lax
from jax.experimental import pallas as pl
from jax.experimental.pallas import tpu as pltpu
from jax.sharding import PartitionSpec as P


def from_behind(shard, axis, by):
    count = lax.axis_size(axis)
    pairs = [(i, i + by) for i in range(count) if 0 <= i + by < count]
    return lax.ppermute(shard, axis, pairs)


def attend(layer_in, qkv_cols, out_cols, modulate, fresh_own, old_keys, old_values, live):
    stream = layer_in.astype(jnp.float32)
    center = jnp.mean(stream, axis=-1, keepdims=True)
    variance = jnp.mean((stream - center) ** 2, axis=-1, keepdims=True)
    normed = (stream - center) / jnp.sqrt(variance + 1e-06) * (1.0 + modulate[0]) + modulate[1]
    normed_b = normed.astype(jnp.bfloat16)
    columns = jnp.einsum(
        "rnd,dc->rnc",
        lax.all_gather(normed_b, "blk", axis=1, tiled=True),
        qkv_cols,
        preferred_element_type=jnp.float32,
    ).astype(jnp.bfloat16)
    projected = lax.all_to_all(columns, "blk", split_axis=1, concat_axis=2, tiled=True)
    num_req, num_rows, width = layer_in.shape
    queries = projected[:, :, :width]
    new_keys = projected[:, :, width : 2 * width]
    new_values = projected[:, :, 2 * width :]
    use_fresh = (fresh_own == 1)[:, None, None]
    keys = jnp.where(use_fresh, new_keys, old_keys)
    values = jnp.where(use_fresh, new_values, old_values)
    num_heads = width // 64
    num_blocks = live.shape[1]
    q_heads = queries.reshape(num_req, num_rows, num_heads, 64)
    live_float = live.astype(jnp.float32)
    run_max = jnp.full((num_req, num_heads, num_rows), -1e30, jnp.float32)
    key_piece = lax.all_gather(keys, "blk", axis=1, tiled=True)
    value_piece = lax.all_gather(values, "blk", axis=1, tiled=True)
    piece_rows = key_piece.shape[1]
    key_heads = key_piece.reshape(num_req, piece_rows, num_heads, 64)
    value_heads = value_piece.reshape(num_req, piece_rows, num_heads, 64)
    scores = (
        jnp.einsum("qrhd,qnhd->qhrn", q_heads, key_heads, preferred_element_type=jnp.float32)
        * 0.125
    )
    block_ids = jnp.arange(piece_rows) // num_rows
    one_hot = (block_ids[:, None] == jnp.arange(num_blocks)[None, :]).astype(jnp.float32)
    usable = jnp.einsum("qb,nb->qn", live_float, one_hot) > 0.5
    usable = usable[:, None, None, :]
    scores = jnp.where(usable, scores, -1e30)
    new_max = jnp.maximum(run_max, jnp.max(scores, axis=-1))
    weights = jnp.where(usable, jnp.exp(scores - new_max[..., None]), 0.0)
    new_sum = jnp.sum(weights, axis=-1)
    new_acc = jnp.einsum(
        "qhrn,qnhd->qhrd", weights, value_heads.astype(jnp.float32), precision=lax.Precision.HIGHEST
    )
    attn = new_acc / new_sum[..., None]
    attn = jnp.transpose(attn, (0, 2, 1, 3)).reshape(num_req, num_rows, width).astype(jnp.bfloat16)
    out_part = jnp.einsum(
        "rnd,dc->rnc",
        lax.all_gather(attn, "blk", axis=1, tiled=True),
        out_cols,
        preferred_element_type=jnp.float32,
    ).astype(jnp.bfloat16)
    mixed_back = lax.all_to_all(out_part, "blk", split_axis=1, concat_axis=2, tiled=True)
    return (stream + modulate[2] * mixed_back.astype(jnp.float32)).astype(jnp.bfloat16)


def pick_request(array, req_idx):
    return lax.dynamic_index_in_dim(array, req_idx, 0, keepdims=True)


def per_device_by_token(hidden, qkv_weight, out_weight, modulation, timestep, fresh, live, k_stale, v_stale):
    section_idx = lax.axis_index("section")
    block_idx = lax.axis_index("blk")
    steps_all = modulation.shape[1]
    pick_row = (jnp.arange(steps_all) == timestep[0]).astype(jnp.float32)
    modulate = jnp.einsum("t,tcd->cd", pick_row, modulation[0], precision=lax.Precision.HIGHEST)
    num_blocks = fresh.shape[2]
    own_column = (jnp.arange(num_blocks) == block_idx).astype(jnp.int32)
    fresh_own = jnp.sum(fresh[0] * own_column[None, :], axis=1)
    qkv_cols = qkv_weight[0]
    out_cols = out_weight[0]
    old_keys = k_stale[0]
    old_values = v_stale[0]
    num_req = hidden.shape[0]
    received = jnp.zeros_like(hidden[0:1])
    first_out = []
    second_out = []
    for tick_idx in range(num_req + 1):
        if tick_idx < num_req:
            own_input = hidden[tick_idx : tick_idx + 1]
        else:
            own_input = jnp.zeros_like(hidden[0:1])
        layer_in = jnp.where(section_idx == 0, own_input, received)
        req_idx = jnp.clip(tick_idx - section_idx, 0, num_req - 1)
        layer_out = attend(
            layer_in,
            qkv_cols,
            out_cols,
            modulate,
            pick_request(fresh_own, req_idx),
            pick_request(old_keys, req_idx),
            pick_request(old_values, req_idx),
            pick_request(live, req_idx),
        )
        if tick_idx < num_req:
            first_out.append(layer_out)
            received = from_behind(layer_out, "section", 1)
        if tick_idx >= 1:
            second_out.append(layer_out)
    result = jnp.where(
        section_idx == 0, jnp.concatenate(first_out, axis=0), jnp.concatenate(second_out, axis=0)
    )
    return result[None]


HEAD = 64
BF16 = jnp.bfloat16
F32 = jnp.float32
NT = (((1,), (1,)), ((), ()))
VMEM = pl.BlockSpec(memory_space=pltpu.VMEM)


def call(body, outs, scratch, cost, *args, specs=None):
    flops, moved = cost
    return pl.pallas_call(
        body,
        out_shape=outs,
        in_specs=specs or [VMEM] * len(args),
        out_specs=jax.tree.map(lambda _: VMEM, outs),
        scratch_shapes=scratch,
        compiler_params=pltpu.CompilerParams(vmem_limit_bytes=24 << 20),
        cost_estimate=pl.CostEstimate(flops=flops, bytes_accessed=moved, transcendentals=0),
    )(*args)


def dot_nt(left, right):
    return lax.dot_general(left, right, NT, preferred_element_type=F32)


def halves(columns):
    mid = columns.shape[0] // 2
    return jnp.concatenate([columns[:mid], columns[mid:]], axis=1)


def pack(cols):
    return jnp.concatenate([cols[:, :128], halves(cols[:, 128:])], axis=0)


def unpack(packed):
    tokens = packed.shape[0] // 3 * 2
    last = packed[tokens:]
    return jnp.concatenate(
        [packed[:tokens], jnp.concatenate([last[:, :HEAD], last[:, HEAD:]], axis=0)], axis=1
    )


def pack_by_parity(cols, odd):
    mid = cols.shape[0] // 2
    even_form = pack(cols)
    odd_form = jnp.concatenate(
        [
            cols[:, HEAD:],
            jnp.concatenate([cols[mid:, :HEAD], cols[:mid, :HEAD]], axis=1),
        ],
        axis=0,
    )
    return jnp.where(odd, odd_form, even_form)


def assemble(blocks, whole, by_heads=False):
    tokens = whole.shape[0]
    n = blocks.shape[0]
    for d in range(0, n, 2):
        even, odd = [group * pow(3, -1, n) % n if by_heads else group for group in (d, d + 1)]
        even_last, odd_last = blocks[even, tokens:].astype(F32), blocks[odd, tokens:].astype(F32)
        left = lax.broadcasted_iota(jnp.int32, even_last.shape, 1) < HEAD
        first = jnp.where(left, even_last, odd_last)
        second = pltpu.roll(jnp.where(left, odd_last, even_last), HEAD, 1)
        at = d // 2 * 384
        whole[:, at : at + 128] = blocks[even, :tokens].astype(whole.dtype)
        whole[:, at + 128 : at + 256] = jnp.concatenate([first, second], axis=0).astype(whole.dtype)
        whole[:, at + 256 : at + 384] = blocks[odd, :tokens].astype(whole.dtype)


def own_columns(ref, rows, me):
    pair = ref[rows, pl.ds(pl.multiple_of(me // 2 * 384, 128), 384)]
    return jnp.where((me & 1) == 1, pair[:, 192:], pair[:, :192])


def norm_into(stream, mod, normed):
    tokens, width = stream.shape
    step = 128
    total = jnp.zeros((tokens, step), F32)
    for at in range(0, width, step):
        total += stream[:, at : at + step]
    center = jnp.sum(total, axis=-1, keepdims=True) / width
    total = jnp.zeros((tokens, step), F32)
    for at in range(0, width, step):
        off = stream[:, at : at + step] - center
        total += off * off
    variance = jnp.sum(total, axis=-1, keepdims=True) / width
    spread = 1.0 / jnp.sqrt(variance + 1e-06)
    for at in range(0, width, step):
        part = (stream[:, at : at + step] - center) * spread
        part = part * (1.0 + mod[0, :, at : at + step]) + mod[1, :, at : at + step]
        normed[:, at : at + step] = part.astype(BF16)


def project(stream, weight, mod, chunks, residual, normed):
    me = lax.axis_index("blk")
    norm_into(stream, mod, normed)
    columns = dot_nt(normed[...], weight[...]).astype(BF16)
    for j in range(3):
        chunks[j][...] = pack(columns[:, 192 * j : 192 * j + 192])
    residual[...] = own_columns(stream, slice(None), me).astype(BF16)


def own_or_other(layer, own, other):
    return jnp.where(lax.axis_index("section") == layer, own, other)


def first_projection(arrived, weight, mod, other_mod, chunk0, chunk1, chunk2, residual, stream, normed, scales):
    rows = stream.shape[0] * 2 // arrived.shape[0]
    half = stream.shape[1] // 2
    n = arrived.shape[0] // 2
    for s in range(2):
        for b in range(n):
            stream[rows * b : rows * b + rows, half * s : half * s + half] = arrived[s * n + b, :rows, :half].astype(F32)
    scales[...] = own_or_other(0, mod[...], other_mod[...])
    project(stream, weight, scales, (chunk0, chunk1, chunk2), residual, normed)


def next_projection(blocks, weight, mod, other_mod, chunk0, chunk1, chunk2, residual, stream, normed, scales):
    assemble(blocks, stream)
    scales[...] = own_or_other(1, mod[...], other_mod[...])
    project(stream, weight, scales, (chunk0, chunk1, chunk2), residual, normed)


def attention(layer, chunk0, chunk1, chunk2, old, fresh, other_fresh, live, attn):
    n = attn.shape[0]
    me, request = lax.axis_index("blk"), lax.axis_index("section")
    first = lax.rem(lax.rem(3 * me, n), 3)
    got = [unpack(chunk[...]) for chunk in (chunk0, chunk1, chunk2)]

    def kind(of):
        at = lax.rem(first + of, 3)
        return jnp.where(at == 0, got[0], jnp.where(at == 1, got[1], got[2]))

    queries = kind(0)
    tokens, width = queries.shape
    heads = width // HEAD
    rows = tokens // n
    token = lax.broadcasted_iota(jnp.int32, (tokens, width), 0)
    key = lax.broadcasted_iota(jnp.int32, (heads * tokens, tokens), 1)
    is_fresh = jnp.zeros((tokens, width), jnp.int32)
    is_live = jnp.zeros((heads * tokens, tokens), jnp.int32)
    for b in range(n):
        flag = own_or_other(layer, fresh[0, request, b], other_fresh[0, request, b])
        is_fresh = jnp.where(token >= b * rows, flag, is_fresh)
        is_live = jnp.where(key >= b * rows, live[request, b], is_live)
    is_fresh, is_live = is_fresh == 1, is_live == 1
    keys = jnp.where(is_fresh, kind(1).astype(F32), old[:, :width].astype(F32)).astype(BF16)
    values = jnp.where(is_fresh, kind(2).astype(F32), old[:, width:].astype(F32)).astype(BF16)
    head_of = lax.broadcasted_iota(jnp.int32, (tokens, width), 1) // HEAD
    queries = queries.astype(F32)
    stacked = jnp.concatenate([jnp.where(head_of == h, queries, 0.0) for h in range(heads)], axis=0)
    scores = dot_nt(stacked.astype(BF16), keys) * 0.125
    scores = jnp.where(is_live, scores, -1e30)
    top = jnp.max(scores, axis=-1, keepdims=True)
    weights = jnp.where(is_live, jnp.exp(scores - top), 0.0)
    total = jnp.sum(weights, axis=-1, keepdims=True)
    mixed = jnp.dot(weights.astype(BF16), values, preferred_element_type=F32) / total
    result = jnp.zeros((tokens, width), F32)
    for h in range(heads):
        result = jnp.where(head_of == h, mixed[h * tokens : (h + 1) * tokens], result)
    packed = pack_by_parity(result, (me & 1) == 1).astype(BF16)
    for d in range(n):
        attn[d] = packed


def layer_columns(layer, blocks, weight, mod, other_mod, residual, whole):
    me = lax.axis_index("blk")
    assemble(blocks, whole, by_heads=True)
    mixed = dot_nt(whole[...], weight[...]).astype(BF16).astype(F32)
    gate = own_or_other(layer, own_columns(mod.at[2], slice(None), me), own_columns(other_mod.at[2], slice(None), me))
    return (residual[...].astype(F32) + gate * mixed).astype(BF16).astype(F32)


def first_output(blocks, weight, mod, other_mod, residual, copies, kept, whole):
    columns = layer_columns(0, blocks, weight, mod, other_mod, residual, whole)
    packed = pack_by_parity(columns, (lax.axis_index("blk") & 1) == 1).astype(BF16)
    for d in range(copies.shape[0]):
        copies[d] = packed
    kept[...] = columns


def last_output(blocks, weight, mod, other_mod, residual, kept, by_token, whole, columns):
    columns[...] = layer_columns(1, blocks, weight, mod, other_mod, residual, whole)
    n = by_token.shape[0] // 2
    rows = columns.shape[0] // n
    for layer, outs in enumerate((kept, columns)):
        for b in range(n):
            by_token[layer * n + b, :rows, :] = outs[rows * b : rows * b + rows, :].astype(BF16)


def first_exchange(hidden, old_keys, old_values, leaving):
    rows, reqs, width = hidden.shape
    n = leaving.shape[0] // reqs
    half = width // 2
    columns = width // n
    second = lax.axis_index("section") == 1
    for s in range(reqs):
        stream, keys, values = [
            jnp.concatenate([ref[i, s : s + 1].astype(F32) for i in range(rows)], axis=0)
            for ref in (hidden, old_keys, old_values)
        ]
        mine = jnp.where(second, stream[:, half:], stream[:, :half]).astype(BF16)
        for b in range(n):
            at = columns * (3 * b % n)
            leaving[s * n + b, :rows, :half] = mine
            leaving[s * n + b, :rows, half:] = jnp.concatenate(
                [keys[:, at : at + columns], values[:, at : at + columns]], axis=1
            ).astype(BF16)


def stale_by_token(arrived, old, rows):
    n = arrived.shape[0] // 2
    per = rows.shape[1] // n
    half = arrived.shape[2] - rows.shape[2]
    for layer in range(2):
        for b in range(n):
            rows[layer, per * b : per * b + per, :] = arrived[layer * n + b, :per, half:].astype(F32)
    old[...] = rows[...].astype(BF16)


def settle_weights(own, other, own_out, other_out, first, first_out, second, second_out, sems):
    at_first = lax.axis_index("section") == 0

    def copies(firsts, seconds):
        pairs = list(zip(firsts + seconds, (first, first_out, second, second_out)))
        return [pltpu.make_async_copy(src, dst, sems.at[i]) for i, (src, dst) in enumerate(pairs)]

    @pl.when(at_first)
    def _():
        started = copies((own, own_out), (other, other_out))
        for copy in started:
            copy.start()
        for copy in started:
            copy.wait()

    @pl.when(jnp.logical_not(at_first))
    def _():
        started = copies((other, other_out), (own, own_out))
        for copy in started:
            copy.start()
        for copy in started:
            copy.wait()


def to_rows(arrived, out, rows):
    n = arrived.shape[0] // 2
    per, columns = out.shape[0], arrived.shape[2]
    for s in range(2):
        for b in range(n):
            rows[s, :per, columns * b : columns * b + columns] = arrived[s * n + b, :per, :].astype(F32)
    for i in range(per):
        out[i] = jnp.concatenate([rows[s, i : i + 1, :] for s in range(2)], axis=0).astype(BF16)


def exchange(blocks, axis):
    return lax.all_to_all(blocks, axis, split_axis=0, concat_axis=0, tiled=True)


def swap_sections(array):
    return lax.ppermute(array, "section", [(0, 1), (1, 0)])


def by_heads(chunks, n):
    inverse = pow(3, -1, n)
    return [
        lax.ppermute(chunk, "blk", [(b, (b + inverse * j) % n) for b in range(n)]) if j else chunk
        for j, chunk in enumerate(chunks)
    ]


def per_device(hidden, qkv_weight, out_weight, modulation, timestep, fresh, live, k_stale, v_stale):
    n = lax.axis_size("blk")
    columns = out_weight.shape[2]
    reqs, rows, width = hidden.shape
    if not (
        columns == 3 * HEAD
        and n % 3 == 1
        and n & (n - 1) == 0
        and reqs == lax.axis_size("section") == 2
        and rows <= 4
    ):
        return per_device_by_token(
            hidden, qkv_weight, out_weight, modulation, timestep, fresh, live, k_stale, v_stale
        )
    tokens = n * rows
    shape = jax.ShapeDtypeStruct
    smem = pl.BlockSpec(memory_space=pltpu.SMEM)
    anywhere = pl.BlockSpec(memory_space=pl.ANY)
    packed = shape((tokens * 3 // 2, 128), BF16)
    copies = shape((n, tokens * 3 // 2, 128), BF16)
    cols = shape((tokens, columns), BF16)

    leaving = call(
        first_exchange,
        shape((reqs * n, 4, width // 2 + 2 * columns), BF16),
        [],
        (0, 1000000),
        jnp.transpose(hidden, (1, 0, 2)),
        jnp.transpose(k_stale[0], (1, 0, 2)),
        jnp.transpose(v_stale[0], (1, 0, 2)),
    )
    arrived = exchange(leaving, ("section", "blk"))

    own_qkv = jnp.swapaxes(qkv_weight[0], 0, 1)
    own_out = jnp.swapaxes(out_weight[0], 0, 1)
    steps = jnp.transpose(modulation, (1, 2, 0, 3))
    mod = lax.dynamic_index_in_dim(steps, timestep[0], 0, keepdims=False)
    weights = call(
        settle_weights,
        [shape(w.shape, BF16) for w in (own_qkv, own_out)] * 2,
        [pltpu.SemaphoreType.DMA((4,))],
        (0, 2 * (own_qkv.size + own_out.size)),
        own_qkv,
        swap_sections(own_qkv),
        own_out,
        swap_sections(own_out),
        specs=[anywhere] * 4,
    )
    mods = (mod, swap_sections(mod))
    flags = (fresh, swap_sections(fresh), live)
    old = call(
        stale_by_token,
        shape((2, tokens, 2 * columns), BF16),
        [pltpu.VMEM((2, tokens, 2 * columns), F32)],
        (0, 200000),
        arrived,
    )

    blocks = arrived
    for layer in range(2):
        *chunks, residual = call(
            next_projection if layer else first_projection,
            [packed, packed, packed, cols],
            [pltpu.VMEM((tokens, width), F32), pltpu.VMEM((tokens, width), BF16), pltpu.VMEM(mod.shape, F32)],
            (2 * tokens * width * 3 * columns, 8 * width * columns),
            blocks,
            weights[2 * layer],
            *mods,
        )
        attn = call(
            functools.partial(attention, layer),
            copies,
            [],
            (8 * tokens * tokens * columns, 300000),
            *by_heads(chunks, n),
            old[layer],
            *flags,
            specs=[VMEM] * 4 + [smem] * 3,
        )
        args = (exchange(attn, "blk"), weights[2 * layer + 1], *mods, residual)
        cost = (2 * tokens * width * columns, 4 * width * columns)
        whole = pltpu.VMEM((tokens, width), BF16)
        if layer == 0:
            leaving, kept = call(first_output, [copies, shape((tokens, columns), F32)], [whole], cost, *args)
            blocks = exchange(leaving, "blk")
        else:
            leaving = call(
                last_output,
                shape((2 * n, 4, columns), BF16),
                [whole, pltpu.VMEM((tokens, columns), F32)],
                cost,
                *args,
                kept,
            )
    result = call(
        to_rows,
        shape((rows, reqs, width), BF16),
        [pltpu.VMEM((2, 8, width), F32)],
        (0, 100000),
        exchange(leaving, ("section", "blk")),
    )
    return jnp.transpose(result, (1, 0, 2))[None]


def solution(mesh):
    return jax.shard_map(
        per_device,
        mesh=mesh,
        in_specs=(
            P(None, "blk", None),
            P("section", None, "blk"),
            P("section", None, "blk"),
            P("section", None, None, None),
            P(),
            P("section", None, None),
            P(),
            P("section", None, "blk", None),
            P("section", None, "blk", None),
        ),
        out_specs=P("section", None, "blk", None),
        check_vma=False,
    )
```

```python
import functools

import jax
import jax.numpy as jnp
from jax import lax
from jax.experimental import pallas as pl
from jax.experimental.pallas import tpu as pltpu
from jax.sharding import PartitionSpec as P


def from_behind(shard, axis, by):
    count = lax.axis_size(axis)
    pairs = [(i, i + by) for i in range(count) if 0 <= i + by < count]
    return lax.ppermute(shard, axis, pairs)


def attend(layer_in, qkv_cols, out_cols, modulate, fresh_own, old_keys, old_values, live):
    stream = layer_in.astype(jnp.float32)
    center = jnp.mean(stream, axis=-1, keepdims=True)
    variance = jnp.mean((stream - center) ** 2, axis=-1, keepdims=True)
    normed = (stream - center) / jnp.sqrt(variance + 1e-06) * (1.0 + modulate[0]) + modulate[1]
    normed_b = normed.astype(jnp.bfloat16)
    columns = jnp.einsum(
        "rnd,dc->rnc",
        lax.all_gather(normed_b, "blk", axis=1, tiled=True),
        qkv_cols,
        preferred_element_type=jnp.float32,
    ).astype(jnp.bfloat16)
    projected = lax.all_to_all(columns, "blk", split_axis=1, concat_axis=2, tiled=True)
    num_req, num_rows, width = layer_in.shape
    queries = projected[:, :, :width]
    new_keys = projected[:, :, width : 2 * width]
    new_values = projected[:, :, 2 * width :]
    use_fresh = (fresh_own == 1)[:, None, None]
    keys = jnp.where(use_fresh, new_keys, old_keys)
    values = jnp.where(use_fresh, new_values, old_values)
    num_heads = width // 64
    num_blocks = live.shape[1]
    q_heads = queries.reshape(num_req, num_rows, num_heads, 64)
    live_float = live.astype(jnp.float32)
    run_max = jnp.full((num_req, num_heads, num_rows), -1e30, jnp.float32)
    key_piece = lax.all_gather(keys, "blk", axis=1, tiled=True)
    value_piece = lax.all_gather(values, "blk", axis=1, tiled=True)
    piece_rows = key_piece.shape[1]
    key_heads = key_piece.reshape(num_req, piece_rows, num_heads, 64)
    value_heads = value_piece.reshape(num_req, piece_rows, num_heads, 64)
    scores = (
        jnp.einsum("qrhd,qnhd->qhrn", q_heads, key_heads, preferred_element_type=jnp.float32)
        * 0.125
    )
    block_ids = jnp.arange(piece_rows) // num_rows
    one_hot = (block_ids[:, None] == jnp.arange(num_blocks)[None, :]).astype(jnp.float32)
    usable = jnp.einsum("qb,nb->qn", live_float, one_hot) > 0.5
    usable = usable[:, None, None, :]
    scores = jnp.where(usable, scores, -1e30)
    new_max = jnp.maximum(run_max, jnp.max(scores, axis=-1))
    weights = jnp.where(usable, jnp.exp(scores - new_max[..., None]), 0.0)
    new_sum = jnp.sum(weights, axis=-1)
    new_acc = jnp.einsum(
        "qhrn,qnhd->qhrd", weights, value_heads.astype(jnp.float32), precision=lax.Precision.HIGHEST
    )
    attn = new_acc / new_sum[..., None]
    attn = jnp.transpose(attn, (0, 2, 1, 3)).reshape(num_req, num_rows, width).astype(jnp.bfloat16)
    out_part = jnp.einsum(
        "rnd,dc->rnc",
        lax.all_gather(attn, "blk", axis=1, tiled=True),
        out_cols,
        preferred_element_type=jnp.float32,
    ).astype(jnp.bfloat16)
    mixed_back = lax.all_to_all(out_part, "blk", split_axis=1, concat_axis=2, tiled=True)
    return (stream + modulate[2] * mixed_back.astype(jnp.float32)).astype(jnp.bfloat16)


def pick_request(array, req_idx):
    return lax.dynamic_index_in_dim(array, req_idx, 0, keepdims=True)


def per_device_by_token(hidden, qkv_weight, out_weight, modulation, timestep, fresh, live, k_stale, v_stale):
    section_idx = lax.axis_index("section")
    block_idx = lax.axis_index("blk")
    steps_all = modulation.shape[1]
    pick_row = (jnp.arange(steps_all) == timestep[0]).astype(jnp.float32)
    modulate = jnp.einsum("t,tcd->cd", pick_row, modulation[0], precision=lax.Precision.HIGHEST)
    num_blocks = fresh.shape[2]
    own_column = (jnp.arange(num_blocks) == block_idx).astype(jnp.int32)
    fresh_own = jnp.sum(fresh[0] * own_column[None, :], axis=1)
    qkv_cols = qkv_weight[0]
    out_cols = out_weight[0]
    old_keys = k_stale[0]
    old_values = v_stale[0]
    num_req = hidden.shape[0]
    received = jnp.zeros_like(hidden[0:1])
    first_out = []
    second_out = []
    for tick_idx in range(num_req + 1):
        if tick_idx < num_req:
            own_input = hidden[tick_idx : tick_idx + 1]
        else:
            own_input = jnp.zeros_like(hidden[0:1])
        layer_in = jnp.where(section_idx == 0, own_input, received)
        req_idx = jnp.clip(tick_idx - section_idx, 0, num_req - 1)
        layer_out = attend(
            layer_in,
            qkv_cols,
            out_cols,
            modulate,
            pick_request(fresh_own, req_idx),
            pick_request(old_keys, req_idx),
            pick_request(old_values, req_idx),
            pick_request(live, req_idx),
        )
        if tick_idx < num_req:
            first_out.append(layer_out)
            received = from_behind(layer_out, "section", 1)
        if tick_idx >= 1:
            second_out.append(layer_out)
    result = jnp.where(
        section_idx == 0, jnp.concatenate(first_out, axis=0), jnp.concatenate(second_out, axis=0)
    )
    return result[None]


HEAD = 64
BF16 = jnp.bfloat16
F32 = jnp.float32
NT = (((1,), (1,)), ((), ()))
VMEM = pl.BlockSpec(memory_space=pltpu.VMEM)
SMEM = pl.BlockSpec(memory_space=pltpu.SMEM)
HBM = pl.BlockSpec(memory_space=pltpu.HBM)
ANY = pl.BlockSpec(memory_space=pl.ANY)


def call(body, outs, scratch, cost, *args, specs=None, spare=40 << 20):
    flops, moved = cost
    return pl.pallas_call(
        body,
        out_shape=outs,
        in_specs=specs or [VMEM] * len(args),
        out_specs=jax.tree.map(lambda _: VMEM, outs),
        scratch_shapes=scratch,
        compiler_params=pltpu.CompilerParams(vmem_limit_bytes=(64 << 20) - spare),
        cost_estimate=pl.CostEstimate(flops=flops, bytes_accessed=moved, transcendentals=0),
    )(*args)


def dot_nt(left, right):
    return lax.dot_general(left, right, NT, preferred_element_type=F32)


def halves(columns):
    mid = columns.shape[0] // 2
    return jnp.concatenate([columns[:mid], columns[mid:]], axis=1)


def pack(cols):
    return jnp.concatenate([cols[:, :128], halves(cols[:, 128:])], axis=0)


def unpack(packed):
    tokens = packed.shape[0] // 3 * 2
    last = packed[tokens:]
    return jnp.concatenate(
        [packed[:tokens], jnp.concatenate([last[:, :HEAD], last[:, HEAD:]], axis=0)], axis=1
    )


def pack_by_parity(cols, odd):
    mid = cols.shape[0] // 2
    even_form = pack(cols)
    odd_form = jnp.concatenate(
        [
            cols[:, HEAD:],
            jnp.concatenate([cols[mid:, :HEAD], cols[:mid, :HEAD]], axis=1),
        ],
        axis=0,
    )
    return jnp.where(odd, odd_form, even_form)


def assemble(blocks, whole, by_heads=False):
    tokens = whole.shape[0]
    n = blocks.shape[0]
    for d in range(0, n, 2):
        even, odd = [group * pow(3, -1, n) % n if by_heads else group for group in (d, d + 1)]
        even_last, odd_last = blocks[even, tokens:].astype(F32), blocks[odd, tokens:].astype(F32)
        left = lax.broadcasted_iota(jnp.int32, even_last.shape, 1) < HEAD
        first = jnp.where(left, even_last, odd_last)
        second = pltpu.roll(jnp.where(left, odd_last, even_last), HEAD, 1)
        at = d // 2 * 384
        whole[:, at : at + 128] = blocks[even, :tokens].astype(whole.dtype)
        whole[:, at + 128 : at + 256] = jnp.concatenate([first, second], axis=0).astype(whole.dtype)
        whole[:, at + 256 : at + 384] = blocks[odd, :tokens].astype(whole.dtype)


def own_columns(ref, rows, me):
    pair = ref[rows, pl.ds(pl.multiple_of(me // 2 * 384, 128), 384)]
    return jnp.where((me & 1) == 1, pair[:, 192:], pair[:, :192])


def norm_into(stream, mod, normed):
    tokens, width = stream.shape
    step = 128
    total = jnp.zeros((tokens, step), F32)
    for at in range(0, width, step):
        total += stream[:, at : at + step]
    center = jnp.sum(total, axis=-1, keepdims=True) / width
    total = jnp.zeros((tokens, step), F32)
    for at in range(0, width, step):
        off = stream[:, at : at + step] - center
        total += off * off
    variance = jnp.sum(total, axis=-1, keepdims=True) / width
    spread = 1.0 / jnp.sqrt(variance + 1e-06)
    for at in range(0, width, step):
        part = (stream[:, at : at + step] - center) * spread
        part = part * (1.0 + mod[0, :, at : at + step]) + mod[1, :, at : at + step]
        normed[:, at : at + step] = part.astype(BF16)


def own_or_other(layer, own, other):
    return jnp.where(lax.axis_index("section") == layer, own, other)


def fetch(layer, own, other, here, sems):
    parts = sems.shape[0]
    rows = here.shape[0] // parts

    def start(source):
        for i in range(parts):
            at = pl.ds(i * rows, rows)
            pltpu.make_async_copy(source.at[at], here.at[at], sems.at[i]).start()

    held = lax.axis_index("section") == layer
    pl.when(held)(lambda: start(own))
    pl.when(jnp.logical_not(held))(lambda: start(other))

    def part(i):
        at = pl.ds(i * rows, rows)
        pltpu.make_async_copy(own.at[at], here.at[at], sems.at[i]).wait()
        return here[at, :]

    return part


def project(stream, part, mod, chunks, residual, normed):
    norm_into(stream, mod, normed)
    residual[...] = own_columns(stream, slice(None), lax.axis_index("blk")).astype(BF16)
    for j in (1, 2, 0):
        chunks[j][...] = pack(dot_nt(normed[...], part(j)).astype(BF16))


def first_projection(arrived, own, other, mod, other_mod, chunk0, chunk1, chunk2, residual, stream, normed, scales, weight, sems):
    part = fetch(0, own, other, weight, sems)
    n = arrived.shape[0]
    rows = stream.shape[0] // n
    for b in range(n):
        stream[rows * b : rows * b + rows, :] = arrived[b, :rows, :].astype(F32)
    scales[...] = own_or_other(0, mod[...], other_mod[...])
    project(stream, part, scales, (chunk0, chunk1, chunk2), residual, normed)


def next_projection(blocks, own, other, mod, other_mod, chunk0, chunk1, chunk2, residual, stream, normed, scales, weight, sems):
    part = fetch(1, own, other, weight, sems)
    assemble(blocks, stream)
    scales[...] = own_or_other(1, mod[...], other_mod[...])
    project(stream, part, scales, (chunk0, chunk1, chunk2), residual, normed)


def attention(layer, chunk0, chunk1, chunk2, old, other_old, mod, other_mod, live, attn):
    n = attn.shape[0]
    me, request = lax.axis_index("blk"), lax.axis_index("section")
    first = lax.rem(lax.rem(3 * me, n), 3)
    got = [unpack(chunk[...]) for chunk in (chunk0, chunk1, chunk2)]

    def kind(of):
        at = lax.rem(first + of, 3)
        return jnp.where(at == 0, got[0], jnp.where(at == 1, got[1], got[2]))

    queries = kind(0)
    tokens, width = queries.shape
    heads = width // HEAD
    rows = tokens // n
    flags = own_or_other(layer, mod[3, :, :128], other_mod[3, :, :128])
    slot = lax.broadcasted_iota(jnp.int32, (tokens, 128), 1)
    block = lax.broadcasted_iota(jnp.int32, (tokens, 128), 0) // rows
    is_fresh = jnp.sum(jnp.where(slot == request * n + block, flags, 0.0), axis=1, keepdims=True) > 0.5
    key = lax.broadcasted_iota(jnp.int32, (1, tokens), 1)
    is_live = jnp.zeros((1, tokens), jnp.int32)
    for b in range(n):
        is_live = jnp.where(key >= b * rows, live[request, b], is_live)
    is_live = is_live == 1
    stale = own_or_other(layer, old[...].astype(F32), other_old[...].astype(F32))
    keys = jnp.where(is_fresh, kind(1).astype(F32), stale[:, :width]).astype(BF16)
    values = jnp.where(is_fresh, kind(2).astype(F32), stale[:, width:]).astype(BF16)
    head_of = lax.broadcasted_iota(jnp.int32, (tokens, width), 1) // HEAD
    queries = queries.astype(F32)
    stacked = jnp.concatenate([jnp.where(head_of == h, queries, 0.0) for h in range(heads)], axis=0)
    scores = dot_nt(stacked.astype(BF16), keys) * 0.125
    scores = jnp.where(is_live, scores, -1e30)
    top = jnp.max(scores, axis=-1, keepdims=True)
    weights = jnp.where(is_live, jnp.exp(scores - top), 0.0)
    total = jnp.sum(weights, axis=-1, keepdims=True)
    mixed = jnp.dot(weights.astype(BF16), values, preferred_element_type=F32) / total
    result = jnp.zeros((tokens, width), F32)
    for h in range(heads):
        result = jnp.where(head_of == h, mixed[h * tokens : (h + 1) * tokens], result)
    packed = pack_by_parity(result, (me & 1) == 1).astype(BF16)
    for d in range(n):
        attn[d] = packed


def layer_columns(layer, blocks, own, other, mod, other_mod, residual, whole, weight, sems):
    me = lax.axis_index("blk")
    part = fetch(layer, own, other, weight, sems)
    assemble(blocks, whole, by_heads=True)
    mixed = dot_nt(whole[...], part(0)).astype(BF16).astype(F32)
    gate = own_or_other(layer, own_columns(mod.at[2], slice(None), me), own_columns(other_mod.at[2], slice(None), me))
    return (residual[...].astype(F32) + gate * mixed).astype(BF16).astype(F32)


def first_output(blocks, own, other, mod, other_mod, residual, copies, kept, whole, weight, sems):
    columns = layer_columns(0, blocks, own, other, mod, other_mod, residual, whole, weight, sems)
    packed = pack_by_parity(columns, (lax.axis_index("blk") & 1) == 1).astype(BF16)
    for d in range(copies.shape[0]):
        copies[d] = packed
    kept[...] = columns


def last_output(blocks, own, other, mod, other_mod, residual, kept, by_token, whole, weight, sems, columns):
    columns[...] = layer_columns(1, blocks, own, other, mod, other_mod, residual, whole, weight, sems)
    n = by_token.shape[0] // 2
    rows = columns.shape[0] // n
    for layer, outs in enumerate((kept, columns)):
        for b in range(n):
            by_token[layer * n + b, :rows, :] = outs[rows * b : rows * b + rows, :].astype(BF16)


def first_exchange(timestep, fresh, hidden, old_keys, old_values, steps, leaving, mod, held, sems):
    copies = [
        pltpu.make_async_copy(steps.at[timestep[0]], mod.at[pl.ds(0, 3)], sems.at[3]),
        *(
            pltpu.make_async_copy(ref, held.at[i], sems.at[i])
            for i, ref in enumerate((hidden, old_keys, old_values))
        ),
    ]
    for copy in copies:
        copy.start()
    rows, reqs, width = hidden.shape
    n = leaving.shape[0]
    columns = width // n
    slot = lax.broadcasted_iota(jnp.int32, (1, width), 1)
    flags = jnp.zeros((1, width), jnp.int32)
    for r in range(reqs):
        for b in range(n):
            flags = jnp.where(slot == r * n + b, fresh[0, r, b], flags)
    mod[3] = flags.astype(F32)
    for copy in copies:
        copy.wait()

    def of_request(which, r):
        return jnp.concatenate([held[which, i, r : r + 1].astype(F32) for i in range(rows)], axis=0)

    mine = jnp.where(lax.axis_index("section") == 0, of_request(0, 0), of_request(0, 1)).astype(BF16)
    stale = [[of_request(which, r) for which in (1, 2)] for r in range(reqs)]
    for b in range(n):
        at = columns * (3 * b % n)
        block = jnp.concatenate([array[:, at : at + columns] for pair in stale for array in pair], axis=1)
        leaving[b, :rows, :] = mine
        for i in range(rows):
            leaving[b, rows : rows + 1, i * 4 * columns : (i + 1) * 4 * columns] = block[i : i + 1].astype(BF16)


def stale_by_token(arrived, keep, give, rows):
    n = arrived.shape[0]
    per = rows.shape[1] // n
    wide = rows.shape[2]
    for b in range(n):
        flat = arrived[b, per : per + 1, :].astype(F32)
        for i in range(per):
            for r in range(2):
                at = (i * 2 + r) * wide
                rows[r, per * b + i : per * b + i + 1, :] = flat[:, at : at + wide]
    first = lax.axis_index("section") == 0
    keep[...] = jnp.where(first, rows[0], rows[1]).astype(BF16)
    give[...] = jnp.where(first, rows[1], rows[0]).astype(BF16)


def to_rows(arrived, out, rows):
    n = arrived.shape[0] // 2
    per, columns = out.shape[0], arrived.shape[2]
    for s in range(2):
        for b in range(n):
            rows[s, :per, columns * b : columns * b + columns] = arrived[s * n + b, :per, :].astype(F32)
    for i in range(per):
        out[i] = jnp.concatenate([rows[s, i : i + 1, :] for s in range(2)], axis=0).astype(BF16)


def exchange(blocks, axis):
    return lax.all_to_all(blocks, axis, split_axis=0, concat_axis=0, tiled=True)


def swap_sections(array):
    return lax.ppermute(array, "section", [(0, 1), (1, 0)])


def by_heads(chunks, n):
    inverse = pow(3, -1, n)
    return [
        lax.ppermute(chunk, "blk", [(b, (b + inverse * j) % n) for b in range(n)]) if j else chunk
        for j, chunk in enumerate(chunks)
    ]


def per_device(hidden, qkv_weight, out_weight, modulation, timestep, fresh, live, k_stale, v_stale):
    n = lax.axis_size("blk")
    columns = out_weight.shape[2]
    reqs, rows, width = hidden.shape
    if not (
        columns == 3 * HEAD
        and n % 3 == 1
        and n & (n - 1) == 0
        and reqs == lax.axis_size("section") == 2
        and rows <= 4
    ):
        return per_device_by_token(
            hidden, qkv_weight, out_weight, modulation, timestep, fresh, live, k_stale, v_stale
        )
    tokens = n * rows
    shape = jax.ShapeDtypeStruct
    packed = shape((tokens * 3 // 2, 128), BF16)
    copies = shape((n, tokens * 3 // 2, 128), BF16)
    cols = shape((tokens, columns), BF16)
    own_qkv = jnp.swapaxes(qkv_weight[0], 0, 1)
    own_out = jnp.swapaxes(out_weight[0], 0, 1)
    qkv = (own_qkv, swap_sections(own_qkv))
    out = (own_out, swap_sections(own_out))

    leaving, mod = call(
        first_exchange,
        [shape((n, 4, width), BF16), shape((4, 1, width), F32)],
        [pltpu.VMEM((3, rows, reqs, width), BF16), pltpu.SemaphoreType.DMA((4,))],
        (0, 1000000),
        timestep,
        fresh,
        jnp.transpose(hidden, (1, 0, 2)),
        jnp.transpose(k_stale[0], (1, 0, 2)),
        jnp.transpose(v_stale[0], (1, 0, 2)),
        jnp.transpose(modulation, (1, 2, 0, 3)),
        specs=[SMEM] * 2 + [HBM] * 4,
        spare=448 << 10,
    )
    mods = (mod, swap_sections(mod))
    arrived = exchange(leaving, "blk")
    keep, give = call(
        stale_by_token,
        [shape((tokens, 2 * columns), BF16)] * 2,
        [pltpu.VMEM((2, tokens, 2 * columns), F32)],
        (0, 200000),
        arrived,
    )
    old = (keep, swap_sections(give))

    blocks = arrived
    for layer in range(2):
        *chunks, residual = call(
            next_projection if layer else first_projection,
            [packed, packed, packed, cols],
            [
                pltpu.VMEM((tokens, width), F32),
                pltpu.VMEM((tokens, width), BF16),
                pltpu.VMEM(mod.shape, F32),
                pltpu.VMEM(own_qkv.shape, BF16),
                pltpu.SemaphoreType.DMA((3,)),
            ],
            (2 * tokens * width * 3 * columns, 8 * width * columns),
            blocks,
            *qkv,
            *mods,
            specs=[VMEM, HBM, ANY, VMEM, VMEM],
            spare=3 << 20,
        )
        attn = call(
            functools.partial(attention, layer),
            copies,
            [],
            (8 * tokens * tokens * columns, 300000),
            *by_heads(chunks, n),
            *old,
            *mods,
            live,
            specs=[VMEM] * 7 + [SMEM],
        )
        args = (exchange(attn, "blk"), *out, *mods, residual)
        cost = (2 * tokens * width * columns, 4 * width * columns)
        held = [pltpu.VMEM((tokens, width), BF16), pltpu.VMEM(own_out.shape, BF16), pltpu.SemaphoreType.DMA((1,))]
        specs = [VMEM, HBM, ANY, VMEM, VMEM, VMEM]
        if layer == 0:
            leaving, kept = call(
                first_output, [copies, shape((tokens, columns), F32)], held, cost, *args, specs=specs
            )
            blocks = exchange(leaving, "blk")
        else:
            leaving = call(
                last_output,
                shape((2 * n, 4, columns), BF16),
                held + [pltpu.VMEM((tokens, columns), F32)],
                cost,
                *args,
                kept,
                specs=specs + [VMEM],
            )
    result = call(
        to_rows,
        shape((rows, reqs, width), BF16),
        [pltpu.VMEM((2, 8, width), F32)],
        (0, 100000),
        exchange(leaving, ("section", "blk")),
    )
    return jnp.transpose(result, (1, 0, 2))[None]


def solution(mesh):
    return jax.shard_map(
        per_device,
        mesh=mesh,
        in_specs=(
            P(None, "blk", None),
            P("section", None, "blk"),
            P("section", None, "blk"),
            P("section", None, None, None),
            P(),
            P("section", None, None),
            P(),
            P("section", None, "blk", None),
            P("section", None, "blk", None),
        ),
        out_specs=P("section", None, "blk", None),
        check_vma=False,
    )
```

```python
import functools

import jax
import jax.numpy as jnp
from jax import lax
from jax.experimental import pallas as pl
from jax.experimental.pallas import tpu as pltpu
from jax.sharding import PartitionSpec as P


def from_behind(shard, axis, by):
    count = lax.axis_size(axis)
    pairs = [(i, i + by) for i in range(count) if 0 <= i + by < count]
    return lax.ppermute(shard, axis, pairs)


def attend(layer_in, qkv_cols, out_cols, modulate, fresh_own, old_keys, old_values, live):
    stream = layer_in.astype(jnp.float32)
    center = jnp.mean(stream, axis=-1, keepdims=True)
    variance = jnp.mean((stream - center) ** 2, axis=-1, keepdims=True)
    normed = (stream - center) / jnp.sqrt(variance + 1e-06) * (1.0 + modulate[0]) + modulate[1]
    normed_b = normed.astype(jnp.bfloat16)
    columns = jnp.einsum(
        "rnd,dc->rnc",
        lax.all_gather(normed_b, "blk", axis=1, tiled=True),
        qkv_cols,
        preferred_element_type=jnp.float32,
    ).astype(jnp.bfloat16)
    projected = lax.all_to_all(columns, "blk", split_axis=1, concat_axis=2, tiled=True)
    num_req, num_rows, width = layer_in.shape
    queries = projected[:, :, :width]
    new_keys = projected[:, :, width : 2 * width]
    new_values = projected[:, :, 2 * width :]
    use_fresh = (fresh_own == 1)[:, None, None]
    keys = jnp.where(use_fresh, new_keys, old_keys)
    values = jnp.where(use_fresh, new_values, old_values)
    num_heads = width // 64
    num_blocks = live.shape[1]
    q_heads = queries.reshape(num_req, num_rows, num_heads, 64)
    live_float = live.astype(jnp.float32)
    run_max = jnp.full((num_req, num_heads, num_rows), -1e30, jnp.float32)
    key_piece = lax.all_gather(keys, "blk", axis=1, tiled=True)
    value_piece = lax.all_gather(values, "blk", axis=1, tiled=True)
    piece_rows = key_piece.shape[1]
    key_heads = key_piece.reshape(num_req, piece_rows, num_heads, 64)
    value_heads = value_piece.reshape(num_req, piece_rows, num_heads, 64)
    scores = (
        jnp.einsum("qrhd,qnhd->qhrn", q_heads, key_heads, preferred_element_type=jnp.float32)
        * 0.125
    )
    block_ids = jnp.arange(piece_rows) // num_rows
    one_hot = (block_ids[:, None] == jnp.arange(num_blocks)[None, :]).astype(jnp.float32)
    usable = jnp.einsum("qb,nb->qn", live_float, one_hot) > 0.5
    usable = usable[:, None, None, :]
    scores = jnp.where(usable, scores, -1e30)
    new_max = jnp.maximum(run_max, jnp.max(scores, axis=-1))
    weights = jnp.where(usable, jnp.exp(scores - new_max[..., None]), 0.0)
    new_sum = jnp.sum(weights, axis=-1)
    new_acc = jnp.einsum(
        "qhrn,qnhd->qhrd", weights, value_heads.astype(jnp.float32), precision=lax.Precision.HIGHEST
    )
    attn = new_acc / new_sum[..., None]
    attn = jnp.transpose(attn, (0, 2, 1, 3)).reshape(num_req, num_rows, width).astype(jnp.bfloat16)
    out_part = jnp.einsum(
        "rnd,dc->rnc",
        lax.all_gather(attn, "blk", axis=1, tiled=True),
        out_cols,
        preferred_element_type=jnp.float32,
    ).astype(jnp.bfloat16)
    mixed_back = lax.all_to_all(out_part, "blk", split_axis=1, concat_axis=2, tiled=True)
    return (stream + modulate[2] * mixed_back.astype(jnp.float32)).astype(jnp.bfloat16)


def pick_request(array, req_idx):
    return lax.dynamic_index_in_dim(array, req_idx, 0, keepdims=True)


def per_device_by_token(hidden, qkv_weight, out_weight, modulation, timestep, fresh, live, k_stale, v_stale):
    section_idx = lax.axis_index("section")
    block_idx = lax.axis_index("blk")
    steps_all = modulation.shape[1]
    pick_row = (jnp.arange(steps_all) == timestep[0]).astype(jnp.float32)
    modulate = jnp.einsum("t,tcd->cd", pick_row, modulation[0], precision=lax.Precision.HIGHEST)
    num_blocks = fresh.shape[2]
    own_column = (jnp.arange(num_blocks) == block_idx).astype(jnp.int32)
    fresh_own = jnp.sum(fresh[0] * own_column[None, :], axis=1)
    qkv_cols = qkv_weight[0]
    out_cols = out_weight[0]
    old_keys = k_stale[0]
    old_values = v_stale[0]
    num_req = hidden.shape[0]
    received = jnp.zeros_like(hidden[0:1])
    first_out = []
    second_out = []
    for tick_idx in range(num_req + 1):
        if tick_idx < num_req:
            own_input = hidden[tick_idx : tick_idx + 1]
        else:
            own_input = jnp.zeros_like(hidden[0:1])
        layer_in = jnp.where(section_idx == 0, own_input, received)
        req_idx = jnp.clip(tick_idx - section_idx, 0, num_req - 1)
        layer_out = attend(
            layer_in,
            qkv_cols,
            out_cols,
            modulate,
            pick_request(fresh_own, req_idx),
            pick_request(old_keys, req_idx),
            pick_request(old_values, req_idx),
            pick_request(live, req_idx),
        )
        if tick_idx < num_req:
            first_out.append(layer_out)
            received = from_behind(layer_out, "section", 1)
        if tick_idx >= 1:
            second_out.append(layer_out)
    result = jnp.where(
        section_idx == 0, jnp.concatenate(first_out, axis=0), jnp.concatenate(second_out, axis=0)
    )
    return result[None]


HEAD = 64
BF16 = jnp.bfloat16
F32 = jnp.float32
NT = (((1,), (1,)), ((), ()))
VMEM = pl.BlockSpec(memory_space=pltpu.VMEM)
SMEM = pl.BlockSpec(memory_space=pltpu.SMEM)
HBM = pl.BlockSpec(memory_space=pltpu.HBM)
ANY = pl.BlockSpec(memory_space=pl.ANY)


def call(body, outs, scratch, cost, *args, specs=None, spare=40 << 20):
    flops, moved = cost
    return pl.pallas_call(
        body,
        out_shape=outs,
        in_specs=specs or [VMEM] * len(args),
        out_specs=jax.tree.map(lambda _: VMEM, outs),
        scratch_shapes=scratch,
        compiler_params=pltpu.CompilerParams(vmem_limit_bytes=(64 << 20) - spare),
        cost_estimate=pl.CostEstimate(flops=flops, bytes_accessed=moved, transcendentals=0),
    )(*args)


def dot_nt(left, right):
    return lax.dot_general(left, right, NT, preferred_element_type=F32)


def halves(columns):
    mid = columns.shape[0] // 2
    return jnp.concatenate([columns[:mid], columns[mid:]], axis=1)


def pack(cols):
    return jnp.concatenate([cols[:, :128], halves(cols[:, 128:])], axis=0)


def unpack(packed):
    tokens = packed.shape[0] // 3 * 2
    last = packed[tokens:]
    return jnp.concatenate(
        [packed[:tokens], jnp.concatenate([last[:, :HEAD], last[:, HEAD:]], axis=0)], axis=1
    )


def pack_by_parity(cols, odd):
    mid = cols.shape[0] // 2
    even_form = pack(cols)
    odd_form = jnp.concatenate(
        [
            cols[:, HEAD:],
            jnp.concatenate([cols[mid:, :HEAD], cols[:mid, :HEAD]], axis=1),
        ],
        axis=0,
    )
    return jnp.where(odd, odd_form, even_form)


def assemble(blocks, whole, by_heads=False):
    tokens = whole.shape[0]
    n = blocks.shape[0]
    for d in range(0, n, 2):
        even, odd = [group * pow(3, -1, n) % n if by_heads else group for group in (d, d + 1)]
        even_last, odd_last = blocks[even, tokens:].astype(F32), blocks[odd, tokens:].astype(F32)
        left = lax.broadcasted_iota(jnp.int32, even_last.shape, 1) < HEAD
        first = jnp.where(left, even_last, odd_last)
        second = pltpu.roll(jnp.where(left, odd_last, even_last), HEAD, 1)
        at = d // 2 * 384
        whole[:, at : at + 128] = blocks[even, :tokens].astype(whole.dtype)
        whole[:, at + 128 : at + 256] = jnp.concatenate([first, second], axis=0).astype(whole.dtype)
        whole[:, at + 256 : at + 384] = blocks[odd, :tokens].astype(whole.dtype)


def own_columns(ref, rows, me):
    pair = ref[rows, pl.ds(pl.multiple_of(me // 2 * 384, 128), 384)]
    return jnp.where((me & 1) == 1, pair[:, 192:], pair[:, :192])


def norm_into(stream, mod, normed):
    tokens, width = stream.shape
    step = 128
    total = jnp.zeros((tokens, step), F32)
    for at in range(0, width, step):
        total += stream[:, at : at + step]
    center = jnp.sum(total, axis=-1, keepdims=True) / width
    total = jnp.zeros((tokens, step), F32)
    for at in range(0, width, step):
        off = stream[:, at : at + step] - center
        total += off * off
    variance = jnp.sum(total, axis=-1, keepdims=True) / width
    spread = 1.0 / jnp.sqrt(variance + 1e-06)
    for at in range(0, width, step):
        part = (stream[:, at : at + step] - center) * spread
        part = part * (1.0 + mod[0, :, at : at + step]) + mod[1, :, at : at + step]
        normed[:, at : at + step] = part.astype(BF16)


def own_or_other(layer, own, other):
    return jnp.where(lax.axis_index("section") == layer, own, other)


def fetch(layer, weights, steps, timestep, here, mod, sems):
    parts = sems.shape[0] - 1
    rows = here.shape[0] // parts

    def copies(which):
        yield pltpu.make_async_copy(steps[which].at[timestep[0]], mod, sems.at[parts])
        for i in range(parts):
            at = pl.ds(i * rows, rows)
            yield pltpu.make_async_copy(weights[which].at[at], here.at[at], sems.at[i])

    def start(which):
        for copy in copies(which):
            copy.start()

    held = lax.axis_index("section") == layer
    pl.when(held)(lambda: start(0))
    pl.when(jnp.logical_not(held))(lambda: start(1))
    first, *rest = copies(0)

    def wait_weight():
        for copy in rest:
            copy.wait()

    return first.wait, wait_weight


def project(stream, weight, waits, mod, chunks, residual, normed):
    wait_mod, wait_weight = waits
    wait_mod()
    norm_into(stream, mod, normed)
    residual[...] = own_columns(stream, slice(None), lax.axis_index("blk")).astype(BF16)
    wait_weight()
    columns = dot_nt(normed[...], weight[...]).astype(BF16)
    for j in range(3):
        chunks[j][...] = pack(columns[:, 192 * j : 192 * j + 192])


def first_projection(timestep, arrived, own, other, steps, other_steps, chunk0, chunk1, chunk2, residual, weight, mod, sems, stream, normed):
    waits = fetch(0, (own, other), (steps, other_steps), timestep, weight, mod, sems)
    n = arrived.shape[0]
    rows = stream.shape[0] // n
    for b in range(n):
        stream[rows * b : rows * b + rows, :] = arrived[b, :rows, :].astype(F32)
    project(stream, weight, waits, mod, (chunk0, chunk1, chunk2), residual, normed)


def next_projection(timestep, blocks, own, other, steps, other_steps, chunk0, chunk1, chunk2, residual, weight, mod, sems, stream, normed):
    waits = fetch(1, (own, other), (steps, other_steps), timestep, weight, mod, sems)
    assemble(blocks, stream)
    project(stream, weight, waits, mod, (chunk0, chunk1, chunk2), residual, normed)


def attention(layer, chunk0, chunk1, chunk2, old, other_old, live, other_out, attn):
    n = attn.shape[0]
    me, request = lax.axis_index("blk"), lax.axis_index("section")
    first = lax.rem(lax.rem(3 * me, n), 3)
    got = [unpack(chunk[...]) for chunk in (chunk0, chunk1, chunk2)]

    def kind(of):
        at = lax.rem(first + of, 3)
        return jnp.where(at == 0, got[0], jnp.where(at == 1, got[1], got[2]))

    queries = kind(0)
    tokens, width = queries.shape
    heads = width // HEAD
    rows = tokens // n
    stale = own_or_other(layer, old[...].astype(F32), other_old[...].astype(F32))
    is_fresh = stale[:, 2 * width : 2 * width + 1] > 0.5
    key = lax.broadcasted_iota(jnp.int32, (1, tokens), 1)
    is_live = jnp.zeros((1, tokens), jnp.int32)
    for b in range(n):
        is_live = jnp.where(key >= b * rows, live[request, b], is_live)
    is_live = is_live == 1
    keys = jnp.where(is_fresh, kind(1).astype(F32), stale[:, :width]).astype(BF16)
    values = jnp.where(is_fresh, kind(2).astype(F32), stale[:, width : 2 * width]).astype(BF16)
    head_of = lax.broadcasted_iota(jnp.int32, (tokens, width), 1) // HEAD
    queries = queries.astype(F32)
    stacked = jnp.concatenate([jnp.where(head_of == h, queries, 0.0) for h in range(heads)], axis=0)
    scores = dot_nt(stacked.astype(BF16), keys) * 0.125
    scores = jnp.where(is_live, scores, -1e30)
    top = jnp.max(scores, axis=-1, keepdims=True)
    weights = jnp.where(is_live, jnp.exp(scores - top), 0.0)
    total = jnp.sum(weights, axis=-1, keepdims=True)
    mixed = jnp.dot(weights.astype(BF16), values, preferred_element_type=F32) / total
    result = jnp.zeros((tokens, width), F32)
    for h in range(heads):
        result = jnp.where(head_of == h, mixed[h * tokens : (h + 1) * tokens], result)
    packed = pack_by_parity(result, (me & 1) == 1).astype(BF16)
    for d in range(n):
        attn[d] = packed


def layer_columns(layer, timestep, blocks, weights, steps, residual, weight, mod, sems, whole):
    me = lax.axis_index("blk")
    wait_mod, wait_weight = fetch(layer, weights, steps, timestep, weight, mod, sems)
    assemble(blocks, whole, by_heads=True)
    wait_mod()
    wait_weight()
    mixed = dot_nt(whole[...], weight[...]).astype(BF16).astype(F32)
    gate = own_columns(mod.at[2], slice(None), me)
    return (residual[...].astype(F32) + gate * mixed).astype(BF16).astype(F32)


def first_output(timestep, blocks, own, other, steps, other_steps, residual, copies, kept, *scratch):
    columns = layer_columns(0, timestep, blocks, (own, other), (steps, other_steps), residual, *scratch)
    packed = pack_by_parity(columns, (lax.axis_index("blk") & 1) == 1).astype(BF16)
    for d in range(copies.shape[0]):
        copies[d] = packed
    kept[...] = columns


def last_output(timestep, blocks, own, other, steps, other_steps, residual, kept, by_token, *scratch):
    *scratch, columns = scratch
    columns[...] = layer_columns(1, timestep, blocks, (own, other), (steps, other_steps), residual, *scratch)
    n = by_token.shape[0] // 2
    rows = columns.shape[0] // n
    for layer, outs in enumerate((kept, columns)):
        for b in range(n):
            by_token[layer * n + b, :rows, :] = outs[rows * b : rows * b + rows, :].astype(BF16)


def first_exchange(hidden, old_keys, old_values, leaving, held, sems):
    copies = [
        pltpu.make_async_copy(ref, held.at[i], sems.at[i])
        for i, ref in enumerate((hidden, old_keys, old_values))
    ]
    for copy in copies:
        copy.start()
    rows, reqs, width = hidden.shape
    n = leaving.shape[0]
    columns = width // n
    for copy in copies:
        copy.wait()

    def of_request(which, r):
        return jnp.concatenate([held[which, i, r : r + 1].astype(F32) for i in range(rows)], axis=0)

    mine = jnp.where(lax.axis_index("section") == 0, of_request(0, 0), of_request(0, 1)).astype(BF16)
    stale = [[of_request(which, r) for which in (1, 2)] for r in range(reqs)]
    for b in range(n):
        at = columns * (3 * b % n)
        block = jnp.concatenate([array[:, at : at + columns] for pair in stale for array in pair], axis=1)
        leaving[b, :rows, :] = mine
        for i in range(rows):
            leaving[b, rows : rows + 1, i * 4 * columns : (i + 1) * 4 * columns] = block[i : i + 1].astype(BF16)


def stale_by_token(arrived, fresh, keep, give, rows):
    n = arrived.shape[0]
    per = rows.shape[1] // n
    wide = rows.shape[2] - 128
    token = lax.broadcasted_iota(jnp.int32, (rows.shape[1], 128), 0)
    for r in range(2):
        flags = jnp.zeros(token.shape, jnp.int32)
        for b in range(n):
            flags = jnp.where(token >= per * b, fresh[0, r, b], flags)
        rows[r, :, wide:] = flags.astype(F32)
    for b in range(n):
        flat = arrived[b, per : per + 1, :].astype(F32)
        for i in range(per):
            for r in range(2):
                at = (i * 2 + r) * wide
                rows[r, per * b + i : per * b + i + 1, :wide] = flat[:, at : at + wide]
    first = lax.axis_index("section") == 0
    keep[...] = jnp.where(first, rows[0], rows[1]).astype(BF16)
    give[...] = jnp.where(first, rows[1], rows[0]).astype(BF16)


def to_rows(arrived, out, rows):
    n = arrived.shape[0] // 2
    per, columns = out.shape[0], arrived.shape[2]
    for s in range(2):
        for b in range(n):
            rows[s, :per, columns * b : columns * b + columns] = arrived[s * n + b, :per, :].astype(F32)
    for i in range(per):
        out[i] = jnp.concatenate([rows[s, i : i + 1, :] for s in range(2)], axis=0).astype(BF16)


def exchange(blocks, axis):
    return lax.all_to_all(blocks, axis, split_axis=0, concat_axis=0, tiled=True)


def swap_sections(array):
    return lax.ppermute(array, "section", [(0, 1), (1, 0)])


def by_heads(chunks, n):
    inverse = pow(3, -1, n)
    return [
        lax.ppermute(chunk, "blk", [(b, (b + inverse * j) % n) for b in range(n)]) if j else chunk
        for j, chunk in enumerate(chunks)
    ]


def per_device(hidden, qkv_weight, out_weight, modulation, timestep, fresh, live, k_stale, v_stale):
    n = lax.axis_size("blk")
    columns = out_weight.shape[2]
    reqs, rows, width = hidden.shape
    if not (
        columns == 3 * HEAD
        and n % 3 == 1
        and n & (n - 1) == 0
        and reqs == lax.axis_size("section") == 2
        and rows <= 4
    ):
        return per_device_by_token(
            hidden, qkv_weight, out_weight, modulation, timestep, fresh, live, k_stale, v_stale
        )
    tokens = n * rows
    shape = jax.ShapeDtypeStruct
    packed = shape((tokens * 3 // 2, 128), BF16)
    copies = shape((n, tokens * 3 // 2, 128), BF16)
    cols = shape((tokens, columns), BF16)
    own_qkv = jnp.swapaxes(qkv_weight[0], 0, 1)
    own_out = jnp.swapaxes(out_weight[0], 0, 1)
    steps = jnp.transpose(modulation, (1, 2, 0, 3))
    qkv = (own_qkv, swap_sections(own_qkv))
    steps = (steps, swap_sections(steps))

    leaving = call(
        first_exchange,
        shape((n, 4, width), BF16),
        [pltpu.VMEM((3, rows, reqs, width), BF16), pltpu.SemaphoreType.DMA((3,))],
        (0, 1000000),
        jnp.transpose(hidden, (1, 0, 2)),
        jnp.transpose(k_stale[0], (1, 0, 2)),
        jnp.transpose(v_stale[0], (1, 0, 2)),
        specs=[HBM] * 3,
        spare=4 << 20,
    )
    arrived, own_out, timestep, fresh, live = lax.optimization_barrier(
        (exchange(leaving, "blk"), own_out, timestep, fresh, live)
    )
    out = (own_out, swap_sections(own_out))
    keep, give = call(
        stale_by_token,
        [shape((tokens, 2 * columns + 128), BF16)] * 2,
        [pltpu.VMEM((2, tokens, 2 * columns + 128), F32)],
        (0, 200000),
        arrived,
        fresh,
        specs=[VMEM, SMEM],
    )
    old = (keep, swap_sections(give))

    def fetched(weight, parts):
        return [
            pltpu.VMEM(weight.shape, BF16),
            pltpu.VMEM(steps[0].shape[1:], F32),
            pltpu.SemaphoreType.DMA((parts + 1,)),
        ]

    blocks = arrived
    for layer in range(2):
        *chunks, residual = call(
            next_projection if layer else first_projection,
            [packed, packed, packed, cols],
            fetched(own_qkv, 12) + [pltpu.VMEM((tokens, width), F32), pltpu.VMEM((tokens, width), BF16)],
            (2 * tokens * width * 3 * columns, 8 * width * columns),
            timestep,
            blocks,
            *qkv,
            *steps,
            specs=[SMEM, VMEM, HBM, ANY, HBM, ANY],
            spare=12 << 20,
        )
        attn = call(
            functools.partial(attention, layer),
            copies,
            [],
            (8 * tokens * tokens * columns, 300000),
            *by_heads(chunks, n),
            *old,
            live,
            out[1],
            specs=[VMEM] * 5 + [SMEM, ANY],
            spare=12 << 20,
        )
        args = (timestep, exchange(attn, "blk"), *out, *steps, residual)
        cost = (2 * tokens * width * columns, 4 * width * columns)
        held = fetched(own_out, 4) + [pltpu.VMEM((tokens, width), BF16)]
        specs = [SMEM, VMEM, HBM, ANY, HBM, ANY, VMEM]
        if layer == 0:
            leaving, kept = call(
                first_output,
                [copies, shape((tokens, columns), F32)],
                held,
                cost,
                *args,
                specs=specs,
                spare=12 << 20,
            )
            blocks = exchange(leaving, "blk")
        else:
            leaving = call(
                last_output,
                shape((2 * n, 4, columns), BF16),
                held + [pltpu.VMEM((tokens, columns), F32)],
                cost,
                *args,
                kept,
                specs=specs + [VMEM],
                spare=12 << 20,
            )
    result = call(
        to_rows,
        shape((rows, reqs, width), BF16),
        [pltpu.VMEM((2, 8, width), F32)],
        (0, 100000),
        exchange(leaving, ("section", "blk")),
    )
    return jnp.transpose(result, (1, 0, 2))[None]


def solution(mesh):
    return jax.shard_map(
        per_device,
        mesh=mesh,
        in_specs=(
            P(None, "blk", None),
            P("section", None, "blk"),
            P("section", None, "blk"),
            P("section", None, None, None),
            P(),
            P("section", None, None),
            P(),
            P("section", None, "blk", None),
            P("section", None, "blk", None),
        ),
        out_specs=P("section", None, "blk", None),
        check_vma=False,
    )
```

```python
import functools

import jax
import jax.numpy as jnp
from jax import lax
from jax.experimental import pallas as pl
from jax.experimental.pallas import tpu as pltpu
from jax.sharding import PartitionSpec as P


def from_behind(shard, axis, by):
    count = lax.axis_size(axis)
    pairs = [(i, i + by) for i in range(count) if 0 <= i + by < count]
    return lax.ppermute(shard, axis, pairs)


def attend(layer_in, qkv_cols, out_cols, modulate, fresh_own, old_keys, old_values, live):
    stream = layer_in.astype(jnp.float32)
    center = jnp.mean(stream, axis=-1, keepdims=True)
    variance = jnp.mean((stream - center) ** 2, axis=-1, keepdims=True)
    normed = (stream - center) / jnp.sqrt(variance + 1e-06) * (1.0 + modulate[0]) + modulate[1]
    normed_b = normed.astype(jnp.bfloat16)
    columns = jnp.einsum(
        "rnd,dc->rnc",
        lax.all_gather(normed_b, "blk", axis=1, tiled=True),
        qkv_cols,
        preferred_element_type=jnp.float32,
    ).astype(jnp.bfloat16)
    projected = lax.all_to_all(columns, "blk", split_axis=1, concat_axis=2, tiled=True)
    num_req, num_rows, width = layer_in.shape
    queries = projected[:, :, :width]
    new_keys = projected[:, :, width : 2 * width]
    new_values = projected[:, :, 2 * width :]
    use_fresh = (fresh_own == 1)[:, None, None]
    keys = jnp.where(use_fresh, new_keys, old_keys)
    values = jnp.where(use_fresh, new_values, old_values)
    num_heads = width // 64
    num_blocks = live.shape[1]
    q_heads = queries.reshape(num_req, num_rows, num_heads, 64)
    live_float = live.astype(jnp.float32)
    run_max = jnp.full((num_req, num_heads, num_rows), -1e30, jnp.float32)
    key_piece = lax.all_gather(keys, "blk", axis=1, tiled=True)
    value_piece = lax.all_gather(values, "blk", axis=1, tiled=True)
    piece_rows = key_piece.shape[1]
    key_heads = key_piece.reshape(num_req, piece_rows, num_heads, 64)
    value_heads = value_piece.reshape(num_req, piece_rows, num_heads, 64)
    scores = (
        jnp.einsum("qrhd,qnhd->qhrn", q_heads, key_heads, preferred_element_type=jnp.float32)
        * 0.125
    )
    block_ids = jnp.arange(piece_rows) // num_rows
    one_hot = (block_ids[:, None] == jnp.arange(num_blocks)[None, :]).astype(jnp.float32)
    usable = jnp.einsum("qb,nb->qn", live_float, one_hot) > 0.5
    usable = usable[:, None, None, :]
    scores = jnp.where(usable, scores, -1e30)
    new_max = jnp.maximum(run_max, jnp.max(scores, axis=-1))
    weights = jnp.where(usable, jnp.exp(scores - new_max[..., None]), 0.0)
    new_sum = jnp.sum(weights, axis=-1)
    new_acc = jnp.einsum(
        "qhrn,qnhd->qhrd", weights, value_heads.astype(jnp.float32), precision=lax.Precision.HIGHEST
    )
    attn = new_acc / new_sum[..., None]
    attn = jnp.transpose(attn, (0, 2, 1, 3)).reshape(num_req, num_rows, width).astype(jnp.bfloat16)
    out_part = jnp.einsum(
        "rnd,dc->rnc",
        lax.all_gather(attn, "blk", axis=1, tiled=True),
        out_cols,
        preferred_element_type=jnp.float32,
    ).astype(jnp.bfloat16)
    mixed_back = lax.all_to_all(out_part, "blk", split_axis=1, concat_axis=2, tiled=True)
    return (stream + modulate[2] * mixed_back.astype(jnp.float32)).astype(jnp.bfloat16)


def pick_request(array, req_idx):
    return lax.dynamic_index_in_dim(array, req_idx, 0, keepdims=True)


def per_device_by_token(hidden, qkv_weight, out_weight, modulation, timestep, fresh, live, k_stale, v_stale):
    section_idx = lax.axis_index("section")
    block_idx = lax.axis_index("blk")
    steps_all = modulation.shape[1]
    pick_row = (jnp.arange(steps_all) == timestep[0]).astype(jnp.float32)
    modulate = jnp.einsum("t,tcd->cd", pick_row, modulation[0], precision=lax.Precision.HIGHEST)
    num_blocks = fresh.shape[2]
    own_column = (jnp.arange(num_blocks) == block_idx).astype(jnp.int32)
    fresh_own = jnp.sum(fresh[0] * own_column[None, :], axis=1)
    qkv_cols = qkv_weight[0]
    out_cols = out_weight[0]
    old_keys = k_stale[0]
    old_values = v_stale[0]
    num_req = hidden.shape[0]
    received = jnp.zeros_like(hidden[0:1])
    first_out = []
    second_out = []
    for tick_idx in range(num_req + 1):
        if tick_idx < num_req:
            own_input = hidden[tick_idx : tick_idx + 1]
        else:
            own_input = jnp.zeros_like(hidden[0:1])
        layer_in = jnp.where(section_idx == 0, own_input, received)
        req_idx = jnp.clip(tick_idx - section_idx, 0, num_req - 1)
        layer_out = attend(
            layer_in,
            qkv_cols,
            out_cols,
            modulate,
            pick_request(fresh_own, req_idx),
            pick_request(old_keys, req_idx),
            pick_request(old_values, req_idx),
            pick_request(live, req_idx),
        )
        if tick_idx < num_req:
            first_out.append(layer_out)
            received = from_behind(layer_out, "section", 1)
        if tick_idx >= 1:
            second_out.append(layer_out)
    result = jnp.where(
        section_idx == 0, jnp.concatenate(first_out, axis=0), jnp.concatenate(second_out, axis=0)
    )
    return result[None]


HEAD = 64
BF16 = jnp.bfloat16
F32 = jnp.float32
NT = (((1,), (1,)), ((), ()))
VMEM = pl.BlockSpec(memory_space=pltpu.VMEM)
SMEM = pl.BlockSpec(memory_space=pltpu.SMEM)
HBM = pl.BlockSpec(memory_space=pltpu.HBM)
ANY = pl.BlockSpec(memory_space=pl.ANY)


def call(body, outs, scratch, cost, *args, specs=None, spare=40 << 20):
    flops, moved = cost
    return pl.pallas_call(
        body,
        out_shape=outs,
        in_specs=specs or [VMEM] * len(args),
        out_specs=jax.tree.map(lambda _: VMEM, outs),
        scratch_shapes=scratch,
        compiler_params=pltpu.CompilerParams(vmem_limit_bytes=(64 << 20) - spare),
        cost_estimate=pl.CostEstimate(flops=flops, bytes_accessed=moved, transcendentals=0),
    )(*args)


def dot_nt(left, right):
    return lax.dot_general(left, right, NT, preferred_element_type=F32)


def halves(columns):
    mid = columns.shape[0] // 2
    return jnp.concatenate([columns[:mid], columns[mid:]], axis=1)


def pack(cols):
    return jnp.concatenate([cols[:, :128], halves(cols[:, 128:])], axis=0)


def unpack(packed):
    tokens = packed.shape[0] // 3 * 2
    last = packed[tokens:]
    return jnp.concatenate(
        [packed[:tokens], jnp.concatenate([last[:, :HEAD], last[:, HEAD:]], axis=0)], axis=1
    )


def pack_by_parity(cols, odd):
    mid = cols.shape[0] // 2
    even_form = pack(cols)
    odd_form = jnp.concatenate(
        [
            cols[:, HEAD:],
            jnp.concatenate([cols[mid:, :HEAD], cols[:mid, :HEAD]], axis=1),
        ],
        axis=0,
    )
    return jnp.where(odd, odd_form, even_form)


def assemble(blocks, whole, by_heads=False):
    tokens = whole.shape[0]
    n = blocks.shape[0]
    for d in range(0, n, 2):
        even, odd = [group * pow(3, -1, n) % n if by_heads else group for group in (d, d + 1)]
        even_last, odd_last = blocks[even, tokens:].astype(F32), blocks[odd, tokens:].astype(F32)
        left = lax.broadcasted_iota(jnp.int32, even_last.shape, 1) < HEAD
        first = jnp.where(left, even_last, odd_last)
        second = pltpu.roll(jnp.where(left, odd_last, even_last), HEAD, 1)
        at = d // 2 * 384
        whole[:, at : at + 128] = blocks[even, :tokens].astype(whole.dtype)
        whole[:, at + 128 : at + 256] = jnp.concatenate([first, second], axis=0).astype(whole.dtype)
        whole[:, at + 256 : at + 384] = blocks[odd, :tokens].astype(whole.dtype)


def own_columns(ref, rows, me):
    pair = ref[rows, pl.ds(pl.multiple_of(me // 2 * 384, 128), 384)]
    return jnp.where((me & 1) == 1, pair[:, 192:], pair[:, :192])


def norm_into(stream, mod, normed):
    tokens, width = stream.shape
    step = 128
    total = jnp.zeros((tokens, step), F32)
    for at in range(0, width, step):
        total += stream[:, at : at + step]
    center = jnp.sum(total, axis=-1, keepdims=True) / width
    total = jnp.zeros((tokens, step), F32)
    for at in range(0, width, step):
        off = stream[:, at : at + step] - center
        total += off * off
    variance = jnp.sum(total, axis=-1, keepdims=True) / width
    spread = 1.0 / jnp.sqrt(variance + 1e-06)
    for at in range(0, width, step):
        part = (stream[:, at : at + step] - center) * spread
        part = part * (1.0 + mod[0, :, at : at + step]) + mod[1, :, at : at + step]
        normed[:, at : at + step] = part.astype(BF16)


def own_or_other(layer, own, other):
    return jnp.where(lax.axis_index("section") == layer, own, other)


def fetch(layer, own, other, here, sems):
    parts = sems.shape[0]
    rows = here.shape[0] // parts

    def copies(source):
        for i in range(parts):
            at = pl.ds(i * rows, rows)
            yield pltpu.make_async_copy(source.at[at], here.at[at], sems.at[i])

    def start(source):
        for copy in copies(source):
            copy.start()

    def wait():
        for copy in copies(own):
            copy.wait()

    held = lax.axis_index("section") == layer
    pl.when(held)(lambda: start(own))
    pl.when(jnp.logical_not(held))(lambda: start(other))
    return wait


def dot_into(layer, left, own, other, product):
    def into(weight):
        product[...] = dot_nt(left[...], weight[...]).astype(product.dtype)

    held = lax.axis_index("section") == layer
    pl.when(held)(lambda: into(own))
    pl.when(jnp.logical_not(held))(lambda: into(other))


def normalise(layer, stream, mod, other_mod, normed, residual, scales):
    scales[...] = own_or_other(layer, mod[...], other_mod[...])
    norm_into(stream, scales, normed)
    residual[...] = own_columns(stream, slice(None), lax.axis_index("blk")).astype(BF16)


def first_projection(arrived, own, other, mod, other_mod, chunk0, chunk1, chunk2, residual, scales, stream, normed, weight, sems):
    wait = fetch(0, own, other, weight, sems)
    n = arrived.shape[0]
    rows = stream.shape[0] // n
    for b in range(n):
        stream[rows * b : rows * b + rows, :] = arrived[b, :rows, :].astype(F32)
    normalise(0, stream, mod, other_mod, normed, residual, scales)
    wait()
    columns = dot_nt(normed[...], weight[...]).astype(BF16)
    for j, chunk in enumerate((chunk0, chunk1, chunk2)):
        chunk[...] = pack(columns[:, 192 * j : 192 * j + 192])


def next_projection(blocks, weight, mod, other_mod, chunk0, chunk1, chunk2, residual, scales, stream, normed):
    assemble(blocks, stream)
    normalise(1, stream, mod, other_mod, normed, residual, scales)
    columns = dot_nt(normed[...], weight[...]).astype(BF16)
    for j, chunk in enumerate((chunk0, chunk1, chunk2)):
        chunk[...] = pack(columns[:, 192 * j : 192 * j + 192])


def attention(layer, chunk0, chunk1, chunk2, old, other_old, live, other_out, attn):
    n = attn.shape[0]
    me, request = lax.axis_index("blk"), lax.axis_index("section")
    first = lax.rem(lax.rem(3 * me, n), 3)
    got = [unpack(chunk[...]) for chunk in (chunk0, chunk1, chunk2)]

    def kind(of):
        at = lax.rem(first + of, 3)
        return jnp.where(at == 0, got[0], jnp.where(at == 1, got[1], got[2]))

    queries = kind(0)
    tokens, width = queries.shape
    heads = width // HEAD
    rows = tokens // n
    stale = own_or_other(layer, old[...].astype(F32), other_old[...].astype(F32))
    is_fresh = stale[:, 2 * width : 2 * width + 1] > 0.5
    key = lax.broadcasted_iota(jnp.int32, (1, tokens), 1)
    is_live = jnp.zeros((1, tokens), jnp.int32)
    for b in range(n):
        is_live = jnp.where(key >= b * rows, live[request, b], is_live)
    is_live = is_live == 1
    keys = jnp.where(is_fresh, kind(1).astype(F32), stale[:, :width]).astype(BF16)
    values = jnp.where(is_fresh, kind(2).astype(F32), stale[:, width : 2 * width]).astype(BF16)
    head_of = lax.broadcasted_iota(jnp.int32, (tokens, width), 1) // HEAD
    queries = queries.astype(F32)
    stacked = jnp.concatenate([jnp.where(head_of == h, queries, 0.0) for h in range(heads)], axis=0)
    scores = dot_nt(stacked.astype(BF16), keys) * 0.125
    scores = jnp.where(is_live, scores, -1e30)
    top = jnp.max(scores, axis=-1, keepdims=True)
    weights = jnp.where(is_live, jnp.exp(scores - top), 0.0)
    total = jnp.sum(weights, axis=-1, keepdims=True)
    mixed = jnp.dot(weights.astype(BF16), values, preferred_element_type=F32) / total
    result = jnp.zeros((tokens, width), F32)
    for h in range(heads):
        result = jnp.where(head_of == h, mixed[h * tokens : (h + 1) * tokens], result)
    packed = pack_by_parity(result, (me & 1) == 1).astype(BF16)
    for d in range(n):
        attn[d] = packed


def layer_columns(layer, blocks, own, other, mod, other_mod, residual, whole, mixed):
    me = lax.axis_index("blk")
    assemble(blocks, whole, by_heads=True)
    dot_into(layer, whole, own, other, mixed)
    gates = own_or_other(layer, mod[2], other_mod[2])
    pairs = [gates[:, at : at + 384] for at in range(0, gates.shape[1], 384)]
    pair = pairs[0]
    for i, other_pair in enumerate(pairs):
        pair = jnp.where(me // 2 == i, other_pair, pair)
    gate = jnp.where((me & 1) == 1, pair[:, 192:], pair[:, :192])
    return (residual[...].astype(F32) + gate * mixed[...].astype(F32)).astype(BF16).astype(F32)


def first_output(blocks, own, other, mod, other_mod, residual, copies, kept, *scratch):
    columns = layer_columns(0, blocks, own, other, mod, other_mod, residual, *scratch)
    packed = pack_by_parity(columns, (lax.axis_index("blk") & 1) == 1).astype(BF16)
    for d in range(copies.shape[0]):
        copies[d] = packed
    kept[...] = columns


def last_output(blocks, own, other, mod, other_mod, residual, kept, by_token, columns, *scratch):
    columns[...] = layer_columns(1, blocks, own, other, mod, other_mod, residual, *scratch)
    n = by_token.shape[0] // 2
    rows = columns.shape[0] // n
    for layer, outs in enumerate((kept, columns)):
        for b in range(n):
            by_token[layer * n + b, :rows, :] = outs[rows * b : rows * b + rows, :].astype(BF16)


def first_exchange(hidden, old_keys, old_values, leaving, held, sems):
    copies = [
        pltpu.make_async_copy(ref, held.at[i], sems.at[i])
        for i, ref in enumerate((hidden, old_keys, old_values))
    ]
    for copy in copies:
        copy.start()
    rows, reqs, width = hidden.shape
    n = leaving.shape[0]
    columns = width // n
    for copy in copies:
        copy.wait()

    def of_request(which, r):
        return jnp.concatenate([held[which, i, r : r + 1].astype(F32) for i in range(rows)], axis=0)

    mine = jnp.where(lax.axis_index("section") == 0, of_request(0, 0), of_request(0, 1)).astype(BF16)
    stale = [[of_request(which, r) for which in (1, 2)] for r in range(reqs)]
    for b in range(n):
        at = columns * (3 * b % n)
        block = jnp.concatenate([array[:, at : at + columns] for pair in stale for array in pair], axis=1)
        leaving[b, :rows, :] = mine
        for i in range(rows):
            leaving[b, rows : rows + 1, i * 4 * columns : (i + 1) * 4 * columns] = block[i : i + 1].astype(BF16)


def stale_by_token(arrived, fresh, own, other, keep, give, weight, rows, sems):
    wait = fetch(1, own, other, weight, sems)
    n = arrived.shape[0]
    per = rows.shape[1] // n
    wide = rows.shape[2] - 128
    token = lax.broadcasted_iota(jnp.int32, (rows.shape[1], 128), 0)
    for r in range(2):
        flags = jnp.zeros(token.shape, jnp.int32)
        for b in range(n):
            flags = jnp.where(token >= per * b, fresh[0, r, b], flags)
        rows[r, :, wide:] = flags.astype(F32)
    for b in range(n):
        flat = arrived[b, per : per + 1, :].astype(F32)
        for i in range(per):
            for r in range(2):
                at = (i * 2 + r) * wide
                rows[r, per * b + i : per * b + i + 1, :wide] = flat[:, at : at + wide]
    first = lax.axis_index("section") == 0
    keep[...] = jnp.where(first, rows[0], rows[1]).astype(BF16)
    give[...] = jnp.where(first, rows[1], rows[0]).astype(BF16)
    wait()


def to_rows(arrived, out, rows):
    n = arrived.shape[0] // 2
    per, columns = out.shape[0], arrived.shape[2]
    for s in range(2):
        for b in range(n):
            rows[s, :per, columns * b : columns * b + columns] = arrived[s * n + b, :per, :].astype(F32)
    for i in range(per):
        out[i] = jnp.concatenate([rows[s, i : i + 1, :] for s in range(2)], axis=0).astype(BF16)


def exchange(blocks, axis):
    return lax.all_to_all(blocks, axis, split_axis=0, concat_axis=0, tiled=True)


def swap_sections(array):
    return lax.ppermute(array, "section", [(0, 1), (1, 0)])


def by_heads(chunks, n):
    inverse = pow(3, -1, n)
    return [
        lax.ppermute(chunk, "blk", [(b, (b + inverse * j) % n) for b in range(n)]) if j else chunk
        for j, chunk in enumerate(chunks)
    ]


def per_device(hidden, qkv_weight, out_weight, modulation, timestep, fresh, live, k_stale, v_stale):
    n = lax.axis_size("blk")
    columns = out_weight.shape[2]
    reqs, rows, width = hidden.shape
    if not (
        columns == 3 * HEAD
        and n % 3 == 1
        and n & (n - 1) == 0
        and reqs == lax.axis_size("section") == 2
        and rows <= 4
    ):
        return per_device_by_token(
            hidden, qkv_weight, out_weight, modulation, timestep, fresh, live, k_stale, v_stale
        )
    tokens = n * rows
    shape = jax.ShapeDtypeStruct
    packed = shape((tokens * 3 // 2, 128), BF16)
    copies = shape((n, tokens * 3 // 2, 128), BF16)
    cols = shape((tokens, columns), BF16)
    own_qkv = jnp.swapaxes(qkv_weight[0], 0, 1)
    own_out = jnp.swapaxes(out_weight[0], 0, 1)
    qkv = (own_qkv, swap_sections(own_qkv))
    steps = jnp.transpose(modulation, (1, 2, 0, 3))
    mod = lax.dynamic_index_in_dim(steps, timestep[0], 0, keepdims=False)

    leaving = call(
        first_exchange,
        shape((n, 4, width), BF16),
        [pltpu.VMEM((3, rows, reqs, width), BF16), pltpu.SemaphoreType.DMA((3,))],
        (0, 1000000),
        jnp.transpose(hidden, (1, 0, 2)),
        jnp.transpose(k_stale[0], (1, 0, 2)),
        jnp.transpose(v_stale[0], (1, 0, 2)),
        specs=[HBM] * 3,
        spare=4 << 20,
    )
    leaving, other_mod = lax.optimization_barrier((leaving, swap_sections(mod)))
    mods = (mod, other_mod)
    arrived, own_out = lax.optimization_barrier((exchange(leaving, "blk"), own_out))
    out = (own_out, swap_sections(own_out))

    blocks = arrived
    for layer in range(2):
        scratch = [
            pltpu.VMEM(mod.shape, F32),
            pltpu.VMEM((tokens, width), F32),
            pltpu.VMEM((tokens, width), BF16),
        ]
        outs = [packed, packed, packed, cols]
        cost = (2 * tokens * width * 3 * columns, 8 * width * columns)
        if layer == 0:
            scratch += [pltpu.VMEM(own_qkv.shape, BF16), pltpu.SemaphoreType.DMA((12,))]
            *chunks, residual = call(
                first_projection,
                outs,
                scratch,
                cost,
                blocks,
                *qkv,
                *mods,
                specs=[VMEM, HBM, ANY, VMEM, VMEM],
                spare=12 << 20,
            )
            arrived, chunks[1] = lax.optimization_barrier((arrived, chunks[1]))
            keep, give, next_qkv = call(
                stale_by_token,
                [shape((tokens, 2 * columns + 128), BF16)] * 2 + [shape(own_qkv.shape, BF16)],
                [pltpu.VMEM((2, tokens, 2 * columns + 128), F32), pltpu.SemaphoreType.DMA((12,))],
                (0, 200000 + 2 * own_qkv.size),
                arrived,
                fresh,
                *qkv,
                specs=[VMEM, SMEM, HBM, ANY],
            )
            old = (keep, swap_sections(give))
        else:
            *chunks, residual = call(next_projection, outs, scratch, cost, blocks, next_qkv, *mods)
        attn = call(
            functools.partial(attention, layer),
            copies,
            [],
            (8 * tokens * tokens * columns, 300000),
            *by_heads(chunks, n),
            *old,
            live,
            out[1],
            specs=[VMEM] * 5 + [SMEM, ANY],
        )
        args = (exchange(attn, "blk"), *out, *mods, residual)
        cost = (2 * tokens * width * columns, 4 * width * columns)
        held = [pltpu.VMEM((tokens, width), BF16), pltpu.VMEM((tokens, columns), BF16)]
        if layer == 0:
            leaving, kept = call(first_output, [copies, shape((tokens, columns), F32)], held, cost, *args)
            blocks = exchange(leaving, "blk")
        else:
            leaving = call(
                last_output,
                shape((2 * n, 4, columns), BF16),
                [pltpu.VMEM((tokens, columns), F32)] + held,
                cost,
                *args,
                kept,
            )
    result = call(
        to_rows,
        shape((rows, reqs, width), BF16),
        [pltpu.VMEM((2, 8, width), F32)],
        (0, 100000),
        exchange(leaving, ("section", "blk")),
    )
    return jnp.transpose(result, (1, 0, 2))[None]


def solution(mesh):
    return jax.shard_map(
        per_device,
        mesh=mesh,
        in_specs=(
            P(None, "blk", None),
            P("section", None, "blk"),
            P("section", None, "blk"),
            P("section", None, None, None),
            P(),
            P("section", None, None),
            P(),
            P("section", None, "blk", None),
            P("section", None, "blk", None),
        ),
        out_specs=P("section", None, "blk", None),
        check_vma=False,
    )
```

```python
import functools

import jax
import jax.numpy as jnp
from jax import lax
from jax.experimental import pallas as pl
from jax.experimental.pallas import tpu as pltpu
from jax.sharding import PartitionSpec as P


def from_behind(shard, axis, by):
    count = lax.axis_size(axis)
    pairs = [(i, i + by) for i in range(count) if 0 <= i + by < count]
    return lax.ppermute(shard, axis, pairs)


def attend(layer_in, qkv_cols, out_cols, modulate, fresh_own, old_keys, old_values, live):
    stream = layer_in.astype(jnp.float32)
    center = jnp.mean(stream, axis=-1, keepdims=True)
    variance = jnp.mean((stream - center) ** 2, axis=-1, keepdims=True)
    normed = (stream - center) / jnp.sqrt(variance + 1e-06) * (1.0 + modulate[0]) + modulate[1]
    normed_b = normed.astype(jnp.bfloat16)
    columns = jnp.einsum(
        "rnd,dc->rnc",
        lax.all_gather(normed_b, "blk", axis=1, tiled=True),
        qkv_cols,
        preferred_element_type=jnp.float32,
    ).astype(jnp.bfloat16)
    projected = lax.all_to_all(columns, "blk", split_axis=1, concat_axis=2, tiled=True)
    num_req, num_rows, width = layer_in.shape
    queries = projected[:, :, :width]
    new_keys = projected[:, :, width : 2 * width]
    new_values = projected[:, :, 2 * width :]
    use_fresh = (fresh_own == 1)[:, None, None]
    keys = jnp.where(use_fresh, new_keys, old_keys)
    values = jnp.where(use_fresh, new_values, old_values)
    num_heads = width // 64
    num_blocks = live.shape[1]
    q_heads = queries.reshape(num_req, num_rows, num_heads, 64)
    live_float = live.astype(jnp.float32)
    run_max = jnp.full((num_req, num_heads, num_rows), -1e30, jnp.float32)
    key_piece = lax.all_gather(keys, "blk", axis=1, tiled=True)
    value_piece = lax.all_gather(values, "blk", axis=1, tiled=True)
    piece_rows = key_piece.shape[1]
    key_heads = key_piece.reshape(num_req, piece_rows, num_heads, 64)
    value_heads = value_piece.reshape(num_req, piece_rows, num_heads, 64)
    scores = (
        jnp.einsum("qrhd,qnhd->qhrn", q_heads, key_heads, preferred_element_type=jnp.float32)
        * 0.125
    )
    block_ids = jnp.arange(piece_rows) // num_rows
    one_hot = (block_ids[:, None] == jnp.arange(num_blocks)[None, :]).astype(jnp.float32)
    usable = jnp.einsum("qb,nb->qn", live_float, one_hot) > 0.5
    usable = usable[:, None, None, :]
    scores = jnp.where(usable, scores, -1e30)
    new_max = jnp.maximum(run_max, jnp.max(scores, axis=-1))
    weights = jnp.where(usable, jnp.exp(scores - new_max[..., None]), 0.0)
    new_sum = jnp.sum(weights, axis=-1)
    new_acc = jnp.einsum(
        "qhrn,qnhd->qhrd", weights, value_heads.astype(jnp.float32), precision=lax.Precision.HIGHEST
    )
    attn = new_acc / new_sum[..., None]
    attn = jnp.transpose(attn, (0, 2, 1, 3)).reshape(num_req, num_rows, width).astype(jnp.bfloat16)
    out_part = jnp.einsum(
        "rnd,dc->rnc",
        lax.all_gather(attn, "blk", axis=1, tiled=True),
        out_cols,
        preferred_element_type=jnp.float32,
    ).astype(jnp.bfloat16)
    mixed_back = lax.all_to_all(out_part, "blk", split_axis=1, concat_axis=2, tiled=True)
    return (stream + modulate[2] * mixed_back.astype(jnp.float32)).astype(jnp.bfloat16)


def pick_request(array, req_idx):
    return lax.dynamic_index_in_dim(array, req_idx, 0, keepdims=True)


def per_device_by_token(hidden, qkv_weight, out_weight, modulation, timestep, fresh, live, k_stale, v_stale):
    section_idx = lax.axis_index("section")
    block_idx = lax.axis_index("blk")
    steps_all = modulation.shape[1]
    pick_row = (jnp.arange(steps_all) == timestep[0]).astype(jnp.float32)
    modulate = jnp.einsum("t,tcd->cd", pick_row, modulation[0], precision=lax.Precision.HIGHEST)
    num_blocks = fresh.shape[2]
    own_column = (jnp.arange(num_blocks) == block_idx).astype(jnp.int32)
    fresh_own = jnp.sum(fresh[0] * own_column[None, :], axis=1)
    qkv_cols = qkv_weight[0]
    out_cols = out_weight[0]
    old_keys = k_stale[0]
    old_values = v_stale[0]
    num_req = hidden.shape[0]
    received = jnp.zeros_like(hidden[0:1])
    first_out = []
    second_out = []
    for tick_idx in range(num_req + 1):
        if tick_idx < num_req:
            own_input = hidden[tick_idx : tick_idx + 1]
        else:
            own_input = jnp.zeros_like(hidden[0:1])
        layer_in = jnp.where(section_idx == 0, own_input, received)
        req_idx = jnp.clip(tick_idx - section_idx, 0, num_req - 1)
        layer_out = attend(
            layer_in,
            qkv_cols,
            out_cols,
            modulate,
            pick_request(fresh_own, req_idx),
            pick_request(old_keys, req_idx),
            pick_request(old_values, req_idx),
            pick_request(live, req_idx),
        )
        if tick_idx < num_req:
            first_out.append(layer_out)
            received = from_behind(layer_out, "section", 1)
        if tick_idx >= 1:
            second_out.append(layer_out)
    result = jnp.where(
        section_idx == 0, jnp.concatenate(first_out, axis=0), jnp.concatenate(second_out, axis=0)
    )
    return result[None]


HEAD = 64
BF16 = jnp.bfloat16
F32 = jnp.float32
NT = (((1,), (1,)), ((), ()))
VMEM = pl.BlockSpec(memory_space=pltpu.VMEM)
SMEM = pl.BlockSpec(memory_space=pltpu.SMEM)
HBM = pl.BlockSpec(memory_space=pltpu.HBM)
ANY = pl.BlockSpec(memory_space=pl.ANY)


def call(body, outs, scratch, cost, *args, specs=None, spare=40 << 20):
    flops, moved = cost
    return pl.pallas_call(
        body,
        out_shape=outs,
        in_specs=specs or [VMEM] * len(args),
        out_specs=jax.tree.map(lambda _: VMEM, outs),
        scratch_shapes=scratch,
        compiler_params=pltpu.CompilerParams(vmem_limit_bytes=(64 << 20) - spare),
        cost_estimate=pl.CostEstimate(flops=flops, bytes_accessed=moved, transcendentals=0),
    )(*args)


def dot_nt(left, right):
    return lax.dot_general(left, right, NT, preferred_element_type=F32)


def halves(columns):
    mid = columns.shape[0] // 2
    return jnp.concatenate([columns[:mid], columns[mid:]], axis=1)


def pack(cols):
    return jnp.concatenate([cols[:, :128], halves(cols[:, 128:])], axis=0)


def unpack(packed):
    tokens = packed.shape[0] // 3 * 2
    last = packed[tokens:]
    return jnp.concatenate(
        [packed[:tokens], jnp.concatenate([last[:, :HEAD], last[:, HEAD:]], axis=0)], axis=1
    )


def pack_by_parity(cols, odd):
    mid = cols.shape[0] // 2
    even_form = pack(cols)
    odd_form = jnp.concatenate(
        [
            cols[:, HEAD:],
            jnp.concatenate([cols[mid:, :HEAD], cols[:mid, :HEAD]], axis=1),
        ],
        axis=0,
    )
    return jnp.where(odd, odd_form, even_form)


def assemble(blocks, whole, by_heads=False):
    tokens = whole.shape[0]
    n = blocks.shape[0]
    for d in range(0, n, 2):
        even, odd = [group * pow(3, -1, n) % n if by_heads else group for group in (d, d + 1)]
        even_last, odd_last = blocks[even, tokens:].astype(F32), blocks[odd, tokens:].astype(F32)
        left = lax.broadcasted_iota(jnp.int32, even_last.shape, 1) < HEAD
        first = jnp.where(left, even_last, odd_last)
        second = pltpu.roll(jnp.where(left, odd_last, even_last), HEAD, 1)
        at = d // 2 * 384
        whole[:, at : at + 128] = blocks[even, :tokens].astype(whole.dtype)
        whole[:, at + 128 : at + 256] = jnp.concatenate([first, second], axis=0).astype(whole.dtype)
        whole[:, at + 256 : at + 384] = blocks[odd, :tokens].astype(whole.dtype)


def own_columns(ref, rows, me):
    pair = ref[rows, pl.ds(pl.multiple_of(me // 2 * 384, 128), 384)]
    return jnp.where((me & 1) == 1, pair[:, 192:], pair[:, :192])


def norm_into(stream, mod, normed):
    tokens, width = stream.shape
    step = 128
    total = jnp.zeros((tokens, step), F32)
    for at in range(0, width, step):
        total += stream[:, at : at + step]
    center = jnp.sum(total, axis=-1, keepdims=True) / width
    total = jnp.zeros((tokens, step), F32)
    for at in range(0, width, step):
        off = stream[:, at : at + step] - center
        total += off * off
    variance = jnp.sum(total, axis=-1, keepdims=True) / width
    spread = 1.0 / jnp.sqrt(variance + 1e-06)
    for at in range(0, width, step):
        part = (stream[:, at : at + step] - center) * spread
        part = part * (1.0 + mod[0, :, at : at + step]) + mod[1, :, at : at + step]
        normed[:, at : at + step] = part.astype(BF16)


def own_or_other(layer, own, other):
    return jnp.where(lax.axis_index("section") == layer, own, other)


def dot_into(layer, left, own, other, product):
    def into(weight):
        product[...] = dot_nt(left[...], weight[...]).astype(product.dtype)

    held = lax.axis_index("section") == layer
    pl.when(held)(lambda: into(own))
    pl.when(jnp.logical_not(held))(lambda: into(other))


def normalise(layer, stream, mod, other_mod, normed, residual, scales):
    scales[...] = own_or_other(layer, mod[...], other_mod[...])
    norm_into(stream, scales, normed)
    residual[...] = own_columns(stream, slice(None), lax.axis_index("blk")).astype(BF16)


def project(layer, stream, own, other, mod, other_mod, chunks, residual, scales, normed, columns):
    normalise(layer, stream, mod, other_mod, normed, residual, scales)
    dot_into(layer, normed, own, other, columns)
    for j, chunk in enumerate(chunks):
        chunk[...] = pack(columns[:, 192 * j : 192 * j + 192])


def first_projection(arrived, own, other, mod, other_mod, chunk0, chunk1, chunk2, residual, stream, *scratch):
    n = arrived.shape[0]
    rows = stream.shape[0] // n
    for b in range(n):
        stream[rows * b : rows * b + rows, :] = arrived[b, :rows, :].astype(F32)
    project(0, stream, own, other, mod, other_mod, (chunk0, chunk1, chunk2), residual, *scratch)


def next_projection(blocks, own, other, mod, other_mod, chunk0, chunk1, chunk2, residual, stream, *scratch):
    assemble(blocks, stream)
    project(1, stream, own, other, mod, other_mod, (chunk0, chunk1, chunk2), residual, *scratch)


def attention(layer, chunk0, chunk1, chunk2, old, fresh, other_fresh, live, other_out, attn):
    n = attn.shape[0]
    me, request = lax.axis_index("blk"), lax.axis_index("section")
    first = lax.rem(lax.rem(3 * me, n), 3)
    got = [unpack(chunk[...]) for chunk in (chunk0, chunk1, chunk2)]

    def kind(of):
        at = lax.rem(first + of, 3)
        return jnp.where(at == 0, got[0], jnp.where(at == 1, got[1], got[2]))

    queries = kind(0)
    tokens, width = queries.shape
    heads = width // HEAD
    rows = tokens // n
    token = lax.broadcasted_iota(jnp.int32, (tokens, 1), 0)
    is_fresh = jnp.zeros((tokens, 1), jnp.int32)
    for b in range(n):
        flag = own_or_other(layer, fresh[0, request, b], other_fresh[0, request, b])
        is_fresh = jnp.where(token >= b * rows, flag, is_fresh)
    is_fresh = is_fresh == 1
    key = lax.broadcasted_iota(jnp.int32, (1, tokens), 1)
    is_live = jnp.zeros((1, tokens), jnp.int32)
    for b in range(n):
        is_live = jnp.where(key >= b * rows, live[request, b], is_live)
    is_live = is_live == 1
    keys = jnp.where(is_fresh, kind(1).astype(F32), old[layer, :, :width].astype(F32)).astype(BF16)
    values = jnp.where(is_fresh, kind(2).astype(F32), old[layer, :, width:].astype(F32)).astype(BF16)
    head_of = lax.broadcasted_iota(jnp.int32, (tokens, width), 1) // HEAD
    queries = queries.astype(F32)
    stacked = jnp.concatenate([jnp.where(head_of == h, queries, 0.0) for h in range(heads)], axis=0)
    scores = dot_nt(stacked.astype(BF16), keys) * 0.125
    scores = jnp.where(is_live, scores, -1e30)
    top = jnp.max(scores, axis=-1, keepdims=True)
    weights = jnp.where(is_live, jnp.exp(scores - top), 0.0)
    total = jnp.sum(weights, axis=-1, keepdims=True)
    mixed = jnp.dot(weights.astype(BF16), values, preferred_element_type=F32) / total
    result = jnp.zeros((tokens, width), F32)
    for h in range(heads):
        result = jnp.where(head_of == h, mixed[h * tokens : (h + 1) * tokens], result)
    packed = pack_by_parity(result, (me & 1) == 1).astype(BF16)
    for d in range(n):
        attn[d] = packed


def layer_columns(layer, blocks, own, other, mod, other_mod, residual, whole, mixed):
    me = lax.axis_index("blk")
    assemble(blocks, whole, by_heads=True)
    dot_into(layer, whole, own, other, mixed)
    gates = own_or_other(layer, mod[2], other_mod[2])
    pairs = [gates[:, at : at + 384] for at in range(0, gates.shape[1], 384)]
    pair = pairs[0]
    for i, other_pair in enumerate(pairs):
        pair = jnp.where(me // 2 == i, other_pair, pair)
    gate = jnp.where((me & 1) == 1, pair[:, 192:], pair[:, :192])
    return (residual[...].astype(F32) + gate * mixed[...].astype(F32)).astype(BF16).astype(F32)


def first_output(blocks, own, other, mod, other_mod, residual, copies, kept, *scratch):
    columns = layer_columns(0, blocks, own, other, mod, other_mod, residual, *scratch)
    packed = pack_by_parity(columns, (lax.axis_index("blk") & 1) == 1).astype(BF16)
    for d in range(copies.shape[0]):
        copies[d] = packed
    kept[...] = columns


def last_output(blocks, own, other, mod, other_mod, residual, kept, by_token, columns, *scratch):
    columns[...] = layer_columns(1, blocks, own, other, mod, other_mod, residual, *scratch)
    n = by_token.shape[0] // 2
    rows = columns.shape[0] // n
    for layer, outs in enumerate((kept, columns)):
        for b in range(n):
            by_token[layer * n + b, :rows, :] = outs[rows * b : rows * b + rows, :].astype(BF16)


def first_exchange(hidden, old_keys, old_values, other_keys, other_values, leaving, held, sems):
    copies = [
        pltpu.make_async_copy(ref, held.at[i], sems.at[i])
        for i, ref in enumerate((hidden, old_keys, old_values, other_keys, other_values))
    ]
    for copy in copies:
        copy.start()
    rows, reqs, width = hidden.shape
    n = leaving.shape[0]
    columns = width // n
    first = lax.axis_index("section") == 0
    for copy in copies:
        copy.wait()

    def of_request(which):
        own = [held[which, i].astype(F32) for i in range(rows)]
        return jnp.concatenate([jnp.where(first, pair[:1], pair[1:]) for pair in own], axis=0)

    mine, *arrays = [of_request(which) for which in range(5)]
    mine = mine.astype(BF16)
    own, other = arrays[:2], arrays[2:]
    stale = [jnp.where(first, a, b) for a, b in zip(own, other)] + [jnp.where(first, b, a) for a, b in zip(own, other)]
    for b in range(n):
        at = columns * (3 * b % n)
        block = jnp.concatenate([array[:, at : at + columns] for array in stale], axis=1)
        leaving[b, :rows, :] = mine
        for i in range(rows):
            leaving[b, rows : rows + 1, i * 4 * columns : (i + 1) * 4 * columns] = block[i : i + 1].astype(BF16)


def stale_by_token(arrived, old, rows):
    n = arrived.shape[0]
    per = rows.shape[1] // n
    wide = rows.shape[2]
    for b in range(n):
        flat = arrived[b, per : per + 1, :].astype(F32)
        for i in range(per):
            for layer in range(2):
                at = (i * 2 + layer) * wide
                rows[layer, per * b + i : per * b + i + 1, :] = flat[:, at : at + wide]
    old[...] = rows[...].astype(BF16)


def to_rows(arrived, out, rows):
    n = arrived.shape[0] // 2
    per, columns = out.shape[0], arrived.shape[2]
    for s in range(2):
        for b in range(n):
            rows[s, :per, columns * b : columns * b + columns] = arrived[s * n + b, :per, :].astype(F32)
    for i in range(per):
        out[i] = jnp.concatenate([rows[s, i : i + 1, :] for s in range(2)], axis=0).astype(BF16)


def exchange(blocks, axis):
    return lax.all_to_all(blocks, axis, split_axis=0, concat_axis=0, tiled=True)


def swap_sections(array):
    return lax.ppermute(array, "section", [(0, 1), (1, 0)])


def by_heads(chunks, n):
    inverse = pow(3, -1, n)
    return [
        lax.ppermute(chunk, "blk", [(b, (b + inverse * j) % n) for b in range(n)]) if j else chunk
        for j, chunk in enumerate(chunks)
    ]


def per_device(hidden, qkv_weight, out_weight, modulation, timestep, fresh, live, k_stale, v_stale):
    n = lax.axis_size("blk")
    columns = out_weight.shape[2]
    reqs, rows, width = hidden.shape
    if not (
        columns == 3 * HEAD
        and n % 3 == 1
        and n & (n - 1) == 0
        and reqs == lax.axis_size("section") == 2
        and rows <= 4
    ):
        return per_device_by_token(
            hidden, qkv_weight, out_weight, modulation, timestep, fresh, live, k_stale, v_stale
        )
    tokens = n * rows
    shape = jax.ShapeDtypeStruct
    packed = shape((tokens * 3 // 2, 128), BF16)
    copies = shape((n, tokens * 3 // 2, 128), BF16)
    cols = shape((tokens, columns), BF16)
    own_qkv = jnp.swapaxes(qkv_weight[0], 0, 1)
    own_out = jnp.swapaxes(out_weight[0], 0, 1)
    steps = jnp.transpose(modulation, (1, 2, 0, 3))
    mod = lax.dynamic_index_in_dim(steps, timestep[0], 0, keepdims=False)
    old_keys = jnp.transpose(k_stale[0], (1, 0, 2))
    old_values = jnp.transpose(v_stale[0], (1, 0, 2))

    leaving = call(
        first_exchange,
        shape((n, 4, width), BF16),
        [pltpu.VMEM((5, rows, reqs, width), BF16), pltpu.SemaphoreType.DMA((5,))],
        (0, 1000000),
        jnp.transpose(hidden, (1, 0, 2)),
        old_keys,
        old_values,
        swap_sections(old_keys),
        swap_sections(old_values),
        specs=[HBM] * 3 + [ANY] * 2,
        spare=4 << 20,
    )
    leaving, other_mod, own_qkv = lax.optimization_barrier((leaving, swap_sections(mod), own_qkv))
    mods = (mod, other_mod)
    qkv = (lax.ppermute(own_qkv, "section", [(0, 0), (1, 1)]), swap_sections(own_qkv))
    arrived, own_out, own_fresh = lax.optimization_barrier((exchange(leaving, "blk"), own_out, fresh))
    out = (own_out, swap_sections(own_out))
    flags = (fresh, swap_sections(own_fresh))

    blocks = arrived
    for layer in range(2):
        *chunks, residual = call(
            next_projection if layer else first_projection,
            [packed, packed, packed, cols],
            [
                pltpu.VMEM((tokens, width), F32),
                pltpu.VMEM(mod.shape, F32),
                pltpu.VMEM((tokens, width), BF16),
                pltpu.VMEM((tokens, 3 * columns), BF16),
            ],
            (2 * tokens * width * 3 * columns, 8 * width * columns),
            blocks,
            *qkv,
            *mods,
        )
        if layer == 0:
            arrived, chunks[1] = lax.optimization_barrier((arrived, chunks[1]))
            old = call(
                stale_by_token,
                shape((2, tokens, 2 * columns), BF16),
                [pltpu.VMEM((2, tokens, 2 * columns), F32)],
                (0, 200000),
                arrived,
            )
        attn = call(
            functools.partial(attention, layer),
            copies,
            [],
            (8 * tokens * tokens * columns, 300000),
            *by_heads(chunks, n),
            old,
            *flags,
            live,
            out[1],
            specs=[VMEM] * 4 + [SMEM] * 3 + [ANY],
        )
        args = (exchange(attn, "blk"), *out, *mods, residual)
        cost = (2 * tokens * width * columns, 4 * width * columns)
        held = [pltpu.VMEM((tokens, width), BF16), pltpu.VMEM((tokens, columns), BF16)]
        if layer == 0:
            leaving, kept = call(first_output, [copies, shape((tokens, columns), F32)], held, cost, *args)
            blocks = exchange(leaving, "blk")
        else:
            leaving = call(
                last_output,
                shape((2 * n, 4, columns), BF16),
                [pltpu.VMEM((tokens, columns), F32)] + held,
                cost,
                *args,
                kept,
            )
    result = call(
        to_rows,
        shape((rows, reqs, width), BF16),
        [pltpu.VMEM((2, 8, width), F32)],
        (0, 100000),
        exchange(leaving, ("section", "blk")),
    )
    return jnp.transpose(result, (1, 0, 2))[None]


def solution(mesh):
    return jax.shard_map(
        per_device,
        mesh=mesh,
        in_specs=(
            P(None, "blk", None),
            P("section", None, "blk"),
            P("section", None, "blk"),
            P("section", None, None, None),
            P(),
            P("section", None, None),
            P(),
            P("section", None, "blk", None),
            P("section", None, "blk", None),
        ),
        out_specs=P("section", None, "blk", None),
        check_vma=False,
    )
```

```python
import functools

import jax
import jax.numpy as jnp
from jax import lax
from jax.experimental import pallas as pl
from jax.experimental.pallas import tpu as pltpu
from jax.sharding import PartitionSpec as P


def from_behind(shard, axis, by):
    count = lax.axis_size(axis)
    pairs = [(i, i + by) for i in range(count) if 0 <= i + by < count]
    return lax.ppermute(shard, axis, pairs)


def attend(layer_in, qkv_cols, out_cols, modulate, fresh_own, old_keys, old_values, live):
    stream = layer_in.astype(jnp.float32)
    center = jnp.mean(stream, axis=-1, keepdims=True)
    variance = jnp.mean((stream - center) ** 2, axis=-1, keepdims=True)
    normed = (stream - center) / jnp.sqrt(variance + 1e-06) * (1.0 + modulate[0]) + modulate[1]
    normed_b = normed.astype(jnp.bfloat16)
    columns = jnp.einsum(
        "rnd,dc->rnc",
        lax.all_gather(normed_b, "blk", axis=1, tiled=True),
        qkv_cols,
        preferred_element_type=jnp.float32,
    ).astype(jnp.bfloat16)
    projected = lax.all_to_all(columns, "blk", split_axis=1, concat_axis=2, tiled=True)
    num_req, num_rows, width = layer_in.shape
    queries = projected[:, :, :width]
    new_keys = projected[:, :, width : 2 * width]
    new_values = projected[:, :, 2 * width :]
    use_fresh = (fresh_own == 1)[:, None, None]
    keys = jnp.where(use_fresh, new_keys, old_keys)
    values = jnp.where(use_fresh, new_values, old_values)
    num_heads = width // 64
    num_blocks = live.shape[1]
    q_heads = queries.reshape(num_req, num_rows, num_heads, 64)
    live_float = live.astype(jnp.float32)
    run_max = jnp.full((num_req, num_heads, num_rows), -1e30, jnp.float32)
    key_piece = lax.all_gather(keys, "blk", axis=1, tiled=True)
    value_piece = lax.all_gather(values, "blk", axis=1, tiled=True)
    piece_rows = key_piece.shape[1]
    key_heads = key_piece.reshape(num_req, piece_rows, num_heads, 64)
    value_heads = value_piece.reshape(num_req, piece_rows, num_heads, 64)
    scores = (
        jnp.einsum("qrhd,qnhd->qhrn", q_heads, key_heads, preferred_element_type=jnp.float32)
        * 0.125
    )
    block_ids = jnp.arange(piece_rows) // num_rows
    one_hot = (block_ids[:, None] == jnp.arange(num_blocks)[None, :]).astype(jnp.float32)
    usable = jnp.einsum("qb,nb->qn", live_float, one_hot) > 0.5
    usable = usable[:, None, None, :]
    scores = jnp.where(usable, scores, -1e30)
    new_max = jnp.maximum(run_max, jnp.max(scores, axis=-1))
    weights = jnp.where(usable, jnp.exp(scores - new_max[..., None]), 0.0)
    new_sum = jnp.sum(weights, axis=-1)
    new_acc = jnp.einsum(
        "qhrn,qnhd->qhrd", weights, value_heads.astype(jnp.float32), precision=lax.Precision.HIGHEST
    )
    attn = new_acc / new_sum[..., None]
    attn = jnp.transpose(attn, (0, 2, 1, 3)).reshape(num_req, num_rows, width).astype(jnp.bfloat16)
    out_part = jnp.einsum(
        "rnd,dc->rnc",
        lax.all_gather(attn, "blk", axis=1, tiled=True),
        out_cols,
        preferred_element_type=jnp.float32,
    ).astype(jnp.bfloat16)
    mixed_back = lax.all_to_all(out_part, "blk", split_axis=1, concat_axis=2, tiled=True)
    return (stream + modulate[2] * mixed_back.astype(jnp.float32)).astype(jnp.bfloat16)


def pick_request(array, req_idx):
    return lax.dynamic_index_in_dim(array, req_idx, 0, keepdims=True)


def per_device_by_token(hidden, qkv_weight, out_weight, modulation, timestep, fresh, live, k_stale, v_stale):
    section_idx = lax.axis_index("section")
    block_idx = lax.axis_index("blk")
    steps_all = modulation.shape[1]
    pick_row = (jnp.arange(steps_all) == timestep[0]).astype(jnp.float32)
    modulate = jnp.einsum("t,tcd->cd", pick_row, modulation[0], precision=lax.Precision.HIGHEST)
    num_blocks = fresh.shape[2]
    own_column = (jnp.arange(num_blocks) == block_idx).astype(jnp.int32)
    fresh_own = jnp.sum(fresh[0] * own_column[None, :], axis=1)
    qkv_cols = qkv_weight[0]
    out_cols = out_weight[0]
    old_keys = k_stale[0]
    old_values = v_stale[0]
    num_req = hidden.shape[0]
    received = jnp.zeros_like(hidden[0:1])
    first_out = []
    second_out = []
    for tick_idx in range(num_req + 1):
        if tick_idx < num_req:
            own_input = hidden[tick_idx : tick_idx + 1]
        else:
            own_input = jnp.zeros_like(hidden[0:1])
        layer_in = jnp.where(section_idx == 0, own_input, received)
        req_idx = jnp.clip(tick_idx - section_idx, 0, num_req - 1)
        layer_out = attend(
            layer_in,
            qkv_cols,
            out_cols,
            modulate,
            pick_request(fresh_own, req_idx),
            pick_request(old_keys, req_idx),
            pick_request(old_values, req_idx),
            pick_request(live, req_idx),
        )
        if tick_idx < num_req:
            first_out.append(layer_out)
            received = from_behind(layer_out, "section", 1)
        if tick_idx >= 1:
            second_out.append(layer_out)
    result = jnp.where(
        section_idx == 0, jnp.concatenate(first_out, axis=0), jnp.concatenate(second_out, axis=0)
    )
    return result[None]


HEAD = 64
BF16 = jnp.bfloat16
F32 = jnp.float32
NT = (((1,), (1,)), ((), ()))
VMEM = pl.BlockSpec(memory_space=pltpu.VMEM)
SMEM = pl.BlockSpec(memory_space=pltpu.SMEM)
HBM = pl.BlockSpec(memory_space=pltpu.HBM)
ANY = pl.BlockSpec(memory_space=pl.ANY)


def call(body, outs, scratch, cost, *args, specs=None, spare=40 << 20):
    flops, moved = cost
    return pl.pallas_call(
        body,
        out_shape=outs,
        in_specs=specs or [VMEM] * len(args),
        out_specs=jax.tree.map(lambda _: VMEM, outs),
        scratch_shapes=scratch,
        compiler_params=pltpu.CompilerParams(vmem_limit_bytes=(64 << 20) - spare),
        cost_estimate=pl.CostEstimate(flops=flops, bytes_accessed=moved, transcendentals=0),
    )(*args)


def dot_nt(left, right):
    return lax.dot_general(left, right, NT, preferred_element_type=F32)


def halves(columns):
    mid = columns.shape[0] // 2
    return jnp.concatenate([columns[:mid], columns[mid:]], axis=1)


def pack(cols):
    return jnp.concatenate([cols[:, :128], halves(cols[:, 128:])], axis=0)


def unpack(packed):
    tokens = packed.shape[0] // 3 * 2
    last = packed[tokens:]
    return jnp.concatenate(
        [packed[:tokens], jnp.concatenate([last[:, :HEAD], last[:, HEAD:]], axis=0)], axis=1
    )


def pack_by_parity(cols, odd):
    mid = cols.shape[0] // 2
    even_form = pack(cols)
    odd_form = jnp.concatenate(
        [
            cols[:, HEAD:],
            jnp.concatenate([cols[mid:, :HEAD], cols[:mid, :HEAD]], axis=1),
        ],
        axis=0,
    )
    return jnp.where(odd, odd_form, even_form)


def assemble(blocks, whole, by_heads=False):
    tokens = whole.shape[0]
    n = blocks.shape[0]
    for d in range(0, n, 2):
        even, odd = [group * pow(3, -1, n) % n if by_heads else group for group in (d, d + 1)]
        even_last, odd_last = blocks[even, tokens:].astype(F32), blocks[odd, tokens:].astype(F32)
        left = lax.broadcasted_iota(jnp.int32, even_last.shape, 1) < HEAD
        first = jnp.where(left, even_last, odd_last)
        second = pltpu.roll(jnp.where(left, odd_last, even_last), HEAD, 1)
        at = d // 2 * 384
        whole[:, at : at + 128] = blocks[even, :tokens].astype(whole.dtype)
        whole[:, at + 128 : at + 256] = jnp.concatenate([first, second], axis=0).astype(whole.dtype)
        whole[:, at + 256 : at + 384] = blocks[odd, :tokens].astype(whole.dtype)


def own_columns(ref, rows, me):
    pair = ref[rows, pl.ds(pl.multiple_of(me // 2 * 384, 128), 384)]
    return jnp.where((me & 1) == 1, pair[:, 192:], pair[:, :192])


def norm_into(stream, mod, normed):
    tokens, width = stream.shape
    step = 128
    total = jnp.zeros((tokens, step), F32)
    for at in range(0, width, step):
        total += stream[:, at : at + step]
    center = jnp.sum(total, axis=-1, keepdims=True) / width
    total = jnp.zeros((tokens, step), F32)
    for at in range(0, width, step):
        off = stream[:, at : at + step] - center
        total += off * off
    variance = jnp.sum(total, axis=-1, keepdims=True) / width
    spread = 1.0 / jnp.sqrt(variance + 1e-06)
    for at in range(0, width, step):
        part = (stream[:, at : at + step] - center) * spread
        part = part * (1.0 + mod[0, :, at : at + step]) + mod[1, :, at : at + step]
        normed[:, at : at + step] = part.astype(BF16)


def own_or_other(layer, own, other):
    return jnp.where(lax.axis_index("section") == layer, own, other)


def dot_into(layer, left, own, other, product):
    def into(weight):
        product[...] = dot_nt(left[...], weight[...]).astype(product.dtype)

    held = lax.axis_index("section") == layer
    pl.when(held)(lambda: into(own))
    pl.when(jnp.logical_not(held))(lambda: into(other))


def normalise(layer, stream, mod, other_mod, normed, residual, scales):
    scales[...] = own_or_other(layer, mod[...], other_mod[...])
    norm_into(stream, scales, normed)
    residual[...] = own_columns(stream, slice(None), lax.axis_index("blk")).astype(BF16)


def chunks_of(columns, chunks):
    for j, chunk in enumerate(chunks):
        chunk[...] = pack(columns[:, 192 * j : 192 * j + 192])


def first_projection(arrived, own, other, mod, other_mod, other_out, chunk0, chunk1, chunk2, residual, stream, scales, normed, columns):
    n = arrived.shape[0]
    rows = stream.shape[0] // n
    for b in range(n):
        stream[rows * b : rows * b + rows, :] = arrived[b, :rows, :].astype(F32)
    normalise(0, stream, mod, other_mod, normed, residual, scales)
    dot_into(0, normed, own, other, columns)
    chunks_of(columns, (chunk0, chunk1, chunk2))


def next_projection(blocks, own, other, mod, other_mod, chunk0, chunk1, chunk2, residual, stream, scales, normed, columns):
    assemble(blocks, stream)
    normalise(1, stream, mod, other_mod, normed, residual, scales)
    dot_into(1, normed, own, other, columns)
    chunks_of(columns, (chunk0, chunk1, chunk2))


def attention(layer, chunk0, chunk1, chunk2, old, fresh, other_fresh, live, attn):
    n = attn.shape[0]
    me, request = lax.axis_index("blk"), lax.axis_index("section")
    first = lax.rem(lax.rem(3 * me, n), 3)
    got = [chunk[...].astype(F32) for chunk in (chunk0, chunk1, chunk2)]

    def kind(of):
        at = lax.rem(first + of, 3)
        return unpack(jnp.where(at == 0, got[0], jnp.where(at == 1, got[1], got[2])))

    queries = kind(0)
    tokens, width = queries.shape
    heads = width // HEAD
    rows = tokens // n
    token = lax.broadcasted_iota(jnp.int32, (tokens, 1), 0)
    is_fresh = jnp.zeros((tokens, 1), jnp.int32)
    for b in range(n):
        flag = own_or_other(layer, fresh[0, request, b], other_fresh[0, request, b])
        is_fresh = jnp.where(token >= b * rows, flag, is_fresh)
    is_fresh = is_fresh == 1
    key = lax.broadcasted_iota(jnp.int32, (1, tokens), 1)
    is_live = jnp.zeros((1, tokens), jnp.int32)
    for b in range(n):
        is_live = jnp.where(key >= b * rows, live[request, b], is_live)
    is_live = is_live == 1
    keys = jnp.where(is_fresh, kind(1), old[layer, :, :width].astype(F32)).astype(BF16)
    values = jnp.where(is_fresh, kind(2), old[layer, :, width:].astype(F32)).astype(BF16)
    head_of = lax.broadcasted_iota(jnp.int32, (tokens, width), 1) // HEAD
    stacked = jnp.concatenate([jnp.where(head_of == h, queries, 0.0) for h in range(heads)], axis=0)
    scores = dot_nt(stacked.astype(BF16), keys) * 0.125
    scores = jnp.where(is_live, scores, -1e30)
    top = jnp.max(scores, axis=-1, keepdims=True)
    weights = jnp.where(is_live, jnp.exp(scores - top), 0.0)
    total = jnp.sum(weights, axis=-1, keepdims=True)
    mixed = jnp.dot(weights.astype(BF16), values, preferred_element_type=F32) * (1.0 / total)
    result = jnp.zeros((tokens, width), F32)
    for h in range(heads):
        result = jnp.where(head_of == h, mixed[h * tokens : (h + 1) * tokens], result)
    packed = pack_by_parity(result, (me & 1) == 1).astype(BF16)
    for d in range(n):
        attn[d] = packed


def layer_columns(layer, blocks, own, other, mod, other_mod, residual, whole, mixed):
    me = lax.axis_index("blk")
    assemble(blocks, whole, by_heads=True)
    dot_into(layer, whole, own, other, mixed)
    gates = own_or_other(layer, mod[2], other_mod[2])
    pairs = [gates[:, at : at + 384] for at in range(0, gates.shape[1], 384)]
    pair = pairs[0]
    for i, other_pair in enumerate(pairs):
        pair = jnp.where(me // 2 == i, other_pair, pair)
    gate = jnp.where((me & 1) == 1, pair[:, 192:], pair[:, :192])
    return (residual[...].astype(F32) + gate * mixed[...].astype(F32)).astype(BF16).astype(F32)


def first_output(blocks, own, other, mod, other_mod, residual, copies, kept, *scratch):
    columns = layer_columns(0, blocks, own, other, mod, other_mod, residual, *scratch)
    packed = pack_by_parity(columns, (lax.axis_index("blk") & 1) == 1).astype(BF16)
    for d in range(copies.shape[0]):
        copies[d] = packed
    kept[...] = columns


def last_output(blocks, own, other, mod, other_mod, residual, kept, by_token, columns, *scratch):
    columns[...] = layer_columns(1, blocks, own, other, mod, other_mod, residual, *scratch)
    n = by_token.shape[0] // 2
    rows = columns.shape[0] // n
    for layer, outs in enumerate((kept, columns)):
        for b in range(n):
            by_token[layer * n + b, :rows, :] = outs[rows * b : rows * b + rows, :].astype(BF16)


def first_exchange(hidden, old_keys, old_values, other_keys, other_values, leaving, held, sems):
    copies = [
        pltpu.make_async_copy(ref, held.at[i], sems.at[i])
        for i, ref in enumerate((hidden, old_keys, old_values, other_keys, other_values))
    ]
    for copy in copies:
        copy.start()
    rows, reqs, width = hidden.shape
    n = leaving.shape[0]
    columns = width // n
    first = lax.axis_index("section") == 0
    for copy in copies:
        copy.wait()

    def of_request(which):
        own = [held[which, i].astype(F32) for i in range(rows)]
        return jnp.concatenate([jnp.where(first, pair[:1], pair[1:]) for pair in own], axis=0)

    mine, *arrays = [of_request(which) for which in range(5)]
    mine = mine.astype(BF16)
    own, other = arrays[:2], arrays[2:]
    stale = [jnp.where(first, a, b) for a, b in zip(own, other)] + [jnp.where(first, b, a) for a, b in zip(own, other)]
    for b in range(n):
        at = columns * (3 * b % n)
        block = jnp.concatenate([array[:, at : at + columns] for array in stale], axis=1)
        leaving[b, :rows, :] = mine
        for i in range(rows):
            leaving[b, rows : rows + 1, i * 4 * columns : (i + 1) * 4 * columns] = block[i : i + 1].astype(BF16)


def stale_by_token(arrived, old, rows):
    n = arrived.shape[0]
    per = rows.shape[1] // n
    wide = rows.shape[2]
    for b in range(n):
        flat = arrived[b, per : per + 1, :].astype(F32)
        for i in range(per):
            for layer in range(2):
                at = (i * 2 + layer) * wide
                rows[layer, per * b + i : per * b + i + 1, :] = flat[:, at : at + wide]
    old[...] = rows[...].astype(BF16)


def to_rows(arrived, out, rows):
    n = arrived.shape[0] // 2
    per, columns = out.shape[0], arrived.shape[2]
    for s in range(2):
        for b in range(n):
            rows[s, :per, columns * b : columns * b + columns] = arrived[s * n + b, :per, :].astype(F32)
    for i in range(per):
        out[i] = jnp.concatenate([rows[s, i : i + 1, :] for s in range(2)], axis=0).astype(BF16)


def exchange(blocks, axis):
    return lax.all_to_all(blocks, axis, split_axis=0, concat_axis=0, tiled=True)


def swap_sections(array):
    return lax.ppermute(array, "section", [(0, 1), (1, 0)])


def by_heads(chunks, n):
    inverse = pow(3, -1, n)
    return [
        lax.ppermute(chunk, "blk", [(b, (b + inverse * j) % n) for b in range(n)]) if j else chunk
        for j, chunk in enumerate(chunks)
    ]


def per_device(hidden, qkv_weight, out_weight, modulation, timestep, fresh, live, k_stale, v_stale):
    n = lax.axis_size("blk")
    columns = out_weight.shape[2]
    reqs, rows, width = hidden.shape
    if not (
        columns == 3 * HEAD
        and n % 3 == 1
        and n & (n - 1) == 0
        and reqs == lax.axis_size("section") == 2
        and rows <= 4
    ):
        return per_device_by_token(
            hidden, qkv_weight, out_weight, modulation, timestep, fresh, live, k_stale, v_stale
        )
    tokens = n * rows
    shape = jax.ShapeDtypeStruct
    packed = shape((tokens * 3 // 2, 128), BF16)
    copies = shape((n, tokens * 3 // 2, 128), BF16)
    cols = shape((tokens, columns), BF16)
    own_qkv = jnp.swapaxes(qkv_weight[0], 0, 1)
    own_out = jnp.swapaxes(out_weight[0], 0, 1)
    steps = jnp.transpose(modulation, (1, 2, 0, 3))
    mod = lax.dynamic_index_in_dim(steps, timestep[0], 0, keepdims=False)
    old_keys = jnp.transpose(k_stale[0], (1, 0, 2))
    old_values = jnp.transpose(v_stale[0], (1, 0, 2))

    leaving = call(
        first_exchange,
        shape((n, 4, width), BF16),
        [pltpu.VMEM((5, rows, reqs, width), BF16), pltpu.SemaphoreType.DMA((5,))],
        (0, 1000000),
        jnp.transpose(hidden, (1, 0, 2)),
        old_keys,
        old_values,
        swap_sections(old_keys),
        swap_sections(old_values),
        specs=[HBM] * 3 + [ANY] * 2,
        spare=4 << 20,
    )
    leaving, other_mod, other_fresh, sent_qkv, sent_out = lax.optimization_barrier(
        (leaving, swap_sections(mod), swap_sections(fresh), own_qkv, own_out)
    )
    mods = (mod, other_mod)
    flags = (fresh, other_fresh)
    other_qkv, other_out = swap_sections(sent_qkv), swap_sections(sent_out)
    out = (own_out, other_out)
    held_qkv = lax.ppermute(sent_qkv, "section", [(0, 0)])
    arrived = exchange(leaving, "blk")

    blocks = arrived
    for layer in range(2):
        *chunks, residual = call(
            next_projection if layer else first_projection,
            [packed, packed, packed, cols],
            [
                pltpu.VMEM((tokens, width), F32),
                pltpu.VMEM(mod.shape, F32),
                pltpu.VMEM((tokens, width), BF16),
                pltpu.VMEM((tokens, 3 * columns), BF16),
            ],
            (2 * tokens * width * 3 * columns, 8 * width * columns),
            blocks,
            *((own_qkv, other_qkv, *mods) if layer else (held_qkv, other_qkv, *mods, other_out)),
            **({} if layer else {"specs": [VMEM] * 5 + [ANY]}),
        )
        if layer == 0:
            arrived, chunks[1] = lax.optimization_barrier((arrived, chunks[1]))
            old = call(
                stale_by_token,
                shape((2, tokens, 2 * columns), BF16),
                [pltpu.VMEM((2, tokens, 2 * columns), F32)],
                (0, 200000),
                arrived,
            )
        attn = call(
            functools.partial(attention, layer),
            copies,
            [],
            (8 * tokens * tokens * columns, 300000),
            *by_heads(chunks, n),
            old,
            *flags,
            live,
            specs=[VMEM] * 4 + [SMEM] * 3,
        )
        args = (exchange(attn, "blk"), *out, *mods, residual)
        cost = (2 * tokens * width * columns, 4 * width * columns)
        held = [pltpu.VMEM((tokens, width), BF16), pltpu.VMEM((tokens, columns), BF16)]
        if layer == 0:
            leaving, kept = call(first_output, [copies, shape((tokens, columns), F32)], held, cost, *args)
            blocks = exchange(leaving, "blk")
        else:
            leaving = call(
                last_output,
                shape((2 * n, 4, columns), BF16),
                [pltpu.VMEM((tokens, columns), F32)] + held,
                cost,
                *args,
                kept,
            )
    result = call(
        to_rows,
        shape((rows, reqs, width), BF16),
        [pltpu.VMEM((2, 8, width), F32)],
        (0, 100000),
        exchange(leaving, ("section", "blk")),
    )
    return jnp.transpose(result, (1, 0, 2))[None]


def solution(mesh):
    return jax.shard_map(
        per_device,
        mesh=mesh,
        in_specs=(
            P(None, "blk", None),
            P("section", None, "blk"),
            P("section", None, "blk"),
            P("section", None, None, None),
            P(),
            P("section", None, None),
            P(),
            P("section", None, "blk", None),
            P("section", None, "blk", None),
        ),
        out_specs=P("section", None, "blk", None),
        check_vma=False,
    )
```

```python
import functools

import jax
import jax.numpy as jnp
from jax import lax
from jax.experimental import pallas as pl
from jax.experimental.pallas import tpu as pltpu
from jax.sharding import PartitionSpec as P


def from_behind(shard, axis, by):
    count = lax.axis_size(axis)
    pairs = [(i, i + by) for i in range(count) if 0 <= i + by < count]
    return lax.ppermute(shard, axis, pairs)


def attend(layer_in, qkv_cols, out_cols, modulate, fresh_own, old_keys, old_values, live):
    stream = layer_in.astype(jnp.float32)
    center = jnp.mean(stream, axis=-1, keepdims=True)
    variance = jnp.mean((stream - center) ** 2, axis=-1, keepdims=True)
    normed = (stream - center) / jnp.sqrt(variance + 1e-06) * (1.0 + modulate[0]) + modulate[1]
    normed_b = normed.astype(jnp.bfloat16)
    columns = jnp.einsum(
        "rnd,dc->rnc",
        lax.all_gather(normed_b, "blk", axis=1, tiled=True),
        qkv_cols,
        preferred_element_type=jnp.float32,
    ).astype(jnp.bfloat16)
    projected = lax.all_to_all(columns, "blk", split_axis=1, concat_axis=2, tiled=True)
    num_req, num_rows, width = layer_in.shape
    queries = projected[:, :, :width]
    new_keys = projected[:, :, width : 2 * width]
    new_values = projected[:, :, 2 * width :]
    use_fresh = (fresh_own == 1)[:, None, None]
    keys = jnp.where(use_fresh, new_keys, old_keys)
    values = jnp.where(use_fresh, new_values, old_values)
    num_heads = width // 64
    num_blocks = live.shape[1]
    q_heads = queries.reshape(num_req, num_rows, num_heads, 64)
    live_float = live.astype(jnp.float32)
    run_max = jnp.full((num_req, num_heads, num_rows), -1e30, jnp.float32)
    key_piece = lax.all_gather(keys, "blk", axis=1, tiled=True)
    value_piece = lax.all_gather(values, "blk", axis=1, tiled=True)
    piece_rows = key_piece.shape[1]
    key_heads = key_piece.reshape(num_req, piece_rows, num_heads, 64)
    value_heads = value_piece.reshape(num_req, piece_rows, num_heads, 64)
    scores = (
        jnp.einsum("qrhd,qnhd->qhrn", q_heads, key_heads, preferred_element_type=jnp.float32)
        * 0.125
    )
    block_ids = jnp.arange(piece_rows) // num_rows
    one_hot = (block_ids[:, None] == jnp.arange(num_blocks)[None, :]).astype(jnp.float32)
    usable = jnp.einsum("qb,nb->qn", live_float, one_hot) > 0.5
    usable = usable[:, None, None, :]
    scores = jnp.where(usable, scores, -1e30)
    new_max = jnp.maximum(run_max, jnp.max(scores, axis=-1))
    weights = jnp.where(usable, jnp.exp(scores - new_max[..., None]), 0.0)
    new_sum = jnp.sum(weights, axis=-1)
    new_acc = jnp.einsum(
        "qhrn,qnhd->qhrd", weights, value_heads.astype(jnp.float32), precision=lax.Precision.HIGHEST
    )
    attn = new_acc / new_sum[..., None]
    attn = jnp.transpose(attn, (0, 2, 1, 3)).reshape(num_req, num_rows, width).astype(jnp.bfloat16)
    out_part = jnp.einsum(
        "rnd,dc->rnc",
        lax.all_gather(attn, "blk", axis=1, tiled=True),
        out_cols,
        preferred_element_type=jnp.float32,
    ).astype(jnp.bfloat16)
    mixed_back = lax.all_to_all(out_part, "blk", split_axis=1, concat_axis=2, tiled=True)
    return (stream + modulate[2] * mixed_back.astype(jnp.float32)).astype(jnp.bfloat16)


def pick_request(array, req_idx):
    return lax.dynamic_index_in_dim(array, req_idx, 0, keepdims=True)


def per_device_by_token(hidden, qkv_weight, out_weight, modulation, timestep, fresh, live, k_stale, v_stale):
    section_idx = lax.axis_index("section")
    block_idx = lax.axis_index("blk")
    steps_all = modulation.shape[1]
    pick_row = (jnp.arange(steps_all) == timestep[0]).astype(jnp.float32)
    modulate = jnp.einsum("t,tcd->cd", pick_row, modulation[0], precision=lax.Precision.HIGHEST)
    num_blocks = fresh.shape[2]
    own_column = (jnp.arange(num_blocks) == block_idx).astype(jnp.int32)
    fresh_own = jnp.sum(fresh[0] * own_column[None, :], axis=1)
    qkv_cols = qkv_weight[0]
    out_cols = out_weight[0]
    old_keys = k_stale[0]
    old_values = v_stale[0]
    num_req = hidden.shape[0]
    received = jnp.zeros_like(hidden[0:1])
    first_out = []
    second_out = []
    for tick_idx in range(num_req + 1):
        if tick_idx < num_req:
            own_input = hidden[tick_idx : tick_idx + 1]
        else:
            own_input = jnp.zeros_like(hidden[0:1])
        layer_in = jnp.where(section_idx == 0, own_input, received)
        req_idx = jnp.clip(tick_idx - section_idx, 0, num_req - 1)
        layer_out = attend(
            layer_in,
            qkv_cols,
            out_cols,
            modulate,
            pick_request(fresh_own, req_idx),
            pick_request(old_keys, req_idx),
            pick_request(old_values, req_idx),
            pick_request(live, req_idx),
        )
        if tick_idx < num_req:
            first_out.append(layer_out)
            received = from_behind(layer_out, "section", 1)
        if tick_idx >= 1:
            second_out.append(layer_out)
    result = jnp.where(
        section_idx == 0, jnp.concatenate(first_out, axis=0), jnp.concatenate(second_out, axis=0)
    )
    return result[None]


HEAD = 64
BF16 = jnp.bfloat16
F32 = jnp.float32
NT = (((1,), (1,)), ((), ()))
VMEM = pl.BlockSpec(memory_space=pltpu.VMEM)
SMEM = pl.BlockSpec(memory_space=pltpu.SMEM)
HBM = pl.BlockSpec(memory_space=pltpu.HBM)
ANY = pl.BlockSpec(memory_space=pl.ANY)


def call(body, outs, scratch, cost, *args, specs=None, spare=40 << 20):
    flops, moved = cost
    return pl.pallas_call(
        body,
        out_shape=outs,
        in_specs=specs or [VMEM] * len(args),
        out_specs=jax.tree.map(lambda _: VMEM, outs),
        scratch_shapes=scratch,
        compiler_params=pltpu.CompilerParams(vmem_limit_bytes=(64 << 20) - spare),
        cost_estimate=pl.CostEstimate(flops=flops, bytes_accessed=moved, transcendentals=0),
    )(*args)


def dot_nt(left, right):
    return lax.dot_general(left, right, NT, preferred_element_type=F32)


def halves(columns):
    mid = columns.shape[0] // 2
    return jnp.concatenate([columns[:mid], columns[mid:]], axis=1)


def pack(cols):
    return jnp.concatenate([cols[:, :128], halves(cols[:, 128:])], axis=0)


def unpack(packed):
    tokens = packed.shape[0] // 3 * 2
    last = packed[tokens:]
    return jnp.concatenate(
        [packed[:tokens], jnp.concatenate([last[:, :HEAD], last[:, HEAD:]], axis=0)], axis=1
    )


def pack_by_parity(cols, odd):
    mid = cols.shape[0] // 2
    even_form = pack(cols)
    odd_form = jnp.concatenate(
        [
            cols[:, HEAD:],
            jnp.concatenate([cols[mid:, :HEAD], cols[:mid, :HEAD]], axis=1),
        ],
        axis=0,
    )
    return jnp.where(odd, odd_form, even_form)


def assemble(blocks, whole, by_heads=False):
    tokens = whole.shape[0]
    n = blocks.shape[0]
    for d in range(0, n, 2):
        even, odd = [group * pow(3, -1, n) % n if by_heads else group for group in (d, d + 1)]
        even_last, odd_last = blocks[even, tokens:].astype(F32), blocks[odd, tokens:].astype(F32)
        left = lax.broadcasted_iota(jnp.int32, even_last.shape, 1) < HEAD
        first = jnp.where(left, even_last, odd_last)
        second = pltpu.roll(jnp.where(left, odd_last, even_last), HEAD, 1)
        at = d // 2 * 384
        whole[:, at : at + 128] = blocks[even, :tokens].astype(whole.dtype)
        whole[:, at + 128 : at + 256] = jnp.concatenate([first, second], axis=0).astype(whole.dtype)
        whole[:, at + 256 : at + 384] = blocks[odd, :tokens].astype(whole.dtype)


def own_columns(ref, rows, me):
    pair = ref[rows, pl.ds(pl.multiple_of(me // 2 * 384, 128), 384)]
    return jnp.where((me & 1) == 1, pair[:, 192:], pair[:, :192])


def norm_into(stream, mod, normed):
    tokens, width = stream.shape
    step = 128
    total = jnp.zeros((tokens, step), F32)
    for at in range(0, width, step):
        total += stream[:, at : at + step]
    center = jnp.sum(total, axis=-1, keepdims=True) / width
    total = jnp.zeros((tokens, step), F32)
    for at in range(0, width, step):
        off = stream[:, at : at + step] - center
        total += off * off
    variance = jnp.sum(total, axis=-1, keepdims=True) / width
    spread = 1.0 / jnp.sqrt(variance + 1e-06)
    for at in range(0, width, step):
        part = (stream[:, at : at + step] - center) * spread
        part = part * (1.0 + mod[0, :, at : at + step]) + mod[1, :, at : at + step]
        normed[:, at : at + step] = part.astype(BF16)


def own_or_other(layer, own, other):
    return jnp.where(lax.axis_index("section") == layer, own, other)


def dot_into(layer, left, own, other, product):
    def into(weight):
        product[...] = dot_nt(left[...], weight[...]).astype(product.dtype)

    held = lax.axis_index("section") == layer
    pl.when(held)(lambda: into(own))
    pl.when(jnp.logical_not(held))(lambda: into(other))


def normalise(layer, stream, mod, other_mod, normed, residual, scales):
    scales[...] = own_or_other(layer, mod[...], other_mod[...])
    norm_into(stream, scales, normed)
    residual[...] = own_columns(stream, slice(None), lax.axis_index("blk")).astype(BF16)


def chunks_of(columns, chunks):
    for j, chunk in enumerate(chunks):
        chunk[...] = pack(columns[:, 192 * j : 192 * j + 192])


def fetch(layer, own, other, here, sems):
    parts = sems.shape[0]
    size = here.shape[0] // parts

    def copies(source):
        for i in range(parts):
            at = pl.ds(i * size, size)
            yield pltpu.make_async_copy(source.at[at], here.at[at], sems.at[i])

    def start(source):
        for copy in copies(source):
            copy.start()

    def wait():
        for copy in copies(own):
            copy.wait()

    held = lax.axis_index("section") == layer
    pl.when(held)(lambda: start(own))
    pl.when(jnp.logical_not(held))(lambda: start(other))
    return wait


def first_projection(arrived, own, other, mod, other_mod, other_out, chunk0, chunk1, chunk2, residual, stream, scales, normed, weight, sems):
    wait = fetch(0, own, other, weight, sems)
    n = arrived.shape[0]
    rows = stream.shape[0] // n
    for b in range(n):
        stream[rows * b : rows * b + rows, :] = arrived[b, :rows, :].astype(F32)
    normalise(0, stream, mod, other_mod, normed, residual, scales)
    wait()
    chunks_of(dot_nt(normed[...], weight[...]).astype(BF16), (chunk0, chunk1, chunk2))


def next_projection(blocks, weight, mod, other_mod, chunk0, chunk1, chunk2, residual, stream, scales, normed):
    assemble(blocks, stream)
    normalise(1, stream, mod, other_mod, normed, residual, scales)
    chunks_of(dot_nt(normed[...], weight[...]).astype(BF16), (chunk0, chunk1, chunk2))


def attention(layer, chunk0, chunk1, chunk2, old, fresh, other_fresh, live, attn):
    n = attn.shape[0]
    me, request = lax.axis_index("blk"), lax.axis_index("section")
    first = lax.rem(lax.rem(3 * me, n), 3)
    got = [chunk[...].astype(F32) for chunk in (chunk0, chunk1, chunk2)]

    def kind(of):
        at = lax.rem(first + of, 3)
        return unpack(jnp.where(at == 0, got[0], jnp.where(at == 1, got[1], got[2])))

    queries = kind(0)
    tokens, width = queries.shape
    heads = width // HEAD
    rows = tokens // n
    token = lax.broadcasted_iota(jnp.int32, (tokens, 1), 0)
    is_fresh = jnp.zeros((tokens, 1), jnp.int32)
    for b in range(n):
        flag = own_or_other(layer, fresh[0, request, b], other_fresh[0, request, b])
        is_fresh = jnp.where(token >= b * rows, flag, is_fresh)
    is_fresh = is_fresh == 1
    key = lax.broadcasted_iota(jnp.int32, (1, tokens), 1)
    is_live = jnp.zeros((1, tokens), jnp.int32)
    for b in range(n):
        is_live = jnp.where(key >= b * rows, live[request, b], is_live)
    is_live = is_live == 1
    keys = jnp.where(is_fresh, kind(1), old[layer, :, :width].astype(F32)).astype(BF16)
    values = jnp.where(is_fresh, kind(2), old[layer, :, width:].astype(F32)).astype(BF16)
    head_of = lax.broadcasted_iota(jnp.int32, (tokens, width), 1) // HEAD
    stacked = jnp.concatenate([jnp.where(head_of == h, queries, 0.0) for h in range(heads)], axis=0)
    scores = dot_nt(stacked.astype(BF16), keys) * 0.125
    scores = jnp.where(is_live, scores, -1e30)
    top = jnp.max(scores, axis=-1, keepdims=True)
    weights = jnp.where(is_live, jnp.exp(scores - top), 0.0)
    total = jnp.sum(weights, axis=-1, keepdims=True)
    mixed = jnp.dot(weights.astype(BF16), values, preferred_element_type=F32) * (1.0 / total)
    result = jnp.zeros((tokens, width), F32)
    for h in range(heads):
        result = jnp.where(head_of == h, mixed[h * tokens : (h + 1) * tokens], result)
    packed = pack_by_parity(result, (me & 1) == 1).astype(BF16)
    for d in range(n):
        attn[d] = packed


def layer_columns(layer, blocks, own, other, mod, other_mod, residual, whole, mixed):
    me = lax.axis_index("blk")
    assemble(blocks, whole, by_heads=True)
    dot_into(layer, whole, own, other, mixed)
    gates = own_or_other(layer, mod[2], other_mod[2])
    pairs = [gates[:, at : at + 384] for at in range(0, gates.shape[1], 384)]
    pair = pairs[0]
    for i, other_pair in enumerate(pairs):
        pair = jnp.where(me // 2 == i, other_pair, pair)
    gate = jnp.where((me & 1) == 1, pair[:, 192:], pair[:, :192])
    return (residual[...].astype(F32) + gate * mixed[...].astype(F32)).astype(BF16).astype(F32)


def first_output(blocks, own, other, mod, other_mod, residual, copies, kept, *scratch):
    columns = layer_columns(0, blocks, own, other, mod, other_mod, residual, *scratch)
    packed = pack_by_parity(columns, (lax.axis_index("blk") & 1) == 1).astype(BF16)
    for d in range(copies.shape[0]):
        copies[d] = packed
    kept[...] = columns


def last_output(blocks, own, other, mod, other_mod, residual, kept, by_token, columns, *scratch):
    columns[...] = layer_columns(1, blocks, own, other, mod, other_mod, residual, *scratch)
    n = by_token.shape[0] // 2
    rows = columns.shape[0] // n
    for layer, outs in enumerate((kept, columns)):
        for b in range(n):
            by_token[layer * n + b, :rows, :] = outs[rows * b : rows * b + rows, :].astype(BF16)


def first_exchange(hidden, old_keys, old_values, other_keys, other_values, leaving, held, sems):
    copies = [
        pltpu.make_async_copy(ref, held.at[i], sems.at[i])
        for i, ref in enumerate((hidden, old_keys, old_values, other_keys, other_values))
    ]
    for copy in copies:
        copy.start()
    rows, reqs, width = hidden.shape
    n = leaving.shape[0]
    columns = width // n
    first = lax.axis_index("section") == 0
    for copy in copies:
        copy.wait()

    def of_request(which):
        own = [held[which, i].astype(F32) for i in range(rows)]
        return jnp.concatenate([jnp.where(first, pair[:1], pair[1:]) for pair in own], axis=0)

    mine, *arrays = [of_request(which) for which in range(5)]
    mine = mine.astype(BF16)
    own, other = arrays[:2], arrays[2:]
    stale = [jnp.where(first, a, b) for a, b in zip(own, other)] + [jnp.where(first, b, a) for a, b in zip(own, other)]
    for b in range(n):
        at = columns * (3 * b % n)
        block = jnp.concatenate([array[:, at : at + columns] for array in stale], axis=1)
        leaving[b, :rows, :] = mine
        for i in range(rows):
            leaving[b, rows : rows + 1, i * 4 * columns : (i + 1) * 4 * columns] = block[i : i + 1].astype(BF16)


def settle(arrived, own, other, old, weight, rows, sems):
    wait = fetch(1, own, other, weight, sems)
    n = arrived.shape[0]
    per = rows.shape[1] // n
    wide = rows.shape[2]
    for b in range(n):
        flat = arrived[b, per : per + 1, :].astype(F32)
        for i in range(per):
            for layer in range(2):
                at = (i * 2 + layer) * wide
                rows[layer, per * b + i : per * b + i + 1, :] = flat[:, at : at + wide]
    old[...] = rows[...].astype(BF16)
    wait()


def to_rows(arrived, out, rows):
    n = arrived.shape[0] // 2
    per, columns = out.shape[0], arrived.shape[2]
    for s in range(2):
        for b in range(n):
            rows[s, :per, columns * b : columns * b + columns] = arrived[s * n + b, :per, :].astype(F32)
    for i in range(per):
        out[i] = jnp.concatenate([rows[s, i : i + 1, :] for s in range(2)], axis=0).astype(BF16)


def exchange(blocks, axis):
    return lax.all_to_all(blocks, axis, split_axis=0, concat_axis=0, tiled=True)


def swap_sections(array):
    return lax.ppermute(array, "section", [(0, 1), (1, 0)])


def by_heads(chunks, n):
    inverse = pow(3, -1, n)
    return [
        lax.ppermute(chunk, "blk", [(b, (b + inverse * j) % n) for b in range(n)]) if j else chunk
        for j, chunk in enumerate(chunks)
    ]


def per_device(hidden, qkv_weight, out_weight, modulation, timestep, fresh, live, k_stale, v_stale):
    n = lax.axis_size("blk")
    columns = out_weight.shape[2]
    reqs, rows, width = hidden.shape
    if not (
        columns == 3 * HEAD
        and n % 3 == 1
        and n & (n - 1) == 0
        and reqs == lax.axis_size("section") == 2
        and rows <= 4
    ):
        return per_device_by_token(
            hidden, qkv_weight, out_weight, modulation, timestep, fresh, live, k_stale, v_stale
        )
    tokens = n * rows
    shape = jax.ShapeDtypeStruct
    packed = shape((tokens * 3 // 2, 128), BF16)
    copies = shape((n, tokens * 3 // 2, 128), BF16)
    cols = shape((tokens, columns), BF16)
    own_qkv = jnp.swapaxes(qkv_weight[0], 0, 1)
    own_out = jnp.swapaxes(out_weight[0], 0, 1)
    steps = jnp.transpose(modulation, (1, 2, 0, 3))
    mod = lax.dynamic_index_in_dim(steps, timestep[0], 0, keepdims=False)
    old_keys = jnp.transpose(k_stale[0], (1, 0, 2))
    old_values = jnp.transpose(v_stale[0], (1, 0, 2))

    small = [swap_sections(array) for array in (old_keys, old_values, mod, fresh)]
    (other_keys, other_values, other_mod, other_fresh), sent_qkv, sent_out = lax.optimization_barrier(
        (small, own_qkv, own_out)
    )
    other_qkv, other_out = swap_sections(sent_qkv), swap_sections(sent_out)
    out = (own_out, other_out)
    leaving = call(
        first_exchange,
        shape((n, 4, width), BF16),
        [pltpu.VMEM((5, rows, reqs, width), BF16), pltpu.SemaphoreType.DMA((5,))],
        (0, 1000000),
        jnp.transpose(hidden, (1, 0, 2)),
        old_keys,
        old_values,
        other_keys,
        other_values,
        specs=[HBM] * 3 + [ANY] * 2,
        spare=4 << 20,
    )
    mods = (mod, other_mod)
    flags = (fresh, other_fresh)
    arrived = exchange(leaving, "blk")

    blocks = arrived
    for layer in range(2):
        scratch = [
            pltpu.VMEM((tokens, width), F32),
            pltpu.VMEM(mod.shape, F32),
            pltpu.VMEM((tokens, width), BF16),
        ]
        outs = [packed, packed, packed, cols]
        cost = (2 * tokens * width * 3 * columns, 8 * width * columns)
        sems = pltpu.SemaphoreType.DMA((36,))
        if layer == 0:
            *chunks, residual = call(
                first_projection,
                outs,
                scratch + [pltpu.VMEM(own_qkv.shape, BF16), sems],
                cost,
                blocks,
                own_qkv,
                other_qkv,
                *mods,
                other_out,
                specs=[VMEM, HBM, ANY, VMEM, VMEM, ANY],
                spare=12 << 20,
            )
            arrived, chunks[1] = lax.optimization_barrier((arrived, chunks[1]))
            old, next_qkv = call(
                settle,
                [shape((2, tokens, 2 * columns), BF16), shape(own_qkv.shape, BF16)],
                [pltpu.VMEM((2, tokens, 2 * columns), F32), sems],
                (0, 200000),
                arrived,
                own_qkv,
                other_qkv,
                specs=[VMEM, HBM, ANY],
            )
        else:
            *chunks, residual = call(next_projection, outs, scratch, cost, blocks, next_qkv, *mods)
        attn = call(
            functools.partial(attention, layer),
            copies,
            [],
            (8 * tokens * tokens * columns, 300000),
            *by_heads(chunks, n),
            old,
            *flags,
            live,
            specs=[VMEM] * 4 + [SMEM] * 3,
        )
        args = (exchange(attn, "blk"), *out, *mods, residual)
        cost = (2 * tokens * width * columns, 4 * width * columns)
        held = [pltpu.VMEM((tokens, width), BF16), pltpu.VMEM((tokens, columns), BF16)]
        if layer == 0:
            leaving, kept = call(first_output, [copies, shape((tokens, columns), F32)], held, cost, *args)
            blocks = exchange(leaving, "blk")
        else:
            leaving = call(
                last_output,
                shape((2 * n, 4, columns), BF16),
                [pltpu.VMEM((tokens, columns), F32)] + held,
                cost,
                *args,
                kept,
            )
    result = call(
        to_rows,
        shape((rows, reqs, width), BF16),
        [pltpu.VMEM((2, 8, width), F32)],
        (0, 100000),
        exchange(leaving, ("section", "blk")),
    )
    return jnp.transpose(result, (1, 0, 2))[None]


def solution(mesh):
    return jax.shard_map(
        per_device,
        mesh=mesh,
        in_specs=(
            P(None, "blk", None),
            P("section", None, "blk"),
            P("section", None, "blk"),
            P("section", None, None, None),
            P(),
            P("section", None, None),
            P(),
            P("section", None, "blk", None),
            P("section", None, "blk", None),
        ),
        out_specs=P("section", None, "blk", None),
        check_vma=False,
    )
```

```python
import functools

import jax
import jax.numpy as jnp
from jax import lax
from jax.experimental import pallas as pl
from jax.experimental.pallas import tpu as pltpu
from jax.sharding import PartitionSpec as P


def from_behind(shard, axis, by):
    count = lax.axis_size(axis)
    pairs = [(i, i + by) for i in range(count) if 0 <= i + by < count]
    return lax.ppermute(shard, axis, pairs)


def attend(layer_in, qkv_cols, out_cols, modulate, fresh_own, old_keys, old_values, live):
    stream = layer_in.astype(jnp.float32)
    center = jnp.mean(stream, axis=-1, keepdims=True)
    variance = jnp.mean((stream - center) ** 2, axis=-1, keepdims=True)
    normed = (stream - center) / jnp.sqrt(variance + 1e-06) * (1.0 + modulate[0]) + modulate[1]
    normed_b = normed.astype(jnp.bfloat16)
    columns = jnp.einsum(
        "rnd,dc->rnc",
        lax.all_gather(normed_b, "blk", axis=1, tiled=True),
        qkv_cols,
        preferred_element_type=jnp.float32,
    ).astype(jnp.bfloat16)
    projected = lax.all_to_all(columns, "blk", split_axis=1, concat_axis=2, tiled=True)
    num_req, num_rows, width = layer_in.shape
    queries = projected[:, :, :width]
    new_keys = projected[:, :, width : 2 * width]
    new_values = projected[:, :, 2 * width :]
    use_fresh = (fresh_own == 1)[:, None, None]
    keys = jnp.where(use_fresh, new_keys, old_keys)
    values = jnp.where(use_fresh, new_values, old_values)
    num_heads = width // 64
    num_blocks = live.shape[1]
    q_heads = queries.reshape(num_req, num_rows, num_heads, 64)
    live_float = live.astype(jnp.float32)
    run_max = jnp.full((num_req, num_heads, num_rows), -1e30, jnp.float32)
    key_piece = lax.all_gather(keys, "blk", axis=1, tiled=True)
    value_piece = lax.all_gather(values, "blk", axis=1, tiled=True)
    piece_rows = key_piece.shape[1]
    key_heads = key_piece.reshape(num_req, piece_rows, num_heads, 64)
    value_heads = value_piece.reshape(num_req, piece_rows, num_heads, 64)
    scores = (
        jnp.einsum("qrhd,qnhd->qhrn", q_heads, key_heads, preferred_element_type=jnp.float32)
        * 0.125
    )
    block_ids = jnp.arange(piece_rows) // num_rows
    one_hot = (block_ids[:, None] == jnp.arange(num_blocks)[None, :]).astype(jnp.float32)
    usable = jnp.einsum("qb,nb->qn", live_float, one_hot) > 0.5
    usable = usable[:, None, None, :]
    scores = jnp.where(usable, scores, -1e30)
    new_max = jnp.maximum(run_max, jnp.max(scores, axis=-1))
    weights = jnp.where(usable, jnp.exp(scores - new_max[..., None]), 0.0)
    new_sum = jnp.sum(weights, axis=-1)
    new_acc = jnp.einsum(
        "qhrn,qnhd->qhrd", weights, value_heads.astype(jnp.float32), precision=lax.Precision.HIGHEST
    )
    attn = new_acc / new_sum[..., None]
    attn = jnp.transpose(attn, (0, 2, 1, 3)).reshape(num_req, num_rows, width).astype(jnp.bfloat16)
    out_part = jnp.einsum(
        "rnd,dc->rnc",
        lax.all_gather(attn, "blk", axis=1, tiled=True),
        out_cols,
        preferred_element_type=jnp.float32,
    ).astype(jnp.bfloat16)
    mixed_back = lax.all_to_all(out_part, "blk", split_axis=1, concat_axis=2, tiled=True)
    return (stream + modulate[2] * mixed_back.astype(jnp.float32)).astype(jnp.bfloat16)


def pick_request(array, req_idx):
    return lax.dynamic_index_in_dim(array, req_idx, 0, keepdims=True)


def per_device_by_token(hidden, qkv_weight, out_weight, modulation, timestep, fresh, live, k_stale, v_stale):
    section_idx = lax.axis_index("section")
    block_idx = lax.axis_index("blk")
    steps_all = modulation.shape[1]
    pick_row = (jnp.arange(steps_all) == timestep[0]).astype(jnp.float32)
    modulate = jnp.einsum("t,tcd->cd", pick_row, modulation[0], precision=lax.Precision.HIGHEST)
    num_blocks = fresh.shape[2]
    own_column = (jnp.arange(num_blocks) == block_idx).astype(jnp.int32)
    fresh_own = jnp.sum(fresh[0] * own_column[None, :], axis=1)
    qkv_cols = qkv_weight[0]
    out_cols = out_weight[0]
    old_keys = k_stale[0]
    old_values = v_stale[0]
    num_req = hidden.shape[0]
    received = jnp.zeros_like(hidden[0:1])
    first_out = []
    second_out = []
    for tick_idx in range(num_req + 1):
        if tick_idx < num_req:
            own_input = hidden[tick_idx : tick_idx + 1]
        else:
            own_input = jnp.zeros_like(hidden[0:1])
        layer_in = jnp.where(section_idx == 0, own_input, received)
        req_idx = jnp.clip(tick_idx - section_idx, 0, num_req - 1)
        layer_out = attend(
            layer_in,
            qkv_cols,
            out_cols,
            modulate,
            pick_request(fresh_own, req_idx),
            pick_request(old_keys, req_idx),
            pick_request(old_values, req_idx),
            pick_request(live, req_idx),
        )
        if tick_idx < num_req:
            first_out.append(layer_out)
            received = from_behind(layer_out, "section", 1)
        if tick_idx >= 1:
            second_out.append(layer_out)
    result = jnp.where(
        section_idx == 0, jnp.concatenate(first_out, axis=0), jnp.concatenate(second_out, axis=0)
    )
    return result[None]


HEAD = 64
BF16 = jnp.bfloat16
F32 = jnp.float32
NT = (((1,), (1,)), ((), ()))
VMEM = pl.BlockSpec(memory_space=pltpu.VMEM)
SMEM = pl.BlockSpec(memory_space=pltpu.SMEM)
HBM = pl.BlockSpec(memory_space=pltpu.HBM)
ANY = pl.BlockSpec(memory_space=pl.ANY)


def call(body, outs, scratch, cost, *args, specs=None, spare=40 << 20):
    flops, moved = cost
    return pl.pallas_call(
        body,
        out_shape=outs,
        in_specs=specs or [VMEM] * len(args),
        out_specs=jax.tree.map(lambda _: VMEM, outs),
        scratch_shapes=scratch,
        compiler_params=pltpu.CompilerParams(vmem_limit_bytes=(64 << 20) - spare),
        cost_estimate=pl.CostEstimate(flops=flops, bytes_accessed=moved, transcendentals=0),
    )(*args)


def dot_nt(left, right):
    return lax.dot_general(left, right, NT, preferred_element_type=F32)


def halves(columns):
    mid = columns.shape[0] // 2
    return jnp.concatenate([columns[:mid], columns[mid:]], axis=1)


def pack(cols):
    return jnp.concatenate([cols[:, :128], halves(cols[:, 128:])], axis=0)


def unpack(packed):
    tokens = packed.shape[0] // 3 * 2
    last = packed[tokens:]
    return jnp.concatenate(
        [packed[:tokens], jnp.concatenate([last[:, :HEAD], last[:, HEAD:]], axis=0)], axis=1
    )


def pack_by_parity(cols, odd):
    mid = cols.shape[0] // 2
    even_form = pack(cols)
    odd_form = jnp.concatenate(
        [
            cols[:, HEAD:],
            jnp.concatenate([cols[mid:, :HEAD], cols[:mid, :HEAD]], axis=1),
        ],
        axis=0,
    )
    return jnp.where(odd, odd_form, even_form)


def assemble(blocks, whole, by_heads=False):
    tokens = whole.shape[0]
    n = blocks.shape[0]
    for d in range(0, n, 2):
        even, odd = [group * pow(3, -1, n) % n if by_heads else group for group in (d, d + 1)]
        even_last, odd_last = blocks[even, tokens:].astype(F32), blocks[odd, tokens:].astype(F32)
        left = lax.broadcasted_iota(jnp.int32, even_last.shape, 1) < HEAD
        first = jnp.where(left, even_last, odd_last)
        second = pltpu.roll(jnp.where(left, odd_last, even_last), HEAD, 1)
        at = d // 2 * 384
        whole[:, at : at + 128] = blocks[even, :tokens].astype(whole.dtype)
        whole[:, at + 128 : at + 256] = jnp.concatenate([first, second], axis=0).astype(whole.dtype)
        whole[:, at + 256 : at + 384] = blocks[odd, :tokens].astype(whole.dtype)


def own_columns(ref, rows, me):
    pair = ref[rows, pl.ds(pl.multiple_of(me // 2 * 384, 128), 384)]
    return jnp.where((me & 1) == 1, pair[:, 192:], pair[:, :192])


def norm_into(stream, mod, normed):
    tokens, width = stream.shape
    step = 128
    total = jnp.zeros((tokens, step), F32)
    for at in range(0, width, step):
        total += stream[:, at : at + step]
    center = jnp.sum(total, axis=-1, keepdims=True) / width
    total = jnp.zeros((tokens, step), F32)
    for at in range(0, width, step):
        off = stream[:, at : at + step] - center
        total += off * off
    variance = jnp.sum(total, axis=-1, keepdims=True) / width
    spread = 1.0 / jnp.sqrt(variance + 1e-06)
    for at in range(0, width, step):
        part = (stream[:, at : at + step] - center) * spread
        part = part * (1.0 + mod[0, :, at : at + step]) + mod[1, :, at : at + step]
        normed[:, at : at + step] = part.astype(BF16)


def own_or_other(layer, own, other):
    return jnp.where(lax.axis_index("section") == layer, own, other)


def dot_into(layer, left, own, other, product):
    def into(weight):
        product[...] = dot_nt(left[...], weight[...]).astype(product.dtype)

    held = lax.axis_index("section") == layer
    pl.when(held)(lambda: into(own))
    pl.when(jnp.logical_not(held))(lambda: into(other))


def normalise(layer, stream, mod, other_mod, normed, residual, scales):
    scales[...] = own_or_other(layer, mod[...], other_mod[...])
    norm_into(stream, scales, normed)
    residual[...] = own_columns(stream, slice(None), lax.axis_index("blk")).astype(BF16)


def chunks_of(columns, chunks):
    for j, chunk in enumerate(chunks):
        chunk[...] = pack(columns[:, 192 * j : 192 * j + 192])


def first_projection(arrived, own, other, mod, other_mod, other_out, chunk0, chunk1, chunk2, residual, stream, scales, normed, columns):
    n = arrived.shape[0]
    rows = stream.shape[0] // n
    for b in range(n):
        stream[rows * b : rows * b + rows, :] = arrived[b, :rows, :].astype(F32)
    normalise(0, stream, mod, other_mod, normed, residual, scales)
    dot_into(0, normed, own, other, columns)
    chunks_of(columns, (chunk0, chunk1, chunk2))


def next_projection(blocks, own, other, mod, other_mod, chunk0, chunk1, chunk2, residual, stream, scales, normed, columns):
    assemble(blocks, stream)
    normalise(1, stream, mod, other_mod, normed, residual, scales)
    dot_into(1, normed, own, other, columns)
    chunks_of(columns, (chunk0, chunk1, chunk2))


def attention(layer, chunk0, chunk1, chunk2, old, fresh, other_fresh, live, attn):
    n = attn.shape[0]
    me, request = lax.axis_index("blk"), lax.axis_index("section")
    first = lax.rem(lax.rem(3 * me, n), 3)
    got = [chunk[...].astype(F32) for chunk in (chunk0, chunk1, chunk2)]

    def kind(of):
        at = lax.rem(first + of, 3)
        return unpack(jnp.where(at == 0, got[0], jnp.where(at == 1, got[1], got[2])))

    queries = kind(0)
    tokens, width = queries.shape
    heads = width // HEAD
    rows = tokens // n
    token = lax.broadcasted_iota(jnp.int32, (tokens, 1), 0)
    is_fresh = jnp.zeros((tokens, 1), jnp.int32)
    for b in range(n):
        flag = own_or_other(layer, fresh[0, request, b], other_fresh[0, request, b])
        is_fresh = jnp.where(token >= b * rows, flag, is_fresh)
    is_fresh = is_fresh == 1
    key = lax.broadcasted_iota(jnp.int32, (1, tokens), 1)
    is_live = jnp.zeros((1, tokens), jnp.int32)
    for b in range(n):
        is_live = jnp.where(key >= b * rows, live[request, b], is_live)
    is_live = is_live == 1
    keys = jnp.where(is_fresh, kind(1), old[layer, :, :width].astype(F32)).astype(BF16)
    values = jnp.where(is_fresh, kind(2), old[layer, :, width:].astype(F32)).astype(BF16)
    head_of = lax.broadcasted_iota(jnp.int32, (tokens, width), 1) // HEAD
    stacked = jnp.concatenate([jnp.where(head_of == h, queries, 0.0) for h in range(heads)], axis=0)
    scores = dot_nt(stacked.astype(BF16), keys) * 0.125
    scores = jnp.where(is_live, scores, -1e30)
    top = jnp.max(scores, axis=-1, keepdims=True)
    weights = jnp.where(is_live, jnp.exp(scores - top), 0.0)
    lane = lax.broadcasted_iota(jnp.int32, (tokens, HEAD), 1)
    values = jnp.concatenate([values, (lane == 0).astype(F32).astype(BF16)], axis=1)
    mixed = jnp.dot(weights.astype(BF16), values, preferred_element_type=F32)
    mixed = mixed[:, :width] * (1.0 / mixed[:, width : width + 1])
    result = jnp.zeros((tokens, width), F32)
    for h in range(heads):
        result = jnp.where(head_of == h, mixed[h * tokens : (h + 1) * tokens], result)
    packed = pack_by_parity(result, (me & 1) == 1).astype(BF16)
    for d in range(n):
        attn[d] = packed


def layer_columns(layer, blocks, own, other, mod, other_mod, residual, whole, mixed):
    me = lax.axis_index("blk")
    assemble(blocks, whole, by_heads=True)
    dot_into(layer, whole, own, other, mixed)
    gates = own_or_other(layer, mod[2], other_mod[2])
    pairs = [gates[:, at : at + 384] for at in range(0, gates.shape[1], 384)]
    pair = pairs[0]
    for i, other_pair in enumerate(pairs):
        pair = jnp.where(me // 2 == i, other_pair, pair)
    gate = jnp.where((me & 1) == 1, pair[:, 192:], pair[:, :192])
    return (residual[...].astype(F32) + gate * mixed[...].astype(F32)).astype(BF16).astype(F32)


def first_output(blocks, own, other, mod, other_mod, residual, copies, kept, *scratch):
    columns = layer_columns(0, blocks, own, other, mod, other_mod, residual, *scratch)
    packed = pack_by_parity(columns, (lax.axis_index("blk") & 1) == 1).astype(BF16)
    for d in range(copies.shape[0]):
        copies[d] = packed
    kept[...] = columns


def last_output(blocks, own, other, mod, other_mod, residual, kept, by_token, columns, *scratch):
    columns[...] = layer_columns(1, blocks, own, other, mod, other_mod, residual, *scratch)
    n = by_token.shape[0] // 2
    rows = columns.shape[0] // n
    for layer, outs in enumerate((kept, columns)):
        for b in range(n):
            by_token[layer * n + b, :rows, :] = outs[rows * b : rows * b + rows, :].astype(BF16)


def first_exchange(hidden, old_keys, old_values, other_keys, other_values, leaving, held, sems):
    copies = [
        pltpu.make_async_copy(ref, held.at[i], sems.at[i])
        for i, ref in enumerate((hidden, old_keys, old_values, other_keys, other_values))
    ]
    for copy in copies:
        copy.start()
    rows, reqs, width = hidden.shape
    n = leaving.shape[0]
    columns = width // n
    first = lax.axis_index("section") == 0
    for copy in copies:
        copy.wait()

    def of_request(which):
        own = [held[which, i].astype(F32) for i in range(rows)]
        return jnp.concatenate([jnp.where(first, pair[:1], pair[1:]) for pair in own], axis=0)

    mine, *arrays = [of_request(which) for which in range(5)]
    mine = mine.astype(BF16)
    own, other = arrays[:2], arrays[2:]
    stale = [jnp.where(first, a, b) for a, b in zip(own, other)] + [jnp.where(first, b, a) for a, b in zip(own, other)]
    for b in range(n):
        at = columns * (3 * b % n)
        block = jnp.concatenate([array[:, at : at + columns] for array in stale], axis=1)
        leaving[b, :rows, :] = mine
        for i in range(rows):
            leaving[b, rows : rows + 1, i * 4 * columns : (i + 1) * 4 * columns] = block[i : i + 1].astype(BF16)


def stale_by_token(arrived, old, rows):
    n = arrived.shape[0]
    per = rows.shape[1] // n
    wide = rows.shape[2]
    for b in range(n):
        flat = arrived[b, per : per + 1, :].astype(F32)
        for i in range(per):
            for layer in range(2):
                at = (i * 2 + layer) * wide
                rows[layer, per * b + i : per * b + i + 1, :] = flat[:, at : at + wide]
    old[...] = rows[...].astype(BF16)


def to_rows(arrived, out, rows):
    n = arrived.shape[0] // 2
    per, columns = out.shape[0], arrived.shape[2]
    for s in range(2):
        for b in range(n):
            rows[s, :per, columns * b : columns * b + columns] = arrived[s * n + b, :per, :].astype(F32)
    for i in range(per):
        out[i] = jnp.concatenate([rows[s, i : i + 1, :] for s in range(2)], axis=0).astype(BF16)


def exchange(blocks, axis):
    return lax.all_to_all(blocks, axis, split_axis=0, concat_axis=0, tiled=True)


def swap_sections(array):
    return lax.ppermute(array, "section", [(0, 1), (1, 0)])


def by_heads(chunks, n):
    inverse = pow(3, -1, n)
    return [
        lax.ppermute(chunk, "blk", [(b, (b + inverse * j) % n) for b in range(n)]) if j else chunk
        for j, chunk in enumerate(chunks)
    ]


def per_device(hidden, qkv_weight, out_weight, modulation, timestep, fresh, live, k_stale, v_stale):
    n = lax.axis_size("blk")
    columns = out_weight.shape[2]
    reqs, rows, width = hidden.shape
    if not (
        columns == 3 * HEAD
        and n % 3 == 1
        and n & (n - 1) == 0
        and reqs == lax.axis_size("section") == 2
        and rows <= 4
    ):
        return per_device_by_token(
            hidden, qkv_weight, out_weight, modulation, timestep, fresh, live, k_stale, v_stale
        )
    tokens = n * rows
    shape = jax.ShapeDtypeStruct
    packed = shape((tokens * 3 // 2, 128), BF16)
    copies = shape((n, tokens * 3 // 2, 128), BF16)
    cols = shape((tokens, columns), BF16)
    own_qkv = jnp.swapaxes(qkv_weight[0], 0, 1)
    own_out = jnp.swapaxes(out_weight[0], 0, 1)
    steps = jnp.transpose(modulation, (1, 2, 0, 3))
    mod = lax.dynamic_index_in_dim(steps, timestep[0], 0, keepdims=False)
    old_keys = jnp.transpose(k_stale[0], (1, 0, 2))
    old_values = jnp.transpose(v_stale[0], (1, 0, 2))

    leaving = call(
        first_exchange,
        shape((n, 4, width), BF16),
        [pltpu.VMEM((5, rows, reqs, width), BF16), pltpu.SemaphoreType.DMA((5,))],
        (0, 1000000),
        jnp.transpose(hidden, (1, 0, 2)),
        old_keys,
        old_values,
        swap_sections(old_keys),
        swap_sections(old_values),
        specs=[HBM] * 3 + [ANY] * 2,
        spare=4 << 20,
    )
    leaving, other_mod, other_fresh, sent_qkv, sent_out = lax.optimization_barrier(
        (leaving, swap_sections(mod), swap_sections(fresh), own_qkv, own_out)
    )
    mods = (mod, other_mod)
    flags = (fresh, other_fresh)
    other_qkv, other_out = swap_sections(sent_qkv), swap_sections(sent_out)
    out = (own_out, other_out)
    arrived, staged = lax.optimization_barrier((exchange(leaving, "blk"), own_qkv))
    held_qkv = lax.ppermute(staged, "section", [(0, 0)])

    blocks = arrived
    for layer in range(2):
        *chunks, residual = call(
            next_projection if layer else first_projection,
            [packed, packed, packed, cols],
            [
                pltpu.VMEM((tokens, width), F32),
                pltpu.VMEM(mod.shape, F32),
                pltpu.VMEM((tokens, width), BF16),
                pltpu.VMEM((tokens, 3 * columns), BF16),
            ],
            (2 * tokens * width * 3 * columns, 8 * width * columns),
            blocks,
            *((own_qkv, other_qkv, *mods) if layer else (held_qkv, other_qkv, *mods, other_out)),
            **({} if layer else {"specs": [VMEM] * 5 + [ANY]}),
        )
        if layer == 0:
            arrived, chunks[1] = lax.optimization_barrier((arrived, chunks[1]))
            old = call(
                stale_by_token,
                shape((2, tokens, 2 * columns), BF16),
                [pltpu.VMEM((2, tokens, 2 * columns), F32)],
                (0, 200000),
                arrived,
            )
        attn = call(
            functools.partial(attention, layer),
            copies,
            [],
            (8 * tokens * tokens * columns, 300000),
            *by_heads(chunks, n),
            old,
            *flags,
            live,
            specs=[VMEM] * 4 + [SMEM] * 3,
        )
        args = (exchange(attn, "blk"), *out, *mods, residual)
        cost = (2 * tokens * width * columns, 4 * width * columns)
        held = [pltpu.VMEM((tokens, width), BF16), pltpu.VMEM((tokens, columns), BF16)]
        if layer == 0:
            leaving, kept = call(first_output, [copies, shape((tokens, columns), F32)], held, cost, *args)
            blocks = exchange(leaving, "blk")
        else:
            leaving = call(
                last_output,
                shape((2 * n, 4, columns), BF16),
                [pltpu.VMEM((tokens, columns), F32)] + held,
                cost,
                *args,
                kept,
            )
    result = call(
        to_rows,
        shape((rows, reqs, width), BF16),
        [pltpu.VMEM((2, 8, width), F32)],
        (0, 100000),
        exchange(leaving, ("section", "blk")),
    )
    return jnp.transpose(result, (1, 0, 2))[None]


def solution(mesh):
    return jax.shard_map(
        per_device,
        mesh=mesh,
        in_specs=(
            P(None, "blk", None),
            P("section", None, "blk"),
            P("section", None, "blk"),
            P("section", None, None, None),
            P(),
            P("section", None, None),
            P(),
            P("section", None, "blk", None),
            P("section", None, "blk", None),
        ),
        out_specs=P("section", None, "blk", None),
        check_vma=False,
    )
```

```python
import functools

import jax
import jax.numpy as jnp
from jax import lax
from jax.experimental import pallas as pl
from jax.experimental.pallas import tpu as pltpu
from jax.sharding import PartitionSpec as P


def from_behind(shard, axis, by):
    count = lax.axis_size(axis)
    pairs = [(i, i + by) for i in range(count) if 0 <= i + by < count]
    return lax.ppermute(shard, axis, pairs)


def attend(layer_in, qkv_cols, out_cols, modulate, fresh_own, old_keys, old_values, live):
    stream = layer_in.astype(jnp.float32)
    center = jnp.mean(stream, axis=-1, keepdims=True)
    variance = jnp.mean((stream - center) ** 2, axis=-1, keepdims=True)
    normed = (stream - center) / jnp.sqrt(variance + 1e-06) * (1.0 + modulate[0]) + modulate[1]
    normed_b = normed.astype(jnp.bfloat16)
    columns = jnp.einsum(
        "rnd,dc->rnc",
        lax.all_gather(normed_b, "blk", axis=1, tiled=True),
        qkv_cols,
        preferred_element_type=jnp.float32,
    ).astype(jnp.bfloat16)
    projected = lax.all_to_all(columns, "blk", split_axis=1, concat_axis=2, tiled=True)
    num_req, num_rows, width = layer_in.shape
    queries = projected[:, :, :width]
    new_keys = projected[:, :, width : 2 * width]
    new_values = projected[:, :, 2 * width :]
    use_fresh = (fresh_own == 1)[:, None, None]
    keys = jnp.where(use_fresh, new_keys, old_keys)
    values = jnp.where(use_fresh, new_values, old_values)
    num_heads = width // 64
    num_blocks = live.shape[1]
    q_heads = queries.reshape(num_req, num_rows, num_heads, 64)
    live_float = live.astype(jnp.float32)
    run_max = jnp.full((num_req, num_heads, num_rows), -1e30, jnp.float32)
    key_piece = lax.all_gather(keys, "blk", axis=1, tiled=True)
    value_piece = lax.all_gather(values, "blk", axis=1, tiled=True)
    piece_rows = key_piece.shape[1]
    key_heads = key_piece.reshape(num_req, piece_rows, num_heads, 64)
    value_heads = value_piece.reshape(num_req, piece_rows, num_heads, 64)
    scores = (
        jnp.einsum("qrhd,qnhd->qhrn", q_heads, key_heads, preferred_element_type=jnp.float32)
        * 0.125
    )
    block_ids = jnp.arange(piece_rows) // num_rows
    one_hot = (block_ids[:, None] == jnp.arange(num_blocks)[None, :]).astype(jnp.float32)
    usable = jnp.einsum("qb,nb->qn", live_float, one_hot) > 0.5
    usable = usable[:, None, None, :]
    scores = jnp.where(usable, scores, -1e30)
    new_max = jnp.maximum(run_max, jnp.max(scores, axis=-1))
    weights = jnp.where(usable, jnp.exp(scores - new_max[..., None]), 0.0)
    new_sum = jnp.sum(weights, axis=-1)
    new_acc = jnp.einsum(
        "qhrn,qnhd->qhrd", weights, value_heads.astype(jnp.float32), precision=lax.Precision.HIGHEST
    )
    attn = new_acc / new_sum[..., None]
    attn = jnp.transpose(attn, (0, 2, 1, 3)).reshape(num_req, num_rows, width).astype(jnp.bfloat16)
    out_part = jnp.einsum(
        "rnd,dc->rnc",
        lax.all_gather(attn, "blk", axis=1, tiled=True),
        out_cols,
        preferred_element_type=jnp.float32,
    ).astype(jnp.bfloat16)
    mixed_back = lax.all_to_all(out_part, "blk", split_axis=1, concat_axis=2, tiled=True)
    return (stream + modulate[2] * mixed_back.astype(jnp.float32)).astype(jnp.bfloat16)


def pick_request(array, req_idx):
    return lax.dynamic_index_in_dim(array, req_idx, 0, keepdims=True)


def per_device_by_token(hidden, qkv_weight, out_weight, modulation, timestep, fresh, live, k_stale, v_stale):
    section_idx = lax.axis_index("section")
    block_idx = lax.axis_index("blk")
    steps_all = modulation.shape[1]
    pick_row = (jnp.arange(steps_all) == timestep[0]).astype(jnp.float32)
    modulate = jnp.einsum("t,tcd->cd", pick_row, modulation[0], precision=lax.Precision.HIGHEST)
    num_blocks = fresh.shape[2]
    own_column = (jnp.arange(num_blocks) == block_idx).astype(jnp.int32)
    fresh_own = jnp.sum(fresh[0] * own_column[None, :], axis=1)
    qkv_cols = qkv_weight[0]
    out_cols = out_weight[0]
    old_keys = k_stale[0]
    old_values = v_stale[0]
    num_req = hidden.shape[0]
    received = jnp.zeros_like(hidden[0:1])
    first_out = []
    second_out = []
    for tick_idx in range(num_req + 1):
        if tick_idx < num_req:
            own_input = hidden[tick_idx : tick_idx + 1]
        else:
            own_input = jnp.zeros_like(hidden[0:1])
        layer_in = jnp.where(section_idx == 0, own_input, received)
        req_idx = jnp.clip(tick_idx - section_idx, 0, num_req - 1)
        layer_out = attend(
            layer_in,
            qkv_cols,
            out_cols,
            modulate,
            pick_request(fresh_own, req_idx),
            pick_request(old_keys, req_idx),
            pick_request(old_values, req_idx),
            pick_request(live, req_idx),
        )
        if tick_idx < num_req:
            first_out.append(layer_out)
            received = from_behind(layer_out, "section", 1)
        if tick_idx >= 1:
            second_out.append(layer_out)
    result = jnp.where(
        section_idx == 0, jnp.concatenate(first_out, axis=0), jnp.concatenate(second_out, axis=0)
    )
    return result[None]


HEAD = 64
BF16 = jnp.bfloat16
F32 = jnp.float32
NT = (((1,), (1,)), ((), ()))
VMEM = pl.BlockSpec(memory_space=pltpu.VMEM)
SMEM = pl.BlockSpec(memory_space=pltpu.SMEM)
HBM = pl.BlockSpec(memory_space=pltpu.HBM)
ANY = pl.BlockSpec(memory_space=pl.ANY)


def call(body, outs, scratch, cost, *args, specs=None, spare=40 << 20):
    flops, moved = cost
    return pl.pallas_call(
        body,
        out_shape=outs,
        in_specs=specs or [VMEM] * len(args),
        out_specs=jax.tree.map(lambda _: VMEM, outs),
        scratch_shapes=scratch,
        compiler_params=pltpu.CompilerParams(vmem_limit_bytes=(64 << 20) - spare),
        cost_estimate=pl.CostEstimate(flops=flops, bytes_accessed=moved, transcendentals=0),
    )(*args)


def dot_nt(left, right):
    return lax.dot_general(left, right, NT, preferred_element_type=F32)


def halves(columns):
    mid = columns.shape[0] // 2
    return jnp.concatenate([columns[:mid], columns[mid:]], axis=1)


def pack(cols):
    return jnp.concatenate([cols[:, :128], halves(cols[:, 128:])], axis=0)


def unpack(packed):
    tokens = packed.shape[0] // 3 * 2
    last = packed[tokens:]
    return jnp.concatenate(
        [packed[:tokens], jnp.concatenate([last[:, :HEAD], last[:, HEAD:]], axis=0)], axis=1
    )


def pack_by_parity(cols, odd):
    mid = cols.shape[0] // 2
    even_form = pack(cols)
    odd_form = jnp.concatenate(
        [
            cols[:, HEAD:],
            jnp.concatenate([cols[mid:, :HEAD], cols[:mid, :HEAD]], axis=1),
        ],
        axis=0,
    )
    return jnp.where(odd, odd_form, even_form)


def assemble(blocks, whole, by_heads=False):
    tokens = whole.shape[0]
    n = blocks.shape[0]
    for d in range(0, n, 2):
        even, odd = [group * pow(3, -1, n) % n if by_heads else group for group in (d, d + 1)]
        even_last, odd_last = blocks[even, tokens:].astype(F32), blocks[odd, tokens:].astype(F32)
        left = lax.broadcasted_iota(jnp.int32, even_last.shape, 1) < HEAD
        first = jnp.where(left, even_last, odd_last)
        second = pltpu.roll(jnp.where(left, odd_last, even_last), HEAD, 1)
        at = d // 2 * 384
        whole[:, at : at + 128] = blocks[even, :tokens].astype(whole.dtype)
        whole[:, at + 128 : at + 256] = jnp.concatenate([first, second], axis=0).astype(whole.dtype)
        whole[:, at + 256 : at + 384] = blocks[odd, :tokens].astype(whole.dtype)


def own_columns(ref, rows, me):
    pair = ref[rows, pl.ds(pl.multiple_of(me // 2 * 384, 128), 384)]
    return jnp.where((me & 1) == 1, pair[:, 192:], pair[:, :192])


def norm_into(stream, mod, normed):
    tokens, width = stream.shape
    step = 128
    total = jnp.zeros((tokens, step), F32)
    for at in range(0, width, step):
        total += stream[:, at : at + step]
    center = jnp.sum(total, axis=-1, keepdims=True) / width
    total = jnp.zeros((tokens, step), F32)
    for at in range(0, width, step):
        off = stream[:, at : at + step] - center
        total += off * off
    variance = jnp.sum(total, axis=-1, keepdims=True) / width
    spread = 1.0 / jnp.sqrt(variance + 1e-06)
    for at in range(0, width, step):
        part = (stream[:, at : at + step] - center) * spread
        part = part * (1.0 + mod[0, :, at : at + step]) + mod[1, :, at : at + step]
        normed[:, at : at + step] = part.astype(BF16)


def own_or_other(layer, own, other):
    return jnp.where(lax.axis_index("section") == layer, own, other)


def dot_into(layer, left, own, other, product):
    def into(weight):
        product[...] = dot_nt(left[...], weight[...]).astype(product.dtype)

    held = lax.axis_index("section") == layer
    pl.when(held)(lambda: into(own))
    pl.when(jnp.logical_not(held))(lambda: into(other))


def normalise(layer, stream, mod, other_mod, normed, residual, scales):
    scales[...] = own_or_other(layer, mod[...], other_mod[...])
    norm_into(stream, scales, normed)
    residual[...] = own_columns(stream, slice(None), lax.axis_index("blk")).astype(BF16)


def chunks_of(columns, chunks):
    for j, chunk in enumerate(chunks):
        chunk[...] = pack(columns[:, 192 * j : 192 * j + 192])


def first_projection(arrived, own, other, mod, other_mod, other_out, chunk0, chunk1, chunk2, residual, stream, scales, normed, columns):
    n = arrived.shape[0]
    rows = stream.shape[0] // n
    for b in range(n):
        stream[rows * b : rows * b + rows, :] = arrived[b, :rows, :].astype(F32)
    normalise(0, stream, mod, other_mod, normed, residual, scales)
    dot_into(0, normed, own, other, columns)
    chunks_of(columns, (chunk0, chunk1, chunk2))


def next_projection(blocks, own, other, mod, other_mod, chunk0, chunk1, chunk2, residual, stream, scales, normed, columns):
    assemble(blocks, stream)
    normalise(1, stream, mod, other_mod, normed, residual, scales)
    dot_into(1, normed, own, other, columns)
    chunks_of(columns, (chunk0, chunk1, chunk2))


def attention(layer, chunk0, chunk1, chunk2, old, fresh, other_fresh, live, attn):
    n = attn.shape[0]
    me, request = lax.axis_index("blk"), lax.axis_index("section")
    first = lax.rem(lax.rem(3 * me, n), 3)
    got = [chunk[...].astype(F32) for chunk in (chunk0, chunk1, chunk2)]

    def kind(of):
        at = lax.rem(first + of, 3)
        return unpack(jnp.where(at == 0, got[0], jnp.where(at == 1, got[1], got[2])))

    queries = kind(0)
    tokens, width = queries.shape
    heads = width // HEAD
    rows = tokens // n
    token = lax.broadcasted_iota(jnp.int32, (tokens, 1), 0)
    is_fresh = jnp.zeros((tokens, 1), jnp.int32)
    for b in range(n):
        flag = own_or_other(layer, fresh[0, request, b], other_fresh[0, request, b])
        is_fresh = jnp.where(token >= b * rows, flag, is_fresh)
    is_fresh = is_fresh == 1
    key = lax.broadcasted_iota(jnp.int32, (1, tokens), 1)
    is_live = jnp.zeros((1, tokens), jnp.int32)
    for b in range(n):
        is_live = jnp.where(key >= b * rows, live[request, b], is_live)
    is_live = is_live == 1
    keys = jnp.where(is_fresh, kind(1), old[layer, :, :width].astype(F32)).astype(BF16)
    values = jnp.where(is_fresh, kind(2), old[layer, :, width:].astype(F32)).astype(BF16)
    head_of = lax.broadcasted_iota(jnp.int32, (tokens, width), 1) // HEAD
    stacked = jnp.concatenate([jnp.where(head_of == h, queries, 0.0) for h in range(heads)], axis=0)
    scores = dot_nt(stacked.astype(BF16), keys) * 0.125
    scores = jnp.where(is_live, scores, -1e30)
    top = jnp.max(scores, axis=-1, keepdims=True)
    weights = jnp.where(is_live, jnp.exp(scores - top), 0.0)
    total = jnp.sum(weights, axis=-1, keepdims=True)
    mixed = jnp.dot(weights.astype(BF16), values, preferred_element_type=F32) * (1.0 / total)
    result = jnp.zeros((tokens, width), F32)
    for h in range(heads):
        result = jnp.where(head_of == h, mixed[h * tokens : (h + 1) * tokens], result)
    packed = pack_by_parity(result, (me & 1) == 1).astype(BF16)
    for d in range(n):
        attn[d] = packed


def layer_columns(layer, blocks, own, other, mod, other_mod, residual, whole, mixed):
    me = lax.axis_index("blk")
    assemble(blocks, whole, by_heads=True)
    dot_into(layer, whole, own, other, mixed)
    gates = own_or_other(layer, mod[2], other_mod[2])
    pairs = [gates[:, at : at + 384] for at in range(0, gates.shape[1], 384)]
    pair = pairs[0]
    for i, other_pair in enumerate(pairs):
        pair = jnp.where(me // 2 == i, other_pair, pair)
    gate = jnp.where((me & 1) == 1, pair[:, 192:], pair[:, :192])
    return (residual[...].astype(F32) + gate * mixed[...].astype(F32)).astype(BF16).astype(F32)


def first_output(blocks, own, other, mod, other_mod, residual, copies, kept, *scratch):
    columns = layer_columns(0, blocks, own, other, mod, other_mod, residual, *scratch)
    packed = pack_by_parity(columns, (lax.axis_index("blk") & 1) == 1).astype(BF16)
    for d in range(copies.shape[0]):
        copies[d] = packed
    kept[...] = columns


def last_output(blocks, own, other, mod, other_mod, residual, kept, by_token, columns, *scratch):
    columns[...] = layer_columns(1, blocks, own, other, mod, other_mod, residual, *scratch)
    n = by_token.shape[0] // 2
    rows = columns.shape[0] // n
    for layer, outs in enumerate((kept, columns)):
        for b in range(n):
            by_token[layer * n + b, :rows, :] = outs[rows * b : rows * b + rows, :].astype(BF16)


def first_exchange(hidden, old_keys, old_values, other_keys, other_values, leaving, held, sems):
    copies = [
        pltpu.make_async_copy(ref, held.at[i], sems.at[i])
        for i, ref in enumerate((hidden, old_keys, old_values, other_keys, other_values))
    ]
    for copy in copies:
        copy.start()
    rows, reqs, width = hidden.shape
    n = leaving.shape[0]
    columns = width // n
    first = lax.axis_index("section") == 0
    for copy in copies:
        copy.wait()

    def of_request(which):
        own = [held[which, i].astype(F32) for i in range(rows)]
        return jnp.concatenate([jnp.where(first, pair[:1], pair[1:]) for pair in own], axis=0)

    mine, *arrays = [of_request(which) for which in range(5)]
    mine = mine.astype(BF16)
    own, other = arrays[:2], arrays[2:]
    stale = [jnp.where(first, a, b) for a, b in zip(own, other)] + [jnp.where(first, b, a) for a, b in zip(own, other)]
    for b in range(n):
        at = columns * (3 * b % n)
        block = jnp.concatenate([array[:, at : at + columns] for array in stale], axis=1)
        leaving[b, :rows, :] = mine
        for i in range(rows):
            leaving[b, rows : rows + 1, i * 4 * columns : (i + 1) * 4 * columns] = block[i : i + 1].astype(BF16)


def stale_by_token(arrived, old, rows):
    n = arrived.shape[0]
    per = rows.shape[1] // n
    wide = rows.shape[2]
    for b in range(n):
        flat = arrived[b, per : per + 1, :].astype(F32)
        for i in range(per):
            for layer in range(2):
                at = (i * 2 + layer) * wide
                rows[layer, per * b + i : per * b + i + 1, :] = flat[:, at : at + wide]
    old[...] = rows[...].astype(BF16)


def to_rows(arrived, out, rows):
    n = arrived.shape[0] // 2
    per, columns = out.shape[0], arrived.shape[2]
    for s in range(2):
        for b in range(n):
            rows[s, :per, columns * b : columns * b + columns] = arrived[s * n + b, :per, :].astype(F32)
    for i in range(per):
        out[i] = jnp.concatenate([rows[s, i : i + 1, :] for s in range(2)], axis=0).astype(BF16)


def exchange(blocks, axis):
    return lax.all_to_all(blocks, axis, split_axis=0, concat_axis=0, tiled=True)


def swap_sections(array):
    return lax.ppermute(array, "section", [(0, 1), (1, 0)])


def by_heads(chunks, n):
    inverse = pow(3, -1, n)
    return [
        lax.ppermute(chunk, "blk", [(b, (b + inverse * j) % n) for b in range(n)]) if j else chunk
        for j, chunk in enumerate(chunks)
    ]


def per_device(hidden, qkv_weight, out_weight, modulation, timestep, fresh, live, k_stale, v_stale):
    n = lax.axis_size("blk")
    columns = out_weight.shape[2]
    reqs, rows, width = hidden.shape
    if not (
        columns == 3 * HEAD
        and n % 3 == 1
        and n & (n - 1) == 0
        and reqs == lax.axis_size("section") == 2
        and rows <= 4
    ):
        return per_device_by_token(
            hidden, qkv_weight, out_weight, modulation, timestep, fresh, live, k_stale, v_stale
        )
    tokens = n * rows
    shape = jax.ShapeDtypeStruct
    packed = shape((tokens * 3 // 2, 128), BF16)
    copies = shape((n, tokens * 3 // 2, 128), BF16)
    cols = shape((tokens, columns), BF16)
    own_qkv = jnp.swapaxes(qkv_weight[0], 0, 1)
    own_out = jnp.swapaxes(out_weight[0], 0, 1)
    steps = jnp.transpose(modulation, (1, 2, 0, 3))
    mod = lax.dynamic_index_in_dim(steps, timestep[0], 0, keepdims=False)
    old_keys = jnp.transpose(k_stale[0], (1, 0, 2))
    old_values = jnp.transpose(v_stale[0], (1, 0, 2))

    other_keys, sent_out = lax.optimization_barrier((swap_sections(old_keys), own_out))
    other_out = swap_sections(sent_out)
    out = (own_out, other_out)
    leaving = call(
        first_exchange,
        shape((n, 4, width), BF16),
        [pltpu.VMEM((5, rows, reqs, width), BF16), pltpu.SemaphoreType.DMA((5,))],
        (0, 1000000),
        jnp.transpose(hidden, (1, 0, 2)),
        old_keys,
        old_values,
        other_keys,
        swap_sections(old_values),
        specs=[HBM] * 3 + [ANY] * 2,
        spare=4 << 20,
    )
    leaving, other_mod, other_fresh, sent_qkv = lax.optimization_barrier(
        (leaving, swap_sections(mod), swap_sections(fresh), own_qkv)
    )
    mods = (mod, other_mod)
    flags = (fresh, other_fresh)
    other_qkv = swap_sections(sent_qkv)
    held_qkv = lax.ppermute(sent_qkv, "section", [(0, 0)])
    arrived = exchange(leaving, "blk")

    blocks = arrived
    for layer in range(2):
        *chunks, residual = call(
            next_projection if layer else first_projection,
            [packed, packed, packed, cols],
            [
                pltpu.VMEM((tokens, width), F32),
                pltpu.VMEM(mod.shape, F32),
                pltpu.VMEM((tokens, width), BF16),
                pltpu.VMEM((tokens, 3 * columns), BF16),
            ],
            (2 * tokens * width * 3 * columns, 8 * width * columns),
            blocks,
            *((own_qkv, other_qkv, *mods) if layer else (held_qkv, other_qkv, *mods, other_out)),
            **({} if layer else {"specs": [VMEM] * 5 + [ANY]}),
        )
        if layer == 0:
            arrived, chunks[1] = lax.optimization_barrier((arrived, chunks[1]))
            old = call(
                stale_by_token,
                shape((2, tokens, 2 * columns), BF16),
                [pltpu.VMEM((2, tokens, 2 * columns), F32)],
                (0, 200000),
                arrived,
            )
        attn = call(
            functools.partial(attention, layer),
            copies,
            [],
            (8 * tokens * tokens * columns, 300000),
            *by_heads(chunks, n),
            old,
            *flags,
            live,
            specs=[VMEM] * 4 + [SMEM] * 3,
        )
        args = (exchange(attn, "blk"), *out, *mods, residual)
        cost = (2 * tokens * width * columns, 4 * width * columns)
        held = [pltpu.VMEM((tokens, width), BF16), pltpu.VMEM((tokens, columns), BF16)]
        if layer == 0:
            leaving, kept = call(first_output, [copies, shape((tokens, columns), F32)], held, cost, *args)
            blocks = exchange(leaving, "blk")
        else:
            leaving = call(
                last_output,
                shape((2 * n, 4, columns), BF16),
                [pltpu.VMEM((tokens, columns), F32)] + held,
                cost,
                *args,
                kept,
            )
    result = call(
        to_rows,
        shape((rows, reqs, width), BF16),
        [pltpu.VMEM((2, 8, width), F32)],
        (0, 100000),
        exchange(leaving, ("section", "blk")),
    )
    return jnp.transpose(result, (1, 0, 2))[None]


def solution(mesh):
    return jax.shard_map(
        per_device,
        mesh=mesh,
        in_specs=(
            P(None, "blk", None),
            P("section", None, "blk"),
            P("section", None, "blk"),
            P("section", None, None, None),
            P(),
            P("section", None, None),
            P(),
            P("section", None, "blk", None),
            P("section", None, "blk", None),
        ),
        out_specs=P("section", None, "blk", None),
        check_vma=False,
    )
```

```python
import functools

import jax
import jax.numpy as jnp
from jax import lax
from jax.experimental import pallas as pl
from jax.experimental.pallas import tpu as pltpu
from jax.sharding import PartitionSpec as P


def from_behind(shard, axis, by):
    count = lax.axis_size(axis)
    pairs = [(i, i + by) for i in range(count) if 0 <= i + by < count]
    return lax.ppermute(shard, axis, pairs)


def attend(layer_in, qkv_cols, out_cols, modulate, fresh_own, old_keys, old_values, live):
    stream = layer_in.astype(jnp.float32)
    center = jnp.mean(stream, axis=-1, keepdims=True)
    variance = jnp.mean((stream - center) ** 2, axis=-1, keepdims=True)
    normed = (stream - center) / jnp.sqrt(variance + 1e-06) * (1.0 + modulate[0]) + modulate[1]
    normed_b = normed.astype(jnp.bfloat16)
    columns = jnp.einsum(
        "rnd,dc->rnc",
        lax.all_gather(normed_b, "blk", axis=1, tiled=True),
        qkv_cols,
        preferred_element_type=jnp.float32,
    ).astype(jnp.bfloat16)
    projected = lax.all_to_all(columns, "blk", split_axis=1, concat_axis=2, tiled=True)
    num_req, num_rows, width = layer_in.shape
    queries = projected[:, :, :width]
    new_keys = projected[:, :, width : 2 * width]
    new_values = projected[:, :, 2 * width :]
    use_fresh = (fresh_own == 1)[:, None, None]
    keys = jnp.where(use_fresh, new_keys, old_keys)
    values = jnp.where(use_fresh, new_values, old_values)
    num_heads = width // 64
    num_blocks = live.shape[1]
    q_heads = queries.reshape(num_req, num_rows, num_heads, 64)
    live_float = live.astype(jnp.float32)
    run_max = jnp.full((num_req, num_heads, num_rows), -1e30, jnp.float32)
    key_piece = lax.all_gather(keys, "blk", axis=1, tiled=True)
    value_piece = lax.all_gather(values, "blk", axis=1, tiled=True)
    piece_rows = key_piece.shape[1]
    key_heads = key_piece.reshape(num_req, piece_rows, num_heads, 64)
    value_heads = value_piece.reshape(num_req, piece_rows, num_heads, 64)
    scores = (
        jnp.einsum("qrhd,qnhd->qhrn", q_heads, key_heads, preferred_element_type=jnp.float32)
        * 0.125
    )
    block_ids = jnp.arange(piece_rows) // num_rows
    one_hot = (block_ids[:, None] == jnp.arange(num_blocks)[None, :]).astype(jnp.float32)
    usable = jnp.einsum("qb,nb->qn", live_float, one_hot) > 0.5
    usable = usable[:, None, None, :]
    scores = jnp.where(usable, scores, -1e30)
    new_max = jnp.maximum(run_max, jnp.max(scores, axis=-1))
    weights = jnp.where(usable, jnp.exp(scores - new_max[..., None]), 0.0)
    new_sum = jnp.sum(weights, axis=-1)
    new_acc = jnp.einsum(
        "qhrn,qnhd->qhrd", weights, value_heads.astype(jnp.float32), precision=lax.Precision.HIGHEST
    )
    attn = new_acc / new_sum[..., None]
    attn = jnp.transpose(attn, (0, 2, 1, 3)).reshape(num_req, num_rows, width).astype(jnp.bfloat16)
    out_part = jnp.einsum(
        "rnd,dc->rnc",
        lax.all_gather(attn, "blk", axis=1, tiled=True),
        out_cols,
        preferred_element_type=jnp.float32,
    ).astype(jnp.bfloat16)
    mixed_back = lax.all_to_all(out_part, "blk", split_axis=1, concat_axis=2, tiled=True)
    return (stream + modulate[2] * mixed_back.astype(jnp.float32)).astype(jnp.bfloat16)


def pick_request(array, req_idx):
    return lax.dynamic_index_in_dim(array, req_idx, 0, keepdims=True)


def per_device_by_token(hidden, qkv_weight, out_weight, modulation, timestep, fresh, live, k_stale, v_stale):
    section_idx = lax.axis_index("section")
    block_idx = lax.axis_index("blk")
    steps_all = modulation.shape[1]
    pick_row = (jnp.arange(steps_all) == timestep[0]).astype(jnp.float32)
    modulate = jnp.einsum("t,tcd->cd", pick_row, modulation[0], precision=lax.Precision.HIGHEST)
    num_blocks = fresh.shape[2]
    own_column = (jnp.arange(num_blocks) == block_idx).astype(jnp.int32)
    fresh_own = jnp.sum(fresh[0] * own_column[None, :], axis=1)
    qkv_cols = qkv_weight[0]
    out_cols = out_weight[0]
    old_keys = k_stale[0]
    old_values = v_stale[0]
    num_req = hidden.shape[0]
    received = jnp.zeros_like(hidden[0:1])
    first_out = []
    second_out = []
    for tick_idx in range(num_req + 1):
        if tick_idx < num_req:
            own_input = hidden[tick_idx : tick_idx + 1]
        else:
            own_input = jnp.zeros_like(hidden[0:1])
        layer_in = jnp.where(section_idx == 0, own_input, received)
        req_idx = jnp.clip(tick_idx - section_idx, 0, num_req - 1)
        layer_out = attend(
            layer_in,
            qkv_cols,
            out_cols,
            modulate,
            pick_request(fresh_own, req_idx),
            pick_request(old_keys, req_idx),
            pick_request(old_values, req_idx),
            pick_request(live, req_idx),
        )
        if tick_idx < num_req:
            first_out.append(layer_out)
            received = from_behind(layer_out, "section", 1)
        if tick_idx >= 1:
            second_out.append(layer_out)
    result = jnp.where(
        section_idx == 0, jnp.concatenate(first_out, axis=0), jnp.concatenate(second_out, axis=0)
    )
    return result[None]


HEAD = 64
BF16 = jnp.bfloat16
F32 = jnp.float32
NT = (((1,), (1,)), ((), ()))
VMEM = pl.BlockSpec(memory_space=pltpu.VMEM)
SMEM = pl.BlockSpec(memory_space=pltpu.SMEM)
HBM = pl.BlockSpec(memory_space=pltpu.HBM)
ANY = pl.BlockSpec(memory_space=pl.ANY)


def call(body, outs, scratch, cost, *args, specs=None, spare=40 << 20):
    flops, moved = cost
    return pl.pallas_call(
        body,
        out_shape=outs,
        in_specs=specs or [VMEM] * len(args),
        out_specs=jax.tree.map(lambda _: VMEM, outs),
        scratch_shapes=scratch,
        compiler_params=pltpu.CompilerParams(vmem_limit_bytes=(64 << 20) - spare),
        cost_estimate=pl.CostEstimate(flops=flops, bytes_accessed=moved, transcendentals=0),
    )(*args)


def pinned(array):
    return pltpu.with_memory_space_constraint(array, pltpu.HBM)


def dot_nt(left, right):
    return lax.dot_general(left, right, NT, preferred_element_type=F32)


def halves(columns):
    mid = columns.shape[0] // 2
    return jnp.concatenate([columns[:mid], columns[mid:]], axis=1)


def pack(cols):
    return jnp.concatenate([cols[:, :128], halves(cols[:, 128:])], axis=0)


def unpack(packed):
    tokens = packed.shape[0] // 3 * 2
    last = packed[tokens:]
    return jnp.concatenate(
        [packed[:tokens], jnp.concatenate([last[:, :HEAD], last[:, HEAD:]], axis=0)], axis=1
    )


def pack_by_parity(cols, odd):
    mid = cols.shape[0] // 2
    even_form = pack(cols)
    odd_form = jnp.concatenate(
        [
            cols[:, HEAD:],
            jnp.concatenate([cols[mid:, :HEAD], cols[:mid, :HEAD]], axis=1),
        ],
        axis=0,
    )
    return jnp.where(odd, odd_form, even_form)


def assemble(blocks, whole, by_heads=False):
    tokens = whole.shape[0]
    n = blocks.shape[0]
    for d in range(0, n, 2):
        even, odd = [group * pow(3, -1, n) % n if by_heads else group for group in (d, d + 1)]
        even_last, odd_last = blocks[even, tokens:].astype(F32), blocks[odd, tokens:].astype(F32)
        left = lax.broadcasted_iota(jnp.int32, even_last.shape, 1) < HEAD
        first = jnp.where(left, even_last, odd_last)
        second = pltpu.roll(jnp.where(left, odd_last, even_last), HEAD, 1)
        at = d // 2 * 384
        whole[:, at : at + 128] = blocks[even, :tokens].astype(whole.dtype)
        whole[:, at + 128 : at + 256] = jnp.concatenate([first, second], axis=0).astype(whole.dtype)
        whole[:, at + 256 : at + 384] = blocks[odd, :tokens].astype(whole.dtype)


def own_columns(ref, rows, me):
    pair = ref[rows, pl.ds(pl.multiple_of(me // 2 * 384, 128), 384)]
    return jnp.where((me & 1) == 1, pair[:, 192:], pair[:, :192])


def norm_into(stream, mod, normed):
    tokens, width = stream.shape
    step = 128
    total = jnp.zeros((tokens, step), F32)
    for at in range(0, width, step):
        total += stream[:, at : at + step]
    center = jnp.sum(total, axis=-1, keepdims=True) / width
    total = jnp.zeros((tokens, step), F32)
    for at in range(0, width, step):
        off = stream[:, at : at + step] - center
        total += off * off
    variance = jnp.sum(total, axis=-1, keepdims=True) / width
    spread = 1.0 / jnp.sqrt(variance + 1e-06)
    for at in range(0, width, step):
        part = (stream[:, at : at + step] - center) * spread
        part = part * (1.0 + mod[0, :, at : at + step]) + mod[1, :, at : at + step]
        normed[:, at : at + step] = part.astype(BF16)


def own_or_other(layer, own, other):
    return jnp.where(lax.axis_index("section") == layer, own, other)


def dot_into(layer, left, own, other, product):
    def into(weight):
        product[...] = dot_nt(left[...], weight[...]).astype(product.dtype)

    held = lax.axis_index("section") == layer
    pl.when(held)(lambda: into(own))
    pl.when(jnp.logical_not(held))(lambda: into(other))


def normalise(layer, stream, mod, other_mod, normed, residual, scales):
    scales[...] = own_or_other(layer, mod[...], other_mod[...])
    norm_into(stream, scales, normed)
    residual[...] = own_columns(stream, slice(None), lax.axis_index("blk")).astype(BF16)


def chunks_of(columns, chunks):
    for j, chunk in enumerate(chunks):
        chunk[...] = pack(columns[:, 192 * j : 192 * j + 192])


def first_projection(arrived, own, other, mod, other_mod, other_out, chunk0, chunk1, chunk2, residual, stream, scales, normed, columns, held, sems):
    holds = lax.axis_index("section") == 0
    parts = sems.shape[0]
    size = held.shape[0] // parts
    copies = [
        pltpu.make_async_copy(own.at[pl.ds(i * size, size)], held.at[pl.ds(i * size, size)], sems.at[i])
        for i in range(parts)
    ]

    @pl.when(holds)
    def _():
        for copy in copies:
            copy.start()

    n = arrived.shape[0]
    rows = stream.shape[0] // n
    for b in range(n):
        stream[rows * b : rows * b + rows, :] = arrived[b, :rows, :].astype(F32)
    normalise(0, stream, mod, other_mod, normed, residual, scales)

    @pl.when(holds)
    def _():
        for copy in copies:
            copy.wait()

    dot_into(0, normed, held, other, columns)
    chunks_of(columns, (chunk0, chunk1, chunk2))


def next_projection(blocks, own, other, mod, other_mod, chunk0, chunk1, chunk2, residual, stream, scales, normed, columns):
    assemble(blocks, stream)
    normalise(1, stream, mod, other_mod, normed, residual, scales)
    dot_into(1, normed, own, other, columns)
    chunks_of(columns, (chunk0, chunk1, chunk2))


def attention(layer, chunk0, chunk1, chunk2, old, fresh, other_fresh, live, attn):
    n = attn.shape[0]
    me, request = lax.axis_index("blk"), lax.axis_index("section")
    first = lax.rem(lax.rem(3 * me, n), 3)
    got = [chunk[...].astype(F32) for chunk in (chunk0, chunk1, chunk2)]

    def kind(of):
        at = lax.rem(first + of, 3)
        return unpack(jnp.where(at == 0, got[0], jnp.where(at == 1, got[1], got[2])))

    queries = kind(0)
    tokens, width = queries.shape
    heads = width // HEAD
    rows = tokens // n
    token = lax.broadcasted_iota(jnp.int32, (tokens, 1), 0)
    is_fresh = jnp.zeros((tokens, 1), jnp.int32)
    for b in range(n):
        flag = own_or_other(layer, fresh[0, request, b], other_fresh[0, request, b])
        is_fresh = jnp.where(token >= b * rows, flag, is_fresh)
    is_fresh = is_fresh == 1
    key = lax.broadcasted_iota(jnp.int32, (1, tokens), 1)
    is_live = jnp.zeros((1, tokens), jnp.int32)
    for b in range(n):
        is_live = jnp.where(key >= b * rows, live[request, b], is_live)
    is_live = is_live == 1
    keys = jnp.where(is_fresh, kind(1), old[layer, :, :width].astype(F32)).astype(BF16)
    values = jnp.where(is_fresh, kind(2), old[layer, :, width:].astype(F32)).astype(BF16)
    head_of = lax.broadcasted_iota(jnp.int32, (tokens, width), 1) // HEAD
    stacked = jnp.concatenate([jnp.where(head_of == h, queries, 0.0) for h in range(heads)], axis=0)
    scores = dot_nt(stacked.astype(BF16), keys) * 0.125
    scores = jnp.where(is_live, scores, -1e30)
    top = jnp.max(scores, axis=-1, keepdims=True)
    weights = jnp.where(is_live, jnp.exp(scores - top), 0.0)
    total = jnp.sum(weights, axis=-1, keepdims=True)
    mixed = jnp.dot(weights.astype(BF16), values, preferred_element_type=F32) * (1.0 / total)
    result = jnp.zeros((tokens, width), F32)
    for h in range(heads):
        result = jnp.where(head_of == h, mixed[h * tokens : (h + 1) * tokens], result)
    packed = pack_by_parity(result, (me & 1) == 1).astype(BF16)
    for d in range(n):
        attn[d] = packed


def layer_columns(layer, blocks, own, other, mod, other_mod, residual, whole, mixed):
    me = lax.axis_index("blk")
    assemble(blocks, whole, by_heads=True)
    dot_into(layer, whole, own, other, mixed)
    gates = own_or_other(layer, mod[2], other_mod[2])
    pairs = [gates[:, at : at + 384] for at in range(0, gates.shape[1], 384)]
    pair = pairs[0]
    for i, other_pair in enumerate(pairs):
        pair = jnp.where(me // 2 == i, other_pair, pair)
    gate = jnp.where((me & 1) == 1, pair[:, 192:], pair[:, :192])
    return (residual[...].astype(F32) + gate * mixed[...].astype(F32)).astype(BF16).astype(F32)


def first_output(blocks, own, other, mod, other_mod, residual, copies, kept, *scratch):
    columns = layer_columns(0, blocks, own, other, mod, other_mod, residual, *scratch)
    packed = pack_by_parity(columns, (lax.axis_index("blk") & 1) == 1).astype(BF16)
    for d in range(copies.shape[0]):
        copies[d] = packed
    kept[...] = columns


def last_output(blocks, own, other, mod, other_mod, residual, kept, by_token, columns, *scratch):
    columns[...] = layer_columns(1, blocks, own, other, mod, other_mod, residual, *scratch)
    n = by_token.shape[0] // 2
    rows = columns.shape[0] // n
    for layer, outs in enumerate((kept, columns)):
        for b in range(n):
            by_token[layer * n + b, :rows, :] = outs[rows * b : rows * b + rows, :].astype(BF16)


def first_exchange(hidden, old_keys, old_values, other_keys, other_values, leaving, held, sems):
    copies = [
        pltpu.make_async_copy(ref, held.at[i], sems.at[i])
        for i, ref in enumerate((hidden, old_keys, old_values, other_keys, other_values))
    ]
    for copy in copies:
        copy.start()
    rows, reqs, width = hidden.shape
    n = leaving.shape[0]
    columns = width // n
    first = lax.axis_index("section") == 0
    for copy in copies:
        copy.wait()

    def of_request(which):
        own = [held[which, i].astype(F32) for i in range(rows)]
        return jnp.concatenate([jnp.where(first, pair[:1], pair[1:]) for pair in own], axis=0)

    mine, *arrays = [of_request(which) for which in range(5)]
    mine = mine.astype(BF16)
    own, other = arrays[:2], arrays[2:]
    stale = [jnp.where(first, a, b) for a, b in zip(own, other)] + [jnp.where(first, b, a) for a, b in zip(own, other)]
    for b in range(n):
        at = columns * (3 * b % n)
        block = jnp.concatenate([array[:, at : at + columns] for array in stale], axis=1)
        leaving[b, :rows, :] = mine
        for i in range(rows):
            leaving[b, rows : rows + 1, i * 4 * columns : (i + 1) * 4 * columns] = block[i : i + 1].astype(BF16)


def stale_by_token(arrived, old, rows):
    n = arrived.shape[0]
    per = rows.shape[1] // n
    wide = rows.shape[2]
    for b in range(n):
        flat = arrived[b, per : per + 1, :].astype(F32)
        for i in range(per):
            for layer in range(2):
                at = (i * 2 + layer) * wide
                rows[layer, per * b + i : per * b + i + 1, :] = flat[:, at : at + wide]
    old[...] = rows[...].astype(BF16)


def to_rows(arrived, out, rows):
    n = arrived.shape[0] // 2
    per, columns = out.shape[0], arrived.shape[2]
    for s in range(2):
        for b in range(n):
            rows[s, :per, columns * b : columns * b + columns] = arrived[s * n + b, :per, :].astype(F32)
    for i in range(per):
        out[i] = jnp.concatenate([rows[s, i : i + 1, :] for s in range(2)], axis=0).astype(BF16)


def exchange(blocks, axis):
    return lax.all_to_all(blocks, axis, split_axis=0, concat_axis=0, tiled=True)


def swap_sections(array):
    return lax.ppermute(array, "section", [(0, 1), (1, 0)])


def by_heads(chunks, n):
    inverse = pow(3, -1, n)
    return [
        lax.ppermute(chunk, "blk", [(b, (b + inverse * j) % n) for b in range(n)]) if j else chunk
        for j, chunk in enumerate(chunks)
    ]


def per_device(hidden, qkv_weight, out_weight, modulation, timestep, fresh, live, k_stale, v_stale):
    n = lax.axis_size("blk")
    columns = out_weight.shape[2]
    reqs, rows, width = hidden.shape
    if not (
        columns == 3 * HEAD
        and n % 3 == 1
        and n & (n - 1) == 0
        and reqs == lax.axis_size("section") == 2
        and rows <= 4
    ):
        return per_device_by_token(
            hidden, qkv_weight, out_weight, modulation, timestep, fresh, live, k_stale, v_stale
        )
    tokens = n * rows
    shape = jax.ShapeDtypeStruct
    packed = shape((tokens * 3 // 2, 128), BF16)
    copies = shape((n, tokens * 3 // 2, 128), BF16)
    cols = shape((tokens, columns), BF16)
    own_qkv = jnp.swapaxes(qkv_weight[0], 0, 1)
    own_out = jnp.swapaxes(out_weight[0], 0, 1)
    steps = jnp.transpose(modulation, (1, 2, 0, 3))
    mod = lax.dynamic_index_in_dim(steps, timestep[0], 0, keepdims=False)
    old_keys = jnp.transpose(k_stale[0], (1, 0, 2))
    old_values = jnp.transpose(v_stale[0], (1, 0, 2))

    small = [swap_sections(array) for array in (old_keys, old_values, mod, fresh)]
    (other_keys, other_values, other_mod, other_fresh), sent_qkv, sent_out = lax.optimization_barrier(
        (small, own_qkv, own_out)
    )
    mods = (mod, other_mod)
    flags = (fresh, other_fresh)
    other_qkv, other_out = swap_sections(sent_qkv), swap_sections(sent_out)
    out = (own_out, other_out)
    leaving = call(
        first_exchange,
        shape((n, 4, width), BF16),
        [pltpu.VMEM((5, rows, reqs, width), BF16), pltpu.SemaphoreType.DMA((5,))],
        (0, 1000000),
        *(pinned(array) for array in (jnp.transpose(hidden, (1, 0, 2)), old_keys, old_values)),
        other_keys,
        other_values,
        specs=[HBM] * 3 + [ANY] * 2,
    )
    arrived = exchange(leaving, "blk")

    blocks = arrived
    for layer in range(2):
        *chunks, residual = call(
            next_projection if layer else first_projection,
            [packed, packed, packed, cols],
            [
                pltpu.VMEM((tokens, width), F32),
                pltpu.VMEM(mod.shape, F32),
                pltpu.VMEM((tokens, width), BF16),
                pltpu.VMEM((tokens, 3 * columns), BF16),
            ]
            + ([] if layer else [pltpu.VMEM(own_qkv.shape, BF16), pltpu.SemaphoreType.DMA((36,))]),
            (2 * tokens * width * 3 * columns, 8 * width * columns),
            blocks,
            *((own_qkv, other_qkv, *mods) if layer else (pinned(own_qkv), other_qkv, *mods, other_out)),
            **({} if layer else {"specs": [VMEM, HBM, VMEM, VMEM, VMEM, ANY]}),
        )
        if layer == 0:
            arrived, chunks[1] = lax.optimization_barrier((arrived, chunks[1]))
            old = call(
                stale_by_token,
                shape((2, tokens, 2 * columns), BF16),
                [pltpu.VMEM((2, tokens, 2 * columns), F32)],
                (0, 200000),
                arrived,
            )
        attn = call(
            functools.partial(attention, layer),
            copies,
            [],
            (8 * tokens * tokens * columns, 300000),
            *by_heads(chunks, n),
            old,
            *flags,
            live,
            specs=[VMEM] * 4 + [SMEM] * 3,
        )
        args = (exchange(attn, "blk"), *out, *mods, residual)
        cost = (2 * tokens * width * columns, 4 * width * columns)
        held = [pltpu.VMEM((tokens, width), BF16), pltpu.VMEM((tokens, columns), BF16)]
        if layer == 0:
            leaving, kept = call(first_output, [copies, shape((tokens, columns), F32)], held, cost, *args)
            blocks = exchange(leaving, "blk")
        else:
            leaving = call(
                last_output,
                shape((2 * n, 4, columns), BF16),
                [pltpu.VMEM((tokens, columns), F32)] + held,
                cost,
                *args,
                kept,
            )
    result = call(
        to_rows,
        shape((rows, reqs, width), BF16),
        [pltpu.VMEM((2, 8, width), F32)],
        (0, 100000),
        exchange(leaving, ("section", "blk")),
    )
    return jnp.transpose(result, (1, 0, 2))[None]


def solution(mesh):
    return jax.shard_map(
        per_device,
        mesh=mesh,
        in_specs=(
            P(None, "blk", None),
            P("section", None, "blk"),
            P("section", None, "blk"),
            P("section", None, None, None),
            P(),
            P("section", None, None),
            P(),
            P("section", None, "blk", None),
            P("section", None, "blk", None),
        ),
        out_specs=P("section", None, "blk", None),
        check_vma=False,
    )
```

```python
import functools

import jax
import jax.numpy as jnp
from jax import lax
from jax.experimental import pallas as pl
from jax.experimental.pallas import tpu as pltpu
from jax.sharding import PartitionSpec as P


def from_behind(shard, axis, by):
    count = lax.axis_size(axis)
    pairs = [(i, i + by) for i in range(count) if 0 <= i + by < count]
    return lax.ppermute(shard, axis, pairs)


def attend(layer_in, qkv_cols, out_cols, modulate, fresh_own, old_keys, old_values, live):
    stream = layer_in.astype(jnp.float32)
    center = jnp.mean(stream, axis=-1, keepdims=True)
    variance = jnp.mean((stream - center) ** 2, axis=-1, keepdims=True)
    normed = (stream - center) / jnp.sqrt(variance + 1e-06) * (1.0 + modulate[0]) + modulate[1]
    normed_b = normed.astype(jnp.bfloat16)
    columns = jnp.einsum(
        "rnd,dc->rnc",
        lax.all_gather(normed_b, "blk", axis=1, tiled=True),
        qkv_cols,
        preferred_element_type=jnp.float32,
    ).astype(jnp.bfloat16)
    projected = lax.all_to_all(columns, "blk", split_axis=1, concat_axis=2, tiled=True)
    num_req, num_rows, width = layer_in.shape
    queries = projected[:, :, :width]
    new_keys = projected[:, :, width : 2 * width]
    new_values = projected[:, :, 2 * width :]
    use_fresh = (fresh_own == 1)[:, None, None]
    keys = jnp.where(use_fresh, new_keys, old_keys)
    values = jnp.where(use_fresh, new_values, old_values)
    num_heads = width // 64
    num_blocks = live.shape[1]
    q_heads = queries.reshape(num_req, num_rows, num_heads, 64)
    live_float = live.astype(jnp.float32)
    run_max = jnp.full((num_req, num_heads, num_rows), -1e30, jnp.float32)
    key_piece = lax.all_gather(keys, "blk", axis=1, tiled=True)
    value_piece = lax.all_gather(values, "blk", axis=1, tiled=True)
    piece_rows = key_piece.shape[1]
    key_heads = key_piece.reshape(num_req, piece_rows, num_heads, 64)
    value_heads = value_piece.reshape(num_req, piece_rows, num_heads, 64)
    scores = (
        jnp.einsum("qrhd,qnhd->qhrn", q_heads, key_heads, preferred_element_type=jnp.float32)
        * 0.125
    )
    block_ids = jnp.arange(piece_rows) // num_rows
    one_hot = (block_ids[:, None] == jnp.arange(num_blocks)[None, :]).astype(jnp.float32)
    usable = jnp.einsum("qb,nb->qn", live_float, one_hot) > 0.5
    usable = usable[:, None, None, :]
    scores = jnp.where(usable, scores, -1e30)
    new_max = jnp.maximum(run_max, jnp.max(scores, axis=-1))
    weights = jnp.where(usable, jnp.exp(scores - new_max[..., None]), 0.0)
    new_sum = jnp.sum(weights, axis=-1)
    new_acc = jnp.einsum(
        "qhrn,qnhd->qhrd", weights, value_heads.astype(jnp.float32), precision=lax.Precision.HIGHEST
    )
    attn = new_acc / new_sum[..., None]
    attn = jnp.transpose(attn, (0, 2, 1, 3)).reshape(num_req, num_rows, width).astype(jnp.bfloat16)
    out_part = jnp.einsum(
        "rnd,dc->rnc",
        lax.all_gather(attn, "blk", axis=1, tiled=True),
        out_cols,
        preferred_element_type=jnp.float32,
    ).astype(jnp.bfloat16)
    mixed_back = lax.all_to_all(out_part, "blk", split_axis=1, concat_axis=2, tiled=True)
    return (stream + modulate[2] * mixed_back.astype(jnp.float32)).astype(jnp.bfloat16)


def pick_request(array, req_idx):
    return lax.dynamic_index_in_dim(array, req_idx, 0, keepdims=True)


def per_device_by_token(hidden, qkv_weight, out_weight, modulation, timestep, fresh, live, k_stale, v_stale):
    section_idx = lax.axis_index("section")
    block_idx = lax.axis_index("blk")
    steps_all = modulation.shape[1]
    pick_row = (jnp.arange(steps_all) == timestep[0]).astype(jnp.float32)
    modulate = jnp.einsum("t,tcd->cd", pick_row, modulation[0], precision=lax.Precision.HIGHEST)
    num_blocks = fresh.shape[2]
    own_column = (jnp.arange(num_blocks) == block_idx).astype(jnp.int32)
    fresh_own = jnp.sum(fresh[0] * own_column[None, :], axis=1)
    qkv_cols = qkv_weight[0]
    out_cols = out_weight[0]
    old_keys = k_stale[0]
    old_values = v_stale[0]
    num_req = hidden.shape[0]
    received = jnp.zeros_like(hidden[0:1])
    first_out = []
    second_out = []
    for tick_idx in range(num_req + 1):
        if tick_idx < num_req:
            own_input = hidden[tick_idx : tick_idx + 1]
        else:
            own_input = jnp.zeros_like(hidden[0:1])
        layer_in = jnp.where(section_idx == 0, own_input, received)
        req_idx = jnp.clip(tick_idx - section_idx, 0, num_req - 1)
        layer_out = attend(
            layer_in,
            qkv_cols,
            out_cols,
            modulate,
            pick_request(fresh_own, req_idx),
            pick_request(old_keys, req_idx),
            pick_request(old_values, req_idx),
            pick_request(live, req_idx),
        )
        if tick_idx < num_req:
            first_out.append(layer_out)
            received = from_behind(layer_out, "section", 1)
        if tick_idx >= 1:
            second_out.append(layer_out)
    result = jnp.where(
        section_idx == 0, jnp.concatenate(first_out, axis=0), jnp.concatenate(second_out, axis=0)
    )
    return result[None]


HEAD = 64
BF16 = jnp.bfloat16
F32 = jnp.float32
NT = (((1,), (1,)), ((), ()))
VMEM = pl.BlockSpec(memory_space=pltpu.VMEM)
SMEM = pl.BlockSpec(memory_space=pltpu.SMEM)
HBM = pl.BlockSpec(memory_space=pltpu.HBM)
ANY = pl.BlockSpec(memory_space=pl.ANY)


def call(body, outs, scratch, cost, *args, specs=None, spare=40 << 20):
    flops, moved = cost
    return pl.pallas_call(
        body,
        out_shape=outs,
        in_specs=specs or [VMEM] * len(args),
        out_specs=jax.tree.map(lambda _: VMEM, outs),
        scratch_shapes=scratch,
        compiler_params=pltpu.CompilerParams(vmem_limit_bytes=(64 << 20) - spare),
        cost_estimate=pl.CostEstimate(flops=flops, bytes_accessed=moved, transcendentals=0),
    )(*args)


def pinned(array):
    return pltpu.with_memory_space_constraint(array, pltpu.HBM)


def dot_nt(left, right):
    return lax.dot_general(left, right, NT, preferred_element_type=F32)


def halves(columns):
    mid = columns.shape[0] // 2
    return jnp.concatenate([columns[:mid], columns[mid:]], axis=1)


def pack(cols):
    return jnp.concatenate([cols[:, :128], halves(cols[:, 128:])], axis=0)


def unpack(packed):
    tokens = packed.shape[0] // 3 * 2
    last = packed[tokens:]
    return jnp.concatenate(
        [packed[:tokens], jnp.concatenate([last[:, :HEAD], last[:, HEAD:]], axis=0)], axis=1
    )


def pack_by_parity(cols, odd):
    mid = cols.shape[0] // 2
    even_form = pack(cols)
    odd_form = jnp.concatenate(
        [
            cols[:, HEAD:],
            jnp.concatenate([cols[mid:, :HEAD], cols[:mid, :HEAD]], axis=1),
        ],
        axis=0,
    )
    return jnp.where(odd, odd_form, even_form)


def assemble(blocks, whole, by_heads=False):
    tokens = whole.shape[0]
    n = blocks.shape[0]
    for d in range(0, n, 2):
        even, odd = [group * pow(3, -1, n) % n if by_heads else group for group in (d, d + 1)]
        even_last, odd_last = blocks[even, tokens:].astype(F32), blocks[odd, tokens:].astype(F32)
        left = lax.broadcasted_iota(jnp.int32, even_last.shape, 1) < HEAD
        first = jnp.where(left, even_last, odd_last)
        second = pltpu.roll(jnp.where(left, odd_last, even_last), HEAD, 1)
        at = d // 2 * 384
        whole[:, at : at + 128] = blocks[even, :tokens].astype(whole.dtype)
        whole[:, at + 128 : at + 256] = jnp.concatenate([first, second], axis=0).astype(whole.dtype)
        whole[:, at + 256 : at + 384] = blocks[odd, :tokens].astype(whole.dtype)


def own_columns(ref, rows, me):
    pair = ref[rows, pl.ds(pl.multiple_of(me // 2 * 384, 128), 384)]
    return jnp.where((me & 1) == 1, pair[:, 192:], pair[:, :192])


def norm_into(stream, mod, normed):
    tokens, width = stream.shape
    step = 128
    total = jnp.zeros((tokens, step), F32)
    for at in range(0, width, step):
        total += stream[:, at : at + step]
    center = jnp.sum(total, axis=-1, keepdims=True) / width
    total = jnp.zeros((tokens, step), F32)
    for at in range(0, width, step):
        off = stream[:, at : at + step] - center
        total += off * off
    variance = jnp.sum(total, axis=-1, keepdims=True) / width
    spread = 1.0 / jnp.sqrt(variance + 1e-06)
    for at in range(0, width, step):
        part = (stream[:, at : at + step] - center) * spread
        part = part * (1.0 + mod[0, :, at : at + step]) + mod[1, :, at : at + step]
        normed[:, at : at + step] = part.astype(BF16)


def own_or_other(layer, own, other):
    return jnp.where(lax.axis_index("section") == layer, own, other)


def dot_into(layer, left, own, other, product):
    def into(weight):
        product[...] = dot_nt(left[...], weight[...]).astype(product.dtype)

    held = lax.axis_index("section") == layer
    pl.when(held)(lambda: into(own))
    pl.when(jnp.logical_not(held))(lambda: into(other))


def normalise(layer, stream, mod, other_mod, normed, residual, scales):
    scales[...] = own_or_other(layer, mod[...], other_mod[...])
    norm_into(stream, scales, normed)
    residual[...] = own_columns(stream, slice(None), lax.axis_index("blk")).astype(BF16)


def chunks_of(columns, chunks):
    for j, chunk in enumerate(chunks):
        chunk[...] = pack(columns[:, 192 * j : 192 * j + 192])


def fetch_if_held(layer, own, first_row, here, sems):
    held = lax.axis_index("section") == layer
    parts = sems.shape[0]
    size = here.shape[0] // parts
    copies = [
        pltpu.make_async_copy(own.at[pl.ds(first_row + i * size, size)], here.at[pl.ds(i * size, size)], sems.at[i])
        for i in range(parts)
    ]

    @pl.when(held)
    def _():
        for copy in copies:
            copy.start()

    def wait():
        @pl.when(held)
        def _():
            for copy in copies:
                copy.wait()

    return wait


def first_projection(arrived, early, own, other, mod, other_mod, other_out, chunk0, chunk1, chunk2, residual, stream, scales, normed, columns, late, sems):
    wait = fetch_if_held(0, own, early.shape[0], late, sems)
    n = arrived.shape[0]
    rows = stream.shape[0] // n
    for b in range(n):
        stream[rows * b : rows * b + rows, :] = arrived[b, :rows, :].astype(F32)
    normalise(0, stream, mod, other_mod, normed, residual, scales)
    wait()
    holds = lax.axis_index("section") == 0
    split = early.shape[0]

    @pl.when(holds)
    def _():
        columns[:, :split] = dot_nt(normed[...], early[...]).astype(BF16)
        columns[:, split:] = dot_nt(normed[...], late[...]).astype(BF16)

    @pl.when(jnp.logical_not(holds))
    def _():
        columns[...] = dot_nt(normed[...], other[...]).astype(BF16)

    chunks_of(columns, (chunk0, chunk1, chunk2))


def next_projection(blocks, own, other, mod, other_mod, chunk0, chunk1, chunk2, residual, stream, scales, normed, columns):
    assemble(blocks, stream)
    normalise(1, stream, mod, other_mod, normed, residual, scales)
    dot_into(1, normed, own, other, columns)
    chunks_of(columns, (chunk0, chunk1, chunk2))


def attention(layer, chunk0, chunk1, chunk2, old, fresh, other_fresh, live, attn):
    n = attn.shape[0]
    me, request = lax.axis_index("blk"), lax.axis_index("section")
    first = lax.rem(lax.rem(3 * me, n), 3)
    got = [chunk[...].astype(F32) for chunk in (chunk0, chunk1, chunk2)]

    def kind(of):
        at = lax.rem(first + of, 3)
        return unpack(jnp.where(at == 0, got[0], jnp.where(at == 1, got[1], got[2])))

    queries = kind(0)
    tokens, width = queries.shape
    heads = width // HEAD
    rows = tokens // n
    token = lax.broadcasted_iota(jnp.int32, (tokens, 1), 0)
    is_fresh = jnp.zeros((tokens, 1), jnp.int32)
    for b in range(n):
        flag = own_or_other(layer, fresh[0, request, b], other_fresh[0, request, b])
        is_fresh = jnp.where(token >= b * rows, flag, is_fresh)
    is_fresh = is_fresh == 1
    key = lax.broadcasted_iota(jnp.int32, (1, tokens), 1)
    is_live = jnp.zeros((1, tokens), jnp.int32)
    for b in range(n):
        is_live = jnp.where(key >= b * rows, live[request, b], is_live)
    is_live = is_live == 1
    keys = jnp.where(is_fresh, kind(1), old[layer, :, :width].astype(F32)).astype(BF16)
    values = jnp.where(is_fresh, kind(2), old[layer, :, width:].astype(F32)).astype(BF16)
    head_of = lax.broadcasted_iota(jnp.int32, (tokens, width), 1) // HEAD
    stacked = jnp.concatenate([jnp.where(head_of == h, queries, 0.0) for h in range(heads)], axis=0)
    scores = dot_nt(stacked.astype(BF16), keys) * 0.125
    scores = jnp.where(is_live, scores, -1e30)
    top = jnp.max(scores, axis=-1, keepdims=True)
    weights = jnp.where(is_live, jnp.exp(scores - top), 0.0)
    total = jnp.sum(weights, axis=-1, keepdims=True)
    mixed = jnp.dot(weights.astype(BF16), values, preferred_element_type=F32) * (1.0 / total)
    result = jnp.zeros((tokens, width), F32)
    for h in range(heads):
        result = jnp.where(head_of == h, mixed[h * tokens : (h + 1) * tokens], result)
    packed = pack_by_parity(result, (me & 1) == 1).astype(BF16)
    for d in range(n):
        attn[d] = packed


def layer_columns(layer, blocks, own, other, mod, other_mod, residual, whole, mixed):
    me = lax.axis_index("blk")
    assemble(blocks, whole, by_heads=True)
    dot_into(layer, whole, own, other, mixed)
    gates = own_or_other(layer, mod[2], other_mod[2])
    pairs = [gates[:, at : at + 384] for at in range(0, gates.shape[1], 384)]
    pair = pairs[0]
    for i, other_pair in enumerate(pairs):
        pair = jnp.where(me // 2 == i, other_pair, pair)
    gate = jnp.where((me & 1) == 1, pair[:, 192:], pair[:, :192])
    return (residual[...].astype(F32) + gate * mixed[...].astype(F32)).astype(BF16).astype(F32)


def first_output(blocks, own, other, mod, other_mod, residual, copies, kept, *scratch):
    columns = layer_columns(0, blocks, own, other, mod, other_mod, residual, *scratch)
    packed = pack_by_parity(columns, (lax.axis_index("blk") & 1) == 1).astype(BF16)
    for d in range(copies.shape[0]):
        copies[d] = packed
    kept[...] = columns


def last_output(blocks, own, other, mod, other_mod, residual, kept, by_token, columns, *scratch):
    columns[...] = layer_columns(1, blocks, own, other, mod, other_mod, residual, *scratch)
    n = by_token.shape[0] // 2
    rows = columns.shape[0] // n
    for layer, outs in enumerate((kept, columns)):
        for b in range(n):
            by_token[layer * n + b, :rows, :] = outs[rows * b : rows * b + rows, :].astype(BF16)


def first_exchange(hidden, old_keys, old_values, other_keys, other_values, weight, leaving, early, held, sems, weight_sems):
    copies = [
        pltpu.make_async_copy(ref, held.at[i], sems.at[i])
        for i, ref in enumerate((hidden, old_keys, old_values, other_keys, other_values))
    ]
    for copy in copies:
        copy.start()
    wait = fetch_if_held(0, weight, 0, early, weight_sems)
    rows, reqs, width = hidden.shape
    n = leaving.shape[0]
    columns = width // n
    first = lax.axis_index("section") == 0
    for copy in copies:
        copy.wait()

    def of_request(which):
        own = [held[which, i].astype(F32) for i in range(rows)]
        return jnp.concatenate([jnp.where(first, pair[:1], pair[1:]) for pair in own], axis=0)

    mine, *arrays = [of_request(which) for which in range(5)]
    mine = mine.astype(BF16)
    own, other = arrays[:2], arrays[2:]
    stale = [jnp.where(first, a, b) for a, b in zip(own, other)] + [jnp.where(first, b, a) for a, b in zip(own, other)]
    for b in range(n):
        at = columns * (3 * b % n)
        block = jnp.concatenate([array[:, at : at + columns] for array in stale], axis=1)
        leaving[b, :rows, :] = mine
        for i in range(rows):
            leaving[b, rows : rows + 1, i * 4 * columns : (i + 1) * 4 * columns] = block[i : i + 1].astype(BF16)
    wait()


def stale_by_token(arrived, old, rows):
    n = arrived.shape[0]
    per = rows.shape[1] // n
    wide = rows.shape[2]
    for b in range(n):
        flat = arrived[b, per : per + 1, :].astype(F32)
        for i in range(per):
            for layer in range(2):
                at = (i * 2 + layer) * wide
                rows[layer, per * b + i : per * b + i + 1, :] = flat[:, at : at + wide]
    old[...] = rows[...].astype(BF16)


def to_rows(arrived, out, rows):
    n = arrived.shape[0] // 2
    per, columns = out.shape[0], arrived.shape[2]
    for s in range(2):
        for b in range(n):
            rows[s, :per, columns * b : columns * b + columns] = arrived[s * n + b, :per, :].astype(F32)
    for i in range(per):
        out[i] = jnp.concatenate([rows[s, i : i + 1, :] for s in range(2)], axis=0).astype(BF16)


def exchange(blocks, axis):
    return lax.all_to_all(blocks, axis, split_axis=0, concat_axis=0, tiled=True)


def swap_sections(array):
    return lax.ppermute(array, "section", [(0, 1), (1, 0)])


def by_heads(chunks, n):
    inverse = pow(3, -1, n)
    return [
        lax.ppermute(chunk, "blk", [(b, (b + inverse * j) % n) for b in range(n)]) if j else chunk
        for j, chunk in enumerate(chunks)
    ]


def per_device(hidden, qkv_weight, out_weight, modulation, timestep, fresh, live, k_stale, v_stale):
    n = lax.axis_size("blk")
    columns = out_weight.shape[2]
    reqs, rows, width = hidden.shape
    if not (
        columns == 3 * HEAD
        and n % 3 == 1
        and n & (n - 1) == 0
        and reqs == lax.axis_size("section") == 2
        and rows <= 4
    ):
        return per_device_by_token(
            hidden, qkv_weight, out_weight, modulation, timestep, fresh, live, k_stale, v_stale
        )
    tokens = n * rows
    shape = jax.ShapeDtypeStruct
    packed = shape((tokens * 3 // 2, 128), BF16)
    copies = shape((n, tokens * 3 // 2, 128), BF16)
    cols = shape((tokens, columns), BF16)
    own_qkv = jnp.swapaxes(qkv_weight[0], 0, 1)
    own_out = jnp.swapaxes(out_weight[0], 0, 1)
    steps = jnp.transpose(modulation, (1, 2, 0, 3))
    mod = lax.dynamic_index_in_dim(steps, timestep[0], 0, keepdims=False)
    old_keys = jnp.transpose(k_stale[0], (1, 0, 2))
    old_values = jnp.transpose(v_stale[0], (1, 0, 2))

    small = [swap_sections(array) for array in (old_keys, old_values, mod, fresh)]
    (other_keys, other_values, other_mod, other_fresh), sent_qkv, sent_out = lax.optimization_barrier(
        (small, own_qkv, own_out)
    )
    mods = (mod, other_mod)
    flags = (fresh, other_fresh)
    other_qkv, other_out = swap_sections(sent_qkv), swap_sections(sent_out)
    out = (own_out, other_out)
    split = 256
    leaving, early = call(
        first_exchange,
        [shape((n, 4, width), BF16), shape((split, width), BF16)],
        [
            pltpu.VMEM((5, rows, reqs, width), BF16),
            pltpu.SemaphoreType.DMA((5,)),
            pltpu.SemaphoreType.DMA((16,)),
        ],
        (0, 1000000),
        *(pinned(array) for array in (jnp.transpose(hidden, (1, 0, 2)), old_keys, old_values)),
        other_keys,
        other_values,
        pinned(own_qkv),
        specs=[HBM] * 3 + [ANY] * 2 + [HBM],
    )
    arrived = exchange(leaving, "blk")

    blocks = arrived
    for layer in range(2):
        *chunks, residual = call(
            next_projection if layer else first_projection,
            [packed, packed, packed, cols],
            [
                pltpu.VMEM((tokens, width), F32),
                pltpu.VMEM(mod.shape, F32),
                pltpu.VMEM((tokens, width), BF16),
                pltpu.VMEM((tokens, 3 * columns), BF16),
            ]
            + ([] if layer else [pltpu.VMEM((3 * columns - split, width), BF16), pltpu.SemaphoreType.DMA((20,))]),
            (2 * tokens * width * 3 * columns, 8 * width * columns),
            blocks,
            *((own_qkv, other_qkv, *mods) if layer else (early, pinned(own_qkv), other_qkv, *mods, other_out)),
            **({} if layer else {"specs": [VMEM, VMEM, HBM, VMEM, VMEM, VMEM, ANY]}),
        )
        if layer == 0:
            arrived, chunks[1] = lax.optimization_barrier((arrived, chunks[1]))
            old = call(
                stale_by_token,
                shape((2, tokens, 2 * columns), BF16),
                [pltpu.VMEM((2, tokens, 2 * columns), F32)],
                (0, 200000),
                arrived,
            )
        attn = call(
            functools.partial(attention, layer),
            copies,
            [],
            (8 * tokens * tokens * columns, 300000),
            *by_heads(chunks, n),
            old,
            *flags,
            live,
            specs=[VMEM] * 4 + [SMEM] * 3,
        )
        args = (exchange(attn, "blk"), *out, *mods, residual)
        cost = (2 * tokens * width * columns, 4 * width * columns)
        held = [pltpu.VMEM((tokens, width), BF16), pltpu.VMEM((tokens, columns), BF16)]
        if layer == 0:
            leaving, kept = call(first_output, [copies, shape((tokens, columns), F32)], held, cost, *args)
            blocks = exchange(leaving, "blk")
        else:
            leaving = call(
                last_output,
                shape((2 * n, 4, columns), BF16),
                [pltpu.VMEM((tokens, columns), F32)] + held,
                cost,
                *args,
                kept,
            )
    result = call(
        to_rows,
        shape((rows, reqs, width), BF16),
        [pltpu.VMEM((2, 8, width), F32)],
        (0, 100000),
        exchange(leaving, ("section", "blk")),
    )
    return jnp.transpose(result, (1, 0, 2))[None]


def solution(mesh):
    return jax.shard_map(
        per_device,
        mesh=mesh,
        in_specs=(
            P(None, "blk", None),
            P("section", None, "blk"),
            P("section", None, "blk"),
            P("section", None, None, None),
            P(),
            P("section", None, None),
            P(),
            P("section", None, "blk", None),
            P("section", None, "blk", None),
        ),
        out_specs=P("section", None, "blk", None),
        check_vma=False,
    )
```

```python
import functools

import jax
import jax.numpy as jnp
from jax import lax
from jax.experimental import pallas as pl
from jax.experimental.pallas import tpu as pltpu
from jax.sharding import PartitionSpec as P


def from_behind(shard, axis, by):
    count = lax.axis_size(axis)
    pairs = [(i, i + by) for i in range(count) if 0 <= i + by < count]
    return lax.ppermute(shard, axis, pairs)


def attend(layer_in, qkv_cols, out_cols, modulate, fresh_own, old_keys, old_values, live):
    stream = layer_in.astype(jnp.float32)
    center = jnp.mean(stream, axis=-1, keepdims=True)
    variance = jnp.mean((stream - center) ** 2, axis=-1, keepdims=True)
    normed = (stream - center) / jnp.sqrt(variance + 1e-06) * (1.0 + modulate[0]) + modulate[1]
    normed_b = normed.astype(jnp.bfloat16)
    columns = jnp.einsum(
        "rnd,dc->rnc",
        lax.all_gather(normed_b, "blk", axis=1, tiled=True),
        qkv_cols,
        preferred_element_type=jnp.float32,
    ).astype(jnp.bfloat16)
    projected = lax.all_to_all(columns, "blk", split_axis=1, concat_axis=2, tiled=True)
    num_req, num_rows, width = layer_in.shape
    queries = projected[:, :, :width]
    new_keys = projected[:, :, width : 2 * width]
    new_values = projected[:, :, 2 * width :]
    use_fresh = (fresh_own == 1)[:, None, None]
    keys = jnp.where(use_fresh, new_keys, old_keys)
    values = jnp.where(use_fresh, new_values, old_values)
    num_heads = width // 64
    num_blocks = live.shape[1]
    q_heads = queries.reshape(num_req, num_rows, num_heads, 64)
    live_float = live.astype(jnp.float32)
    run_max = jnp.full((num_req, num_heads, num_rows), -1e30, jnp.float32)
    key_piece = lax.all_gather(keys, "blk", axis=1, tiled=True)
    value_piece = lax.all_gather(values, "blk", axis=1, tiled=True)
    piece_rows = key_piece.shape[1]
    key_heads = key_piece.reshape(num_req, piece_rows, num_heads, 64)
    value_heads = value_piece.reshape(num_req, piece_rows, num_heads, 64)
    scores = (
        jnp.einsum("qrhd,qnhd->qhrn", q_heads, key_heads, preferred_element_type=jnp.float32)
        * 0.125
    )
    block_ids = jnp.arange(piece_rows) // num_rows
    one_hot = (block_ids[:, None] == jnp.arange(num_blocks)[None, :]).astype(jnp.float32)
    usable = jnp.einsum("qb,nb->qn", live_float, one_hot) > 0.5
    usable = usable[:, None, None, :]
    scores = jnp.where(usable, scores, -1e30)
    new_max = jnp.maximum(run_max, jnp.max(scores, axis=-1))
    weights = jnp.where(usable, jnp.exp(scores - new_max[..., None]), 0.0)
    new_sum = jnp.sum(weights, axis=-1)
    new_acc = jnp.einsum(
        "qhrn,qnhd->qhrd", weights, value_heads.astype(jnp.float32), precision=lax.Precision.HIGHEST
    )
    attn = new_acc / new_sum[..., None]
    attn = jnp.transpose(attn, (0, 2, 1, 3)).reshape(num_req, num_rows, width).astype(jnp.bfloat16)
    out_part = jnp.einsum(
        "rnd,dc->rnc",
        lax.all_gather(attn, "blk", axis=1, tiled=True),
        out_cols,
        preferred_element_type=jnp.float32,
    ).astype(jnp.bfloat16)
    mixed_back = lax.all_to_all(out_part, "blk", split_axis=1, concat_axis=2, tiled=True)
    return (stream + modulate[2] * mixed_back.astype(jnp.float32)).astype(jnp.bfloat16)


def pick_request(array, req_idx):
    return lax.dynamic_index_in_dim(array, req_idx, 0, keepdims=True)


def per_device_by_token(hidden, qkv_weight, out_weight, modulation, timestep, fresh, live, k_stale, v_stale):
    section_idx = lax.axis_index("section")
    block_idx = lax.axis_index("blk")
    steps_all = modulation.shape[1]
    pick_row = (jnp.arange(steps_all) == timestep[0]).astype(jnp.float32)
    modulate = jnp.einsum("t,tcd->cd", pick_row, modulation[0], precision=lax.Precision.HIGHEST)
    num_blocks = fresh.shape[2]
    own_column = (jnp.arange(num_blocks) == block_idx).astype(jnp.int32)
    fresh_own = jnp.sum(fresh[0] * own_column[None, :], axis=1)
    qkv_cols = qkv_weight[0]
    out_cols = out_weight[0]
    old_keys = k_stale[0]
    old_values = v_stale[0]
    num_req = hidden.shape[0]
    received = jnp.zeros_like(hidden[0:1])
    first_out = []
    second_out = []
    for tick_idx in range(num_req + 1):
        if tick_idx < num_req:
            own_input = hidden[tick_idx : tick_idx + 1]
        else:
            own_input = jnp.zeros_like(hidden[0:1])
        layer_in = jnp.where(section_idx == 0, own_input, received)
        req_idx = jnp.clip(tick_idx - section_idx, 0, num_req - 1)
        layer_out = attend(
            layer_in,
            qkv_cols,
            out_cols,
            modulate,
            pick_request(fresh_own, req_idx),
            pick_request(old_keys, req_idx),
            pick_request(old_values, req_idx),
            pick_request(live, req_idx),
        )
        if tick_idx < num_req:
            first_out.append(layer_out)
            received = from_behind(layer_out, "section", 1)
        if tick_idx >= 1:
            second_out.append(layer_out)
    result = jnp.where(
        section_idx == 0, jnp.concatenate(first_out, axis=0), jnp.concatenate(second_out, axis=0)
    )
    return result[None]


HEAD = 64
BF16 = jnp.bfloat16
F32 = jnp.float32
NT = (((1,), (1,)), ((), ()))
VMEM = pl.BlockSpec(memory_space=pltpu.VMEM)
SMEM = pl.BlockSpec(memory_space=pltpu.SMEM)
HBM = pl.BlockSpec(memory_space=pltpu.HBM)
ANY = pl.BlockSpec(memory_space=pl.ANY)


def call(body, outs, scratch, cost, *args, specs=None, spare=40 << 20):
    flops, moved = cost
    return pl.pallas_call(
        body,
        out_shape=outs,
        in_specs=specs or [VMEM] * len(args),
        out_specs=jax.tree.map(lambda _: VMEM, outs),
        scratch_shapes=scratch,
        compiler_params=pltpu.CompilerParams(vmem_limit_bytes=(64 << 20) - spare),
        cost_estimate=pl.CostEstimate(flops=flops, bytes_accessed=moved, transcendentals=0),
    )(*args)


def pinned(array):
    return pltpu.with_memory_space_constraint(array, pltpu.HBM)


def dot_nt(left, right):
    return lax.dot_general(left, right, NT, preferred_element_type=F32)


def halves(columns):
    mid = columns.shape[0] // 2
    return jnp.concatenate([columns[:mid], columns[mid:]], axis=1)


def pack(cols):
    return jnp.concatenate([cols[:, :128], halves(cols[:, 128:])], axis=0)


def unpack(packed):
    tokens = packed.shape[0] // 3 * 2
    last = packed[tokens:]
    return jnp.concatenate(
        [packed[:tokens], jnp.concatenate([last[:, :HEAD], last[:, HEAD:]], axis=0)], axis=1
    )


def pack_by_parity(cols, odd):
    mid = cols.shape[0] // 2
    even_form = pack(cols)
    odd_form = jnp.concatenate(
        [
            cols[:, HEAD:],
            jnp.concatenate([cols[mid:, :HEAD], cols[:mid, :HEAD]], axis=1),
        ],
        axis=0,
    )
    return jnp.where(odd, odd_form, even_form)


def assemble(blocks, whole, by_heads=False):
    tokens = whole.shape[0]
    n = blocks.shape[0]
    for d in range(0, n, 2):
        even, odd = [group * pow(3, -1, n) % n if by_heads else group for group in (d, d + 1)]
        even_last, odd_last = blocks[even, tokens:].astype(F32), blocks[odd, tokens:].astype(F32)
        left = lax.broadcasted_iota(jnp.int32, even_last.shape, 1) < HEAD
        first = jnp.where(left, even_last, odd_last)
        second = pltpu.roll(jnp.where(left, odd_last, even_last), HEAD, 1)
        at = d // 2 * 384
        whole[:, at : at + 128] = blocks[even, :tokens].astype(whole.dtype)
        whole[:, at + 128 : at + 256] = jnp.concatenate([first, second], axis=0).astype(whole.dtype)
        whole[:, at + 256 : at + 384] = blocks[odd, :tokens].astype(whole.dtype)


def own_columns(ref, rows, me):
    pair = ref[rows, pl.ds(pl.multiple_of(me // 2 * 384, 128), 384)]
    return jnp.where((me & 1) == 1, pair[:, 192:], pair[:, :192])


def norm_into(stream, mod, normed):
    tokens, width = stream.shape
    step = 128
    total = jnp.zeros((tokens, step), F32)
    for at in range(0, width, step):
        total += stream[:, at : at + step]
    center = jnp.sum(total, axis=-1, keepdims=True) / width
    total = jnp.zeros((tokens, step), F32)
    for at in range(0, width, step):
        off = stream[:, at : at + step] - center
        total += off * off
    variance = jnp.sum(total, axis=-1, keepdims=True) / width
    spread = 1.0 / jnp.sqrt(variance + 1e-06)
    for at in range(0, width, step):
        part = (stream[:, at : at + step] - center) * spread
        part = part * (1.0 + mod[0, :, at : at + step]) + mod[1, :, at : at + step]
        normed[:, at : at + step] = part.astype(BF16)


def own_or_other(layer, own, other):
    return jnp.where(lax.axis_index("section") == layer, own, other)


def dot_into(layer, left, own, other, product):
    def into(weight):
        product[...] = dot_nt(left[...], weight[...]).astype(product.dtype)

    held = lax.axis_index("section") == layer
    pl.when(held)(lambda: into(own))
    pl.when(jnp.logical_not(held))(lambda: into(other))


def normalise(layer, stream, mod, other_mod, normed, residual, scales):
    scales[...] = own_or_other(layer, mod[...], other_mod[...])
    norm_into(stream, scales, normed)
    residual[...] = own_columns(stream, slice(None), lax.axis_index("blk")).astype(BF16)


def chunks_of(columns, chunks):
    for j, chunk in enumerate(chunks):
        chunk[...] = pack(columns[:, 192 * j : 192 * j + 192])


def first_projection(arrived, own, other, mod, other_mod, other_out, chunk0, chunk1, chunk2, residual, stream, scales, normed, columns, held, sems):
    holds = lax.axis_index("section") == 0
    parts = sems.shape[0]
    size = held.shape[0] // parts
    copies = [
        pltpu.make_async_copy(own.at[pl.ds(i * size, size)], held.at[pl.ds(i * size, size)], sems.at[i])
        for i in range(parts)
    ]

    @pl.when(holds)
    def _():
        for copy in copies:
            copy.start()

    n = arrived.shape[0]
    rows = stream.shape[0] // n
    for b in range(n):
        stream[rows * b : rows * b + rows, :] = arrived[b, :rows, :].astype(F32)
    normalise(0, stream, mod, other_mod, normed, residual, scales)

    @pl.when(holds)
    def _():
        for copy in copies:
            copy.wait()

    dot_into(0, normed, held, other, columns)
    chunks_of(columns, (chunk0, chunk1, chunk2))


def next_projection(blocks, own, other, mod, other_mod, chunk0, chunk1, chunk2, residual, stream, scales, normed, columns):
    assemble(blocks, stream)
    normalise(1, stream, mod, other_mod, normed, residual, scales)
    dot_into(1, normed, own, other, columns)
    chunks_of(columns, (chunk0, chunk1, chunk2))


def attention(layer, chunk0, chunk1, chunk2, old, fresh, other_fresh, live, attn):
    n = attn.shape[0]
    me, request = lax.axis_index("blk"), lax.axis_index("section")
    first = lax.rem(lax.rem(3 * me, n), 3)
    got = [chunk[...].astype(F32) for chunk in (chunk0, chunk1, chunk2)]

    def kind(of):
        at = lax.rem(first + of, 3)
        return unpack(jnp.where(at == 0, got[0], jnp.where(at == 1, got[1], got[2])))

    queries = kind(0)
    tokens, width = queries.shape
    heads = width // HEAD
    rows = tokens // n
    token = lax.broadcasted_iota(jnp.int32, (tokens, 1), 0)
    is_fresh = jnp.zeros((tokens, 1), jnp.int32)
    for b in range(n):
        flag = own_or_other(layer, fresh[0, request, b], other_fresh[0, request, b])
        is_fresh = jnp.where(token >= b * rows, flag, is_fresh)
    is_fresh = is_fresh == 1
    key = lax.broadcasted_iota(jnp.int32, (1, tokens), 1)
    is_live = jnp.zeros((1, tokens), jnp.int32)
    for b in range(n):
        is_live = jnp.where(key >= b * rows, live[request, b], is_live)
    is_live = is_live == 1
    keys = jnp.where(is_fresh, kind(1), old[layer, :, :width].astype(F32)).astype(BF16)
    values = jnp.where(is_fresh, kind(2), old[layer, :, width:].astype(F32)).astype(BF16)
    head_of = lax.broadcasted_iota(jnp.int32, (tokens, width), 1) // HEAD
    stacked = jnp.concatenate([jnp.where(head_of == h, queries, 0.0) for h in range(heads)], axis=0)
    scores = dot_nt(stacked.astype(BF16), keys) * 0.125
    scores = jnp.where(is_live, scores, -1e30)
    top = jnp.max(scores, axis=-1, keepdims=True)
    weights = jnp.where(is_live, jnp.exp(scores - top), 0.0)
    total = jnp.sum(weights, axis=-1, keepdims=True)
    mixed = jnp.dot(weights.astype(BF16), values, preferred_element_type=F32) * (1.0 / total)
    result = jnp.zeros((tokens, width), F32)
    for h in range(heads):
        result = jnp.where(head_of == h, mixed[h * tokens : (h + 1) * tokens], result)
    packed = pack_by_parity(result, (me & 1) == 1).astype(BF16)
    for d in range(n):
        attn[d] = packed


def layer_columns(layer, blocks, own, other, mod, other_mod, residual, whole, mixed):
    me = lax.axis_index("blk")
    assemble(blocks, whole, by_heads=True)
    dot_into(layer, whole, own, other, mixed)
    gates = own_or_other(layer, mod[2], other_mod[2])
    pairs = [gates[:, at : at + 384] for at in range(0, gates.shape[1], 384)]
    pair = pairs[0]
    for i, other_pair in enumerate(pairs):
        pair = jnp.where(me // 2 == i, other_pair, pair)
    gate = jnp.where((me & 1) == 1, pair[:, 192:], pair[:, :192])
    return (residual[...].astype(F32) + gate * mixed[...].astype(F32)).astype(BF16).astype(F32)


def first_output(blocks, own, other, mod, other_mod, residual, copies, kept, *scratch):
    columns = layer_columns(0, blocks, own, other, mod, other_mod, residual, *scratch)
    packed = pack_by_parity(columns, (lax.axis_index("blk") & 1) == 1).astype(BF16)
    for d in range(copies.shape[0]):
        copies[d] = packed
    kept[...] = columns


def last_output(blocks, own, other, mod, other_mod, residual, kept, by_token, columns, *scratch):
    columns[...] = layer_columns(1, blocks, own, other, mod, other_mod, residual, *scratch)
    n = by_token.shape[0] // 2
    rows = columns.shape[0] // n
    for layer, outs in enumerate((kept, columns)):
        for b in range(n):
            by_token[layer * n + b, :rows, :] = outs[rows * b : rows * b + rows, :].astype(BF16)


def first_exchange(hidden, old_keys, old_values, other_keys, other_values, leaving, held, sems):
    copies = [
        pltpu.make_async_copy(ref, held.at[i], sems.at[i])
        for i, ref in enumerate((hidden, old_keys, old_values, other_keys, other_values))
    ]
    for copy in copies:
        copy.start()
    rows, reqs, width = hidden.shape
    n = leaving.shape[0]
    columns = width // n
    first = lax.axis_index("section") == 0
    for copy in copies:
        copy.wait()

    def of_request(which):
        own = [held[which, i].astype(F32) for i in range(rows)]
        return jnp.concatenate([jnp.where(first, pair[:1], pair[1:]) for pair in own], axis=0)

    mine, *arrays = [of_request(which) for which in range(5)]
    mine = mine.astype(BF16)
    own, other = arrays[:2], arrays[2:]
    stale = [jnp.where(first, a, b) for a, b in zip(own, other)] + [jnp.where(first, b, a) for a, b in zip(own, other)]
    for b in range(n):
        at = columns * (3 * b % n)
        block = jnp.concatenate([array[:, at : at + columns] for array in stale], axis=1)
        leaving[b, :rows, :] = mine
        for i in range(rows):
            leaving[b, rows : rows + 1, i * 4 * columns : (i + 1) * 4 * columns] = block[i : i + 1].astype(BF16)


def stale_by_token(arrived, old, rows):
    n = arrived.shape[0]
    per = rows.shape[1] // n
    wide = rows.shape[2]
    for b in range(n):
        flat = arrived[b, per : per + 1, :].astype(F32)
        for i in range(per):
            for layer in range(2):
                at = (i * 2 + layer) * wide
                rows[layer, per * b + i : per * b + i + 1, :] = flat[:, at : at + wide]
    old[...] = rows[...].astype(BF16)


def to_rows(arrived, out, rows):
    n = arrived.shape[0] // 2
    per, columns = out.shape[0], arrived.shape[2]
    for s in range(2):
        for b in range(n):
            rows[s, :per, columns * b : columns * b + columns] = arrived[s * n + b, :per, :].astype(F32)
    for i in range(per):
        out[i] = jnp.concatenate([rows[s, i : i + 1, :] for s in range(2)], axis=0).astype(BF16)


def exchange(blocks, axis):
    return lax.all_to_all(blocks, axis, split_axis=0, concat_axis=0, tiled=True)


def swap_sections(array):
    return lax.ppermute(array, "section", [(0, 1), (1, 0)])


def by_heads(chunks, n):
    inverse = pow(3, -1, n)
    return [
        lax.ppermute(chunk, "blk", [(b, (b + inverse * j) % n) for b in range(n)]) if j else chunk
        for j, chunk in enumerate(chunks)
    ]


def per_device(hidden, qkv_weight, out_weight, modulation, timestep, fresh, live, k_stale, v_stale):
    n = lax.axis_size("blk")
    columns = out_weight.shape[2]
    reqs, rows, width = hidden.shape
    if not (
        columns == 3 * HEAD
        and n % 3 == 1
        and n & (n - 1) == 0
        and reqs == lax.axis_size("section") == 2
        and rows <= 4
    ):
        return per_device_by_token(
            hidden, qkv_weight, out_weight, modulation, timestep, fresh, live, k_stale, v_stale
        )
    tokens = n * rows
    shape = jax.ShapeDtypeStruct
    packed = shape((tokens * 3 // 2, 128), BF16)
    copies = shape((n, tokens * 3 // 2, 128), BF16)
    cols = shape((tokens, columns), BF16)
    own_qkv = jnp.swapaxes(qkv_weight[0], 0, 1)
    own_out = jnp.swapaxes(out_weight[0], 0, 1)
    steps = jnp.transpose(modulation, (1, 2, 0, 3))
    old_keys = jnp.transpose(k_stale[0], (1, 0, 2))
    old_values = jnp.transpose(v_stale[0], (1, 0, 2))

    other_keys, other_values, timestep = lax.optimization_barrier(
        (swap_sections(old_keys), swap_sections(old_values), timestep)
    )
    mod = lax.dynamic_index_in_dim(steps, timestep[0], 0, keepdims=False)
    other_mod, other_fresh, sent_qkv, sent_out = lax.optimization_barrier(
        (swap_sections(mod), swap_sections(fresh), own_qkv, own_out)
    )
    mods = (mod, other_mod)
    flags = (fresh, other_fresh)
    other_qkv, other_out = swap_sections(sent_qkv), swap_sections(sent_out)
    out = (own_out, other_out)
    leaving = call(
        first_exchange,
        shape((n, 4, width), BF16),
        [pltpu.VMEM((5, rows, reqs, width), BF16), pltpu.SemaphoreType.DMA((5,))],
        (0, 1000000),
        *(pinned(array) for array in (jnp.transpose(hidden, (1, 0, 2)), old_keys, old_values)),
        other_keys,
        other_values,
        specs=[HBM] * 3 + [ANY] * 2,
    )
    arrived = exchange(leaving, "blk")

    blocks = arrived
    for layer in range(2):
        *chunks, residual = call(
            next_projection if layer else first_projection,
            [packed, packed, packed, cols],
            [
                pltpu.VMEM((tokens, width), F32),
                pltpu.VMEM(mod.shape, F32),
                pltpu.VMEM((tokens, width), BF16),
                pltpu.VMEM((tokens, 3 * columns), BF16),
            ]
            + ([] if layer else [pltpu.VMEM(own_qkv.shape, BF16), pltpu.SemaphoreType.DMA((36,))]),
            (2 * tokens * width * 3 * columns, 8 * width * columns),
            blocks,
            *((own_qkv, other_qkv, *mods) if layer else (pinned(own_qkv), other_qkv, *mods, other_out)),
            **({} if layer else {"specs": [VMEM, HBM, VMEM, VMEM, VMEM, ANY]}),
        )
        if layer == 0:
            arrived, chunks[1] = lax.optimization_barrier((arrived, chunks[1]))
            old = call(
                stale_by_token,
                shape((2, tokens, 2 * columns), BF16),
                [pltpu.VMEM((2, tokens, 2 * columns), F32)],
                (0, 200000),
                arrived,
            )
        attn = call(
            functools.partial(attention, layer),
            copies,
            [],
            (8 * tokens * tokens * columns, 300000),
            *by_heads(chunks, n),
            old,
            *flags,
            live,
            specs=[VMEM] * 4 + [SMEM] * 3,
        )
        args = (exchange(attn, "blk"), *out, *mods, residual)
        cost = (2 * tokens * width * columns, 4 * width * columns)
        held = [pltpu.VMEM((tokens, width), BF16), pltpu.VMEM((tokens, columns), BF16)]
        if layer == 0:
            leaving, kept = call(first_output, [copies, shape((tokens, columns), F32)], held, cost, *args)
            blocks = exchange(leaving, "blk")
        else:
            leaving = call(
                last_output,
                shape((2 * n, 4, columns), BF16),
                [pltpu.VMEM((tokens, columns), F32)] + held,
                cost,
                *args,
                kept,
            )
    result = call(
        to_rows,
        shape((rows, reqs, width), BF16),
        [pltpu.VMEM((2, 8, width), F32)],
        (0, 100000),
        exchange(leaving, ("section", "blk")),
    )
    return jnp.transpose(result, (1, 0, 2))[None]


def solution(mesh):
    return jax.shard_map(
        per_device,
        mesh=mesh,
        in_specs=(
            P(None, "blk", None),
            P("section", None, "blk"),
            P("section", None, "blk"),
            P("section", None, None, None),
            P(),
            P("section", None, None),
            P(),
            P("section", None, "blk", None),
            P("section", None, "blk", None),
        ),
        out_specs=P("section", None, "blk", None),
        check_vma=False,
    )
```

```python
import functools

import jax
import jax.numpy as jnp
from jax import lax
from jax.experimental import pallas as pl
from jax.experimental.pallas import tpu as pltpu
from jax.sharding import PartitionSpec as P


def from_behind(shard, axis, by):
    count = lax.axis_size(axis)
    pairs = [(i, i + by) for i in range(count) if 0 <= i + by < count]
    return lax.ppermute(shard, axis, pairs)


def attend(layer_in, qkv_cols, out_cols, modulate, fresh_own, old_keys, old_values, live):
    stream = layer_in.astype(jnp.float32)
    center = jnp.mean(stream, axis=-1, keepdims=True)
    variance = jnp.mean((stream - center) ** 2, axis=-1, keepdims=True)
    normed = (stream - center) / jnp.sqrt(variance + 1e-06) * (1.0 + modulate[0]) + modulate[1]
    normed_b = normed.astype(jnp.bfloat16)
    columns = jnp.einsum(
        "rnd,dc->rnc",
        lax.all_gather(normed_b, "blk", axis=1, tiled=True),
        qkv_cols,
        preferred_element_type=jnp.float32,
    ).astype(jnp.bfloat16)
    projected = lax.all_to_all(columns, "blk", split_axis=1, concat_axis=2, tiled=True)
    num_req, num_rows, width = layer_in.shape
    queries = projected[:, :, :width]
    new_keys = projected[:, :, width : 2 * width]
    new_values = projected[:, :, 2 * width :]
    use_fresh = (fresh_own == 1)[:, None, None]
    keys = jnp.where(use_fresh, new_keys, old_keys)
    values = jnp.where(use_fresh, new_values, old_values)
    num_heads = width // 64
    num_blocks = live.shape[1]
    q_heads = queries.reshape(num_req, num_rows, num_heads, 64)
    live_float = live.astype(jnp.float32)
    run_max = jnp.full((num_req, num_heads, num_rows), -1e30, jnp.float32)
    key_piece = lax.all_gather(keys, "blk", axis=1, tiled=True)
    value_piece = lax.all_gather(values, "blk", axis=1, tiled=True)
    piece_rows = key_piece.shape[1]
    key_heads = key_piece.reshape(num_req, piece_rows, num_heads, 64)
    value_heads = value_piece.reshape(num_req, piece_rows, num_heads, 64)
    scores = (
        jnp.einsum("qrhd,qnhd->qhrn", q_heads, key_heads, preferred_element_type=jnp.float32)
        * 0.125
    )
    block_ids = jnp.arange(piece_rows) // num_rows
    one_hot = (block_ids[:, None] == jnp.arange(num_blocks)[None, :]).astype(jnp.float32)
    usable = jnp.einsum("qb,nb->qn", live_float, one_hot) > 0.5
    usable = usable[:, None, None, :]
    scores = jnp.where(usable, scores, -1e30)
    new_max = jnp.maximum(run_max, jnp.max(scores, axis=-1))
    weights = jnp.where(usable, jnp.exp(scores - new_max[..., None]), 0.0)
    new_sum = jnp.sum(weights, axis=-1)
    new_acc = jnp.einsum(
        "qhrn,qnhd->qhrd", weights, value_heads.astype(jnp.float32), precision=lax.Precision.HIGHEST
    )
    attn = new_acc / new_sum[..., None]
    attn = jnp.transpose(attn, (0, 2, 1, 3)).reshape(num_req, num_rows, width).astype(jnp.bfloat16)
    out_part = jnp.einsum(
        "rnd,dc->rnc",
        lax.all_gather(attn, "blk", axis=1, tiled=True),
        out_cols,
        preferred_element_type=jnp.float32,
    ).astype(jnp.bfloat16)
    mixed_back = lax.all_to_all(out_part, "blk", split_axis=1, concat_axis=2, tiled=True)
    return (stream + modulate[2] * mixed_back.astype(jnp.float32)).astype(jnp.bfloat16)


def pick_request(array, req_idx):
    return lax.dynamic_index_in_dim(array, req_idx, 0, keepdims=True)


def per_device_by_token(hidden, qkv_weight, out_weight, modulation, timestep, fresh, live, k_stale, v_stale):
    section_idx = lax.axis_index("section")
    block_idx = lax.axis_index("blk")
    steps_all = modulation.shape[1]
    pick_row = (jnp.arange(steps_all) == timestep[0]).astype(jnp.float32)
    modulate = jnp.einsum("t,tcd->cd", pick_row, modulation[0], precision=lax.Precision.HIGHEST)
    num_blocks = fresh.shape[2]
    own_column = (jnp.arange(num_blocks) == block_idx).astype(jnp.int32)
    fresh_own = jnp.sum(fresh[0] * own_column[None, :], axis=1)
    qkv_cols = qkv_weight[0]
    out_cols = out_weight[0]
    old_keys = k_stale[0]
    old_values = v_stale[0]
    num_req = hidden.shape[0]
    received = jnp.zeros_like(hidden[0:1])
    first_out = []
    second_out = []
    for tick_idx in range(num_req + 1):
        if tick_idx < num_req:
            own_input = hidden[tick_idx : tick_idx + 1]
        else:
            own_input = jnp.zeros_like(hidden[0:1])
        layer_in = jnp.where(section_idx == 0, own_input, received)
        req_idx = jnp.clip(tick_idx - section_idx, 0, num_req - 1)
        layer_out = attend(
            layer_in,
            qkv_cols,
            out_cols,
            modulate,
            pick_request(fresh_own, req_idx),
            pick_request(old_keys, req_idx),
            pick_request(old_values, req_idx),
            pick_request(live, req_idx),
        )
        if tick_idx < num_req:
            first_out.append(layer_out)
            received = from_behind(layer_out, "section", 1)
        if tick_idx >= 1:
            second_out.append(layer_out)
    result = jnp.where(
        section_idx == 0, jnp.concatenate(first_out, axis=0), jnp.concatenate(second_out, axis=0)
    )
    return result[None]


HEAD = 64
BF16 = jnp.bfloat16
F32 = jnp.float32
NT = (((1,), (1,)), ((), ()))
VMEM = pl.BlockSpec(memory_space=pltpu.VMEM)
SMEM = pl.BlockSpec(memory_space=pltpu.SMEM)
HBM = pl.BlockSpec(memory_space=pltpu.HBM)
ANY = pl.BlockSpec(memory_space=pl.ANY)


def call(body, outs, scratch, cost, *args, specs=None, spare=40 << 20):
    flops, moved = cost
    return pl.pallas_call(
        body,
        out_shape=outs,
        in_specs=specs or [VMEM] * len(args),
        out_specs=jax.tree.map(lambda _: VMEM, outs),
        scratch_shapes=scratch,
        compiler_params=pltpu.CompilerParams(vmem_limit_bytes=(64 << 20) - spare),
        cost_estimate=pl.CostEstimate(flops=flops, bytes_accessed=moved, transcendentals=0),
    )(*args)


def pinned(array):
    return pltpu.with_memory_space_constraint(array, pltpu.HBM)


def dot_nt(left, right):
    return lax.dot_general(left, right, NT, preferred_element_type=F32)


def halves(columns):
    mid = columns.shape[0] // 2
    return jnp.concatenate([columns[:mid], columns[mid:]], axis=1)


def pack(cols):
    return jnp.concatenate([cols[:, :128], halves(cols[:, 128:])], axis=0)


def unpack(packed):
    tokens = packed.shape[0] // 3 * 2
    last = packed[tokens:]
    return jnp.concatenate(
        [packed[:tokens], jnp.concatenate([last[:, :HEAD], last[:, HEAD:]], axis=0)], axis=1
    )


def pack_by_parity(cols, odd):
    mid = cols.shape[0] // 2
    even_form = pack(cols)
    odd_form = jnp.concatenate(
        [
            cols[:, HEAD:],
            jnp.concatenate([cols[mid:, :HEAD], cols[:mid, :HEAD]], axis=1),
        ],
        axis=0,
    )
    return jnp.where(odd, odd_form, even_form)


def assemble(blocks, whole, by_heads=False):
    tokens = whole.shape[0]
    n = blocks.shape[0]
    for d in range(0, n, 2):
        even, odd = [group * pow(3, -1, n) % n if by_heads else group for group in (d, d + 1)]
        even_last, odd_last = blocks[even, tokens:].astype(F32), blocks[odd, tokens:].astype(F32)
        left = lax.broadcasted_iota(jnp.int32, even_last.shape, 1) < HEAD
        first = jnp.where(left, even_last, odd_last)
        second = pltpu.roll(jnp.where(left, odd_last, even_last), HEAD, 1)
        at = d // 2 * 384
        whole[:, at : at + 128] = blocks[even, :tokens].astype(whole.dtype)
        whole[:, at + 128 : at + 256] = jnp.concatenate([first, second], axis=0).astype(whole.dtype)
        whole[:, at + 256 : at + 384] = blocks[odd, :tokens].astype(whole.dtype)


def own_columns(ref, rows, me):
    pair = ref[rows, pl.ds(pl.multiple_of(me // 2 * 384, 128), 384)]
    return jnp.where((me & 1) == 1, pair[:, 192:], pair[:, :192])


def norm_into(stream, mod, normed):
    tokens, width = stream.shape
    step = 128
    total = jnp.zeros((tokens, step), F32)
    for at in range(0, width, step):
        total += stream[:, at : at + step]
    center = jnp.sum(total, axis=-1, keepdims=True) / width
    total = jnp.zeros((tokens, step), F32)
    for at in range(0, width, step):
        off = stream[:, at : at + step] - center
        total += off * off
    variance = jnp.sum(total, axis=-1, keepdims=True) / width
    spread = 1.0 / jnp.sqrt(variance + 1e-06)
    for at in range(0, width, step):
        part = (stream[:, at : at + step] - center) * spread
        part = part * (1.0 + mod[0, :, at : at + step]) + mod[1, :, at : at + step]
        normed[:, at : at + step] = part.astype(BF16)


def own_or_other(layer, own, other):
    return jnp.where(lax.axis_index("section") == layer, own, other)


def dot_into(layer, left, own, other, product):
    def into(weight):
        product[...] = dot_nt(left[...], weight[...]).astype(product.dtype)

    held = lax.axis_index("section") == layer
    pl.when(held)(lambda: into(own))
    pl.when(jnp.logical_not(held))(lambda: into(other))


def normalise(layer, stream, mod, other_mod, normed, residual, scales):
    scales[...] = own_or_other(layer, mod[...], other_mod[...])
    norm_into(stream, scales, normed)
    residual[...] = own_columns(stream, slice(None), lax.axis_index("blk")).astype(BF16)


def chunks_of(columns, chunks):
    for j, chunk in enumerate(chunks):
        chunk[...] = pack(columns[:, 192 * j : 192 * j + 192])


def first_projection(arrived, own, other, mod, other_mod, other_out, chunk0, chunk1, chunk2, residual, stream, scales, normed, columns, held, sems):
    holds = lax.axis_index("section") == 0
    parts = sems.shape[0]
    size = held.shape[0] // parts
    copies = [
        pltpu.make_async_copy(own.at[pl.ds(i * size, size)], held.at[pl.ds(i * size, size)], sems.at[i])
        for i in range(parts)
    ]

    @pl.when(holds)
    def _():
        for copy in copies:
            copy.start()

    n = arrived.shape[0]
    rows = stream.shape[0] // n
    for b in range(n):
        stream[rows * b : rows * b + rows, :] = arrived[b, :rows, :].astype(F32)
    normalise(0, stream, mod, other_mod, normed, residual, scales)

    @pl.when(holds)
    def _():
        for copy in copies:
            copy.wait()

    dot_into(0, normed, held, other, columns)
    chunks_of(columns, (chunk0, chunk1, chunk2))


def next_projection(blocks, own, other, mod, other_mod, chunk0, chunk1, chunk2, residual, stream, scales, normed, columns):
    assemble(blocks, stream)
    normalise(1, stream, mod, other_mod, normed, residual, scales)
    dot_into(1, normed, own, other, columns)
    chunks_of(columns, (chunk0, chunk1, chunk2))


def attention(layer, chunk0, chunk1, chunk2, old, fresh, other_fresh, live, attn):
    n = attn.shape[0]
    me, request = lax.axis_index("blk"), lax.axis_index("section")
    first = lax.rem(lax.rem(3 * me, n), 3)
    got = [chunk[...].astype(F32) for chunk in (chunk0, chunk1, chunk2)]

    def kind(of):
        at = lax.rem(first + of, 3)
        return unpack(jnp.where(at == 0, got[0], jnp.where(at == 1, got[1], got[2])))

    queries = kind(0)
    tokens, width = queries.shape
    heads = width // HEAD
    rows = tokens // n
    token = lax.broadcasted_iota(jnp.int32, (tokens, 1), 0)
    is_fresh = jnp.zeros((tokens, 1), jnp.int32)
    for b in range(n):
        flag = own_or_other(layer, fresh[0, request, b], other_fresh[0, request, b])
        is_fresh = jnp.where(token >= b * rows, flag, is_fresh)
    is_fresh = is_fresh == 1
    key = lax.broadcasted_iota(jnp.int32, (1, tokens), 1)
    is_live = jnp.zeros((1, tokens), jnp.int32)
    for b in range(n):
        is_live = jnp.where(key >= b * rows, live[request, b], is_live)
    is_live = is_live == 1
    keys = jnp.where(is_fresh, kind(1), old[layer, :, :width].astype(F32)).astype(BF16)
    values = jnp.where(is_fresh, kind(2), old[layer, :, width:].astype(F32)).astype(BF16)
    head_of = lax.broadcasted_iota(jnp.int32, (tokens, width), 1) // HEAD
    stacked = jnp.concatenate([jnp.where(head_of == h, queries, 0.0) for h in range(heads)], axis=0)
    scores = dot_nt(stacked.astype(BF16), keys) * 0.125
    scores = jnp.where(is_live, scores, -1e30)
    top = jnp.max(scores, axis=-1, keepdims=True)
    weights = jnp.where(is_live, jnp.exp(scores - top), 0.0)
    total = jnp.sum(weights, axis=-1, keepdims=True)
    mixed = jnp.dot(weights.astype(BF16), values, preferred_element_type=F32) * (1.0 / total)
    result = jnp.zeros((tokens, width), F32)
    for h in range(heads):
        result = jnp.where(head_of == h, mixed[h * tokens : (h + 1) * tokens], result)
    packed = pack_by_parity(result, (me & 1) == 1).astype(BF16)
    for d in range(n):
        attn[d] = packed


def layer_columns(layer, blocks, own, other, mod, other_mod, residual, whole, mixed):
    me = lax.axis_index("blk")
    assemble(blocks, whole, by_heads=True)
    dot_into(layer, whole, own, other, mixed)
    gates = own_or_other(layer, mod[2], other_mod[2])
    pairs = [gates[:, at : at + 384] for at in range(0, gates.shape[1], 384)]
    pair = pairs[0]
    for i, other_pair in enumerate(pairs):
        pair = jnp.where(me // 2 == i, other_pair, pair)
    gate = jnp.where((me & 1) == 1, pair[:, 192:], pair[:, :192])
    return (residual[...].astype(F32) + gate * mixed[...].astype(F32)).astype(BF16).astype(F32)


def first_output(blocks, own, other, mod, other_mod, residual, copies, kept, *scratch):
    columns = layer_columns(0, blocks, own, other, mod, other_mod, residual, *scratch)
    packed = pack_by_parity(columns, (lax.axis_index("blk") & 1) == 1).astype(BF16)
    for d in range(copies.shape[0]):
        copies[d] = packed
    kept[...] = columns


def last_output(blocks, own, other, mod, other_mod, residual, kept, by_token, columns, *scratch):
    columns[...] = layer_columns(1, blocks, own, other, mod, other_mod, residual, *scratch)
    n = by_token.shape[0] // 2
    rows = columns.shape[0] // n
    for layer, outs in enumerate((kept, columns)):
        for b in range(n):
            by_token[layer * n + b, :rows, :] = outs[rows * b : rows * b + rows, :].astype(BF16)


def first_exchange(hidden, old_keys, old_values, other_keys, other_values, leaving, held, sems):
    copies = [
        pltpu.make_async_copy(ref, held.at[i], sems.at[i])
        for i, ref in enumerate((hidden, old_keys, old_values, other_keys, other_values))
    ]
    for copy in copies:
        copy.start()
    rows, reqs, width = hidden.shape
    n = leaving.shape[0]
    columns = width // n
    first = lax.axis_index("section") == 0
    for copy in copies:
        copy.wait()

    def of_request(which):
        own = [held[which, i].astype(F32) for i in range(rows)]
        return jnp.concatenate([jnp.where(first, pair[:1], pair[1:]) for pair in own], axis=0)

    mine, *arrays = [of_request(which) for which in range(5)]
    mine = mine.astype(BF16)
    own, other = arrays[:2], arrays[2:]
    stale = [jnp.where(first, a, b) for a, b in zip(own, other)] + [jnp.where(first, b, a) for a, b in zip(own, other)]
    for b in range(n):
        at = columns * (3 * b % n)
        block = jnp.concatenate([array[:, at : at + columns] for array in stale], axis=1)
        leaving[b, :rows, :] = mine
        for i in range(rows):
            leaving[b, rows : rows + 1, i * 4 * columns : (i + 1) * 4 * columns] = block[i : i + 1].astype(BF16)


def stale_by_token(arrived, old, rows):
    n = arrived.shape[0]
    per = rows.shape[1] // n
    wide = rows.shape[2]
    for b in range(n):
        flat = arrived[b, per : per + 1, :].astype(F32)
        for i in range(per):
            for layer in range(2):
                at = (i * 2 + layer) * wide
                rows[layer, per * b + i : per * b + i + 1, :] = flat[:, at : at + wide]
    old[...] = rows[...].astype(BF16)


def to_rows(arrived, out, rows):
    n = arrived.shape[0] // 2
    per, columns = out.shape[0], arrived.shape[2]
    for s in range(2):
        for b in range(n):
            rows[s, :per, columns * b : columns * b + columns] = arrived[s * n + b, :per, :].astype(F32)
    for i in range(per):
        out[i] = jnp.concatenate([rows[s, i : i + 1, :] for s in range(2)], axis=0).astype(BF16)


def exchange(blocks, axis):
    return lax.all_to_all(blocks, axis, split_axis=0, concat_axis=0, tiled=True)


def swap_sections(array):
    return lax.ppermute(array, "section", [(0, 1), (1, 0)])


def by_heads(chunks, n):
    inverse = pow(3, -1, n)
    return [
        lax.ppermute(chunk, "blk", [(b, (b + inverse * j) % n) for b in range(n)]) if j else chunk
        for j, chunk in enumerate(chunks)
    ]


def per_device(hidden, qkv_weight, out_weight, modulation, timestep, fresh, live, k_stale, v_stale):
    n = lax.axis_size("blk")
    columns = out_weight.shape[2]
    reqs, rows, width = hidden.shape
    if not (
        columns == 3 * HEAD
        and n % 3 == 1
        and n & (n - 1) == 0
        and reqs == lax.axis_size("section") == 2
        and rows <= 4
    ):
        return per_device_by_token(
            hidden, qkv_weight, out_weight, modulation, timestep, fresh, live, k_stale, v_stale
        )
    tokens = n * rows
    shape = jax.ShapeDtypeStruct
    packed = shape((tokens * 3 // 2, 128), BF16)
    copies = shape((n, tokens * 3 // 2, 128), BF16)
    cols = shape((tokens, columns), BF16)
    own_qkv = jnp.swapaxes(qkv_weight[0], 0, 1)
    own_out = jnp.swapaxes(out_weight[0], 0, 1)
    steps = jnp.transpose(modulation, (1, 2, 0, 3))
    old_keys = jnp.transpose(k_stale[0], (1, 0, 2))
    old_values = jnp.transpose(v_stale[0], (1, 0, 2))

    other_keys, other_values, timestep, sent_fresh = lax.optimization_barrier(
        (swap_sections(old_keys), swap_sections(old_values), timestep, fresh)
    )
    mod = lax.dynamic_index_in_dim(steps, timestep[0], 0, keepdims=False)
    other_mod, other_fresh, sent_qkv, sent_out = lax.optimization_barrier(
        (swap_sections(mod), swap_sections(sent_fresh), own_qkv, own_out)
    )
    mods = (mod, other_mod)
    flags = (fresh, other_fresh)
    other_qkv, other_out = swap_sections(sent_qkv), swap_sections(sent_out)
    out = (own_out, other_out)
    leaving = call(
        first_exchange,
        shape((n, 4, width), BF16),
        [pltpu.VMEM((5, rows, reqs, width), BF16), pltpu.SemaphoreType.DMA((5,))],
        (0, 1000000),
        *(pinned(array) for array in (jnp.transpose(hidden, (1, 0, 2)), old_keys, old_values)),
        other_keys,
        other_values,
        specs=[HBM] * 3 + [ANY] * 2,
    )
    arrived = exchange(leaving, "blk")

    blocks = arrived
    for layer in range(2):
        *chunks, residual = call(
            next_projection if layer else first_projection,
            [packed, packed, packed, cols],
            [
                pltpu.VMEM((tokens, width), F32),
                pltpu.VMEM(mod.shape, F32),
                pltpu.VMEM((tokens, width), BF16),
                pltpu.VMEM((tokens, 3 * columns), BF16),
            ]
            + ([] if layer else [pltpu.VMEM(own_qkv.shape, BF16), pltpu.SemaphoreType.DMA((36,))]),
            (2 * tokens * width * 3 * columns, 8 * width * columns),
            blocks,
            *((own_qkv, other_qkv, *mods) if layer else (pinned(own_qkv), other_qkv, *mods, other_out)),
            **({} if layer else {"specs": [VMEM, HBM, VMEM, VMEM, VMEM, ANY]}),
        )
        if layer == 0:
            arrived, chunks[1] = lax.optimization_barrier((arrived, chunks[1]))
            old = call(
                stale_by_token,
                shape((2, tokens, 2 * columns), BF16),
                [pltpu.VMEM((2, tokens, 2 * columns), F32)],
                (0, 200000),
                arrived,
            )
        attn = call(
            functools.partial(attention, layer),
            copies,
            [],
            (8 * tokens * tokens * columns, 300000),
            *by_heads(chunks, n),
            old,
            *flags,
            live,
            specs=[VMEM] * 4 + [SMEM] * 3,
        )
        args = (exchange(attn, "blk"), *out, *mods, residual)
        cost = (2 * tokens * width * columns, 4 * width * columns)
        held = [pltpu.VMEM((tokens, width), BF16), pltpu.VMEM((tokens, columns), BF16)]
        if layer == 0:
            leaving, kept = call(first_output, [copies, shape((tokens, columns), F32)], held, cost, *args)
            blocks = exchange(leaving, "blk")
        else:
            leaving = call(
                last_output,
                shape((2 * n, 4, columns), BF16),
                [pltpu.VMEM((tokens, columns), F32)] + held,
                cost,
                *args,
                kept,
            )
    result = call(
        to_rows,
        shape((rows, reqs, width), BF16),
        [pltpu.VMEM((2, 8, width), F32)],
        (0, 100000),
        exchange(leaving, ("section", "blk")),
    )
    return jnp.transpose(result, (1, 0, 2))[None]


def solution(mesh):
    return jax.shard_map(
        per_device,
        mesh=mesh,
        in_specs=(
            P(None, "blk", None),
            P("section", None, "blk"),
            P("section", None, "blk"),
            P("section", None, None, None),
            P(),
            P("section", None, None),
            P(),
            P("section", None, "blk", None),
            P("section", None, "blk", None),
        ),
        out_specs=P("section", None, "blk", None),
        check_vma=False,
    )
```

```python
import functools

import jax
import jax.numpy as jnp
from jax import lax
from jax.experimental import pallas as pl
from jax.experimental.pallas import tpu as pltpu
from jax.sharding import PartitionSpec as P


def from_behind(shard, axis, by):
    count = lax.axis_size(axis)
    pairs = [(i, i + by) for i in range(count) if 0 <= i + by < count]
    return lax.ppermute(shard, axis, pairs)


def attend(layer_in, qkv_cols, out_cols, modulate, fresh_own, old_keys, old_values, live):
    stream = layer_in.astype(jnp.float32)
    center = jnp.mean(stream, axis=-1, keepdims=True)
    variance = jnp.mean((stream - center) ** 2, axis=-1, keepdims=True)
    normed = (stream - center) / jnp.sqrt(variance + 1e-06) * (1.0 + modulate[0]) + modulate[1]
    normed_b = normed.astype(jnp.bfloat16)
    columns = jnp.einsum(
        "rnd,dc->rnc",
        lax.all_gather(normed_b, "blk", axis=1, tiled=True),
        qkv_cols,
        preferred_element_type=jnp.float32,
    ).astype(jnp.bfloat16)
    projected = lax.all_to_all(columns, "blk", split_axis=1, concat_axis=2, tiled=True)
    num_req, num_rows, width = layer_in.shape
    queries = projected[:, :, :width]
    new_keys = projected[:, :, width : 2 * width]
    new_values = projected[:, :, 2 * width :]
    use_fresh = (fresh_own == 1)[:, None, None]
    keys = jnp.where(use_fresh, new_keys, old_keys)
    values = jnp.where(use_fresh, new_values, old_values)
    num_heads = width // 64
    num_blocks = live.shape[1]
    q_heads = queries.reshape(num_req, num_rows, num_heads, 64)
    live_float = live.astype(jnp.float32)
    run_max = jnp.full((num_req, num_heads, num_rows), -1e30, jnp.float32)
    key_piece = lax.all_gather(keys, "blk", axis=1, tiled=True)
    value_piece = lax.all_gather(values, "blk", axis=1, tiled=True)
    piece_rows = key_piece.shape[1]
    key_heads = key_piece.reshape(num_req, piece_rows, num_heads, 64)
    value_heads = value_piece.reshape(num_req, piece_rows, num_heads, 64)
    scores = (
        jnp.einsum("qrhd,qnhd->qhrn", q_heads, key_heads, preferred_element_type=jnp.float32)
        * 0.125
    )
    block_ids = jnp.arange(piece_rows) // num_rows
    one_hot = (block_ids[:, None] == jnp.arange(num_blocks)[None, :]).astype(jnp.float32)
    usable = jnp.einsum("qb,nb->qn", live_float, one_hot) > 0.5
    usable = usable[:, None, None, :]
    scores = jnp.where(usable, scores, -1e30)
    new_max = jnp.maximum(run_max, jnp.max(scores, axis=-1))
    weights = jnp.where(usable, jnp.exp(scores - new_max[..., None]), 0.0)
    new_sum = jnp.sum(weights, axis=-1)
    new_acc = jnp.einsum(
        "qhrn,qnhd->qhrd", weights, value_heads.astype(jnp.float32), precision=lax.Precision.HIGHEST
    )
    attn = new_acc / new_sum[..., None]
    attn = jnp.transpose(attn, (0, 2, 1, 3)).reshape(num_req, num_rows, width).astype(jnp.bfloat16)
    out_part = jnp.einsum(
        "rnd,dc->rnc",
        lax.all_gather(attn, "blk", axis=1, tiled=True),
        out_cols,
        preferred_element_type=jnp.float32,
    ).astype(jnp.bfloat16)
    mixed_back = lax.all_to_all(out_part, "blk", split_axis=1, concat_axis=2, tiled=True)
    return (stream + modulate[2] * mixed_back.astype(jnp.float32)).astype(jnp.bfloat16)


def pick_request(array, req_idx):
    return lax.dynamic_index_in_dim(array, req_idx, 0, keepdims=True)


def per_device_by_token(hidden, qkv_weight, out_weight, modulation, timestep, fresh, live, k_stale, v_stale):
    section_idx = lax.axis_index("section")
    block_idx = lax.axis_index("blk")
    steps_all = modulation.shape[1]
    pick_row = (jnp.arange(steps_all) == timestep[0]).astype(jnp.float32)
    modulate = jnp.einsum("t,tcd->cd", pick_row, modulation[0], precision=lax.Precision.HIGHEST)
    num_blocks = fresh.shape[2]
    own_column = (jnp.arange(num_blocks) == block_idx).astype(jnp.int32)
    fresh_own = jnp.sum(fresh[0] * own_column[None, :], axis=1)
    qkv_cols = qkv_weight[0]
    out_cols = out_weight[0]
    old_keys = k_stale[0]
    old_values = v_stale[0]
    num_req = hidden.shape[0]
    received = jnp.zeros_like(hidden[0:1])
    first_out = []
    second_out = []
    for tick_idx in range(num_req + 1):
        if tick_idx < num_req:
            own_input = hidden[tick_idx : tick_idx + 1]
        else:
            own_input = jnp.zeros_like(hidden[0:1])
        layer_in = jnp.where(section_idx == 0, own_input, received)
        req_idx = jnp.clip(tick_idx - section_idx, 0, num_req - 1)
        layer_out = attend(
            layer_in,
            qkv_cols,
            out_cols,
            modulate,
            pick_request(fresh_own, req_idx),
            pick_request(old_keys, req_idx),
            pick_request(old_values, req_idx),
            pick_request(live, req_idx),
        )
        if tick_idx < num_req:
            first_out.append(layer_out)
            received = from_behind(layer_out, "section", 1)
        if tick_idx >= 1:
            second_out.append(layer_out)
    result = jnp.where(
        section_idx == 0, jnp.concatenate(first_out, axis=0), jnp.concatenate(second_out, axis=0)
    )
    return result[None]


HEAD = 64
HOME = 1
BF16 = jnp.bfloat16
F32 = jnp.float32
NT = (((1,), (1,)), ((), ()))
VMEM = pl.BlockSpec(memory_space=pltpu.VMEM)
SMEM = pl.BlockSpec(memory_space=pltpu.SMEM)
HBM = pl.BlockSpec(memory_space=pltpu.HBM)
ANY = pl.BlockSpec(memory_space=pl.ANY)


def call(body, outs, scratch, cost, *args, specs=None, spare=40 << 20):
    flops, moved = cost
    return pl.pallas_call(
        body,
        out_shape=outs,
        in_specs=specs or [VMEM] * len(args),
        out_specs=jax.tree.map(lambda _: VMEM, outs),
        scratch_shapes=scratch,
        compiler_params=pltpu.CompilerParams(vmem_limit_bytes=(64 << 20) - spare),
        cost_estimate=pl.CostEstimate(flops=flops, bytes_accessed=moved, transcendentals=0),
    )(*args)


def pinned(array):
    return pltpu.with_memory_space_constraint(array, pltpu.HBM)


def dot_nt(left, right):
    return lax.dot_general(left, right, NT, preferred_element_type=F32)


def halves(columns):
    mid = columns.shape[0] // 2
    return jnp.concatenate([columns[:mid], columns[mid:]], axis=1)


def pack(cols):
    return jnp.concatenate([cols[:, :128], halves(cols[:, 128:])], axis=0)


def unpack(packed):
    tokens = packed.shape[0] // 3 * 2
    last = packed[tokens:]
    return jnp.concatenate(
        [packed[:tokens], jnp.concatenate([last[:, :HEAD], last[:, HEAD:]], axis=0)], axis=1
    )


def pack_by_parity(cols, odd):
    mid = cols.shape[0] // 2
    even_form = pack(cols)
    odd_form = jnp.concatenate(
        [
            cols[:, HEAD:],
            jnp.concatenate([cols[mid:, :HEAD], cols[:mid, :HEAD]], axis=1),
        ],
        axis=0,
    )
    return jnp.where(odd, odd_form, even_form)


def assemble(blocks, whole, by_heads=False):
    tokens = whole.shape[0]
    n = blocks.shape[0]
    for d in range(0, n, 2):
        even, odd = [(group - HOME) * pow(3, -1, n) % n if by_heads else group for group in (d, d + 1)]
        even_last, odd_last = blocks[even, tokens:].astype(F32), blocks[odd, tokens:].astype(F32)
        left = lax.broadcasted_iota(jnp.int32, even_last.shape, 1) < HEAD
        first = jnp.where(left, even_last, odd_last)
        second = pltpu.roll(jnp.where(left, odd_last, even_last), HEAD, 1)
        at = d // 2 * 384
        whole[:, at : at + 128] = blocks[even, :tokens].astype(whole.dtype)
        whole[:, at + 128 : at + 256] = jnp.concatenate([first, second], axis=0).astype(whole.dtype)
        whole[:, at + 256 : at + 384] = blocks[odd, :tokens].astype(whole.dtype)


def own_columns(ref, rows, me):
    pair = ref[rows, pl.ds(pl.multiple_of(me // 2 * 384, 128), 384)]
    return jnp.where((me & 1) == 1, pair[:, 192:], pair[:, :192])


def norm_into(stream, mod, normed):
    tokens, width = stream.shape
    step = 128
    total = jnp.zeros((tokens, step), F32)
    for at in range(0, width, step):
        total += stream[:, at : at + step]
    center = jnp.sum(total, axis=-1, keepdims=True) / width
    total = jnp.zeros((tokens, step), F32)
    for at in range(0, width, step):
        off = stream[:, at : at + step] - center
        total += off * off
    variance = jnp.sum(total, axis=-1, keepdims=True) / width
    spread = 1.0 / jnp.sqrt(variance + 1e-06)
    for at in range(0, width, step):
        part = (stream[:, at : at + step] - center) * spread
        part = part * (1.0 + mod[0, :, at : at + step]) + mod[1, :, at : at + step]
        normed[:, at : at + step] = part.astype(BF16)


def own_or_other(layer, own, other):
    return jnp.where(lax.axis_index("section") == layer, own, other)


def dot_into(layer, left, own, other, product):
    def into(weight):
        product[...] = dot_nt(left[...], weight[...]).astype(product.dtype)

    held = lax.axis_index("section") == layer
    pl.when(held)(lambda: into(own))
    pl.when(jnp.logical_not(held))(lambda: into(other))


def normalise(layer, stream, mod, other_mod, normed, residual, scales):
    scales[...] = own_or_other(layer, mod[...], other_mod[...])
    norm_into(stream, scales, normed)
    residual[...] = own_columns(stream, slice(None), lax.axis_index("blk")).astype(BF16)


def chunks_of(columns, chunks):
    for j, chunk in enumerate(chunks):
        chunk[...] = pack(columns[:, 192 * j : 192 * j + 192])


def first_projection(arrived, own, other, mod, other_mod, other_out, chunk0, chunk1, chunk2, residual, stream, scales, normed, columns, held, sems):
    holds = lax.axis_index("section") == 0
    parts = sems.shape[0]
    size = held.shape[0] // parts
    copies = [
        pltpu.make_async_copy(own.at[pl.ds(i * size, size)], held.at[pl.ds(i * size, size)], sems.at[i])
        for i in range(parts)
    ]

    @pl.when(holds)
    def _():
        for copy in copies:
            copy.start()

    n = arrived.shape[0]
    rows = stream.shape[0] // n
    for b in range(n):
        stream[rows * b : rows * b + rows, :] = arrived[b, :rows, :].astype(F32)
    normalise(0, stream, mod, other_mod, normed, residual, scales)

    @pl.when(holds)
    def _():
        for at in range(0, held.shape[0], 256):
            end = min(at + 256, held.shape[0])
            for copy in copies[at // size : end // size]:
                copy.wait()
            columns[:, at:end] = dot_nt(normed[...], held[at:end, :]).astype(BF16)

    @pl.when(jnp.logical_not(holds))
    def _():
        columns[...] = dot_nt(normed[...], other[...]).astype(BF16)

    chunks_of(columns, (chunk0, chunk1, chunk2))


def next_projection(blocks, own, other, mod, other_mod, chunk0, chunk1, chunk2, residual, stream, scales, normed, columns):
    assemble(blocks, stream)
    normalise(1, stream, mod, other_mod, normed, residual, scales)
    dot_into(1, normed, own, other, columns)
    chunks_of(columns, (chunk0, chunk1, chunk2))


def attention(layer, chunk0, chunk1, chunk2, old, fresh, other_fresh, live, attn):
    n = attn.shape[0]
    me, request = lax.axis_index("blk"), lax.axis_index("section")
    first = lax.rem(lax.rem(3 * me + HOME, n), 3)
    got = [chunk[...].astype(F32) for chunk in (chunk0, chunk1, chunk2)]

    def kind(of):
        at = lax.rem(first + of, 3)
        return unpack(jnp.where(at == 0, got[0], jnp.where(at == 1, got[1], got[2])))

    queries = kind(0)
    tokens, width = queries.shape
    heads = width // HEAD
    rows = tokens // n
    token = lax.broadcasted_iota(jnp.int32, (tokens, 1), 0)
    is_fresh = jnp.zeros((tokens, 1), jnp.int32)
    for b in range(n):
        flag = own_or_other(layer, fresh[0, request, b], other_fresh[0, request, b])
        is_fresh = jnp.where(token >= b * rows, flag, is_fresh)
    is_fresh = is_fresh == 1
    key = lax.broadcasted_iota(jnp.int32, (1, tokens), 1)
    is_live = jnp.zeros((1, tokens), jnp.int32)
    for b in range(n):
        is_live = jnp.where(key >= b * rows, live[request, b], is_live)
    is_live = is_live == 1
    keys = jnp.where(is_fresh, kind(1), old[layer, :, :width].astype(F32)).astype(BF16)
    values = jnp.where(is_fresh, kind(2), old[layer, :, width:].astype(F32)).astype(BF16)
    head_of = lax.broadcasted_iota(jnp.int32, (tokens, width), 1) // HEAD
    stacked = jnp.concatenate([jnp.where(head_of == h, queries, 0.0) for h in range(heads)], axis=0)
    scores = dot_nt(stacked.astype(BF16), keys) * 0.125
    scores = jnp.where(is_live, scores, -1e30)
    top = jnp.max(scores, axis=-1, keepdims=True)
    weights = jnp.where(is_live, jnp.exp(scores - top), 0.0)
    total = jnp.sum(weights, axis=-1, keepdims=True)
    mixed = jnp.dot(weights.astype(BF16), values, preferred_element_type=F32) * (1.0 / total)
    result = jnp.zeros((tokens, width), F32)
    for h in range(heads):
        result = jnp.where(head_of == h, mixed[h * tokens : (h + 1) * tokens], result)
    packed = pack_by_parity(result, ((me + HOME) & 1) == 1).astype(BF16)
    for d in range(n):
        attn[d] = packed


def layer_columns(layer, blocks, own, other, mod, other_mod, residual, whole, mixed):
    me = lax.axis_index("blk")
    assemble(blocks, whole, by_heads=True)
    dot_into(layer, whole, own, other, mixed)
    gates = own_or_other(layer, mod[2], other_mod[2])
    pairs = [gates[:, at : at + 384] for at in range(0, gates.shape[1], 384)]
    pair = pairs[0]
    for i, other_pair in enumerate(pairs):
        pair = jnp.where(me // 2 == i, other_pair, pair)
    gate = jnp.where((me & 1) == 1, pair[:, 192:], pair[:, :192])
    return (residual[...].astype(F32) + gate * mixed[...].astype(F32)).astype(BF16).astype(F32)


def first_output(blocks, own, other, mod, other_mod, residual, copies, kept, *scratch):
    columns = layer_columns(0, blocks, own, other, mod, other_mod, residual, *scratch)
    packed = pack_by_parity(columns, (lax.axis_index("blk") & 1) == 1).astype(BF16)
    for d in range(copies.shape[0]):
        copies[d] = packed
    kept[...] = columns


def last_output(blocks, own, other, mod, other_mod, residual, kept, by_token, columns, *scratch):
    columns[...] = layer_columns(1, blocks, own, other, mod, other_mod, residual, *scratch)
    n = by_token.shape[0] // 2
    rows = columns.shape[0] // n
    for layer, outs in enumerate((kept, columns)):
        for b in range(n):
            by_token[layer * n + b, :rows, :] = outs[rows * b : rows * b + rows, :].astype(BF16)


def first_exchange(hidden, old_keys, old_values, other_keys, other_values, leaving, held, sems):
    copies = [
        pltpu.make_async_copy(ref, held.at[i], sems.at[i])
        for i, ref in enumerate((hidden, old_keys, old_values, other_keys, other_values))
    ]
    for copy in copies:
        copy.start()
    rows, reqs, width = hidden.shape
    n = leaving.shape[0]
    columns = width // n
    first = lax.axis_index("section") == 0
    for copy in copies:
        copy.wait()

    def of_request(which):
        own = [held[which, i].astype(F32) for i in range(rows)]
        return jnp.concatenate([jnp.where(first, pair[:1], pair[1:]) for pair in own], axis=0)

    mine, *arrays = [of_request(which) for which in range(5)]
    mine = mine.astype(BF16)
    own, other = arrays[:2], arrays[2:]
    stale = [jnp.where(first, a, b) for a, b in zip(own, other)] + [jnp.where(first, b, a) for a, b in zip(own, other)]
    for b in range(n):
        at = columns * ((3 * b + HOME) % n)
        block = jnp.concatenate([array[:, at : at + columns] for array in stale], axis=1)
        leaving[b, :rows, :] = mine
        for i in range(rows):
            leaving[b, rows : rows + 1, i * 4 * columns : (i + 1) * 4 * columns] = block[i : i + 1].astype(BF16)


def stale_by_token(arrived, old, rows):
    n = arrived.shape[0]
    per = rows.shape[1] // n
    wide = rows.shape[2]
    for b in range(n):
        flat = arrived[b, per : per + 1, :].astype(F32)
        for i in range(per):
            for layer in range(2):
                at = (i * 2 + layer) * wide
                rows[layer, per * b + i : per * b + i + 1, :] = flat[:, at : at + wide]
    old[...] = rows[...].astype(BF16)


def to_rows(arrived, out, rows):
    n = arrived.shape[0] // 2
    per, columns = out.shape[0], arrived.shape[2]
    for s in range(2):
        for b in range(n):
            rows[s, :per, columns * b : columns * b + columns] = arrived[s * n + b, :per, :].astype(F32)
    for i in range(per):
        out[i] = jnp.concatenate([rows[s, i : i + 1, :] for s in range(2)], axis=0).astype(BF16)


def exchange(blocks, axis):
    return lax.all_to_all(blocks, axis, split_axis=0, concat_axis=0, tiled=True)


def swap_sections(array):
    return lax.ppermute(array, "section", [(0, 1), (1, 0)])


def by_heads(chunks, n):
    inverse = pow(3, -1, n)
    return [
        lax.ppermute(chunk, "blk", [(b, (b + inverse * (j - HOME)) % n) for b in range(n)]) if j != HOME else chunk
        for j, chunk in enumerate(chunks)
    ]


def per_device(hidden, qkv_weight, out_weight, modulation, timestep, fresh, live, k_stale, v_stale):
    n = lax.axis_size("blk")
    columns = out_weight.shape[2]
    reqs, rows, width = hidden.shape
    if not (
        columns == 3 * HEAD
        and n % 3 == 1
        and n & (n - 1) == 0
        and reqs == lax.axis_size("section") == 2
        and rows <= 4
    ):
        return per_device_by_token(
            hidden, qkv_weight, out_weight, modulation, timestep, fresh, live, k_stale, v_stale
        )
    tokens = n * rows
    shape = jax.ShapeDtypeStruct
    packed = shape((tokens * 3 // 2, 128), BF16)
    copies = shape((n, tokens * 3 // 2, 128), BF16)
    cols = shape((tokens, columns), BF16)
    own_qkv = jnp.swapaxes(qkv_weight[0], 0, 1)
    own_out = jnp.swapaxes(out_weight[0], 0, 1)
    steps = jnp.transpose(modulation, (1, 2, 0, 3))
    old_keys = jnp.transpose(k_stale[0], (1, 0, 2))
    old_values = jnp.transpose(v_stale[0], (1, 0, 2))

    other_keys, other_values, timestep, sent_fresh = lax.optimization_barrier(
        (swap_sections(old_keys), swap_sections(old_values), timestep, fresh)
    )
    mod = lax.dynamic_index_in_dim(steps, timestep[0], 0, keepdims=False)
    other_mod, other_fresh, sent_qkv, sent_out = lax.optimization_barrier(
        (swap_sections(mod), swap_sections(sent_fresh), own_qkv, own_out)
    )
    mods = (mod, other_mod)
    flags = (fresh, other_fresh)
    other_qkv, other_out = swap_sections(sent_qkv), swap_sections(sent_out)
    out = (own_out, other_out)
    leaving = call(
        first_exchange,
        shape((n, 4, width), BF16),
        [pltpu.VMEM((5, rows, reqs, width), BF16), pltpu.SemaphoreType.DMA((5,))],
        (0, 1000000),
        *(pinned(array) for array in (jnp.transpose(hidden, (1, 0, 2)), old_keys, old_values)),
        other_keys,
        other_values,
        specs=[HBM] * 3 + [ANY] * 2,
    )
    arrived = exchange(leaving, "blk")

    blocks = arrived
    for layer in range(2):
        *chunks, residual = call(
            next_projection if layer else first_projection,
            [packed, packed, packed, cols],
            [
                pltpu.VMEM((tokens, width), F32),
                pltpu.VMEM(mod.shape, F32),
                pltpu.VMEM((tokens, width), BF16),
                pltpu.VMEM((tokens, 3 * columns), BF16),
            ]
            + ([] if layer else [pltpu.VMEM(own_qkv.shape, BF16), pltpu.SemaphoreType.DMA((9,))]),
            (2 * tokens * width * 3 * columns, 8 * width * columns),
            blocks,
            *((own_qkv, other_qkv, *mods) if layer else (pinned(own_qkv), other_qkv, *mods, other_out)),
            **({} if layer else {"specs": [VMEM, HBM, VMEM, VMEM, VMEM, ANY]}),
        )
        if layer == 0:
            arrived, chunks[1] = lax.optimization_barrier((arrived, chunks[1]))
            old = call(
                stale_by_token,
                shape((2, tokens, 2 * columns), BF16),
                [pltpu.VMEM((2, tokens, 2 * columns), F32)],
                (0, 200000),
                arrived,
            )
        attn = call(
            functools.partial(attention, layer),
            copies,
            [],
            (8 * tokens * tokens * columns, 300000),
            *by_heads(chunks, n),
            old,
            *flags,
            live,
            specs=[VMEM] * 4 + [SMEM] * 3,
        )
        args = (exchange(attn, "blk"), *out, *mods, residual)
        cost = (2 * tokens * width * columns, 4 * width * columns)
        held = [pltpu.VMEM((tokens, width), BF16), pltpu.VMEM((tokens, columns), BF16)]
        if layer == 0:
            leaving, kept = call(first_output, [copies, shape((tokens, columns), F32)], held, cost, *args)
            blocks = exchange(leaving, "blk")
        else:
            leaving = call(
                last_output,
                shape((2 * n, 4, columns), BF16),
                [pltpu.VMEM((tokens, columns), F32)] + held,
                cost,
                *args,
                kept,
            )
    result = call(
        to_rows,
        shape((rows, reqs, width), BF16),
        [pltpu.VMEM((2, 8, width), F32)],
        (0, 100000),
        exchange(leaving, ("section", "blk")),
    )
    return jnp.transpose(result, (1, 0, 2))[None]


def solution(mesh):
    return jax.shard_map(
        per_device,
        mesh=mesh,
        in_specs=(
            P(None, "blk", None),
            P("section", None, "blk"),
            P("section", None, "blk"),
            P("section", None, None, None),
            P(),
            P("section", None, None),
            P(),
            P("section", None, "blk", None),
            P("section", None, "blk", None),
        ),
        out_specs=P("section", None, "blk", None),
        check_vma=False,
    )
```

```python
import functools

import jax
import jax.numpy as jnp
from jax import lax
from jax.experimental import pallas as pl
from jax.experimental.pallas import tpu as pltpu
from jax.sharding import PartitionSpec as P


def from_behind(shard, axis, by):
    count = lax.axis_size(axis)
    pairs = [(i, i + by) for i in range(count) if 0 <= i + by < count]
    return lax.ppermute(shard, axis, pairs)


def attend(layer_in, qkv_cols, out_cols, modulate, fresh_own, old_keys, old_values, live):
    stream = layer_in.astype(jnp.float32)
    center = jnp.mean(stream, axis=-1, keepdims=True)
    variance = jnp.mean((stream - center) ** 2, axis=-1, keepdims=True)
    normed = (stream - center) / jnp.sqrt(variance + 1e-06) * (1.0 + modulate[0]) + modulate[1]
    normed_b = normed.astype(jnp.bfloat16)
    columns = jnp.einsum(
        "rnd,dc->rnc",
        lax.all_gather(normed_b, "blk", axis=1, tiled=True),
        qkv_cols,
        preferred_element_type=jnp.float32,
    ).astype(jnp.bfloat16)
    projected = lax.all_to_all(columns, "blk", split_axis=1, concat_axis=2, tiled=True)
    num_req, num_rows, width = layer_in.shape
    queries = projected[:, :, :width]
    new_keys = projected[:, :, width : 2 * width]
    new_values = projected[:, :, 2 * width :]
    use_fresh = (fresh_own == 1)[:, None, None]
    keys = jnp.where(use_fresh, new_keys, old_keys)
    values = jnp.where(use_fresh, new_values, old_values)
    num_heads = width // 64
    num_blocks = live.shape[1]
    q_heads = queries.reshape(num_req, num_rows, num_heads, 64)
    live_float = live.astype(jnp.float32)
    run_max = jnp.full((num_req, num_heads, num_rows), -1e30, jnp.float32)
    key_piece = lax.all_gather(keys, "blk", axis=1, tiled=True)
    value_piece = lax.all_gather(values, "blk", axis=1, tiled=True)
    piece_rows = key_piece.shape[1]
    key_heads = key_piece.reshape(num_req, piece_rows, num_heads, 64)
    value_heads = value_piece.reshape(num_req, piece_rows, num_heads, 64)
    scores = (
        jnp.einsum("qrhd,qnhd->qhrn", q_heads, key_heads, preferred_element_type=jnp.float32)
        * 0.125
    )
    block_ids = jnp.arange(piece_rows) // num_rows
    one_hot = (block_ids[:, None] == jnp.arange(num_blocks)[None, :]).astype(jnp.float32)
    usable = jnp.einsum("qb,nb->qn", live_float, one_hot) > 0.5
    usable = usable[:, None, None, :]
    scores = jnp.where(usable, scores, -1e30)
    new_max = jnp.maximum(run_max, jnp.max(scores, axis=-1))
    weights = jnp.where(usable, jnp.exp(scores - new_max[..., None]), 0.0)
    new_sum = jnp.sum(weights, axis=-1)
    new_acc = jnp.einsum(
        "qhrn,qnhd->qhrd", weights, value_heads.astype(jnp.float32), precision=lax.Precision.HIGHEST
    )
    attn = new_acc / new_sum[..., None]
    attn = jnp.transpose(attn, (0, 2, 1, 3)).reshape(num_req, num_rows, width).astype(jnp.bfloat16)
    out_part = jnp.einsum(
        "rnd,dc->rnc",
        lax.all_gather(attn, "blk", axis=1, tiled=True),
        out_cols,
        preferred_element_type=jnp.float32,
    ).astype(jnp.bfloat16)
    mixed_back = lax.all_to_all(out_part, "blk", split_axis=1, concat_axis=2, tiled=True)
    return (stream + modulate[2] * mixed_back.astype(jnp.float32)).astype(jnp.bfloat16)


def pick_request(array, req_idx):
    return lax.dynamic_index_in_dim(array, req_idx, 0, keepdims=True)


def per_device_by_token(hidden, qkv_weight, out_weight, modulation, timestep, fresh, live, k_stale, v_stale):
    section_idx = lax.axis_index("section")
    block_idx = lax.axis_index("blk")
    steps_all = modulation.shape[1]
    pick_row = (jnp.arange(steps_all) == timestep[0]).astype(jnp.float32)
    modulate = jnp.einsum("t,tcd->cd", pick_row, modulation[0], precision=lax.Precision.HIGHEST)
    num_blocks = fresh.shape[2]
    own_column = (jnp.arange(num_blocks) == block_idx).astype(jnp.int32)
    fresh_own = jnp.sum(fresh[0] * own_column[None, :], axis=1)
    qkv_cols = qkv_weight[0]
    out_cols = out_weight[0]
    old_keys = k_stale[0]
    old_values = v_stale[0]
    num_req = hidden.shape[0]
    received = jnp.zeros_like(hidden[0:1])
    first_out = []
    second_out = []
    for tick_idx in range(num_req + 1):
        if tick_idx < num_req:
            own_input = hidden[tick_idx : tick_idx + 1]
        else:
            own_input = jnp.zeros_like(hidden[0:1])
        layer_in = jnp.where(section_idx == 0, own_input, received)
        req_idx = jnp.clip(tick_idx - section_idx, 0, num_req - 1)
        layer_out = attend(
            layer_in,
            qkv_cols,
            out_cols,
            modulate,
            pick_request(fresh_own, req_idx),
            pick_request(old_keys, req_idx),
            pick_request(old_values, req_idx),
            pick_request(live, req_idx),
        )
        if tick_idx < num_req:
            first_out.append(layer_out)
            received = from_behind(layer_out, "section", 1)
        if tick_idx >= 1:
            second_out.append(layer_out)
    result = jnp.where(
        section_idx == 0, jnp.concatenate(first_out, axis=0), jnp.concatenate(second_out, axis=0)
    )
    return result[None]


HEAD = 64
BF16 = jnp.bfloat16
F32 = jnp.float32
NT = (((1,), (1,)), ((), ()))
VMEM = pl.BlockSpec(memory_space=pltpu.VMEM)
SMEM = pl.BlockSpec(memory_space=pltpu.SMEM)
HBM = pl.BlockSpec(memory_space=pltpu.HBM)
ANY = pl.BlockSpec(memory_space=pl.ANY)


def call(body, outs, scratch, cost, *args, specs=None, spare=40 << 20):
    flops, moved = cost
    return pl.pallas_call(
        body,
        out_shape=outs,
        in_specs=specs or [VMEM] * len(args),
        out_specs=jax.tree.map(lambda _: VMEM, outs),
        scratch_shapes=scratch,
        compiler_params=pltpu.CompilerParams(vmem_limit_bytes=(64 << 20) - spare),
        cost_estimate=pl.CostEstimate(flops=flops, bytes_accessed=moved, transcendentals=0),
    )(*args)


def pinned(array):
    return pltpu.with_memory_space_constraint(array, pltpu.HBM)


def dot_nt(left, right):
    return lax.dot_general(left, right, NT, preferred_element_type=F32)


def halves(columns):
    mid = columns.shape[0] // 2
    return jnp.concatenate([columns[:mid], columns[mid:]], axis=1)


def group_of(device, n):
    return (3 * device + 2 * (device % 2)) % n


def owner_of(group, n):
    return (group - 2 * (group % 2)) * pow(3, -1, n) % n


def pack(cols):
    return jnp.concatenate([cols[:, :128], halves(cols[:, 128:])], axis=0)


def unpack(packed):
    tokens = packed.shape[0] // 3 * 2
    last = packed[tokens:]
    return jnp.concatenate(
        [packed[:tokens], jnp.concatenate([last[:, :HEAD], last[:, HEAD:]], axis=0)], axis=1
    )


def pack_by_parity(cols, odd):
    mid = cols.shape[0] // 2
    even_form = pack(cols)
    odd_form = jnp.concatenate(
        [
            cols[:, HEAD:],
            jnp.concatenate([cols[mid:, :HEAD], cols[:mid, :HEAD]], axis=1),
        ],
        axis=0,
    )
    return jnp.where(odd, odd_form, even_form)


def assemble(blocks, whole, by_heads=False):
    tokens = whole.shape[0]
    n = blocks.shape[0]
    for d in range(0, n, 2):
        even, odd = [owner_of(group, n) if by_heads else group for group in (d, d + 1)]
        even_last, odd_last = blocks[even, tokens:].astype(F32), blocks[odd, tokens:].astype(F32)
        left = lax.broadcasted_iota(jnp.int32, even_last.shape, 1) < HEAD
        first = jnp.where(left, even_last, odd_last)
        second = pltpu.roll(jnp.where(left, odd_last, even_last), HEAD, 1)
        at = d // 2 * 384
        whole[:, at : at + 128] = blocks[even, :tokens].astype(whole.dtype)
        whole[:, at + 128 : at + 256] = jnp.concatenate([first, second], axis=0).astype(whole.dtype)
        whole[:, at + 256 : at + 384] = blocks[odd, :tokens].astype(whole.dtype)


def own_columns(ref, rows, me):
    pair = ref[rows, pl.ds(pl.multiple_of(me // 2 * 384, 128), 384)]
    return jnp.where((me & 1) == 1, pair[:, 192:], pair[:, :192])


def norm_into(stream, mod, normed):
    tokens, width = stream.shape
    step = 128
    total = jnp.zeros((tokens, step), F32)
    for at in range(0, width, step):
        total += stream[:, at : at + step]
    center = jnp.sum(total, axis=-1, keepdims=True) / width
    total = jnp.zeros((tokens, step), F32)
    for at in range(0, width, step):
        off = stream[:, at : at + step] - center
        total += off * off
    variance = jnp.sum(total, axis=-1, keepdims=True) / width
    spread = 1.0 / jnp.sqrt(variance + 1e-06)
    for at in range(0, width, step):
        part = (stream[:, at : at + step] - center) * spread
        part = part * (1.0 + mod[0, :, at : at + step]) + mod[1, :, at : at + step]
        normed[:, at : at + step] = part.astype(BF16)


def own_or_other(layer, own, other):
    return jnp.where(lax.axis_index("section") == layer, own, other)


def dot_into(layer, left, own, other, product):
    def into(weight):
        product[...] = dot_nt(left[...], weight[...]).astype(product.dtype)

    held = lax.axis_index("section") == layer
    pl.when(held)(lambda: into(own))
    pl.when(jnp.logical_not(held))(lambda: into(other))


def normalise(layer, stream, mod, other_mod, normed, residual, scales):
    scales[...] = own_or_other(layer, mod[...], other_mod[...])
    norm_into(stream, scales, normed)
    residual[...] = own_columns(stream, slice(None), lax.axis_index("blk")).astype(BF16)


def chunks_of(columns, chunks):
    odd = (lax.axis_index("blk") & 1) == 1
    first, middle, last = [pack(columns[:, at : at + 192].astype(F32)) for at in range(0, 576, 192)]
    for chunk, value in zip(chunks, (jnp.where(odd, last, first), middle, jnp.where(odd, first, last))):
        chunk[...] = value.astype(BF16)


def first_projection(arrived, own, other, mod, other_mod, other_out, chunk0, chunk1, chunk2, residual, stream, scales, normed, columns, held, sems):
    holds = lax.axis_index("section") == 0
    parts = sems.shape[0]
    size = held.shape[0] // parts
    copies = [
        pltpu.make_async_copy(own.at[pl.ds(i * size, size)], held.at[pl.ds(i * size, size)], sems.at[i])
        for i in range(parts)
    ]

    @pl.when(holds)
    def _():
        for copy in copies:
            copy.start()

    n = arrived.shape[0]
    rows = stream.shape[0] // n
    for b in range(n):
        stream[rows * b : rows * b + rows, :] = arrived[b, :rows, :].astype(F32)
    normalise(0, stream, mod, other_mod, normed, residual, scales)

    @pl.when(holds)
    def _():
        for copy in copies:
            copy.wait()

    dot_into(0, normed, held, other, columns)
    chunks_of(columns, (chunk0, chunk1, chunk2))


def next_projection(blocks, own, other, mod, other_mod, chunk0, chunk1, chunk2, residual, stream, scales, normed, columns):
    assemble(blocks, stream)
    normalise(1, stream, mod, other_mod, normed, residual, scales)
    dot_into(1, normed, own, other, columns)
    chunks_of(columns, (chunk0, chunk1, chunk2))


def attention(layer, chunk0, chunk1, chunk2, old, fresh, other_fresh, live, attn):
    n = attn.shape[0]
    me, request = lax.axis_index("blk"), lax.axis_index("section")
    inverse = pow(3, -1, n)
    odd = me & 1
    sign = 1 - 2 * odd
    sender1 = lax.rem(me - sign * inverse + 2 * n, n)
    sender2 = lax.rem(me - sign * 2 * inverse + 2 * n, n)
    kinds = ((3 * me + 2 * odd) // n, (3 * sender1 + 1) // n, (3 * sender2 + 2 - 2 * odd) // n)
    got = [chunk[...].astype(F32) for chunk in (chunk0, chunk1, chunk2)]

    def kind(which):
        return unpack(jnp.where(kinds[0] == which, got[0], jnp.where(kinds[1] == which, got[1], got[2])))

    queries = kind(0)
    tokens, width = queries.shape
    heads = width // HEAD
    rows = tokens // n
    token = lax.broadcasted_iota(jnp.int32, (tokens, 1), 0)
    is_fresh = jnp.zeros((tokens, 1), jnp.int32)
    for b in range(n):
        flag = own_or_other(layer, fresh[0, request, b], other_fresh[0, request, b])
        is_fresh = jnp.where(token >= b * rows, flag, is_fresh)
    is_fresh = is_fresh == 1
    key = lax.broadcasted_iota(jnp.int32, (1, tokens), 1)
    is_live = jnp.zeros((1, tokens), jnp.int32)
    for b in range(n):
        is_live = jnp.where(key >= b * rows, live[request, b], is_live)
    is_live = is_live == 1
    keys = jnp.where(is_fresh, kind(1), old[layer, :, :width].astype(F32)).astype(BF16)
    values = jnp.where(is_fresh, kind(2), old[layer, :, width:].astype(F32)).astype(BF16)
    head_of = lax.broadcasted_iota(jnp.int32, (tokens, width), 1) // HEAD
    stacked = jnp.concatenate([jnp.where(head_of == h, queries, 0.0) for h in range(heads)], axis=0)
    scores = dot_nt(stacked.astype(BF16), keys) * 0.125
    scores = jnp.where(is_live, scores, -1e30)
    top = jnp.max(scores, axis=-1, keepdims=True)
    weights = jnp.where(is_live, jnp.exp(scores - top), 0.0)
    total = jnp.sum(weights, axis=-1, keepdims=True)
    mixed = jnp.dot(weights.astype(BF16), values, preferred_element_type=F32) * (1.0 / total)
    result = jnp.zeros((tokens, width), F32)
    for h in range(heads):
        result = jnp.where(head_of == h, mixed[h * tokens : (h + 1) * tokens], result)
    packed = pack_by_parity(result, (me & 1) == 1).astype(BF16)
    for d in range(n):
        attn[d] = packed


def layer_columns(layer, blocks, own, other, mod, other_mod, residual, whole, mixed):
    me = lax.axis_index("blk")
    assemble(blocks, whole, by_heads=True)
    dot_into(layer, whole, own, other, mixed)
    gates = own_or_other(layer, mod[2], other_mod[2])
    pairs = [gates[:, at : at + 384] for at in range(0, gates.shape[1], 384)]
    pair = pairs[0]
    for i, other_pair in enumerate(pairs):
        pair = jnp.where(me // 2 == i, other_pair, pair)
    gate = jnp.where((me & 1) == 1, pair[:, 192:], pair[:, :192])
    return (residual[...].astype(F32) + gate * mixed[...].astype(F32)).astype(BF16).astype(F32)


def first_output(blocks, own, other, mod, other_mod, residual, copies, kept, *scratch):
    columns = layer_columns(0, blocks, own, other, mod, other_mod, residual, *scratch)
    packed = pack_by_parity(columns, (lax.axis_index("blk") & 1) == 1).astype(BF16)
    for d in range(copies.shape[0]):
        copies[d] = packed
    kept[...] = columns


def last_output(blocks, own, other, mod, other_mod, residual, kept, by_token, columns, *scratch):
    columns[...] = layer_columns(1, blocks, own, other, mod, other_mod, residual, *scratch)
    n = by_token.shape[0] // 2
    rows = columns.shape[0] // n
    for layer, outs in enumerate((kept, columns)):
        for b in range(n):
            by_token[layer * n + b, :rows, :] = outs[rows * b : rows * b + rows, :].astype(BF16)


def first_exchange(hidden, old_keys, old_values, other_keys, other_values, leaving, held, sems):
    copies = [
        pltpu.make_async_copy(ref, held.at[i], sems.at[i])
        for i, ref in enumerate((hidden, old_keys, old_values, other_keys, other_values))
    ]
    for copy in copies:
        copy.start()
    rows, reqs, width = hidden.shape
    n = leaving.shape[0]
    columns = width // n
    first = lax.axis_index("section") == 0
    for copy in copies:
        copy.wait()

    def of_request(which):
        own = [held[which, i].astype(F32) for i in range(rows)]
        return jnp.concatenate([jnp.where(first, pair[:1], pair[1:]) for pair in own], axis=0)

    mine, *arrays = [of_request(which) for which in range(5)]
    mine = mine.astype(BF16)
    own, other = arrays[:2], arrays[2:]
    stale = [jnp.where(first, a, b) for a, b in zip(own, other)] + [jnp.where(first, b, a) for a, b in zip(own, other)]
    for b in range(n):
        at = columns * group_of(b, n)
        block = jnp.concatenate([array[:, at : at + columns] for array in stale], axis=1)
        leaving[b, :rows, :] = mine
        for i in range(rows):
            leaving[b, rows : rows + 1, i * 4 * columns : (i + 1) * 4 * columns] = block[i : i + 1].astype(BF16)


def stale_by_token(arrived, old, rows):
    n = arrived.shape[0]
    per = rows.shape[1] // n
    wide = rows.shape[2]
    for b in range(n):
        flat = arrived[b, per : per + 1, :].astype(F32)
        for i in range(per):
            for layer in range(2):
                at = (i * 2 + layer) * wide
                rows[layer, per * b + i : per * b + i + 1, :] = flat[:, at : at + wide]
    old[...] = rows[...].astype(BF16)


def to_rows(arrived, out, rows):
    n = arrived.shape[0] // 2
    per, columns = out.shape[0], arrived.shape[2]
    for s in range(2):
        for b in range(n):
            rows[s, :per, columns * b : columns * b + columns] = arrived[s * n + b, :per, :].astype(F32)
    for i in range(per):
        out[i] = jnp.concatenate([rows[s, i : i + 1, :] for s in range(2)], axis=0).astype(BF16)


def exchange(blocks, axis):
    return lax.all_to_all(blocks, axis, split_axis=0, concat_axis=0, tiled=True)


def swap_sections(array):
    return lax.ppermute(array, "section", [(0, 1), (1, 0)])


def by_heads(chunks, n):
    inverse = pow(3, -1, n)
    kept, middle, other = chunks
    pairs1 = [(b, (b + (inverse if b % 2 else -inverse)) % n) for b in range(n)]
    pairs2 = [(b, (b + (-2 * inverse if b % 2 else 2 * inverse)) % n) for b in range(n)]
    return kept, lax.ppermute(middle, "blk", pairs1), lax.ppermute(other, "blk", pairs2)


def per_device(hidden, qkv_weight, out_weight, modulation, timestep, fresh, live, k_stale, v_stale):
    n = lax.axis_size("blk")
    columns = out_weight.shape[2]
    reqs, rows, width = hidden.shape
    if not (
        columns == 3 * HEAD
        and n % 3 == 1
        and n & (n - 1) == 0
        and reqs == lax.axis_size("section") == 2
        and rows <= 4
    ):
        return per_device_by_token(
            hidden, qkv_weight, out_weight, modulation, timestep, fresh, live, k_stale, v_stale
        )
    tokens = n * rows
    shape = jax.ShapeDtypeStruct
    packed = shape((tokens * 3 // 2, 128), BF16)
    copies = shape((n, tokens * 3 // 2, 128), BF16)
    cols = shape((tokens, columns), BF16)
    own_qkv = jnp.swapaxes(qkv_weight[0], 0, 1)
    own_out = jnp.swapaxes(out_weight[0], 0, 1)
    steps = jnp.transpose(modulation, (1, 2, 0, 3))
    old_keys = jnp.transpose(k_stale[0], (1, 0, 2))
    old_values = jnp.transpose(v_stale[0], (1, 0, 2))

    other_keys, other_values, timestep, sent_fresh = lax.optimization_barrier(
        (swap_sections(old_keys), swap_sections(old_values), timestep, fresh)
    )
    mod = lax.dynamic_index_in_dim(steps, timestep[0], 0, keepdims=False)
    other_mod, other_fresh, sent_qkv, sent_out = lax.optimization_barrier(
        (swap_sections(mod), swap_sections(sent_fresh), own_qkv, own_out)
    )
    mods = (mod, other_mod)
    flags = (fresh, other_fresh)
    other_qkv, other_out = swap_sections(sent_qkv), swap_sections(sent_out)
    out = (own_out, other_out)
    leaving = call(
        first_exchange,
        shape((n, 4, width), BF16),
        [pltpu.VMEM((5, rows, reqs, width), BF16), pltpu.SemaphoreType.DMA((5,))],
        (0, 1000000),
        *(pinned(array) for array in (jnp.transpose(hidden, (1, 0, 2)), old_keys, old_values)),
        other_keys,
        other_values,
        specs=[HBM] * 3 + [ANY] * 2,
    )
    arrived = exchange(leaving, "blk")

    blocks = arrived
    for layer in range(2):
        *chunks, residual = call(
            next_projection if layer else first_projection,
            [packed, packed, packed, cols],
            [
                pltpu.VMEM((tokens, width), F32),
                pltpu.VMEM(mod.shape, F32),
                pltpu.VMEM((tokens, width), BF16),
                pltpu.VMEM((tokens, 3 * columns), BF16),
            ]
            + ([] if layer else [pltpu.VMEM(own_qkv.shape, BF16), pltpu.SemaphoreType.DMA((36,))]),
            (2 * tokens * width * 3 * columns, 8 * width * columns),
            blocks,
            *((own_qkv, other_qkv, *mods) if layer else (pinned(own_qkv), other_qkv, *mods, other_out)),
            **({} if layer else {"specs": [VMEM, HBM, VMEM, VMEM, VMEM, ANY]}),
        )
        if layer == 0:
            arrived, chunks[1] = lax.optimization_barrier((arrived, chunks[1]))
            old = call(
                stale_by_token,
                shape((2, tokens, 2 * columns), BF16),
                [pltpu.VMEM((2, tokens, 2 * columns), F32)],
                (0, 200000),
                arrived,
            )
        attn = call(
            functools.partial(attention, layer),
            copies,
            [],
            (8 * tokens * tokens * columns, 300000),
            *by_heads(chunks, n),
            old,
            *flags,
            live,
            specs=[VMEM] * 4 + [SMEM] * 3,
        )
        args = (exchange(attn, "blk"), *out, *mods, residual)
        cost = (2 * tokens * width * columns, 4 * width * columns)
        held = [pltpu.VMEM((tokens, width), BF16), pltpu.VMEM((tokens, columns), BF16)]
        if layer == 0:
            leaving, kept = call(first_output, [copies, shape((tokens, columns), F32)], held, cost, *args)
            blocks = exchange(leaving, "blk")
        else:
            leaving = call(
                last_output,
                shape((2 * n, 4, columns), BF16),
                [pltpu.VMEM((tokens, columns), F32)] + held,
                cost,
                *args,
                kept,
            )
    result = call(
        to_rows,
        shape((rows, reqs, width), BF16),
        [pltpu.VMEM((2, 8, width), F32)],
        (0, 100000),
        exchange(leaving, ("section", "blk")),
    )
    return jnp.transpose(result, (1, 0, 2))[None]


def solution(mesh):
    return jax.shard_map(
        per_device,
        mesh=mesh,
        in_specs=(
            P(None, "blk", None),
            P("section", None, "blk"),
            P("section", None, "blk"),
            P("section", None, None, None),
            P(),
            P("section", None, None),
            P(),
            P("section", None, "blk", None),
            P("section", None, "blk", None),
        ),
        out_specs=P("section", None, "blk", None),
        check_vma=False,
    )
```

```python
import functools

import jax
import jax.numpy as jnp
from jax import lax
from jax.experimental import pallas as pl
from jax.experimental.pallas import tpu as pltpu
from jax.sharding import PartitionSpec as P


def from_behind(shard, axis, by):
    count = lax.axis_size(axis)
    pairs = [(i, i + by) for i in range(count) if 0 <= i + by < count]
    return lax.ppermute(shard, axis, pairs)


def attend(layer_in, qkv_cols, out_cols, modulate, fresh_own, old_keys, old_values, live):
    stream = layer_in.astype(jnp.float32)
    center = jnp.mean(stream, axis=-1, keepdims=True)
    variance = jnp.mean((stream - center) ** 2, axis=-1, keepdims=True)
    normed = (stream - center) / jnp.sqrt(variance + 1e-06) * (1.0 + modulate[0]) + modulate[1]
    normed_b = normed.astype(jnp.bfloat16)
    columns = jnp.einsum(
        "rnd,dc->rnc",
        lax.all_gather(normed_b, "blk", axis=1, tiled=True),
        qkv_cols,
        preferred_element_type=jnp.float32,
    ).astype(jnp.bfloat16)
    projected = lax.all_to_all(columns, "blk", split_axis=1, concat_axis=2, tiled=True)
    num_req, num_rows, width = layer_in.shape
    queries = projected[:, :, :width]
    new_keys = projected[:, :, width : 2 * width]
    new_values = projected[:, :, 2 * width :]
    use_fresh = (fresh_own == 1)[:, None, None]
    keys = jnp.where(use_fresh, new_keys, old_keys)
    values = jnp.where(use_fresh, new_values, old_values)
    num_heads = width // 64
    num_blocks = live.shape[1]
    q_heads = queries.reshape(num_req, num_rows, num_heads, 64)
    live_float = live.astype(jnp.float32)
    run_max = jnp.full((num_req, num_heads, num_rows), -1e30, jnp.float32)
    key_piece = lax.all_gather(keys, "blk", axis=1, tiled=True)
    value_piece = lax.all_gather(values, "blk", axis=1, tiled=True)
    piece_rows = key_piece.shape[1]
    key_heads = key_piece.reshape(num_req, piece_rows, num_heads, 64)
    value_heads = value_piece.reshape(num_req, piece_rows, num_heads, 64)
    scores = (
        jnp.einsum("qrhd,qnhd->qhrn", q_heads, key_heads, preferred_element_type=jnp.float32)
        * 0.125
    )
    block_ids = jnp.arange(piece_rows) // num_rows
    one_hot = (block_ids[:, None] == jnp.arange(num_blocks)[None, :]).astype(jnp.float32)
    usable = jnp.einsum("qb,nb->qn", live_float, one_hot) > 0.5
    usable = usable[:, None, None, :]
    scores = jnp.where(usable, scores, -1e30)
    new_max = jnp.maximum(run_max, jnp.max(scores, axis=-1))
    weights = jnp.where(usable, jnp.exp(scores - new_max[..., None]), 0.0)
    new_sum = jnp.sum(weights, axis=-1)
    new_acc = jnp.einsum(
        "qhrn,qnhd->qhrd", weights, value_heads.astype(jnp.float32), precision=lax.Precision.HIGHEST
    )
    attn = new_acc / new_sum[..., None]
    attn = jnp.transpose(attn, (0, 2, 1, 3)).reshape(num_req, num_rows, width).astype(jnp.bfloat16)
    out_part = jnp.einsum(
        "rnd,dc->rnc",
        lax.all_gather(attn, "blk", axis=1, tiled=True),
        out_cols,
        preferred_element_type=jnp.float32,
    ).astype(jnp.bfloat16)
    mixed_back = lax.all_to_all(out_part, "blk", split_axis=1, concat_axis=2, tiled=True)
    return (stream + modulate[2] * mixed_back.astype(jnp.float32)).astype(jnp.bfloat16)


def pick_request(array, req_idx):
    return lax.dynamic_index_in_dim(array, req_idx, 0, keepdims=True)


def per_device_by_token(hidden, qkv_weight, out_weight, modulation, timestep, fresh, live, k_stale, v_stale):
    section_idx = lax.axis_index("section")
    block_idx = lax.axis_index("blk")
    steps_all = modulation.shape[1]
    pick_row = (jnp.arange(steps_all) == timestep[0]).astype(jnp.float32)
    modulate = jnp.einsum("t,tcd->cd", pick_row, modulation[0], precision=lax.Precision.HIGHEST)
    num_blocks = fresh.shape[2]
    own_column = (jnp.arange(num_blocks) == block_idx).astype(jnp.int32)
    fresh_own = jnp.sum(fresh[0] * own_column[None, :], axis=1)
    qkv_cols = qkv_weight[0]
    out_cols = out_weight[0]
    old_keys = k_stale[0]
    old_values = v_stale[0]
    num_req = hidden.shape[0]
    received = jnp.zeros_like(hidden[0:1])
    first_out = []
    second_out = []
    for tick_idx in range(num_req + 1):
        if tick_idx < num_req:
            own_input = hidden[tick_idx : tick_idx + 1]
        else:
            own_input = jnp.zeros_like(hidden[0:1])
        layer_in = jnp.where(section_idx == 0, own_input, received)
        req_idx = jnp.clip(tick_idx - section_idx, 0, num_req - 1)
        layer_out = attend(
            layer_in,
            qkv_cols,
            out_cols,
            modulate,
            pick_request(fresh_own, req_idx),
            pick_request(old_keys, req_idx),
            pick_request(old_values, req_idx),
            pick_request(live, req_idx),
        )
        if tick_idx < num_req:
            first_out.append(layer_out)
            received = from_behind(layer_out, "section", 1)
        if tick_idx >= 1:
            second_out.append(layer_out)
    result = jnp.where(
        section_idx == 0, jnp.concatenate(first_out, axis=0), jnp.concatenate(second_out, axis=0)
    )
    return result[None]


HEAD = 64
BF16 = jnp.bfloat16
F32 = jnp.float32
NT = (((1,), (1,)), ((), ()))
VMEM = pl.BlockSpec(memory_space=pltpu.VMEM)
SMEM = pl.BlockSpec(memory_space=pltpu.SMEM)
HBM = pl.BlockSpec(memory_space=pltpu.HBM)
ANY = pl.BlockSpec(memory_space=pl.ANY)


def call(body, outs, scratch, cost, *args, specs=None, spare=40 << 20):
    flops, moved = cost
    return pl.pallas_call(
        body,
        out_shape=outs,
        in_specs=specs or [VMEM] * len(args),
        out_specs=jax.tree.map(lambda _: VMEM, outs),
        scratch_shapes=scratch,
        compiler_params=pltpu.CompilerParams(vmem_limit_bytes=(64 << 20) - spare),
        cost_estimate=pl.CostEstimate(flops=flops, bytes_accessed=moved, transcendentals=0),
    )(*args)


def pinned(array):
    return pltpu.with_memory_space_constraint(array, pltpu.HBM)


def dot_nt(left, right):
    return lax.dot_general(left, right, NT, preferred_element_type=F32)


def halves(columns):
    mid = columns.shape[0] // 2
    return jnp.concatenate([columns[:mid], columns[mid:]], axis=1)


def group_of(device, n):
    return (3 * device + 2 * (device % 2)) % n


def owner_of(group, n):
    return (group - 2 * (group % 2)) * pow(3, -1, n) % n


def pack(cols):
    return jnp.concatenate([cols[:, :128], halves(cols[:, 128:])], axis=0)


def unpack(packed):
    tokens = packed.shape[0] // 3 * 2
    last = packed[tokens:]
    return jnp.concatenate(
        [packed[:tokens], jnp.concatenate([last[:, :HEAD], last[:, HEAD:]], axis=0)], axis=1
    )


def pack_by_parity(cols, odd):
    mid = cols.shape[0] // 2
    even_form = pack(cols)
    odd_form = jnp.concatenate(
        [
            cols[:, HEAD:],
            jnp.concatenate([cols[mid:, :HEAD], cols[:mid, :HEAD]], axis=1),
        ],
        axis=0,
    )
    return jnp.where(odd, odd_form, even_form)


def assemble(blocks, whole, by_heads=False):
    tokens = whole.shape[0]
    n = blocks.shape[0]
    for d in range(0, n, 2):
        even, odd = [owner_of(group, n) if by_heads else group for group in (d, d + 1)]
        even_last, odd_last = blocks[even, tokens:].astype(F32), blocks[odd, tokens:].astype(F32)
        left = lax.broadcasted_iota(jnp.int32, even_last.shape, 1) < HEAD
        first = jnp.where(left, even_last, odd_last)
        second = pltpu.roll(jnp.where(left, odd_last, even_last), HEAD, 1)
        at = d // 2 * 384
        whole[:, at : at + 128] = blocks[even, :tokens].astype(whole.dtype)
        whole[:, at + 128 : at + 256] = jnp.concatenate([first, second], axis=0).astype(whole.dtype)
        whole[:, at + 256 : at + 384] = blocks[odd, :tokens].astype(whole.dtype)


def own_columns(ref, rows, me):
    pair = ref[rows, pl.ds(pl.multiple_of(me // 2 * 384, 128), 384)]
    return jnp.where((me & 1) == 1, pair[:, 192:], pair[:, :192])


def norm_into(stream, mod, normed):
    tokens, width = stream.shape
    step = 128
    total = jnp.zeros((tokens, step), F32)
    for at in range(0, width, step):
        total += stream[:, at : at + step]
    center = jnp.sum(total, axis=-1, keepdims=True) / width
    total = jnp.zeros((tokens, step), F32)
    for at in range(0, width, step):
        off = stream[:, at : at + step] - center
        total += off * off
    variance = jnp.sum(total, axis=-1, keepdims=True) / width
    spread = 1.0 / jnp.sqrt(variance + 1e-06)
    for at in range(0, width, step):
        part = (stream[:, at : at + step] - center) * spread
        part = part * (1.0 + mod[0, :, at : at + step]) + mod[1, :, at : at + step]
        normed[:, at : at + step] = part.astype(BF16)


def own_or_other(layer, own, other):
    return jnp.where(lax.axis_index("section") == layer, own, other)


def dot_into(layer, left, own, other, product):
    def into(weight):
        product[...] = dot_nt(left[...], weight[...]).astype(product.dtype)

    held = lax.axis_index("section") == layer
    pl.when(held)(lambda: into(own))
    pl.when(jnp.logical_not(held))(lambda: into(other))


def normalise(stream, mod, normed, residual):
    norm_into(stream, mod, normed)
    residual[...] = own_columns(stream, slice(None), lax.axis_index("blk")).astype(BF16)


def chunks_of(columns, chunks):
    odd = (lax.axis_index("blk") & 1) == 1
    first, middle, last = [pack(columns[:, at : at + 192].astype(F32)) for at in range(0, 576, 192)]
    for chunk, value in zip(chunks, (jnp.where(odd, last, first), middle, jnp.where(odd, first, last))):
        chunk[...] = value.astype(BF16)


def first_projection(arrived, own, other, mod, other_out, chunk0, chunk1, chunk2, residual, stream, normed, columns, held, sems):
    holds = lax.axis_index("section") == 0
    parts = sems.shape[0]
    size = held.shape[0] // parts
    copies = [
        pltpu.make_async_copy(own.at[pl.ds(i * size, size)], held.at[pl.ds(i * size, size)], sems.at[i])
        for i in range(parts)
    ]

    @pl.when(holds)
    def _():
        for copy in copies:
            copy.start()

    n = arrived.shape[0]
    rows = stream.shape[0] // n
    for b in range(n):
        stream[rows * b : rows * b + rows, :] = arrived[b, :rows, :].astype(F32)
    normalise(stream, mod, normed, residual)

    @pl.when(holds)
    def _():
        for copy in copies:
            copy.wait()

    dot_into(0, normed, held, other, columns)
    chunks_of(columns, (chunk0, chunk1, chunk2))


def next_projection(blocks, own, other, mod, chunk0, chunk1, chunk2, residual, stream, normed, columns):
    assemble(blocks, stream)
    normalise(stream, mod, normed, residual)
    dot_into(1, normed, own, other, columns)
    chunks_of(columns, (chunk0, chunk1, chunk2))


def attention(layer, chunk0, chunk1, chunk2, old, fresh, other_fresh, live, attn):
    n = attn.shape[0]
    me, request = lax.axis_index("blk"), lax.axis_index("section")
    inverse = pow(3, -1, n)
    odd = me & 1
    sign = 1 - 2 * odd
    sender1 = lax.rem(me - sign * inverse + 2 * n, n)
    sender2 = lax.rem(me - sign * 2 * inverse + 2 * n, n)
    kinds = ((3 * me + 2 * odd) // n, (3 * sender1 + 1) // n, (3 * sender2 + 2 - 2 * odd) // n)
    got = [chunk[...].astype(F32) for chunk in (chunk0, chunk1, chunk2)]

    def kind(which):
        return unpack(jnp.where(kinds[0] == which, got[0], jnp.where(kinds[1] == which, got[1], got[2])))

    queries = kind(0)
    tokens, width = queries.shape
    heads = width // HEAD
    rows = tokens // n
    token = lax.broadcasted_iota(jnp.int32, (tokens, 1), 0)
    is_fresh = jnp.zeros((tokens, 1), jnp.int32)
    for b in range(n):
        flag = own_or_other(layer, fresh[0, request, b], other_fresh[0, request, b])
        is_fresh = jnp.where(token >= b * rows, flag, is_fresh)
    is_fresh = is_fresh == 1
    key = lax.broadcasted_iota(jnp.int32, (1, tokens), 1)
    is_live = jnp.zeros((1, tokens), jnp.int32)
    for b in range(n):
        is_live = jnp.where(key >= b * rows, live[request, b], is_live)
    is_live = is_live == 1
    keys = jnp.where(is_fresh, kind(1), old[layer, :, :width].astype(F32)).astype(BF16)
    values = jnp.where(is_fresh, kind(2), old[layer, :, width:].astype(F32)).astype(BF16)
    head_of = lax.broadcasted_iota(jnp.int32, (tokens, width), 1) // HEAD
    stacked = jnp.concatenate([jnp.where(head_of == h, queries, 0.0) for h in range(heads)], axis=0)
    scores = dot_nt(stacked.astype(BF16), keys) * 0.125
    scores = jnp.where(is_live, scores, -1e30)
    top = jnp.max(scores, axis=-1, keepdims=True)
    weights = jnp.where(is_live, jnp.exp(scores - top), 0.0)
    total = jnp.sum(weights, axis=-1, keepdims=True)
    mixed = jnp.dot(weights.astype(BF16), values, preferred_element_type=F32) * (1.0 / total)
    result = jnp.zeros((tokens, width), F32)
    for h in range(heads):
        result = jnp.where(head_of == h, mixed[h * tokens : (h + 1) * tokens], result)
    packed = pack_by_parity(result, (me & 1) == 1).astype(BF16)
    for d in range(n):
        attn[d] = packed


def layer_columns(layer, blocks, own, other, mod, residual, whole, mixed):
    assemble(blocks, whole, by_heads=True)
    dot_into(layer, whole, own, other, mixed)
    gate = own_columns(mod.at[2], slice(None), lax.axis_index("blk"))
    return (residual[...].astype(F32) + gate * mixed[...].astype(F32)).astype(BF16).astype(F32)


def first_output(blocks, own, other, mod, residual, copies, kept, *scratch):
    columns = layer_columns(0, blocks, own, other, mod, residual, *scratch)
    packed = pack_by_parity(columns, (lax.axis_index("blk") & 1) == 1).astype(BF16)
    for d in range(copies.shape[0]):
        copies[d] = packed
    kept[...] = columns


def last_output(blocks, own, other, mod, residual, kept, by_token, columns, *scratch):
    columns[...] = layer_columns(1, blocks, own, other, mod, residual, *scratch)
    n = by_token.shape[0] // 2
    rows = columns.shape[0] // n
    for layer, outs in enumerate((kept, columns)):
        for b in range(n):
            by_token[layer * n + b, :rows, :] = outs[rows * b : rows * b + rows, :].astype(BF16)


def first_exchange(hidden, old_keys, old_values, other_keys, other_values, mod, other_mod, leaving, first_mod, held, sems):
    copies = [
        pltpu.make_async_copy(ref, held.at[i], sems.at[i])
        for i, ref in enumerate((hidden, old_keys, old_values, other_keys, other_values))
    ]
    for copy in copies:
        copy.start()
    rows, reqs, width = hidden.shape
    n = leaving.shape[0]
    columns = width // n
    first = lax.axis_index("section") == 0
    first_mod[...] = own_or_other(0, mod[...], other_mod[...])
    for copy in copies:
        copy.wait()

    def of_request(which):
        own = [held[which, i].astype(F32) for i in range(rows)]
        return jnp.concatenate([jnp.where(first, pair[:1], pair[1:]) for pair in own], axis=0)

    mine, *arrays = [of_request(which) for which in range(5)]
    mine = mine.astype(BF16)
    own, other = arrays[:2], arrays[2:]
    stale = [jnp.where(first, a, b) for a, b in zip(own, other)] + [jnp.where(first, b, a) for a, b in zip(own, other)]
    for b in range(n):
        at = columns * group_of(b, n)
        block = jnp.concatenate([array[:, at : at + columns] for array in stale], axis=1)
        leaving[b, :rows, :] = mine
        for i in range(rows):
            leaving[b, rows : rows + 1, i * 4 * columns : (i + 1) * 4 * columns] = block[i : i + 1].astype(BF16)


def stale_by_token(arrived, mod, other_mod, old, second_mod, rows):
    n = arrived.shape[0]
    per = rows.shape[1] // n
    wide = rows.shape[2]
    for b in range(n):
        flat = arrived[b, per : per + 1, :].astype(F32)
        for i in range(per):
            for layer in range(2):
                at = (i * 2 + layer) * wide
                rows[layer, per * b + i : per * b + i + 1, :] = flat[:, at : at + wide]
    old[...] = rows[...].astype(BF16)
    second_mod[...] = own_or_other(1, mod[...], other_mod[...])


def to_rows(arrived, out, rows):
    n = arrived.shape[0] // 2
    per, columns = out.shape[0], arrived.shape[2]
    for s in range(2):
        for b in range(n):
            rows[s, :per, columns * b : columns * b + columns] = arrived[s * n + b, :per, :].astype(F32)
    for i in range(per):
        out[i] = jnp.concatenate([rows[s, i : i + 1, :] for s in range(2)], axis=0).astype(BF16)


def exchange(blocks, axis):
    return lax.all_to_all(blocks, axis, split_axis=0, concat_axis=0, tiled=True)


def swap_sections(array):
    return lax.ppermute(array, "section", [(0, 1), (1, 0)])


def by_heads(chunks, n):
    inverse = pow(3, -1, n)
    kept, middle, other = chunks
    pairs1 = [(b, (b + (inverse if b % 2 else -inverse)) % n) for b in range(n)]
    pairs2 = [(b, (b + (-2 * inverse if b % 2 else 2 * inverse)) % n) for b in range(n)]
    return kept, lax.ppermute(middle, "blk", pairs1), lax.ppermute(other, "blk", pairs2)


def per_device(hidden, qkv_weight, out_weight, modulation, timestep, fresh, live, k_stale, v_stale):
    n = lax.axis_size("blk")
    columns = out_weight.shape[2]
    reqs, rows, width = hidden.shape
    if not (
        columns == 3 * HEAD
        and n % 3 == 1
        and n & (n - 1) == 0
        and reqs == lax.axis_size("section") == 2
        and rows <= 4
    ):
        return per_device_by_token(
            hidden, qkv_weight, out_weight, modulation, timestep, fresh, live, k_stale, v_stale
        )
    tokens = n * rows
    shape = jax.ShapeDtypeStruct
    packed = shape((tokens * 3 // 2, 128), BF16)
    copies = shape((n, tokens * 3 // 2, 128), BF16)
    cols = shape((tokens, columns), BF16)
    own_qkv = jnp.swapaxes(qkv_weight[0], 0, 1)
    own_out = jnp.swapaxes(out_weight[0], 0, 1)
    steps = jnp.transpose(modulation, (1, 2, 0, 3))
    old_keys = jnp.transpose(k_stale[0], (1, 0, 2))
    old_values = jnp.transpose(v_stale[0], (1, 0, 2))

    other_keys, other_values, timestep, sent_fresh = lax.optimization_barrier(
        (swap_sections(old_keys), swap_sections(old_values), timestep, fresh)
    )
    mod = lax.dynamic_index_in_dim(steps, timestep[0], 0, keepdims=False)
    other_mod, other_fresh, sent_qkv, sent_out = lax.optimization_barrier(
        (swap_sections(mod), swap_sections(sent_fresh), own_qkv, own_out)
    )
    mods = (mod, other_mod)
    flags = (fresh, other_fresh)
    other_qkv, other_out = swap_sections(sent_qkv), swap_sections(sent_out)
    out = (own_out, other_out)
    leaving, layer_mod = call(
        first_exchange,
        [shape((n, 4, width), BF16), shape(mod.shape, F32)],
        [pltpu.VMEM((5, rows, reqs, width), BF16), pltpu.SemaphoreType.DMA((5,))],
        (0, 1000000),
        *(pinned(array) for array in (jnp.transpose(hidden, (1, 0, 2)), old_keys, old_values)),
        other_keys,
        other_values,
        *mods,
        specs=[HBM] * 3 + [ANY] * 2 + [VMEM] * 2,
    )
    arrived = exchange(leaving, "blk")

    blocks = arrived
    for layer in range(2):
        *chunks, residual = call(
            next_projection if layer else first_projection,
            [packed, packed, packed, cols],
            [
                pltpu.VMEM((tokens, width), F32),
                pltpu.VMEM((tokens, width), BF16),
                pltpu.VMEM((tokens, 3 * columns), BF16),
            ]
            + ([] if layer else [pltpu.VMEM(own_qkv.shape, BF16), pltpu.SemaphoreType.DMA((12,))]),
            (2 * tokens * width * 3 * columns, 8 * width * columns),
            blocks,
            *((own_qkv, other_qkv, layer_mod) if layer else (pinned(own_qkv), other_qkv, layer_mod, other_out)),
            **({} if layer else {"specs": [VMEM, HBM, VMEM, VMEM, ANY]}),
        )
        if layer == 0:
            arrived, chunks[1] = lax.optimization_barrier((arrived, chunks[1]))
            old, next_mod = call(
                stale_by_token,
                [shape((2, tokens, 2 * columns), BF16), shape(mod.shape, F32)],
                [pltpu.VMEM((2, tokens, 2 * columns), F32)],
                (0, 200000),
                arrived,
                *mods,
            )
        attn = call(
            functools.partial(attention, layer),
            copies,
            [],
            (8 * tokens * tokens * columns, 300000),
            *by_heads(chunks, n),
            old,
            *flags,
            live,
            specs=[VMEM] * 4 + [SMEM] * 3,
        )
        args = (exchange(attn, "blk"), *out, layer_mod, residual)
        cost = (2 * tokens * width * columns, 4 * width * columns)
        held = [pltpu.VMEM((tokens, width), BF16), pltpu.VMEM((tokens, columns), BF16)]
        if layer == 0:
            leaving, kept = call(first_output, [copies, shape((tokens, columns), F32)], held, cost, *args)
            blocks, layer_mod = exchange(leaving, "blk"), next_mod
        else:
            leaving = call(
                last_output,
                shape((2 * n, 4, columns), BF16),
                [pltpu.VMEM((tokens, columns), F32)] + held,
                cost,
                *args,
                kept,
            )
    result = call(
        to_rows,
        shape((rows, reqs, width), BF16),
        [pltpu.VMEM((2, 8, width), F32)],
        (0, 100000),
        exchange(leaving, ("section", "blk")),
    )
    return jnp.transpose(result, (1, 0, 2))[None]


def solution(mesh):
    return jax.shard_map(
        per_device,
        mesh=mesh,
        in_specs=(
            P(None, "blk", None),
            P("section", None, "blk"),
            P("section", None, "blk"),
            P("section", None, None, None),
            P(),
            P("section", None, None),
            P(),
            P("section", None, "blk", None),
            P("section", None, "blk", None),
        ),
        out_specs=P("section", None, "blk", None),
        check_vma=False,
    )
```

```python
import functools

import jax
import jax.numpy as jnp
from jax import lax
from jax.experimental import pallas as pl
from jax.experimental.pallas import tpu as pltpu
from jax.sharding import PartitionSpec as P


def from_behind(shard, axis, by):
    count = lax.axis_size(axis)
    pairs = [(i, i + by) for i in range(count) if 0 <= i + by < count]
    return lax.ppermute(shard, axis, pairs)


def attend(layer_in, qkv_cols, out_cols, modulate, fresh_own, old_keys, old_values, live):
    stream = layer_in.astype(jnp.float32)
    center = jnp.mean(stream, axis=-1, keepdims=True)
    variance = jnp.mean((stream - center) ** 2, axis=-1, keepdims=True)
    normed = (stream - center) / jnp.sqrt(variance + 1e-06) * (1.0 + modulate[0]) + modulate[1]
    normed_b = normed.astype(jnp.bfloat16)
    columns = jnp.einsum(
        "rnd,dc->rnc",
        lax.all_gather(normed_b, "blk", axis=1, tiled=True),
        qkv_cols,
        preferred_element_type=jnp.float32,
    ).astype(jnp.bfloat16)
    projected = lax.all_to_all(columns, "blk", split_axis=1, concat_axis=2, tiled=True)
    num_req, num_rows, width = layer_in.shape
    queries = projected[:, :, :width]
    new_keys = projected[:, :, width : 2 * width]
    new_values = projected[:, :, 2 * width :]
    use_fresh = (fresh_own == 1)[:, None, None]
    keys = jnp.where(use_fresh, new_keys, old_keys)
    values = jnp.where(use_fresh, new_values, old_values)
    num_heads = width // 64
    num_blocks = live.shape[1]
    q_heads = queries.reshape(num_req, num_rows, num_heads, 64)
    live_float = live.astype(jnp.float32)
    run_max = jnp.full((num_req, num_heads, num_rows), -1e30, jnp.float32)
    key_piece = lax.all_gather(keys, "blk", axis=1, tiled=True)
    value_piece = lax.all_gather(values, "blk", axis=1, tiled=True)
    piece_rows = key_piece.shape[1]
    key_heads = key_piece.reshape(num_req, piece_rows, num_heads, 64)
    value_heads = value_piece.reshape(num_req, piece_rows, num_heads, 64)
    scores = (
        jnp.einsum("qrhd,qnhd->qhrn", q_heads, key_heads, preferred_element_type=jnp.float32)
        * 0.125
    )
    block_ids = jnp.arange(piece_rows) // num_rows
    one_hot = (block_ids[:, None] == jnp.arange(num_blocks)[None, :]).astype(jnp.float32)
    usable = jnp.einsum("qb,nb->qn", live_float, one_hot) > 0.5
    usable = usable[:, None, None, :]
    scores = jnp.where(usable, scores, -1e30)
    new_max = jnp.maximum(run_max, jnp.max(scores, axis=-1))
    weights = jnp.where(usable, jnp.exp(scores - new_max[..., None]), 0.0)
    new_sum = jnp.sum(weights, axis=-1)
    new_acc = jnp.einsum(
        "qhrn,qnhd->qhrd", weights, value_heads.astype(jnp.float32), precision=lax.Precision.HIGHEST
    )
    attn = new_acc / new_sum[..., None]
    attn = jnp.transpose(attn, (0, 2, 1, 3)).reshape(num_req, num_rows, width).astype(jnp.bfloat16)
    out_part = jnp.einsum(
        "rnd,dc->rnc",
        lax.all_gather(attn, "blk", axis=1, tiled=True),
        out_cols,
        preferred_element_type=jnp.float32,
    ).astype(jnp.bfloat16)
    mixed_back = lax.all_to_all(out_part, "blk", split_axis=1, concat_axis=2, tiled=True)
    return (stream + modulate[2] * mixed_back.astype(jnp.float32)).astype(jnp.bfloat16)


def pick_request(array, req_idx):
    return lax.dynamic_index_in_dim(array, req_idx, 0, keepdims=True)


def per_device_by_token(hidden, qkv_weight, out_weight, modulation, timestep, fresh, live, k_stale, v_stale):
    section_idx = lax.axis_index("section")
    block_idx = lax.axis_index("blk")
    steps_all = modulation.shape[1]
    pick_row = (jnp.arange(steps_all) == timestep[0]).astype(jnp.float32)
    modulate = jnp.einsum("t,tcd->cd", pick_row, modulation[0], precision=lax.Precision.HIGHEST)
    num_blocks = fresh.shape[2]
    own_column = (jnp.arange(num_blocks) == block_idx).astype(jnp.int32)
    fresh_own = jnp.sum(fresh[0] * own_column[None, :], axis=1)
    qkv_cols = qkv_weight[0]
    out_cols = out_weight[0]
    old_keys = k_stale[0]
    old_values = v_stale[0]
    num_req = hidden.shape[0]
    received = jnp.zeros_like(hidden[0:1])
    first_out = []
    second_out = []
    for tick_idx in range(num_req + 1):
        if tick_idx < num_req:
            own_input = hidden[tick_idx : tick_idx + 1]
        else:
            own_input = jnp.zeros_like(hidden[0:1])
        layer_in = jnp.where(section_idx == 0, own_input, received)
        req_idx = jnp.clip(tick_idx - section_idx, 0, num_req - 1)
        layer_out = attend(
            layer_in,
            qkv_cols,
            out_cols,
            modulate,
            pick_request(fresh_own, req_idx),
            pick_request(old_keys, req_idx),
            pick_request(old_values, req_idx),
            pick_request(live, req_idx),
        )
        if tick_idx < num_req:
            first_out.append(layer_out)
            received = from_behind(layer_out, "section", 1)
        if tick_idx >= 1:
            second_out.append(layer_out)
    result = jnp.where(
        section_idx == 0, jnp.concatenate(first_out, axis=0), jnp.concatenate(second_out, axis=0)
    )
    return result[None]


HEAD = 64
BF16 = jnp.bfloat16
F32 = jnp.float32
NT = (((1,), (1,)), ((), ()))
VMEM = pl.BlockSpec(memory_space=pltpu.VMEM)
SMEM = pl.BlockSpec(memory_space=pltpu.SMEM)
HBM = pl.BlockSpec(memory_space=pltpu.HBM)
ANY = pl.BlockSpec(memory_space=pl.ANY)


def call(body, outs, scratch, cost, *args, specs=None, spare=40 << 20):
    flops, moved = cost
    return pl.pallas_call(
        body,
        out_shape=outs,
        in_specs=specs or [VMEM] * len(args),
        out_specs=jax.tree.map(lambda _: VMEM, outs),
        scratch_shapes=scratch,
        compiler_params=pltpu.CompilerParams(vmem_limit_bytes=(64 << 20) - spare),
        cost_estimate=pl.CostEstimate(flops=flops, bytes_accessed=moved, transcendentals=0),
    )(*args)


def pinned(array):
    return pltpu.with_memory_space_constraint(array, pltpu.HBM)


def dot_nt(left, right):
    return lax.dot_general(left, right, NT, preferred_element_type=F32)


def halves(columns):
    mid = columns.shape[0] // 2
    return jnp.concatenate([columns[:mid], columns[mid:]], axis=1)


def group_of(device, n):
    return (3 * device + 2 * (device % 2)) % n


def owner_of(group, n):
    return (group - 2 * (group % 2)) * pow(3, -1, n) % n


def pack(cols):
    return jnp.concatenate([cols[:, :128], halves(cols[:, 128:])], axis=0)


def unpack(packed):
    tokens = packed.shape[0] // 3 * 2
    last = packed[tokens:]
    return jnp.concatenate(
        [packed[:tokens], jnp.concatenate([last[:, :HEAD], last[:, HEAD:]], axis=0)], axis=1
    )


def pack_by_parity(cols, odd):
    mid = cols.shape[0] // 2
    even_form = pack(cols)
    odd_form = jnp.concatenate(
        [
            cols[:, HEAD:],
            jnp.concatenate([cols[mid:, :HEAD], cols[:mid, :HEAD]], axis=1),
        ],
        axis=0,
    )
    return jnp.where(odd, odd_form, even_form)


def assemble(blocks, whole, by_heads=False):
    tokens = whole.shape[0]
    n = blocks.shape[0]
    for d in range(0, n, 2):
        even, odd = [owner_of(group, n) if by_heads else group for group in (d, d + 1)]
        even_last, odd_last = blocks[even, tokens:].astype(F32), blocks[odd, tokens:].astype(F32)
        left = lax.broadcasted_iota(jnp.int32, even_last.shape, 1) < HEAD
        first = jnp.where(left, even_last, odd_last)
        second = pltpu.roll(jnp.where(left, odd_last, even_last), HEAD, 1)
        at = d // 2 * 384
        whole[:, at : at + 128] = blocks[even, :tokens].astype(whole.dtype)
        whole[:, at + 128 : at + 256] = jnp.concatenate([first, second], axis=0).astype(whole.dtype)
        whole[:, at + 256 : at + 384] = blocks[odd, :tokens].astype(whole.dtype)


def own_columns(ref, rows, me):
    pair = ref[rows, pl.ds(pl.multiple_of(me // 2 * 384, 128), 384)]
    return jnp.where((me & 1) == 1, pair[:, 192:], pair[:, :192])


def norm_into(stream, mod, normed):
    tokens, width = stream.shape
    step = 128
    total = jnp.zeros((tokens, step), F32)
    for at in range(0, width, step):
        total += stream[:, at : at + step]
    center = jnp.sum(total, axis=-1, keepdims=True) / width
    total = jnp.zeros((tokens, step), F32)
    for at in range(0, width, step):
        off = stream[:, at : at + step] - center
        total += off * off
    variance = jnp.sum(total, axis=-1, keepdims=True) / width
    spread = 1.0 / jnp.sqrt(variance + 1e-06)
    for at in range(0, width, step):
        part = (stream[:, at : at + step] - center) * spread
        part = part * (1.0 + mod[0, :, at : at + step]) + mod[1, :, at : at + step]
        normed[:, at : at + step] = part.astype(BF16)


def own_or_other(layer, own, other):
    return jnp.where(lax.axis_index("section") == layer, own, other)


def dot_into(layer, left, own, other, product):
    def into(weight):
        product[...] = dot_nt(left[...], weight[...]).astype(product.dtype)

    held = lax.axis_index("section") == layer
    pl.when(held)(lambda: into(own))
    pl.when(jnp.logical_not(held))(lambda: into(other))


def normalise(stream, mod, normed, residual):
    norm_into(stream, mod, normed)
    residual[...] = own_columns(stream, slice(None), lax.axis_index("blk")).astype(BF16)


def chunks_of(columns, chunks):
    odd = (lax.axis_index("blk") & 1) == 1
    first, middle, last = [pack(columns[:, at : at + 192].astype(F32)) for at in range(0, 576, 192)]
    for chunk, value in zip(chunks, (jnp.where(odd, last, first), middle, jnp.where(odd, first, last))):
        chunk[...] = value.astype(BF16)


def first_projection(arrived, own, other, mod, other_out, chunk0, chunk1, chunk2, residual, stream, normed, columns, held, sems):
    holds = lax.axis_index("section") == 0
    parts = sems.shape[0]
    size = held.shape[0] // parts
    copies = [
        pltpu.make_async_copy(own.at[pl.ds(i * size, size)], held.at[pl.ds(i * size, size)], sems.at[i])
        for i in range(parts)
    ]

    @pl.when(holds)
    def _():
        for copy in copies:
            copy.start()

    n = arrived.shape[0]
    rows = stream.shape[0] // n
    for b in range(n):
        stream[rows * b : rows * b + rows, :] = arrived[b, :rows, :].astype(F32)
    normalise(stream, mod, normed, residual)

    @pl.when(holds)
    def _():
        for copy in copies:
            copy.wait()

    dot_into(0, normed, held, other, columns)
    chunks_of(columns, (chunk0, chunk1, chunk2))


def next_projection(blocks, own, other, mod, chunk0, chunk1, chunk2, residual, stream, normed, columns):
    assemble(blocks, stream)
    normalise(stream, mod, normed, residual)
    dot_into(1, normed, own, other, columns)
    chunks_of(columns, (chunk0, chunk1, chunk2))


def attention(layer, chunk0, chunk1, chunk2, old, fresh, other_fresh, live, attn):
    n = attn.shape[0]
    me, request = lax.axis_index("blk"), lax.axis_index("section")
    inverse = pow(3, -1, n)
    odd = me & 1
    sign = 1 - 2 * odd
    sender1 = lax.rem(me - sign * inverse + 2 * n, n)
    sender2 = lax.rem(me - sign * 2 * inverse + 2 * n, n)
    kinds = ((3 * me + 2 * odd) // n, (3 * sender1 + 1) // n, (3 * sender2 + 2 - 2 * odd) // n)
    got = [chunk[...].astype(F32) for chunk in (chunk0, chunk1, chunk2)]

    def kind(which):
        return unpack(jnp.where(kinds[0] == which, got[0], jnp.where(kinds[1] == which, got[1], got[2])))

    queries = kind(0)
    tokens, width = queries.shape
    heads = width // HEAD
    rows = tokens // n
    token = lax.broadcasted_iota(jnp.int32, (tokens, 1), 0)
    is_fresh = jnp.zeros((tokens, 1), jnp.int32)
    for b in range(n):
        flag = own_or_other(layer, fresh[0, request, b], other_fresh[0, request, b])
        is_fresh = jnp.where(token >= b * rows, flag, is_fresh)
    is_fresh = is_fresh == 1
    key = lax.broadcasted_iota(jnp.int32, (1, tokens), 1)
    is_live = jnp.zeros((1, tokens), jnp.int32)
    for b in range(n):
        is_live = jnp.where(key >= b * rows, live[request, b], is_live)
    is_live = is_live == 1
    keys = jnp.where(is_fresh, kind(1), old[layer, :, :width].astype(F32)).astype(BF16)
    values = jnp.where(is_fresh, kind(2), old[layer, :, width:].astype(F32)).astype(BF16)
    head_of = lax.broadcasted_iota(jnp.int32, (tokens, width), 1) // HEAD
    stacked = jnp.concatenate([jnp.where(head_of == h, queries, 0.0) for h in range(heads)], axis=0)
    scores = dot_nt(stacked.astype(BF16), keys) * 0.125
    scores = jnp.where(is_live, scores, -1e30)
    top = jnp.max(scores, axis=-1, keepdims=True)
    weights = jnp.where(is_live, jnp.exp(scores - top), 0.0)
    total = jnp.sum(weights, axis=-1, keepdims=True)
    mixed = jnp.dot(weights.astype(BF16), values, preferred_element_type=F32) * (1.0 / total)
    result = jnp.zeros((tokens, width), F32)
    for h in range(heads):
        result = jnp.where(head_of == h, mixed[h * tokens : (h + 1) * tokens], result)
    packed = pack_by_parity(result, (me & 1) == 1).astype(BF16)
    for d in range(n):
        attn[d] = packed


def layer_columns(layer, blocks, own, other, mod, residual, whole, mixed):
    assemble(blocks, whole, by_heads=True)
    dot_into(layer, whole, own, other, mixed)
    gate = own_columns(mod.at[2], slice(None), lax.axis_index("blk"))
    return (residual[...].astype(F32) + gate * mixed[...].astype(F32)).astype(BF16).astype(F32)


def first_output(blocks, own, other, mod, residual, copies, kept, *scratch):
    columns = layer_columns(0, blocks, own, other, mod, residual, *scratch)
    packed = pack_by_parity(columns, (lax.axis_index("blk") & 1) == 1).astype(BF16)
    for d in range(copies.shape[0]):
        copies[d] = packed
    kept[...] = columns


def last_output(blocks, own, other, mod, residual, kept, by_token, columns, *scratch):
    columns[...] = layer_columns(1, blocks, own, other, mod, residual, *scratch)
    n = by_token.shape[0] // 2
    rows = columns.shape[0] // n
    for layer, outs in enumerate((kept, columns)):
        for b in range(n):
            by_token[layer * n + b, :rows, :] = outs[rows * b : rows * b + rows, :].astype(BF16)


def first_exchange(hidden, old_keys, old_values, other_keys, other_values, mod, other_mod, leaving, first_mod, held, sems):
    copies = [
        pltpu.make_async_copy(ref, held.at[i], sems.at[i])
        for i, ref in enumerate((hidden, old_keys, old_values, other_keys, other_values))
    ]
    for copy in copies:
        copy.start()
    rows, reqs, width = hidden.shape
    n = leaving.shape[0]
    columns = width // n
    first = lax.axis_index("section") == 0
    first_mod[...] = own_or_other(0, mod[...], other_mod[...])
    for copy in copies:
        copy.wait()

    def of_request(which):
        own = [held[which, i].astype(F32) for i in range(rows)]
        return jnp.concatenate([jnp.where(first, pair[:1], pair[1:]) for pair in own], axis=0)

    mine, *arrays = [of_request(which) for which in range(5)]
    mine = mine.astype(BF16)
    own, other = arrays[:2], arrays[2:]
    stale = [jnp.where(first, a, b) for a, b in zip(own, other)] + [jnp.where(first, b, a) for a, b in zip(own, other)]
    for b in range(n):
        at = columns * group_of(b, n) // 128 * 128
        block = jnp.concatenate([array[:, at : at + 256] for array in stale], axis=1)
        leaving[b, :rows, :] = mine
        for i in range(rows):
            leaving[b, rows : rows + 1, i * 1024 : (i + 1) * 1024] = block[i : i + 1].astype(BF16)


def stale_by_token(arrived, mod, other_mod, old, second_mod, rows):
    n = arrived.shape[0]
    per = rows.shape[1] // n
    wide = rows.shape[2]
    for b in range(n):
        flat = arrived[b, per : per + 1, :].astype(F32)
        for i in range(per):
            for layer in range(2):
                at = (i * 2 + layer) * wide
                rows[layer, per * b + i : per * b + i + 1, :] = flat[:, at : at + wide]
    odd = (lax.axis_index("blk") & 1) == 1
    for layer in range(2):
        pair = [rows[layer, :, at : at + 256] for at in (0, 256)]
        old[layer] = jnp.concatenate([jnp.where(odd, part[:, 64:], part[:, :192]) for part in pair], axis=1).astype(BF16)
    second_mod[...] = own_or_other(1, mod[...], other_mod[...])


def to_rows(arrived, out, rows):
    n = arrived.shape[0] // 2
    per, columns = out.shape[0], arrived.shape[2]
    for s in range(2):
        for b in range(n):
            rows[s, :per, columns * b : columns * b + columns] = arrived[s * n + b, :per, :].astype(F32)
    for i in range(per):
        out[i] = jnp.concatenate([rows[s, i : i + 1, :] for s in range(2)], axis=0).astype(BF16)


def exchange(blocks, axis):
    return lax.all_to_all(blocks, axis, split_axis=0, concat_axis=0, tiled=True)


def swap_sections(array):
    return lax.ppermute(array, "section", [(0, 1), (1, 0)])


def by_heads(chunks, n):
    inverse = pow(3, -1, n)
    kept, middle, other = chunks
    pairs1 = [(b, (b + (inverse if b % 2 else -inverse)) % n) for b in range(n)]
    pairs2 = [(b, (b + (-2 * inverse if b % 2 else 2 * inverse)) % n) for b in range(n)]
    return kept, lax.ppermute(middle, "blk", pairs1), lax.ppermute(other, "blk", pairs2)


def per_device(hidden, qkv_weight, out_weight, modulation, timestep, fresh, live, k_stale, v_stale):
    n = lax.axis_size("blk")
    columns = out_weight.shape[2]
    reqs, rows, width = hidden.shape
    if not (
        columns == 3 * HEAD
        and n % 3 == 1
        and n & (n - 1) == 0
        and reqs == lax.axis_size("section") == 2
        and rows <= 4
    ):
        return per_device_by_token(
            hidden, qkv_weight, out_weight, modulation, timestep, fresh, live, k_stale, v_stale
        )
    tokens = n * rows
    shape = jax.ShapeDtypeStruct
    packed = shape((tokens * 3 // 2, 128), BF16)
    copies = shape((n, tokens * 3 // 2, 128), BF16)
    cols = shape((tokens, columns), BF16)
    own_qkv = jnp.swapaxes(qkv_weight[0], 0, 1)
    own_out = jnp.swapaxes(out_weight[0], 0, 1)
    steps = jnp.transpose(modulation, (1, 2, 0, 3))
    old_keys = jnp.transpose(k_stale[0], (1, 0, 2))
    old_values = jnp.transpose(v_stale[0], (1, 0, 2))

    other_keys, other_values, timestep, sent_fresh = lax.optimization_barrier(
        (swap_sections(old_keys), swap_sections(old_values), timestep, fresh)
    )
    mod = lax.dynamic_index_in_dim(steps, timestep[0], 0, keepdims=False)
    other_mod, other_fresh, sent_qkv, sent_out = lax.optimization_barrier(
        (swap_sections(mod), swap_sections(sent_fresh), own_qkv, own_out)
    )
    mods = (mod, other_mod)
    flags = (fresh, other_fresh)
    other_qkv, other_out = swap_sections(sent_qkv), swap_sections(sent_out)
    out = (own_out, other_out)
    leaving, layer_mod = call(
        first_exchange,
        [shape((n, 4, width), BF16), shape(mod.shape, F32)],
        [pltpu.VMEM((5, rows, reqs, width), BF16), pltpu.SemaphoreType.DMA((5,))],
        (0, 1000000),
        *(pinned(array) for array in (jnp.transpose(hidden, (1, 0, 2)), old_keys, old_values)),
        other_keys,
        other_values,
        *mods,
        specs=[HBM] * 3 + [ANY] * 2 + [VMEM] * 2,
    )
    arrived = exchange(leaving, "blk")

    blocks = arrived
    for layer in range(2):
        *chunks, residual = call(
            next_projection if layer else first_projection,
            [packed, packed, packed, cols],
            [
                pltpu.VMEM((tokens, width), F32),
                pltpu.VMEM((tokens, width), BF16),
                pltpu.VMEM((tokens, 3 * columns), BF16),
            ]
            + ([] if layer else [pltpu.VMEM(own_qkv.shape, BF16), pltpu.SemaphoreType.DMA((12,))]),
            (2 * tokens * width * 3 * columns, 8 * width * columns),
            blocks,
            *((own_qkv, other_qkv, layer_mod) if layer else (pinned(own_qkv), other_qkv, layer_mod, other_out)),
            **({} if layer else {"specs": [VMEM, HBM, VMEM, VMEM, ANY]}),
        )
        if layer == 0:
            arrived, chunks[1] = lax.optimization_barrier((arrived, chunks[1]))
            old, next_mod = call(
                stale_by_token,
                [shape((2, tokens, 2 * columns), BF16), shape(mod.shape, F32)],
                [pltpu.VMEM((2, tokens, 512), F32)],
                (0, 200000),
                arrived,
                *mods,
            )
        attn = call(
            functools.partial(attention, layer),
            copies,
            [],
            (8 * tokens * tokens * columns, 300000),
            *by_heads(chunks, n),
            old,
            *flags,
            live,
            specs=[VMEM] * 4 + [SMEM] * 3,
        )
        args = (exchange(attn, "blk"), *out, layer_mod, residual)
        cost = (2 * tokens * width * columns, 4 * width * columns)
        held = [pltpu.VMEM((tokens, width), BF16), pltpu.VMEM((tokens, columns), BF16)]
        if layer == 0:
            leaving, kept = call(first_output, [copies, shape((tokens, columns), F32)], held, cost, *args)
            blocks, layer_mod = exchange(leaving, "blk"), next_mod
        else:
            leaving = call(
                last_output,
                shape((2 * n, 4, columns), BF16),
                [pltpu.VMEM((tokens, columns), F32)] + held,
                cost,
                *args,
                kept,
            )
    result = call(
        to_rows,
        shape((rows, reqs, width), BF16),
        [pltpu.VMEM((2, 8, width), F32)],
        (0, 100000),
        exchange(leaving, ("section", "blk")),
    )
    return jnp.transpose(result, (1, 0, 2))[None]


def solution(mesh):
    return jax.shard_map(
        per_device,
        mesh=mesh,
        in_specs=(
            P(None, "blk", None),
            P("section", None, "blk"),
            P("section", None, "blk"),
            P("section", None, None, None),
            P(),
            P("section", None, None),
            P(),
            P("section", None, "blk", None),
            P("section", None, "blk", None),
        ),
        out_specs=P("section", None, "blk", None),
        check_vma=False,
    )
```

```python
import functools

import jax
import jax.numpy as jnp
from jax import lax
from jax.experimental import pallas as pl
from jax.experimental.pallas import tpu as pltpu
from jax.sharding import PartitionSpec as P


def from_behind(shard, axis, by):
    count = lax.axis_size(axis)
    pairs = [(i, i + by) for i in range(count) if 0 <= i + by < count]
    return lax.ppermute(shard, axis, pairs)


def attend(layer_in, qkv_cols, out_cols, modulate, fresh_own, old_keys, old_values, live):
    stream = layer_in.astype(jnp.float32)
    center = jnp.mean(stream, axis=-1, keepdims=True)
    variance = jnp.mean((stream - center) ** 2, axis=-1, keepdims=True)
    normed = (stream - center) / jnp.sqrt(variance + 1e-06) * (1.0 + modulate[0]) + modulate[1]
    normed_b = normed.astype(jnp.bfloat16)
    columns = jnp.einsum(
        "rnd,dc->rnc",
        lax.all_gather(normed_b, "blk", axis=1, tiled=True),
        qkv_cols,
        preferred_element_type=jnp.float32,
    ).astype(jnp.bfloat16)
    projected = lax.all_to_all(columns, "blk", split_axis=1, concat_axis=2, tiled=True)
    num_req, num_rows, width = layer_in.shape
    queries = projected[:, :, :width]
    new_keys = projected[:, :, width : 2 * width]
    new_values = projected[:, :, 2 * width :]
    use_fresh = (fresh_own == 1)[:, None, None]
    keys = jnp.where(use_fresh, new_keys, old_keys)
    values = jnp.where(use_fresh, new_values, old_values)
    num_heads = width // 64
    num_blocks = live.shape[1]
    q_heads = queries.reshape(num_req, num_rows, num_heads, 64)
    live_float = live.astype(jnp.float32)
    run_max = jnp.full((num_req, num_heads, num_rows), -1e30, jnp.float32)
    key_piece = lax.all_gather(keys, "blk", axis=1, tiled=True)
    value_piece = lax.all_gather(values, "blk", axis=1, tiled=True)
    piece_rows = key_piece.shape[1]
    key_heads = key_piece.reshape(num_req, piece_rows, num_heads, 64)
    value_heads = value_piece.reshape(num_req, piece_rows, num_heads, 64)
    scores = (
        jnp.einsum("qrhd,qnhd->qhrn", q_heads, key_heads, preferred_element_type=jnp.float32)
        * 0.125
    )
    block_ids = jnp.arange(piece_rows) // num_rows
    one_hot = (block_ids[:, None] == jnp.arange(num_blocks)[None, :]).astype(jnp.float32)
    usable = jnp.einsum("qb,nb->qn", live_float, one_hot) > 0.5
    usable = usable[:, None, None, :]
    scores = jnp.where(usable, scores, -1e30)
    new_max = jnp.maximum(run_max, jnp.max(scores, axis=-1))
    weights = jnp.where(usable, jnp.exp(scores - new_max[..., None]), 0.0)
    new_sum = jnp.sum(weights, axis=-1)
    new_acc = jnp.einsum(
        "qhrn,qnhd->qhrd", weights, value_heads.astype(jnp.float32), precision=lax.Precision.HIGHEST
    )
    attn = new_acc / new_sum[..., None]
    attn = jnp.transpose(attn, (0, 2, 1, 3)).reshape(num_req, num_rows, width).astype(jnp.bfloat16)
    out_part = jnp.einsum(
        "rnd,dc->rnc",
        lax.all_gather(attn, "blk", axis=1, tiled=True),
        out_cols,
        preferred_element_type=jnp.float32,
    ).astype(jnp.bfloat16)
    mixed_back = lax.all_to_all(out_part, "blk", split_axis=1, concat_axis=2, tiled=True)
    return (stream + modulate[2] * mixed_back.astype(jnp.float32)).astype(jnp.bfloat16)


def pick_request(array, req_idx):
    return lax.dynamic_index_in_dim(array, req_idx, 0, keepdims=True)


def per_device_by_token(hidden, qkv_weight, out_weight, modulation, timestep, fresh, live, k_stale, v_stale):
    section_idx = lax.axis_index("section")
    block_idx = lax.axis_index("blk")
    steps_all = modulation.shape[1]
    pick_row = (jnp.arange(steps_all) == timestep[0]).astype(jnp.float32)
    modulate = jnp.einsum("t,tcd->cd", pick_row, modulation[0], precision=lax.Precision.HIGHEST)
    num_blocks = fresh.shape[2]
    own_column = (jnp.arange(num_blocks) == block_idx).astype(jnp.int32)
    fresh_own = jnp.sum(fresh[0] * own_column[None, :], axis=1)
    qkv_cols = qkv_weight[0]
    out_cols = out_weight[0]
    old_keys = k_stale[0]
    old_values = v_stale[0]
    num_req = hidden.shape[0]
    received = jnp.zeros_like(hidden[0:1])
    first_out = []
    second_out = []
    for tick_idx in range(num_req + 1):
        if tick_idx < num_req:
            own_input = hidden[tick_idx : tick_idx + 1]
        else:
            own_input = jnp.zeros_like(hidden[0:1])
        layer_in = jnp.where(section_idx == 0, own_input, received)
        req_idx = jnp.clip(tick_idx - section_idx, 0, num_req - 1)
        layer_out = attend(
            layer_in,
            qkv_cols,
            out_cols,
            modulate,
            pick_request(fresh_own, req_idx),
            pick_request(old_keys, req_idx),
            pick_request(old_values, req_idx),
            pick_request(live, req_idx),
        )
        if tick_idx < num_req:
            first_out.append(layer_out)
            received = from_behind(layer_out, "section", 1)
        if tick_idx >= 1:
            second_out.append(layer_out)
    result = jnp.where(
        section_idx == 0, jnp.concatenate(first_out, axis=0), jnp.concatenate(second_out, axis=0)
    )
    return result[None]


HEAD = 64
BF16 = jnp.bfloat16
F32 = jnp.float32
NT = (((1,), (1,)), ((), ()))
VMEM = pl.BlockSpec(memory_space=pltpu.VMEM)
SMEM = pl.BlockSpec(memory_space=pltpu.SMEM)
HBM = pl.BlockSpec(memory_space=pltpu.HBM)
ANY = pl.BlockSpec(memory_space=pl.ANY)


def call(body, outs, scratch, cost, *args, specs=None, spare=40 << 20):
    flops, moved = cost
    return pl.pallas_call(
        body,
        out_shape=outs,
        in_specs=specs or [VMEM] * len(args),
        out_specs=jax.tree.map(lambda _: VMEM, outs),
        scratch_shapes=scratch,
        compiler_params=pltpu.CompilerParams(vmem_limit_bytes=(64 << 20) - spare),
        cost_estimate=pl.CostEstimate(flops=flops, bytes_accessed=moved, transcendentals=0),
    )(*args)


def pinned(array):
    return pltpu.with_memory_space_constraint(array, pltpu.HBM)


def dot_nt(left, right):
    return lax.dot_general(left, right, NT, preferred_element_type=F32)


def halves(columns):
    mid = columns.shape[0] // 2
    return jnp.concatenate([columns[:mid], columns[mid:]], axis=1)


def group_of(device, n):
    return (3 * device + 2 * (device % 2)) % n


def owner_of(group, n):
    return (group - 2 * (group % 2)) * pow(3, -1, n) % n


def pack(cols):
    return jnp.concatenate([cols[:, :128], halves(cols[:, 128:])], axis=0)


def unpack(packed):
    tokens = packed.shape[0] // 3 * 2
    last = packed[tokens:]
    return jnp.concatenate(
        [packed[:tokens], jnp.concatenate([last[:, :HEAD], last[:, HEAD:]], axis=0)], axis=1
    )


def pack_by_parity(cols, odd):
    mid = cols.shape[0] // 2
    even_form = pack(cols)
    odd_form = jnp.concatenate(
        [
            cols[:, HEAD:],
            jnp.concatenate([cols[mid:, :HEAD], cols[:mid, :HEAD]], axis=1),
        ],
        axis=0,
    )
    return jnp.where(odd, odd_form, even_form)


def assemble(blocks, whole, by_heads=False):
    tokens = whole.shape[0]
    n = blocks.shape[0]
    for d in range(0, n, 2):
        even, odd = [owner_of(group, n) if by_heads else group for group in (d, d + 1)]
        even_last, odd_last = blocks[even, tokens:].astype(F32), blocks[odd, tokens:].astype(F32)
        left = lax.broadcasted_iota(jnp.int32, even_last.shape, 1) < HEAD
        first = jnp.where(left, even_last, odd_last)
        second = pltpu.roll(jnp.where(left, odd_last, even_last), HEAD, 1)
        at = d // 2 * 384
        whole[:, at : at + 128] = blocks[even, :tokens].astype(whole.dtype)
        whole[:, at + 128 : at + 256] = jnp.concatenate([first, second], axis=0).astype(whole.dtype)
        whole[:, at + 256 : at + 384] = blocks[odd, :tokens].astype(whole.dtype)


def own_columns(ref, rows, me):
    pair = ref[rows, pl.ds(pl.multiple_of(me // 2 * 384, 128), 384)]
    return jnp.where((me & 1) == 1, pair[:, 192:], pair[:, :192])


def norm_into(stream, mod, normed):
    tokens, width = stream.shape
    step = 128
    total = jnp.zeros((tokens, step), F32)
    for at in range(0, width, step):
        total += stream[:, at : at + step]
    center = jnp.sum(total, axis=-1, keepdims=True) / width
    total = jnp.zeros((tokens, step), F32)
    for at in range(0, width, step):
        off = stream[:, at : at + step] - center
        total += off * off
    variance = jnp.sum(total, axis=-1, keepdims=True) / width
    spread = 1.0 / jnp.sqrt(variance + 1e-06)
    for at in range(0, width, step):
        part = (stream[:, at : at + step] - center) * spread
        part = part * (1.0 + mod[0, :, at : at + step]) + mod[1, :, at : at + step]
        normed[:, at : at + step] = part.astype(BF16)


def own_or_other(layer, own, other):
    return jnp.where(lax.axis_index("section") == layer, own, other)


def dot_into(layer, left, own, other, product):
    def into(weight):
        product[...] = dot_nt(left[...], weight[...]).astype(product.dtype)

    held = lax.axis_index("section") == layer
    pl.when(held)(lambda: into(own))
    pl.when(jnp.logical_not(held))(lambda: into(other))


def normalise(stream, mod, normed, residual):
    norm_into(stream, mod, normed)
    residual[...] = own_columns(stream, slice(None), lax.axis_index("blk")).astype(BF16)


def chunks_of(columns, chunks):
    odd = (lax.axis_index("blk") & 1) == 1
    first, middle, last = [pack(columns[:, at : at + 192].astype(F32)) for at in range(0, 576, 192)]
    for chunk, value in zip(chunks, (jnp.where(odd, last, first), middle, jnp.where(odd, first, last))):
        chunk[...] = value.astype(BF16)


def first_projection(arrived, own, other, mod, other_out, chunk0, chunk1, chunk2, residual, stream, normed, columns, held, sems):
    holds = lax.axis_index("section") == 0
    parts = sems.shape[0]
    size = held.shape[0] // parts
    copies = [
        pltpu.make_async_copy(own.at[pl.ds(i * size, size)], held.at[pl.ds(i * size, size)], sems.at[i])
        for i in range(parts)
    ]

    @pl.when(holds)
    def _():
        for i, copy in enumerate(copies):
            copy.start(priority=i % 2)

    n = arrived.shape[0]
    rows = stream.shape[0] // n
    for b in range(n):
        stream[rows * b : rows * b + rows, :] = arrived[b, :rows, :].astype(F32)
    normalise(stream, mod, normed, residual)

    @pl.when(holds)
    def _():
        for copy in copies:
            copy.wait()

    dot_into(0, normed, held, other, columns)
    chunks_of(columns, (chunk0, chunk1, chunk2))


def next_projection(blocks, own, other, mod, chunk0, chunk1, chunk2, residual, stream, normed, columns):
    assemble(blocks, stream)
    normalise(stream, mod, normed, residual)
    dot_into(1, normed, own, other, columns)
    chunks_of(columns, (chunk0, chunk1, chunk2))


def attention(layer, chunk0, chunk1, chunk2, old, fresh, other_fresh, live, attn):
    n = attn.shape[0]
    me, request = lax.axis_index("blk"), lax.axis_index("section")
    inverse = pow(3, -1, n)
    odd = me & 1
    sign = 1 - 2 * odd
    sender1 = lax.rem(me - sign * inverse + 2 * n, n)
    sender2 = lax.rem(me - sign * 2 * inverse + 2 * n, n)
    kinds = ((3 * me + 2 * odd) // n, (3 * sender1 + 1) // n, (3 * sender2 + 2 - 2 * odd) // n)
    got = [chunk[...].astype(F32) for chunk in (chunk0, chunk1, chunk2)]

    def kind(which):
        return unpack(jnp.where(kinds[0] == which, got[0], jnp.where(kinds[1] == which, got[1], got[2])))

    queries = kind(0)
    tokens, width = queries.shape
    heads = width // HEAD
    rows = tokens // n
    token = lax.broadcasted_iota(jnp.int32, (tokens, 1), 0)
    is_fresh = jnp.zeros((tokens, 1), jnp.int32)
    for b in range(n):
        flag = own_or_other(layer, fresh[0, request, b], other_fresh[0, request, b])
        is_fresh = jnp.where(token >= b * rows, flag, is_fresh)
    is_fresh = is_fresh == 1
    key = lax.broadcasted_iota(jnp.int32, (1, tokens), 1)
    is_live = jnp.zeros((1, tokens), jnp.int32)
    for b in range(n):
        is_live = jnp.where(key >= b * rows, live[request, b], is_live)
    is_live = is_live == 1
    keys = jnp.where(is_fresh, kind(1), old[layer, :, :width].astype(F32)).astype(BF16)
    values = jnp.where(is_fresh, kind(2), old[layer, :, width:].astype(F32)).astype(BF16)
    head_of = lax.broadcasted_iota(jnp.int32, (tokens, width), 1) // HEAD
    stacked = jnp.concatenate([jnp.where(head_of == h, queries, 0.0) for h in range(heads)], axis=0)
    scores = dot_nt(stacked.astype(BF16), keys) * 0.125
    scores = jnp.where(is_live, scores, -1e30)
    top = jnp.max(scores, axis=-1, keepdims=True)
    weights = jnp.where(is_live, jnp.exp(scores - top), 0.0)
    total = jnp.sum(weights, axis=-1, keepdims=True)
    mixed = jnp.dot(weights.astype(BF16), values, preferred_element_type=F32) * (1.0 / total)
    result = jnp.zeros((tokens, width), F32)
    for h in range(heads):
        result = jnp.where(head_of == h, mixed[h * tokens : (h + 1) * tokens], result)
    packed = pack_by_parity(result, (me & 1) == 1).astype(BF16)
    for d in range(n):
        attn[d] = packed


def layer_columns(layer, blocks, own, other, mod, residual, whole, mixed):
    assemble(blocks, whole, by_heads=True)
    dot_into(layer, whole, own, other, mixed)
    gate = own_columns(mod.at[2], slice(None), lax.axis_index("blk"))
    return (residual[...].astype(F32) + gate * mixed[...].astype(F32)).astype(BF16).astype(F32)


def first_output(blocks, own, other, mod, residual, copies, kept, *scratch):
    columns = layer_columns(0, blocks, own, other, mod, residual, *scratch)
    packed = pack_by_parity(columns, (lax.axis_index("blk") & 1) == 1).astype(BF16)
    for d in range(copies.shape[0]):
        copies[d] = packed
    kept[...] = columns


def last_output(blocks, own, other, mod, residual, kept, by_token, columns, *scratch):
    columns[...] = layer_columns(1, blocks, own, other, mod, residual, *scratch)
    n = by_token.shape[0] // 2
    rows = columns.shape[0] // n
    for layer, outs in enumerate((kept, columns)):
        for b in range(n):
            by_token[layer * n + b, :rows, :] = outs[rows * b : rows * b + rows, :].astype(BF16)


def first_exchange(hidden, old_keys, old_values, other_keys, other_values, mod, other_mod, leaving, first_mod, held, sems):
    copies = [
        pltpu.make_async_copy(ref, held.at[i], sems.at[i])
        for i, ref in enumerate((hidden, old_keys, old_values, other_keys, other_values))
    ]
    for copy in copies:
        copy.start()
    rows, reqs, width = hidden.shape
    n = leaving.shape[0]
    columns = width // n
    first = lax.axis_index("section") == 0
    first_mod[...] = own_or_other(0, mod[...], other_mod[...])
    for copy in copies:
        copy.wait()

    def of_request(which):
        own = [held[which, i].astype(F32) for i in range(rows)]
        return jnp.concatenate([jnp.where(first, pair[:1], pair[1:]) for pair in own], axis=0)

    mine, *arrays = [of_request(which) for which in range(5)]
    mine = mine.astype(BF16)
    own, other = arrays[:2], arrays[2:]
    stale = [jnp.where(first, a, b) for a, b in zip(own, other)] + [jnp.where(first, b, a) for a, b in zip(own, other)]
    for b in range(n):
        at = columns * group_of(b, n)
        block = jnp.concatenate([array[:, at : at + columns] for array in stale], axis=1)
        leaving[b, :rows, :] = mine
        for i in range(rows):
            leaving[b, rows : rows + 1, i * 4 * columns : (i + 1) * 4 * columns] = block[i : i + 1].astype(BF16)


def stale_by_token(arrived, mod, other_mod, old, second_mod, rows):
    n = arrived.shape[0]
    per = rows.shape[1] // n
    wide = rows.shape[2]
    for b in range(n):
        flat = arrived[b, per : per + 1, :].astype(F32)
        for i in range(per):
            for layer in range(2):
                at = (i * 2 + layer) * wide
                rows[layer, per * b + i : per * b + i + 1, :] = flat[:, at : at + wide]
    old[...] = rows[...].astype(BF16)
    second_mod[...] = own_or_other(1, mod[...], other_mod[...])


def to_rows(arrived, out, rows):
    n = arrived.shape[0] // 2
    per, columns = out.shape[0], arrived.shape[2]
    for s in range(2):
        for b in range(n):
            rows[s, :per, columns * b : columns * b + columns] = arrived[s * n + b, :per, :].astype(F32)
    for i in range(per):
        out[i] = jnp.concatenate([rows[s, i : i + 1, :] for s in range(2)], axis=0).astype(BF16)


def exchange(blocks, axis):
    return lax.all_to_all(blocks, axis, split_axis=0, concat_axis=0, tiled=True)


def swap_sections(array):
    return lax.ppermute(array, "section", [(0, 1), (1, 0)])


def by_heads(chunks, n):
    inverse = pow(3, -1, n)
    kept, middle, other = chunks
    pairs1 = [(b, (b + (inverse if b % 2 else -inverse)) % n) for b in range(n)]
    pairs2 = [(b, (b + (-2 * inverse if b % 2 else 2 * inverse)) % n) for b in range(n)]
    return kept, lax.ppermute(middle, "blk", pairs1), lax.ppermute(other, "blk", pairs2)


def per_device(hidden, qkv_weight, out_weight, modulation, timestep, fresh, live, k_stale, v_stale):
    n = lax.axis_size("blk")
    columns = out_weight.shape[2]
    reqs, rows, width = hidden.shape
    if not (
        columns == 3 * HEAD
        and n % 3 == 1
        and n & (n - 1) == 0
        and reqs == lax.axis_size("section") == 2
        and rows <= 4
    ):
        return per_device_by_token(
            hidden, qkv_weight, out_weight, modulation, timestep, fresh, live, k_stale, v_stale
        )
    tokens = n * rows
    shape = jax.ShapeDtypeStruct
    packed = shape((tokens * 3 // 2, 128), BF16)
    copies = shape((n, tokens * 3 // 2, 128), BF16)
    cols = shape((tokens, columns), BF16)
    own_qkv = jnp.swapaxes(qkv_weight[0], 0, 1)
    own_out = jnp.swapaxes(out_weight[0], 0, 1)
    steps = jnp.transpose(modulation, (1, 2, 0, 3))
    old_keys = jnp.transpose(k_stale[0], (1, 0, 2))
    old_values = jnp.transpose(v_stale[0], (1, 0, 2))

    other_keys, other_values, timestep, sent_fresh = lax.optimization_barrier(
        (swap_sections(old_keys), swap_sections(old_values), timestep, fresh)
    )
    mod = lax.dynamic_index_in_dim(steps, timestep[0], 0, keepdims=False)
    other_mod, other_fresh, sent_qkv, sent_out = lax.optimization_barrier(
        (swap_sections(mod), swap_sections(sent_fresh), own_qkv, own_out)
    )
    mods = (mod, other_mod)
    flags = (fresh, other_fresh)
    other_qkv, other_out = swap_sections(sent_qkv), swap_sections(sent_out)
    out = (own_out, other_out)
    leaving, layer_mod = call(
        first_exchange,
        [shape((n, 4, width), BF16), shape(mod.shape, F32)],
        [pltpu.VMEM((5, rows, reqs, width), BF16), pltpu.SemaphoreType.DMA((5,))],
        (0, 1000000),
        *(pinned(array) for array in (jnp.transpose(hidden, (1, 0, 2)), old_keys, old_values)),
        other_keys,
        other_values,
        *mods,
        specs=[HBM] * 3 + [ANY] * 2 + [VMEM] * 2,
    )
    arrived = exchange(leaving, "blk")

    blocks = arrived
    for layer in range(2):
        *chunks, residual = call(
            next_projection if layer else first_projection,
            [packed, packed, packed, cols],
            [
                pltpu.VMEM((tokens, width), F32),
                pltpu.VMEM((tokens, width), BF16),
                pltpu.VMEM((tokens, 3 * columns), BF16),
            ]
            + ([] if layer else [pltpu.VMEM(own_qkv.shape, BF16), pltpu.SemaphoreType.DMA((12,))]),
            (2 * tokens * width * 3 * columns, 8 * width * columns),
            blocks,
            *((own_qkv, other_qkv, layer_mod) if layer else (pinned(own_qkv), other_qkv, layer_mod, other_out)),
            **({} if layer else {"specs": [VMEM, HBM, VMEM, VMEM, ANY]}),
        )
        if layer == 0:
            arrived, chunks[1] = lax.optimization_barrier((arrived, chunks[1]))
            old, next_mod = call(
                stale_by_token,
                [shape((2, tokens, 2 * columns), BF16), shape(mod.shape, F32)],
                [pltpu.VMEM((2, tokens, 2 * columns), F32)],
                (0, 200000),
                arrived,
                *mods,
            )
        attn = call(
            functools.partial(attention, layer),
            copies,
            [],
            (8 * tokens * tokens * columns, 300000),
            *by_heads(chunks, n),
            old,
            *flags,
            live,
            specs=[VMEM] * 4 + [SMEM] * 3,
        )
        args = (exchange(attn, "blk"), *out, layer_mod, residual)
        cost = (2 * tokens * width * columns, 4 * width * columns)
        held = [pltpu.VMEM((tokens, width), BF16), pltpu.VMEM((tokens, columns), BF16)]
        if layer == 0:
            leaving, kept = call(first_output, [copies, shape((tokens, columns), F32)], held, cost, *args)
            blocks, layer_mod = exchange(leaving, "blk"), next_mod
        else:
            leaving = call(
                last_output,
                shape((2 * n, 4, columns), BF16),
                [pltpu.VMEM((tokens, columns), F32)] + held,
                cost,
                *args,
                kept,
            )
    result = call(
        to_rows,
        shape((rows, reqs, width), BF16),
        [pltpu.VMEM((2, 8, width), F32)],
        (0, 100000),
        exchange(leaving, ("section", "blk")),
    )
    return jnp.transpose(result, (1, 0, 2))[None]


def solution(mesh):
    return jax.shard_map(
        per_device,
        mesh=mesh,
        in_specs=(
            P(None, "blk", None),
            P("section", None, "blk"),
            P("section", None, "blk"),
            P("section", None, None, None),
            P(),
            P("section", None, None),
            P(),
            P("section", None, "blk", None),
            P("section", None, "blk", None),
        ),
        out_specs=P("section", None, "blk", None),
        check_vma=False,
    )
```

```python
import functools

import jax
import jax.numpy as jnp
from jax import lax
from jax.experimental import pallas as pl
from jax.experimental.pallas import tpu as pltpu
from jax.sharding import PartitionSpec as P


def from_behind(shard, axis, by):
    count = lax.axis_size(axis)
    pairs = [(i, i + by) for i in range(count) if 0 <= i + by < count]
    return lax.ppermute(shard, axis, pairs)


def attend(layer_in, qkv_cols, out_cols, modulate, fresh_own, old_keys, old_values, live):
    stream = layer_in.astype(jnp.float32)
    center = jnp.mean(stream, axis=-1, keepdims=True)
    variance = jnp.mean((stream - center) ** 2, axis=-1, keepdims=True)
    normed = (stream - center) / jnp.sqrt(variance + 1e-06) * (1.0 + modulate[0]) + modulate[1]
    normed_b = normed.astype(jnp.bfloat16)
    columns = jnp.einsum(
        "rnd,dc->rnc",
        lax.all_gather(normed_b, "blk", axis=1, tiled=True),
        qkv_cols,
        preferred_element_type=jnp.float32,
    ).astype(jnp.bfloat16)
    projected = lax.all_to_all(columns, "blk", split_axis=1, concat_axis=2, tiled=True)
    num_req, num_rows, width = layer_in.shape
    queries = projected[:, :, :width]
    new_keys = projected[:, :, width : 2 * width]
    new_values = projected[:, :, 2 * width :]
    use_fresh = (fresh_own == 1)[:, None, None]
    keys = jnp.where(use_fresh, new_keys, old_keys)
    values = jnp.where(use_fresh, new_values, old_values)
    num_heads = width // 64
    num_blocks = live.shape[1]
    q_heads = queries.reshape(num_req, num_rows, num_heads, 64)
    live_float = live.astype(jnp.float32)
    run_max = jnp.full((num_req, num_heads, num_rows), -1e30, jnp.float32)
    key_piece = lax.all_gather(keys, "blk", axis=1, tiled=True)
    value_piece = lax.all_gather(values, "blk", axis=1, tiled=True)
    piece_rows = key_piece.shape[1]
    key_heads = key_piece.reshape(num_req, piece_rows, num_heads, 64)
    value_heads = value_piece.reshape(num_req, piece_rows, num_heads, 64)
    scores = (
        jnp.einsum("qrhd,qnhd->qhrn", q_heads, key_heads, preferred_element_type=jnp.float32)
        * 0.125
    )
    block_ids = jnp.arange(piece_rows) // num_rows
    one_hot = (block_ids[:, None] == jnp.arange(num_blocks)[None, :]).astype(jnp.float32)
    usable = jnp.einsum("qb,nb->qn", live_float, one_hot) > 0.5
    usable = usable[:, None, None, :]
    scores = jnp.where(usable, scores, -1e30)
    new_max = jnp.maximum(run_max, jnp.max(scores, axis=-1))
    weights = jnp.where(usable, jnp.exp(scores - new_max[..., None]), 0.0)
    new_sum = jnp.sum(weights, axis=-1)
    new_acc = jnp.einsum(
        "qhrn,qnhd->qhrd", weights, value_heads.astype(jnp.float32), precision=lax.Precision.HIGHEST
    )
    attn = new_acc / new_sum[..., None]
    attn = jnp.transpose(attn, (0, 2, 1, 3)).reshape(num_req, num_rows, width).astype(jnp.bfloat16)
    out_part = jnp.einsum(
        "rnd,dc->rnc",
        lax.all_gather(attn, "blk", axis=1, tiled=True),
        out_cols,
        preferred_element_type=jnp.float32,
    ).astype(jnp.bfloat16)
    mixed_back = lax.all_to_all(out_part, "blk", split_axis=1, concat_axis=2, tiled=True)
    return (stream + modulate[2] * mixed_back.astype(jnp.float32)).astype(jnp.bfloat16)


def pick_request(array, req_idx):
    return lax.dynamic_index_in_dim(array, req_idx, 0, keepdims=True)


def per_device_by_token(hidden, qkv_weight, out_weight, modulation, timestep, fresh, live, k_stale, v_stale):
    section_idx = lax.axis_index("section")
    block_idx = lax.axis_index("blk")
    steps_all = modulation.shape[1]
    pick_row = (jnp.arange(steps_all) == timestep[0]).astype(jnp.float32)
    modulate = jnp.einsum("t,tcd->cd", pick_row, modulation[0], precision=lax.Precision.HIGHEST)
    num_blocks = fresh.shape[2]
    own_column = (jnp.arange(num_blocks) == block_idx).astype(jnp.int32)
    fresh_own = jnp.sum(fresh[0] * own_column[None, :], axis=1)
    qkv_cols = qkv_weight[0]
    out_cols = out_weight[0]
    old_keys = k_stale[0]
    old_values = v_stale[0]
    num_req = hidden.shape[0]
    received = jnp.zeros_like(hidden[0:1])
    first_out = []
    second_out = []
    for tick_idx in range(num_req + 1):
        if tick_idx < num_req:
            own_input = hidden[tick_idx : tick_idx + 1]
        else:
            own_input = jnp.zeros_like(hidden[0:1])
        layer_in = jnp.where(section_idx == 0, own_input, received)
        req_idx = jnp.clip(tick_idx - section_idx, 0, num_req - 1)
        layer_out = attend(
            layer_in,
            qkv_cols,
            out_cols,
            modulate,
            pick_request(fresh_own, req_idx),
            pick_request(old_keys, req_idx),
            pick_request(old_values, req_idx),
            pick_request(live, req_idx),
        )
        if tick_idx < num_req:
            first_out.append(layer_out)
            received = from_behind(layer_out, "section", 1)
        if tick_idx >= 1:
            second_out.append(layer_out)
    result = jnp.where(
        section_idx == 0, jnp.concatenate(first_out, axis=0), jnp.concatenate(second_out, axis=0)
    )
    return result[None]


HEAD = 64
BF16 = jnp.bfloat16
F32 = jnp.float32
NT = (((1,), (1,)), ((), ()))
VMEM = pl.BlockSpec(memory_space=pltpu.VMEM)
SMEM = pl.BlockSpec(memory_space=pltpu.SMEM)
HBM = pl.BlockSpec(memory_space=pltpu.HBM)
ANY = pl.BlockSpec(memory_space=pl.ANY)


def call(body, outs, scratch, cost, *args, specs=None, spare=40 << 20):
    flops, moved = cost
    return pl.pallas_call(
        body,
        out_shape=outs,
        in_specs=specs or [VMEM] * len(args),
        out_specs=jax.tree.map(lambda _: VMEM, outs),
        scratch_shapes=scratch,
        compiler_params=pltpu.CompilerParams(vmem_limit_bytes=(64 << 20) - spare),
        cost_estimate=pl.CostEstimate(flops=flops, bytes_accessed=moved, transcendentals=0),
    )(*args)


def pinned(array):
    return pltpu.with_memory_space_constraint(array, pltpu.HBM)


def dot_nt(left, right):
    return lax.dot_general(left, right, NT, preferred_element_type=F32)


def halves(columns):
    mid = columns.shape[0] // 2
    return jnp.concatenate([columns[:mid], columns[mid:]], axis=1)


def group_of(device, n):
    return (3 * device + 2 * (device % 2)) % n


def owner_of(group, n):
    return (group - 2 * (group % 2)) * pow(3, -1, n) % n


def pack(cols):
    return jnp.concatenate([cols[:, :128], halves(cols[:, 128:])], axis=0)


def unpack(packed):
    tokens = packed.shape[0] // 3 * 2
    last = packed[tokens:]
    return jnp.concatenate(
        [packed[:tokens], jnp.concatenate([last[:, :HEAD], last[:, HEAD:]], axis=0)], axis=1
    )


def pack_by_parity(cols, odd):
    mid = cols.shape[0] // 2
    even_form = pack(cols)
    odd_form = jnp.concatenate(
        [
            cols[:, HEAD:],
            jnp.concatenate([cols[mid:, :HEAD], cols[:mid, :HEAD]], axis=1),
        ],
        axis=0,
    )
    return jnp.where(odd, odd_form, even_form)


def assemble(blocks, whole, by_heads=False):
    tokens = whole.shape[0]
    n = blocks.shape[0]
    for d in range(0, n, 2):
        even, odd = [owner_of(group, n) if by_heads else group for group in (d, d + 1)]
        even_last, odd_last = blocks[even, tokens:].astype(F32), blocks[odd, tokens:].astype(F32)
        left = lax.broadcasted_iota(jnp.int32, even_last.shape, 1) < HEAD
        first = jnp.where(left, even_last, odd_last)
        second = pltpu.roll(jnp.where(left, odd_last, even_last), HEAD, 1)
        at = d // 2 * 384
        whole[:, at : at + 128] = blocks[even, :tokens].astype(whole.dtype)
        whole[:, at + 128 : at + 256] = jnp.concatenate([first, second], axis=0).astype(whole.dtype)
        whole[:, at + 256 : at + 384] = blocks[odd, :tokens].astype(whole.dtype)


def own_columns(ref, rows, me):
    pair = ref[rows, pl.ds(pl.multiple_of(me // 2 * 384, 128), 384)]
    return jnp.where((me & 1) == 1, pair[:, 192:], pair[:, :192])


def norm_into(stream, mod, normed):
    tokens, width = stream.shape
    step = 128
    total = jnp.zeros((tokens, step), F32)
    for at in range(0, width, step):
        total += stream[:, at : at + step]
    center = jnp.sum(total, axis=-1, keepdims=True) / width
    total = jnp.zeros((tokens, step), F32)
    for at in range(0, width, step):
        off = stream[:, at : at + step] - center
        total += off * off
    variance = jnp.sum(total, axis=-1, keepdims=True) / width
    spread = 1.0 / jnp.sqrt(variance + 1e-06)
    for at in range(0, width, step):
        part = (stream[:, at : at + step] - center) * spread
        part = part * (1.0 + mod[0, :, at : at + step]) + mod[1, :, at : at + step]
        normed[:, at : at + step] = part.astype(BF16)


def own_or_other(layer, own, other):
    return jnp.where(lax.axis_index("section") == layer, own, other)


def dot_into(layer, left, own, other, product):
    def into(weight):
        product[...] = dot_nt(left[...], weight[...]).astype(product.dtype)

    held = lax.axis_index("section") == layer
    pl.when(held)(lambda: into(own))
    pl.when(jnp.logical_not(held))(lambda: into(other))


def normalise(stream, mod, normed, residual):
    norm_into(stream, mod, normed)
    residual[...] = own_columns(stream, slice(None), lax.axis_index("blk")).astype(BF16)


def chunks_of(columns, chunks):
    odd = (lax.axis_index("blk") & 1) == 1
    first, middle, last = [pack(columns[:, at : at + 192].astype(F32)) for at in range(0, 576, 192)]
    for chunk, value in zip(chunks, (jnp.where(odd, last, first), middle, jnp.where(odd, first, last))):
        chunk[...] = value.astype(BF16)


def first_projection(arrived, own, other, mod, other_out, chunk0, chunk1, chunk2, residual, stream, normed, columns, held, sems):
    holds = lax.axis_index("section") == 0
    parts = sems.shape[0]
    size = held.shape[0] // parts
    copies = [
        pltpu.make_async_copy(own.at[pl.ds(i * size, size)], held.at[pl.ds(i * size, size)], sems.at[i])
        for i in range(parts)
    ]

    @pl.when(holds)
    def _():
        for copy in copies:
            copy.start()

    n = arrived.shape[0]
    rows = stream.shape[0] // n
    for b in range(n):
        stream[rows * b : rows * b + rows, :] = arrived[b, :rows, :].astype(F32)
    normalise(stream, mod, normed, residual)

    @pl.when(holds)
    def _():
        for copy in copies:
            copy.wait()

    dot_into(0, normed, held, other, columns)
    chunks_of(columns, (chunk0, chunk1, chunk2))


def next_projection(blocks, own, other, mod, chunk0, chunk1, chunk2, residual, stream, normed, columns):
    assemble(blocks, stream)
    normalise(stream, mod, normed, residual)
    dot_into(1, normed, own, other, columns)
    chunks_of(columns, (chunk0, chunk1, chunk2))


def attention(layer, chunk0, chunk1, chunk2, old, fresh, other_fresh, live, attn):
    n = attn.shape[0]
    me, request = lax.axis_index("blk"), lax.axis_index("section")
    inverse = pow(3, -1, n)
    odd = me & 1
    sign = 1 - 2 * odd
    sender1 = lax.rem(me - sign * inverse + 2 * n, n)
    sender2 = lax.rem(me - sign * 2 * inverse + 2 * n, n)
    kinds = ((3 * me + 2 * odd) // n, (3 * sender1 + 1) // n, (3 * sender2 + 2 - 2 * odd) // n)
    got = [chunk[...].astype(F32) for chunk in (chunk0, chunk1, chunk2)]

    def kind(which):
        return unpack(jnp.where(kinds[0] == which, got[0], jnp.where(kinds[1] == which, got[1], got[2])))

    queries = kind(0)
    tokens, width = queries.shape
    heads = width // HEAD
    rows = tokens // n
    token = lax.broadcasted_iota(jnp.int32, (tokens, 1), 0)
    is_fresh = jnp.zeros((tokens, 1), jnp.int32)
    for b in range(n):
        flag = own_or_other(layer, fresh[0, request, b], other_fresh[0, request, b])
        is_fresh = jnp.where(token >= b * rows, flag, is_fresh)
    is_fresh = is_fresh == 1
    key = lax.broadcasted_iota(jnp.int32, (1, tokens), 1)
    is_live = jnp.zeros((1, tokens), jnp.int32)
    for b in range(n):
        is_live = jnp.where(key >= b * rows, live[request, b], is_live)
    is_live = is_live == 1
    keys = jnp.where(is_fresh, kind(1), old[layer, :, :width].astype(F32)).astype(BF16)
    values = jnp.where(is_fresh, kind(2), old[layer, :, width:].astype(F32)).astype(BF16)
    head_of = lax.broadcasted_iota(jnp.int32, (tokens, width), 1) // HEAD
    stacked = jnp.concatenate([jnp.where(head_of == h, queries, 0.0) for h in range(heads)], axis=0)
    scores = dot_nt(stacked.astype(BF16), keys) * 0.125
    scores = jnp.where(is_live, scores, -1e30)
    top = jnp.max(scores, axis=-1, keepdims=True)
    weights = jnp.where(is_live, jnp.exp(scores - top), 0.0)
    total = jnp.sum(weights, axis=-1, keepdims=True)
    mixed = jnp.dot(weights.astype(BF16), values, preferred_element_type=F32) * (1.0 / total)
    result = jnp.zeros((tokens, width), F32)
    for h in range(heads):
        result = jnp.where(head_of == h, mixed[h * tokens : (h + 1) * tokens], result)
    packed = pack_by_parity(result, (me & 1) == 1).astype(BF16)
    for d in range(n):
        attn[d] = packed


def layer_columns(layer, blocks, own, other, mod, residual, whole, mixed):
    assemble(blocks, whole, by_heads=True)
    dot_into(layer, whole, own, other, mixed)
    gate = own_columns(mod.at[2], slice(None), lax.axis_index("blk"))
    return (residual[...].astype(F32) + gate * mixed[...].astype(F32)).astype(BF16).astype(F32)


def first_output(blocks, own, other, mod, residual, copies, kept, *scratch):
    columns = layer_columns(0, blocks, own, other, mod, residual, *scratch)
    packed = pack_by_parity(columns, (lax.axis_index("blk") & 1) == 1).astype(BF16)
    for d in range(copies.shape[0]):
        copies[d] = packed
    kept[...] = columns


def last_output(blocks, own, other, mod, residual, kept, by_token, columns, *scratch):
    columns[...] = layer_columns(1, blocks, own, other, mod, residual, *scratch)
    n = by_token.shape[0] // 2
    rows = columns.shape[0] // n
    for layer, outs in enumerate((kept, columns)):
        for b in range(n):
            by_token[layer * n + b, :rows, :] = outs[rows * b : rows * b + rows, :].astype(BF16)


def stage_rows(hidden, old_keys, old_values, staged, sems):
    copies = [
        pltpu.make_async_copy(ref, staged.at[i], sems.at[i]) for i, ref in enumerate((hidden, old_keys, old_values))
    ]
    for copy in copies:
        copy.start()
    for copy in copies:
        copy.wait()


def first_exchange(staged, other_keys, other_values, mod, other_mod, leaving, first_mod):
    _, rows, reqs, width = staged.shape
    n = leaving.shape[0]
    columns = width // n
    first = lax.axis_index("section") == 0
    first_mod[...] = own_or_other(0, mod[...], other_mod[...])
    held = [staged.at[0], staged.at[1], staged.at[2], other_keys, other_values]

    def of_request(which):
        own = [held[which][i].astype(F32) for i in range(rows)]
        return jnp.concatenate([jnp.where(first, pair[:1], pair[1:]) for pair in own], axis=0)

    mine, *arrays = [of_request(which) for which in range(5)]
    mine = mine.astype(BF16)
    own, other = arrays[:2], arrays[2:]
    stale = [jnp.where(first, a, b) for a, b in zip(own, other)] + [jnp.where(first, b, a) for a, b in zip(own, other)]
    for b in range(n):
        at = columns * group_of(b, n)
        block = jnp.concatenate([array[:, at : at + columns] for array in stale], axis=1)
        leaving[b, :rows, :] = mine
        for i in range(rows):
            leaving[b, rows : rows + 1, i * 4 * columns : (i + 1) * 4 * columns] = block[i : i + 1].astype(BF16)


def stale_by_token(arrived, mod, other_mod, old, second_mod, rows):
    n = arrived.shape[0]
    per = rows.shape[1] // n
    wide = rows.shape[2]
    for b in range(n):
        flat = arrived[b, per : per + 1, :].astype(F32)
        for i in range(per):
            for layer in range(2):
                at = (i * 2 + layer) * wide
                rows[layer, per * b + i : per * b + i + 1, :] = flat[:, at : at + wide]
    old[...] = rows[...].astype(BF16)
    second_mod[...] = own_or_other(1, mod[...], other_mod[...])


def to_rows(arrived, out, rows):
    n = arrived.shape[0] // 2
    per, columns = out.shape[0], arrived.shape[2]
    for s in range(2):
        for b in range(n):
            rows[s, :per, columns * b : columns * b + columns] = arrived[s * n + b, :per, :].astype(F32)
    for i in range(per):
        out[i] = jnp.concatenate([rows[s, i : i + 1, :] for s in range(2)], axis=0).astype(BF16)


def exchange(blocks, axis):
    return lax.all_to_all(blocks, axis, split_axis=0, concat_axis=0, tiled=True)


def swap_sections(array):
    return lax.ppermute(array, "section", [(0, 1), (1, 0)])


def by_heads(chunks, n):
    inverse = pow(3, -1, n)
    kept, middle, other = chunks
    pairs1 = [(b, (b + (inverse if b % 2 else -inverse)) % n) for b in range(n)]
    pairs2 = [(b, (b + (-2 * inverse if b % 2 else 2 * inverse)) % n) for b in range(n)]
    return kept, lax.ppermute(middle, "blk", pairs1), lax.ppermute(other, "blk", pairs2)


def per_device(hidden, qkv_weight, out_weight, modulation, timestep, fresh, live, k_stale, v_stale):
    n = lax.axis_size("blk")
    columns = out_weight.shape[2]
    reqs, rows, width = hidden.shape
    if not (
        columns == 3 * HEAD
        and n % 3 == 1
        and n & (n - 1) == 0
        and reqs == lax.axis_size("section") == 2
        and rows <= 4
    ):
        return per_device_by_token(
            hidden, qkv_weight, out_weight, modulation, timestep, fresh, live, k_stale, v_stale
        )
    tokens = n * rows
    shape = jax.ShapeDtypeStruct
    packed = shape((tokens * 3 // 2, 128), BF16)
    copies = shape((n, tokens * 3 // 2, 128), BF16)
    cols = shape((tokens, columns), BF16)
    own_qkv = jnp.swapaxes(qkv_weight[0], 0, 1)
    own_out = jnp.swapaxes(out_weight[0], 0, 1)
    steps = jnp.transpose(modulation, (1, 2, 0, 3))
    old_keys = jnp.transpose(k_stale[0], (1, 0, 2))
    old_values = jnp.transpose(v_stale[0], (1, 0, 2))

    other_keys, other_values, timestep, sent_fresh = lax.optimization_barrier(
        (swap_sections(old_keys), swap_sections(old_values), timestep, fresh)
    )
    mod = lax.dynamic_index_in_dim(steps, timestep[0], 0, keepdims=False)
    staged = call(
        stage_rows,
        shape((3, rows, reqs, width), BF16),
        [pltpu.SemaphoreType.DMA((3,))],
        (0, 200000),
        *(pinned(array) for array in (jnp.transpose(hidden, (1, 0, 2)), old_keys, old_values)),
        specs=[HBM] * 3,
    )
    other_mod, other_fresh, sent_qkv, sent_out, staged = lax.optimization_barrier(
        (swap_sections(mod), swap_sections(sent_fresh), own_qkv, own_out, staged)
    )
    mods = (mod, other_mod)
    flags = (fresh, other_fresh)
    other_qkv, other_out = swap_sections(sent_qkv), swap_sections(sent_out)
    out = (own_out, other_out)
    leaving, layer_mod = call(
        first_exchange,
        [shape((n, 4, width), BF16), shape(mod.shape, F32)],
        [],
        (0, 1000000),
        staged,
        other_keys,
        other_values,
        *mods,
    )
    arrived = exchange(leaving, "blk")

    blocks = arrived
    for layer in range(2):
        *chunks, residual = call(
            next_projection if layer else first_projection,
            [packed, packed, packed, cols],
            [
                pltpu.VMEM((tokens, width), F32),
                pltpu.VMEM((tokens, width), BF16),
                pltpu.VMEM((tokens, 3 * columns), BF16),
            ]
            + ([] if layer else [pltpu.VMEM(own_qkv.shape, BF16), pltpu.SemaphoreType.DMA((12,))]),
            (2 * tokens * width * 3 * columns, 8 * width * columns),
            blocks,
            *((own_qkv, other_qkv, layer_mod) if layer else (pinned(own_qkv), other_qkv, layer_mod, other_out)),
            **({} if layer else {"specs": [VMEM, HBM, VMEM, VMEM, ANY]}),
        )
        if layer == 0:
            arrived, chunks[1] = lax.optimization_barrier((arrived, chunks[1]))
            old, next_mod = call(
                stale_by_token,
                [shape((2, tokens, 2 * columns), BF16), shape(mod.shape, F32)],
                [pltpu.VMEM((2, tokens, 2 * columns), F32)],
                (0, 200000),
                arrived,
                *mods,
            )
        attn = call(
            functools.partial(attention, layer),
            copies,
            [],
            (8 * tokens * tokens * columns, 300000),
            *by_heads(chunks, n),
            old,
            *flags,
            live,
            specs=[VMEM] * 4 + [SMEM] * 3,
        )
        args = (exchange(attn, "blk"), *out, layer_mod, residual)
        cost = (2 * tokens * width * columns, 4 * width * columns)
        held = [pltpu.VMEM((tokens, width), BF16), pltpu.VMEM((tokens, columns), BF16)]
        if layer == 0:
            leaving, kept = call(first_output, [copies, shape((tokens, columns), F32)], held, cost, *args)
            blocks, layer_mod = exchange(leaving, "blk"), next_mod
        else:
            leaving = call(
                last_output,
                shape((2 * n, 4, columns), BF16),
                [pltpu.VMEM((tokens, columns), F32)] + held,
                cost,
                *args,
                kept,
            )
    result = call(
        to_rows,
        shape((rows, reqs, width), BF16),
        [pltpu.VMEM((2, 8, width), F32)],
        (0, 100000),
        exchange(leaving, ("section", "blk")),
    )
    return jnp.transpose(result, (1, 0, 2))[None]


def solution(mesh):
    return jax.shard_map(
        per_device,
        mesh=mesh,
        in_specs=(
            P(None, "blk", None),
            P("section", None, "blk"),
            P("section", None, "blk"),
            P("section", None, None, None),
            P(),
            P("section", None, None),
            P(),
            P("section", None, "blk", None),
            P("section", None, "blk", None),
        ),
        out_specs=P("section", None, "blk", None),
        check_vma=False,
    )
```

```python
import functools

import jax
import jax.numpy as jnp
from jax import lax
from jax.experimental import pallas as pl
from jax.experimental.pallas import tpu as pltpu
from jax.sharding import PartitionSpec as P


def from_behind(shard, axis, by):
    count = lax.axis_size(axis)
    pairs = [(i, i + by) for i in range(count) if 0 <= i + by < count]
    return lax.ppermute(shard, axis, pairs)


def attend(layer_in, qkv_cols, out_cols, modulate, fresh_own, old_keys, old_values, live):
    stream = layer_in.astype(jnp.float32)
    center = jnp.mean(stream, axis=-1, keepdims=True)
    variance = jnp.mean((stream - center) ** 2, axis=-1, keepdims=True)
    normed = (stream - center) / jnp.sqrt(variance + 1e-06) * (1.0 + modulate[0]) + modulate[1]
    normed_b = normed.astype(jnp.bfloat16)
    columns = jnp.einsum(
        "rnd,dc->rnc",
        lax.all_gather(normed_b, "blk", axis=1, tiled=True),
        qkv_cols,
        preferred_element_type=jnp.float32,
    ).astype(jnp.bfloat16)
    projected = lax.all_to_all(columns, "blk", split_axis=1, concat_axis=2, tiled=True)
    num_req, num_rows, width = layer_in.shape
    queries = projected[:, :, :width]
    new_keys = projected[:, :, width : 2 * width]
    new_values = projected[:, :, 2 * width :]
    use_fresh = (fresh_own == 1)[:, None, None]
    keys = jnp.where(use_fresh, new_keys, old_keys)
    values = jnp.where(use_fresh, new_values, old_values)
    num_heads = width // 64
    num_blocks = live.shape[1]
    q_heads = queries.reshape(num_req, num_rows, num_heads, 64)
    live_float = live.astype(jnp.float32)
    run_max = jnp.full((num_req, num_heads, num_rows), -1e30, jnp.float32)
    key_piece = lax.all_gather(keys, "blk", axis=1, tiled=True)
    value_piece = lax.all_gather(values, "blk", axis=1, tiled=True)
    piece_rows = key_piece.shape[1]
    key_heads = key_piece.reshape(num_req, piece_rows, num_heads, 64)
    value_heads = value_piece.reshape(num_req, piece_rows, num_heads, 64)
    scores = (
        jnp.einsum("qrhd,qnhd->qhrn", q_heads, key_heads, preferred_element_type=jnp.float32)
        * 0.125
    )
    block_ids = jnp.arange(piece_rows) // num_rows
    one_hot = (block_ids[:, None] == jnp.arange(num_blocks)[None, :]).astype(jnp.float32)
    usable = jnp.einsum("qb,nb->qn", live_float, one_hot) > 0.5
    usable = usable[:, None, None, :]
    scores = jnp.where(usable, scores, -1e30)
    new_max = jnp.maximum(run_max, jnp.max(scores, axis=-1))
    weights = jnp.where(usable, jnp.exp(scores - new_max[..., None]), 0.0)
    new_sum = jnp.sum(weights, axis=-1)
    new_acc = jnp.einsum(
        "qhrn,qnhd->qhrd", weights, value_heads.astype(jnp.float32), precision=lax.Precision.HIGHEST
    )
    attn = new_acc / new_sum[..., None]
    attn = jnp.transpose(attn, (0, 2, 1, 3)).reshape(num_req, num_rows, width).astype(jnp.bfloat16)
    out_part = jnp.einsum(
        "rnd,dc->rnc",
        lax.all_gather(attn, "blk", axis=1, tiled=True),
        out_cols,
        preferred_element_type=jnp.float32,
    ).astype(jnp.bfloat16)
    mixed_back = lax.all_to_all(out_part, "blk", split_axis=1, concat_axis=2, tiled=True)
    return (stream + modulate[2] * mixed_back.astype(jnp.float32)).astype(jnp.bfloat16)


def pick_request(array, req_idx):
    return lax.dynamic_index_in_dim(array, req_idx, 0, keepdims=True)


def per_device_by_token(hidden, qkv_weight, out_weight, modulation, timestep, fresh, live, k_stale, v_stale):
    section_idx = lax.axis_index("section")
    block_idx = lax.axis_index("blk")
    steps_all = modulation.shape[1]
    pick_row = (jnp.arange(steps_all) == timestep[0]).astype(jnp.float32)
    modulate = jnp.einsum("t,tcd->cd", pick_row, modulation[0], precision=lax.Precision.HIGHEST)
    num_blocks = fresh.shape[2]
    own_column = (jnp.arange(num_blocks) == block_idx).astype(jnp.int32)
    fresh_own = jnp.sum(fresh[0] * own_column[None, :], axis=1)
    qkv_cols = qkv_weight[0]
    out_cols = out_weight[0]
    old_keys = k_stale[0]
    old_values = v_stale[0]
    num_req = hidden.shape[0]
    received = jnp.zeros_like(hidden[0:1])
    first_out = []
    second_out = []
    for tick_idx in range(num_req + 1):
        if tick_idx < num_req:
            own_input = hidden[tick_idx : tick_idx + 1]
        else:
            own_input = jnp.zeros_like(hidden[0:1])
        layer_in = jnp.where(section_idx == 0, own_input, received)
        req_idx = jnp.clip(tick_idx - section_idx, 0, num_req - 1)
        layer_out = attend(
            layer_in,
            qkv_cols,
            out_cols,
            modulate,
            pick_request(fresh_own, req_idx),
            pick_request(old_keys, req_idx),
            pick_request(old_values, req_idx),
            pick_request(live, req_idx),
        )
        if tick_idx < num_req:
            first_out.append(layer_out)
            received = from_behind(layer_out, "section", 1)
        if tick_idx >= 1:
            second_out.append(layer_out)
    result = jnp.where(
        section_idx == 0, jnp.concatenate(first_out, axis=0), jnp.concatenate(second_out, axis=0)
    )
    return result[None]


HEAD = 64
BF16 = jnp.bfloat16
F32 = jnp.float32
NT = (((1,), (1,)), ((), ()))
VMEM = pl.BlockSpec(memory_space=pltpu.VMEM)
SMEM = pl.BlockSpec(memory_space=pltpu.SMEM)
HBM = pl.BlockSpec(memory_space=pltpu.HBM)
ANY = pl.BlockSpec(memory_space=pl.ANY)


def call(body, outs, scratch, cost, *args, specs=None, spare=40 << 20):
    flops, moved = cost
    return pl.pallas_call(
        body,
        out_shape=outs,
        in_specs=specs or [VMEM] * len(args),
        out_specs=jax.tree.map(lambda _: VMEM, outs),
        scratch_shapes=scratch,
        compiler_params=pltpu.CompilerParams(vmem_limit_bytes=(64 << 20) - spare),
        cost_estimate=pl.CostEstimate(flops=flops, bytes_accessed=moved, transcendentals=0),
    )(*args)


def pinned(array):
    return pltpu.with_memory_space_constraint(array, pltpu.HBM)


def dot_nt(left, right):
    return lax.dot_general(left, right, NT, preferred_element_type=F32)


def halves(columns):
    mid = columns.shape[0] // 2
    return jnp.concatenate([columns[:mid], columns[mid:]], axis=1)


def group_of(device, n):
    return (3 * device + 2 * (device % 2)) % n


def owner_of(group, n):
    return (group - 2 * (group % 2)) * pow(3, -1, n) % n


def pack(cols):
    return jnp.concatenate([cols[:, :128], halves(cols[:, 128:])], axis=0)


def unpack(packed):
    tokens = packed.shape[0] // 3 * 2
    last = packed[tokens:]
    return jnp.concatenate(
        [packed[:tokens], jnp.concatenate([last[:, :HEAD], last[:, HEAD:]], axis=0)], axis=1
    )


def pack_by_parity(cols, odd):
    mid = cols.shape[0] // 2
    even_form = pack(cols)
    odd_form = jnp.concatenate(
        [
            cols[:, HEAD:],
            jnp.concatenate([cols[mid:, :HEAD], cols[:mid, :HEAD]], axis=1),
        ],
        axis=0,
    )
    return jnp.where(odd, odd_form, even_form)


def assemble(blocks, whole, by_heads=False):
    tokens = whole.shape[0]
    n = blocks.shape[0]
    for d in range(0, n, 2):
        even, odd = [owner_of(group, n) if by_heads else group for group in (d, d + 1)]
        even_last, odd_last = blocks[even, tokens:].astype(F32), blocks[odd, tokens:].astype(F32)
        left = lax.broadcasted_iota(jnp.int32, even_last.shape, 1) < HEAD
        first = jnp.where(left, even_last, odd_last)
        second = pltpu.roll(jnp.where(left, odd_last, even_last), HEAD, 1)
        at = d // 2 * 384
        whole[:, at : at + 128] = blocks[even, :tokens].astype(whole.dtype)
        whole[:, at + 128 : at + 256] = jnp.concatenate([first, second], axis=0).astype(whole.dtype)
        whole[:, at + 256 : at + 384] = blocks[odd, :tokens].astype(whole.dtype)


def own_columns(ref, rows, me):
    pair = ref[rows, pl.ds(pl.multiple_of(me // 2 * 384, 128), 384)]
    return jnp.where((me & 1) == 1, pair[:, 192:], pair[:, :192])


def norm_into(stream, mod, normed):
    tokens, width = stream.shape
    step = 128
    total = jnp.zeros((tokens, step), F32)
    for at in range(0, width, step):
        total += stream[:, at : at + step]
    center = jnp.sum(total, axis=-1, keepdims=True) / width
    total = jnp.zeros((tokens, step), F32)
    for at in range(0, width, step):
        off = stream[:, at : at + step] - center
        total += off * off
    variance = jnp.sum(total, axis=-1, keepdims=True) / width
    spread = 1.0 / jnp.sqrt(variance + 1e-06)
    for at in range(0, width, step):
        part = (stream[:, at : at + step] - center) * spread
        part = part * (1.0 + mod[0, :, at : at + step]) + mod[1, :, at : at + step]
        normed[:, at : at + step] = part.astype(BF16)


def own_or_other(layer, own, other):
    return jnp.where(lax.axis_index("section") == layer, own, other)


def dot_into(layer, left, own, other, product):
    def into(weight):
        product[...] = dot_nt(left[...], weight[...]).astype(product.dtype)

    held = lax.axis_index("section") == layer
    pl.when(held)(lambda: into(own))
    pl.when(jnp.logical_not(held))(lambda: into(other))


def normalise(stream, mod, normed, residual):
    norm_into(stream, mod, normed)
    residual[...] = own_columns(stream, slice(None), lax.axis_index("blk")).astype(BF16)


def chunks_of(columns, chunks):
    odd = (lax.axis_index("blk") & 1) == 1
    first, middle, last = [pack(columns[:, at : at + 192].astype(F32)) for at in range(0, 576, 192)]
    for chunk, value in zip(chunks, (jnp.where(odd, last, first), middle, jnp.where(odd, first, last))):
        chunk[...] = value.astype(BF16)


def first_projection(arrived, own, other, mod, other_out, chunk0, chunk1, chunk2, residual, stream, normed, columns, held, sems):
    holds = lax.axis_index("section") == 0
    parts = sems.shape[0]
    size = held.shape[0] // parts
    copies = [
        pltpu.make_async_copy(own.at[pl.ds(i * size, size)], held.at[pl.ds(i * size, size)], sems.at[i])
        for i in range(parts)
    ]

    @pl.when(holds)
    def _():
        for i, copy in enumerate(copies):
            copy.start(priority=i % 2)

    n = arrived.shape[0]
    rows = stream.shape[0] // n
    for b in range(n):
        stream[rows * b : rows * b + rows, :] = arrived[b, :rows, :].astype(F32)
    normalise(stream, mod, normed, residual)

    @pl.when(holds)
    def _():
        for copy in copies:
            copy.wait()

    dot_into(0, normed, held, other, columns)
    chunks_of(columns, (chunk0, chunk1, chunk2))


def next_projection(blocks, own, other, mod, chunk0, chunk1, chunk2, residual, stream, normed, columns):
    assemble(blocks, stream)
    normalise(stream, mod, normed, residual)
    dot_into(1, normed, own, other, columns)
    chunks_of(columns, (chunk0, chunk1, chunk2))


def attention(layer, chunk0, chunk1, chunk2, old, fresh, other_fresh, live, attn):
    n = attn.shape[0]
    me, request = lax.axis_index("blk"), lax.axis_index("section")
    inverse = pow(3, -1, n)
    odd = me & 1
    sign = 1 - 2 * odd
    sender1 = lax.rem(me - sign * inverse + 2 * n, n)
    sender2 = lax.rem(me - sign * 2 * inverse + 2 * n, n)
    kinds = ((3 * me + 2 * odd) // n, (3 * sender1 + 1) // n, (3 * sender2 + 2 - 2 * odd) // n)
    got = [chunk[...].astype(F32) for chunk in (chunk0, chunk1, chunk2)]

    def kind(which):
        return unpack(jnp.where(kinds[0] == which, got[0], jnp.where(kinds[1] == which, got[1], got[2])))

    queries = kind(0)
    tokens, width = queries.shape
    heads = width // HEAD
    rows = tokens // n
    token = lax.broadcasted_iota(jnp.int32, (tokens, 1), 0)
    is_fresh = jnp.zeros((tokens, 1), jnp.int32)
    for b in range(n):
        flag = own_or_other(layer, fresh[0, request, b], other_fresh[0, request, b])
        is_fresh = jnp.where(token >= b * rows, flag, is_fresh)
    is_fresh = is_fresh == 1
    key = lax.broadcasted_iota(jnp.int32, (1, tokens), 1)
    is_live = jnp.zeros((1, tokens), jnp.int32)
    for b in range(n):
        is_live = jnp.where(key >= b * rows, live[request, b], is_live)
    is_live = is_live == 1
    keys = jnp.where(is_fresh, kind(1), old[layer, :, :width].astype(F32)).astype(BF16)
    values = jnp.where(is_fresh, kind(2), old[layer, :, width:].astype(F32)).astype(BF16)
    head_of = lax.broadcasted_iota(jnp.int32, (tokens, width), 1) // HEAD
    stacked = jnp.concatenate([jnp.where(head_of == h, queries, 0.0) for h in range(heads)], axis=0)
    scores = dot_nt(stacked.astype(BF16), keys) * 0.125
    scores = jnp.where(is_live, scores, -1e30)
    top = jnp.max(scores, axis=-1, keepdims=True)
    weights = jnp.where(is_live, jnp.exp(scores - top), 0.0)
    total = jnp.sum(weights, axis=-1, keepdims=True)
    mixed = jnp.dot(weights.astype(BF16), values, preferred_element_type=F32) * (1.0 / total)
    result = jnp.zeros((tokens, width), F32)
    for h in range(heads):
        result = jnp.where(head_of == h, mixed[h * tokens : (h + 1) * tokens], result)
    packed = pack_by_parity(result, (me & 1) == 1).astype(BF16)
    for d in range(n):
        attn[d] = packed


def layer_columns(layer, blocks, own, other, mod, residual, whole, mixed):
    assemble(blocks, whole, by_heads=True)
    dot_into(layer, whole, own, other, mixed)
    gate = own_columns(mod.at[2], slice(None), lax.axis_index("blk"))
    return (residual[...].astype(F32) + gate * mixed[...].astype(F32)).astype(BF16).astype(F32)


def first_output(blocks, own, other, mod, residual, copies, kept, *scratch):
    columns = layer_columns(0, blocks, own, other, mod, residual, *scratch)
    packed = pack_by_parity(columns, (lax.axis_index("blk") & 1) == 1).astype(BF16)
    for d in range(copies.shape[0]):
        copies[d] = packed
    kept[...] = columns


def last_output(blocks, own, other, mod, residual, kept, by_token, columns, *scratch):
    columns[...] = layer_columns(1, blocks, own, other, mod, residual, *scratch)
    n = by_token.shape[0] // 2
    rows = columns.shape[0] // n
    for layer, outs in enumerate((kept, columns)):
        for b in range(n):
            by_token[layer * n + b, :rows, :] = outs[rows * b : rows * b + rows, :].astype(BF16)


def stage_rows(hidden, old_keys, old_values, staged, sems):
    copies = [
        pltpu.make_async_copy(ref, staged.at[i], sems.at[i]) for i, ref in enumerate((hidden, old_keys, old_values))
    ]
    for copy in copies:
        copy.start()
    for copy in copies:
        copy.wait()


def first_exchange(staged, other_keys, other_values, mod, other_mod, leaving, first_mod):
    _, rows, reqs, width = staged.shape
    n = leaving.shape[0]
    columns = width // n
    first = lax.axis_index("section") == 0
    first_mod[...] = own_or_other(0, mod[...], other_mod[...])
    held = [staged.at[0], staged.at[1], staged.at[2], other_keys, other_values]

    def of_request(which):
        own = [held[which][i].astype(F32) for i in range(rows)]
        return jnp.concatenate([jnp.where(first, pair[:1], pair[1:]) for pair in own], axis=0)

    mine, *arrays = [of_request(which) for which in range(5)]
    mine = mine.astype(BF16)
    own, other = arrays[:2], arrays[2:]
    stale = [jnp.where(first, a, b) for a, b in zip(own, other)] + [jnp.where(first, b, a) for a, b in zip(own, other)]
    for b in range(n):
        at = columns * group_of(b, n)
        block = jnp.concatenate([array[:, at : at + columns] for array in stale], axis=1)
        leaving[b, :rows, :] = mine
        for i in range(rows):
            leaving[b, rows : rows + 1, i * 4 * columns : (i + 1) * 4 * columns] = block[i : i + 1].astype(BF16)


def stale_by_token(arrived, mod, other_mod, old, second_mod, rows):
    n = arrived.shape[0]
    per = rows.shape[1] // n
    wide = rows.shape[2]
    for b in range(n):
        flat = arrived[b, per : per + 1, :].astype(F32)
        for i in range(per):
            for layer in range(2):
                at = (i * 2 + layer) * wide
                rows[layer, per * b + i : per * b + i + 1, :] = flat[:, at : at + wide]
    old[...] = rows[...].astype(BF16)
    second_mod[...] = own_or_other(1, mod[...], other_mod[...])


def to_rows(arrived, out, rows):
    n = arrived.shape[0] // 2
    per, columns = out.shape[0], arrived.shape[2]
    for s in range(2):
        for b in range(n):
            rows[s, :per, columns * b : columns * b + columns] = arrived[s * n + b, :per, :].astype(F32)
    for i in range(per):
        out[i] = jnp.concatenate([rows[s, i : i + 1, :] for s in range(2)], axis=0).astype(BF16)


def exchange(blocks, axis):
    return lax.all_to_all(blocks, axis, split_axis=0, concat_axis=0, tiled=True)


def swap_sections(array):
    return lax.ppermute(array, "section", [(0, 1), (1, 0)])


def by_heads(chunks, n):
    inverse = pow(3, -1, n)
    kept, middle, other = chunks
    pairs1 = [(b, (b + (inverse if b % 2 else -inverse)) % n) for b in range(n)]
    pairs2 = [(b, (b + (-2 * inverse if b % 2 else 2 * inverse)) % n) for b in range(n)]
    return kept, lax.ppermute(middle, "blk", pairs1), lax.ppermute(other, "blk", pairs2)


def per_device(hidden, qkv_weight, out_weight, modulation, timestep, fresh, live, k_stale, v_stale):
    n = lax.axis_size("blk")
    columns = out_weight.shape[2]
    reqs, rows, width = hidden.shape
    if not (
        columns == 3 * HEAD
        and n % 3 == 1
        and n & (n - 1) == 0
        and reqs == lax.axis_size("section") == 2
        and rows <= 4
    ):
        return per_device_by_token(
            hidden, qkv_weight, out_weight, modulation, timestep, fresh, live, k_stale, v_stale
        )
    tokens = n * rows
    shape = jax.ShapeDtypeStruct
    packed = shape((tokens * 3 // 2, 128), BF16)
    copies = shape((n, tokens * 3 // 2, 128), BF16)
    cols = shape((tokens, columns), BF16)
    own_qkv = jnp.swapaxes(qkv_weight[0], 0, 1)
    own_out = jnp.swapaxes(out_weight[0], 0, 1)
    steps = jnp.transpose(modulation, (1, 2, 0, 3))
    old_keys = jnp.transpose(k_stale[0], (1, 0, 2))
    old_values = jnp.transpose(v_stale[0], (1, 0, 2))

    other_keys, other_values, timestep, sent_fresh = lax.optimization_barrier(
        (swap_sections(old_keys), swap_sections(old_values), timestep, fresh)
    )
    mod = lax.dynamic_index_in_dim(steps, timestep[0], 0, keepdims=False)
    staged = call(
        stage_rows,
        shape((3, rows, reqs, width), BF16),
        [pltpu.SemaphoreType.DMA((3,))],
        (0, 200000),
        *(pinned(array) for array in (jnp.transpose(hidden, (1, 0, 2)), old_keys, old_values)),
        specs=[HBM] * 3,
    )
    other_mod, other_fresh, sent_qkv, sent_out, staged = lax.optimization_barrier(
        (swap_sections(mod), swap_sections(sent_fresh), own_qkv, own_out, staged)
    )
    mods = (mod, other_mod)
    flags = (fresh, other_fresh)
    other_qkv, other_out = swap_sections(sent_qkv), swap_sections(sent_out)
    out = (own_out, other_out)
    leaving, layer_mod = call(
        first_exchange,
        [shape((n, 4, width), BF16), shape(mod.shape, F32)],
        [],
        (0, 1000000),
        staged,
        other_keys,
        other_values,
        *mods,
    )
    arrived = exchange(leaving, "blk")

    blocks = arrived
    for layer in range(2):
        *chunks, residual = call(
            next_projection if layer else first_projection,
            [packed, packed, packed, cols],
            [
                pltpu.VMEM((tokens, width), F32),
                pltpu.VMEM((tokens, width), BF16),
                pltpu.VMEM((tokens, 3 * columns), BF16),
            ]
            + ([] if layer else [pltpu.VMEM(own_qkv.shape, BF16), pltpu.SemaphoreType.DMA((12,))]),
            (2 * tokens * width * 3 * columns, 8 * width * columns),
            blocks,
            *((own_qkv, other_qkv, layer_mod) if layer else (pinned(own_qkv), other_qkv, layer_mod, other_out)),
            **({} if layer else {"specs": [VMEM, HBM, VMEM, VMEM, ANY]}),
        )
        if layer == 0:
            arrived, chunks[1] = lax.optimization_barrier((arrived, chunks[1]))
            old, next_mod = call(
                stale_by_token,
                [shape((2, tokens, 2 * columns), BF16), shape(mod.shape, F32)],
                [pltpu.VMEM((2, tokens, 2 * columns), F32)],
                (0, 200000),
                arrived,
                *mods,
            )
        attn = call(
            functools.partial(attention, layer),
            copies,
            [],
            (8 * tokens * tokens * columns, 300000),
            *by_heads(chunks, n),
            old,
            *flags,
            live,
            specs=[VMEM] * 4 + [SMEM] * 3,
        )
        args = (exchange(attn, "blk"), *out, layer_mod, residual)
        cost = (2 * tokens * width * columns, 4 * width * columns)
        held = [pltpu.VMEM((tokens, width), BF16), pltpu.VMEM((tokens, columns), BF16)]
        if layer == 0:
            leaving, kept = call(first_output, [copies, shape((tokens, columns), F32)], held, cost, *args)
            blocks, layer_mod = exchange(leaving, "blk"), next_mod
        else:
            leaving = call(
                last_output,
                shape((2 * n, 4, columns), BF16),
                [pltpu.VMEM((tokens, columns), F32)] + held,
                cost,
                *args,
                kept,
            )
    result = call(
        to_rows,
        shape((rows, reqs, width), BF16),
        [pltpu.VMEM((2, 8, width), F32)],
        (0, 100000),
        exchange(leaving, ("section", "blk")),
    )
    return jnp.transpose(result, (1, 0, 2))[None]


def solution(mesh):
    return jax.shard_map(
        per_device,
        mesh=mesh,
        in_specs=(
            P(None, "blk", None),
            P("section", None, "blk"),
            P("section", None, "blk"),
            P("section", None, None, None),
            P(),
            P("section", None, None),
            P(),
            P("section", None, "blk", None),
            P("section", None, "blk", None),
        ),
        out_specs=P("section", None, "blk", None),
        check_vma=False,
    )
```
